32 devices in a mesh: ctx: 4 (over z), fsdp: 8 (over y, x, core).
Axes of the slice: x: 2, y: 2, z: 4, core: 2. Of those that a mesh axis runs over, the one named last changes fastest.
Arguments:
- layer_input: bfloat16 [8, 1024, 2048], P('fsdp', 'ctx'), may hold values from -6 to 6
- cotangent: bfloat16 [8, 1024, 2048], P('fsdp', 'ctx'), may hold values from -6 to 6
- positions: int32 [8, 1024], replicated, may hold values from 0 to 1023, as said below
- w_attn: bfloat16 [4, 2048, 2048], P(None, 'ctx', 'fsdp'), may hold values from -0.24527766 to 0.24527766
- w_ffn: bfloat16 [3, 2048, 4, 2048], P(None, 'ctx', None, 'fsdp'), may hold values from -0.125 to 0.125
- gains: float32 [4, 2048], replicated, may hold values from 0.5 to 1.5
- mom_attn: float32 [4, 2048, 2048], P(None, 'ctx', 'fsdp'), may hold values from -160 to 160
- mom_ffn: float32 [3, 2048, 4, 2048], P(None, 'ctx', None, 'fsdp'), may hold values from -160 to 160
- gain_mom: float32 [4, 2048], replicated, may hold values from -160 to 160
Outputs:
- layer_output: bfloat16 [8, 1024, 2048], P('fsdp', 'ctx')
- grad_input: float32 [8, 1024, 2048], P('fsdp', 'ctx')
- grad_attn: float32 [4, 2048, 2048], P(None, 'ctx', 'fsdp')
- grad_ffn: float32 [3, 2048, 4, 2048], P(None, 'ctx', None, 'fsdp')
- grad_gains: float32 [4, 2048], replicated
- new_mom_attn: float32 [4, 2048, 2048], P(None, 'ctx', 'fsdp')
- new_mom_ffn: float32 [3, 2048, 4, 2048], P(None, 'ctx', None, 'fsdp')
- new_gain_mom: float32 [4, 2048], replicated
- step_attn: float32 [4, 2048, 2048], P(None, 'ctx', 'fsdp')
- step_ffn: float32 [3, 2048, 4, 2048], P(None, 'ctx', None, 'fsdp')
- step_gains: float32 [4, 2048], replicated
The draws below stay inside these ranges and needn't reach their ends.
Inputs may be any that keep to these rules, and one draw needn't show every extreme that they name: Each position of a sequence stands in exactly one slot. The 256 slots that begin at slot c * 256 hold block j of 128 positions and then block 7 - j, in order; j differs from c to c.
All inputs are finite; a program needn't handle non-finite values.
Results may differ from the reference program's by a relative error of at most 0.03.
Values may be sent and summed in bfloat16 or wider, within the bound.
A program may use at most 320 MiB of HBM per device.

```python
import jax
import jax.numpy as jnp
from jax import lax

D = 2048
HEADS = 16
SEQ_LEN = 1024
NS_STEPS = 3
HEAD_DIM = 128
BLOCKS = 4
SEQS = 8
HALF = 128
TOKENS = 8192


def draw_positions(key, part):
    pair_count = SEQ_LEN // (2 * HALF)
    seq_keys = jax.random.split(key, SEQS)

    def shuffle(seq_key):
        return jax.random.permutation(seq_key, pair_count)
    orders = jax.vmap(shuffle)(seq_keys)
    slots = jnp.arange(SEQ_LEN, dtype=jnp.int32)
    owner = slots // (2 * HALF)
    within = slots % (2 * HALF)
    chosen = orders[:, owner]
    block_index = jnp.where(within < HALF, chosen, 2 * pair_count - 1 - chosen)
    return (block_index * HALF + within % HALF).astype(jnp.int32)


def draw_w_attn(key, part):
    first_key, second_key = jax.random.split(key)
    base = jax.random.truncated_normal(first_key, -4.0, 4.0, (4, D, D), jnp.float32)
    columns = jnp.arange(D, dtype=jnp.float32) / D
    spread = 10.0 ** jax.random.uniform(second_key, (2, 1, D), jnp.float32)
    rising = 3.0 ** (0.5 * columns)
    scales = jnp.concatenate([spread * rising * 0.16, jnp.ones((2, 1, D), jnp.float32)], axis=0)
    return (base * scales * D ** (-0.5)).astype(jnp.bfloat16)


def levels(rng, shape, cuts, smallest, largest):
    def one(axis_at, parts):
        draws = jax.random.uniform(jax.random.fold_in(jax.random.fold_in(rng, 6), axis_at), (parts,), jnp.float32, smallest / len(cuts), largest / len(cuts))
        return jnp.repeat(jnp.exp(draws), shape[axis_at] // parts).reshape((-1,) + (1,) * (len(shape) - axis_at - 1))

    factor_of = one(*cuts[0])
    for cut in cuts[1:]:
        factor_of = factor_of * one(*cut)
    return factor_of


def noise(stream_key, shape, deviation, limit, pieces=(), held_as=jnp.bfloat16):
    factor_of = levels(stream_key, shape, pieces, -0.22, 0.18) if pieces else 1.0
    drawn = jax.random.normal(stream_key, shape, jnp.float32) * deviation * factor_of
    return jnp.minimum(jnp.maximum(drawn, -limit), limit).astype(held_as)


def setup_inputs(seed: int = 0) -> dict:
    keys = jax.random.split(jax.random.key(seed), 10)
    return {
        "layer_input": noise(keys[0], (SEQS, SEQ_LEN, D), 1.0, 6.0, ((0, 8), (1, 4))),
        "cotangent": noise(keys[1], (SEQS, SEQ_LEN, D), 1.0, 6.0, ((0, 8), (1, 4))),
        "positions": draw_positions(jax.random.fold_in(keys[9], 71), 0),
        "w_attn": draw_w_attn(jax.random.fold_in(keys[9], 71), 0),
        "w_ffn": noise(keys[4], (3, D, BLOCKS, D), D ** -0.5, 0.125, ((1, 4), (3, 8))),
        "gains": jnp.clip(1.0 + 0.1 * jax.random.normal(keys[5], (4, D), jnp.float32), 0.5, 1.5),
        "mom_attn": noise(keys[6], (4, D, D), (0.3 * TOKENS ** 0.5), 160.0, ((1, 4), (2, 8)), jnp.float32),
        "mom_ffn": noise(keys[7], (3, D, BLOCKS, D), (0.3 * TOKENS ** 0.5), 160.0, ((1, 4), (3, 8)), jnp.float32),
        "gain_mom": noise(keys[8], (4, D), (0.3 * TOKENS ** 0.5), 160.0, (), jnp.float32),
    }


@jax.custom_vjp
def low(v):
    return lax.optimization_barrier(v.astype(jnp.bfloat16)).astype(jnp.float32)

@jax.custom_vjp
def low_back(v):
    return v

def low_keep(v):
    return (low(v), None)

def low_pass(kept, grad):
    return (grad,)

def back_keep(v):
    return (v, None)

def back_low(kept, grad):
    return (low(grad),)
low.defvjp(low_keep, low_pass)
low_back.defvjp(back_keep, back_low)
epsilon = 1e-06
rope_theta = 500000.0
quintic_one = 3.4445
quintic_two = -4.775
quintic_three = 2.0315
momentum = 0.95
muon_rate = 1.0
gain_rate = 0.0005

def rms_norm(operand, gain):
    return operand * lax.rsqrt(lax.optimization_barrier(jnp.mean(operand * operand, axis=-1, keepdims=True)) + epsilon) * gain

def rotary_tables(slot_order):
    half_dim = HEAD_DIM // 2
    inverse = rope_theta ** (-(jnp.arange(half_dim, dtype=jnp.float32) * 2.0) / HEAD_DIM)
    angles = slot_order.astype(jnp.float32)[..., None] * inverse
    angles = jnp.concatenate([angles, angles], axis=-1)
    return (jnp.cos(angles)[..., None, :], jnp.sin(angles)[..., None, :])

def rotate(operand, cosine_table, sine_table):
    half_dim = operand.shape[-1] // 2
    flipped = jnp.concatenate([-operand[..., half_dim:], operand[..., :half_dim]], axis=-1)
    return operand * cosine_table + flipped * sine_table

def block_forward(inputs, slot_order, w_attn, w_ffn, gains):
    highest = lax.Precision.HIGHEST
    groups, length, width = inputs.shape
    projected = jnp.einsum('gsd,jde->jgse', inputs, w_attn[:3], precision=highest)
    query_raw = low_back(projected[0])
    key_raw = low_back(projected[1])
    value_rows = low(low_back(projected[2]))
    query_norm = rms_norm(query_raw, gains[0])
    key_norm = rms_norm(key_raw, gains[1])
    cosine_table, sine_table = rotary_tables(slot_order)
    head_shape = (groups, length, HEADS, HEAD_DIM)
    query_rows = low(rotate(query_norm.reshape(head_shape), cosine_table, sine_table) * HEAD_DIM ** (-0.5))
    key_rows = low(rotate(key_norm.reshape(head_shape), cosine_table, sine_table))
    value_heads = value_rows.reshape(head_shape)
    scores = low_back(jnp.einsum('gqhe,gkhe->ghqk', query_rows, key_rows, precision=highest))
    causal = slot_order[:, None, :, None] >= slot_order[:, None, None, :]
    scores = jnp.where(causal, scores, -1e+30)
    probabilities = low(jax.nn.softmax(scores, axis=-1))
    attn_mixed = jnp.einsum('ghqk,gkhe->gqhe', probabilities, value_heads, precision=highest)
    attn_mixed = low(low_back(attn_mixed.reshape(groups, length, width)))
    attn_out = low_back(jnp.einsum('gse,de->gsd', attn_mixed, w_attn[3], precision=highest))
    hidden_in = inputs + rms_norm(attn_out, gains[2])
    mlp_input = low(hidden_in)
    gate_value = low_back(jnp.einsum('gsd,dbj->gsbj', mlp_input, w_ffn[0], precision=highest))
    up_value = low_back(jnp.einsum('gsd,dbj->gsbj', mlp_input, w_ffn[1], precision=highest))
    hidden = low(jax.nn.silu(gate_value) * up_value)
    mlp_out = low_back(jnp.einsum('gsbj,dbj->gsd', hidden, w_ffn[2], precision=highest))
    return hidden_in + rms_norm(mlp_out, gains[3])

def orthogonalize(unit_matrix):
    highest = lax.Precision.HIGHEST
    for iteration in range(NS_STEPS):
        gram_part = low(jnp.dot(unit_matrix, unit_matrix.T, precision=highest))
        product = jnp.dot(gram_part, unit_matrix, precision=highest)
        product_two = jnp.dot(gram_part, low(product), precision=highest)
        unit_matrix = low(quintic_one * unit_matrix + quintic_two * product + quintic_three * product_two)
    return unit_matrix

def reference(layer_input, cotangent, positions, w_attn, w_ffn, gains, mom_attn, mom_ffn, gain_mom):
    group_size = max(1, min(SEQS, 2048 // SEQ_LEN))
    while SEQS % group_size:
        group_size -= 1
    group_count = SEQS // group_size

    def forward_all(inputs, attn_weights, ffn_weights, gain_rows):
        batched = inputs.reshape(group_count, group_size, SEQ_LEN, D)
        orders = positions.reshape(group_count, group_size, SEQ_LEN)
        group_step = jax.checkpoint(lambda operands: block_forward(operands[0], operands[1], attn_weights, ffn_weights, gain_rows))
        return lax.map(group_step, (batched, orders)).reshape(SEQS, SEQ_LEN, D)
    primals = (layer_input.astype(jnp.float32), w_attn.astype(jnp.float32), w_ffn.astype(jnp.float32), gains)
    result, pullback = jax.vjp(forward_all, *primals)
    grad_input, grad_attn, grad_ffn, grad_gains = pullback(cotangent.astype(jnp.float32))
    new_mom_attn = momentum * mom_attn + grad_attn
    new_mom_ffn = momentum * mom_ffn + grad_ffn
    new_gain_mom = momentum * gain_mom + grad_gains
    ffn_units = jnp.transpose(new_mom_ffn, (0, 2, 1, 3)).reshape(3 * BLOCKS, D, D)
    all_units = jnp.concatenate([new_mom_attn, ffn_units], axis=0)
    unit_norms = jnp.sqrt(lax.optimization_barrier(jnp.sum(all_units * all_units, axis=(1, 2))))
    unit_start = low(all_units / (unit_norms + 1e-07)[:, None, None])
    orthogonal = lax.map(orthogonalize, unit_start)
    unit_steps = -muon_rate * orthogonal
    step_attn = unit_steps[:4]
    step_ffn = jnp.transpose(unit_steps[4:].reshape(3, BLOCKS, D, D), (0, 2, 1, 3))
    step_gains = -gain_rate * new_gain_mom
    return (result.astype(jnp.bfloat16), grad_input, grad_attn, grad_ffn, grad_gains, new_mom_attn, new_mom_ffn, new_gain_mom, step_attn, step_ffn, step_gains)
```

```python
import functools
import jax
import jax.numpy as jnp
from jax import lax
from jax.sharding import PartitionSpec as P

NS_STEPS = 3
HEAD_DIM = 128
UNITS_ATTN = 4

epsilon = 1e-06
rope_theta = 500000.0
quintic_one = 3.4445
quintic_two = -4.775
quintic_three = 2.0315
momentum = 0.95
muon_rate = 1.0
gain_rate = 0.0005
BOTH = ("ctx", "fsdp")
bf16 = jnp.bfloat16
f32 = jnp.float32


def dot(a, b, ca, cb):
    return lax.dot_general(a, b, (((ca,), (cb,)), ((), ())), preferred_element_type=f32)


def token_rows(operand):
    return lax.all_gather(operand, "fsdp", axis=0, tiled=True)


def token_sums(operand):
    return lax.psum_scatter(operand.astype(bf16), "fsdp", scatter_dimension=0, tiled=True).astype(f32)


def norm_stats(first_sum, second_sum):
    got = lax.all_gather(jnp.stack([first_sum, second_sum]), "fsdp", axis=0, tiled=False)
    total = jnp.sum(got, axis=0)
    return total[0], total[1]


def rms_back(upstream, normed, inv_scale):
    return inv_scale * (upstream - normed * jnp.mean(upstream * normed, axis=-1, keepdims=True))


def rotary_tables(slot_order):
    half_dim = HEAD_DIM // 2
    inverse = rope_theta ** (-(jnp.arange(half_dim, dtype=f32) * 2.0) / HEAD_DIM)
    angles = slot_order.astype(f32)[..., None] * inverse
    angles = jnp.concatenate([angles, angles], axis=-1)
    return (jnp.cos(angles)[..., None, :], jnp.sin(angles)[..., None, :])


def rotate(operand, cosine_table, sine_table):
    half_dim = operand.shape[-1] // 2
    flipped = jnp.concatenate([-operand[..., half_dim:], operand[..., :half_dim]], axis=-1)
    return operand * cosine_table + flipped * sine_table


def unrotate(upstream, cosine_table, sine_table):
    half_dim = upstream.shape[-1] // 2
    shifted = upstream * sine_table
    flipped = jnp.concatenate([shifted[..., half_dim:], -shifted[..., :half_dim]], axis=-1)
    return upstream * cosine_table + flipped


def masked_scores(query_rows, key_rows, pos):
    scores = jnp.einsum("gqhe,gkhe->ghqk", query_rows, key_rows, preferred_element_type=f32)
    causal = pos[:, None, :, None] >= pos[:, None, None, :]
    return jnp.where(causal, scores, -1e30)


def attend(query_rows, key_rows, value_rows, pos):
    scores = masked_scores(query_rows, key_rows, pos)
    row_max = jnp.max(scores, axis=-1, keepdims=True)
    weights = jnp.exp(scores - row_max)
    row_total = jnp.sum(weights, axis=-1, keepdims=True)
    probabilities = (weights / row_total).astype(bf16)
    attn_mixed = jnp.einsum("ghqk,gkhe->gqhe", probabilities, value_rows, preferred_element_type=f32)
    return attn_mixed.astype(bf16), row_max + jnp.log(row_total)


def attend_back(query_rows, key_rows, value_rows, pos, grad_mixed, log_total):
    scores = masked_scores(query_rows, key_rows, pos)
    probabilities = jnp.exp(scores - log_total)
    grad_probs = jnp.einsum("gqhe,gkhe->ghqk", grad_mixed, value_rows, preferred_element_type=f32)
    grad_value = jnp.einsum(
        "ghqk,gqhe->gkhe", probabilities.astype(bf16), grad_mixed, preferred_element_type=f32
    )
    inner_sum = jnp.sum(grad_probs * probabilities, axis=-1, keepdims=True)
    grad_scores = (probabilities * (grad_probs - inner_sum)).astype(bf16)
    grad_query = jnp.einsum("ghqk,gkhe->gqhe", grad_scores, key_rows, preferred_element_type=f32)
    grad_key = jnp.einsum("ghqk,gqhe->gkhe", grad_scores, query_rows, preferred_element_type=f32)
    return grad_query, grad_key, grad_value


def shards(C, F, layer_input, cotangent, positions, w_attn, w_ffn, gains, mom_attn, mom_ffn, gain_mom):
    z = lax.axis_index("ctx")
    f = lax.axis_index("fsdp")
    local_rows, width = layer_input.shape[1], layer_input.shape[2]
    seq_total, seq_length = positions.shape
    dz, head_cols = w_attn.shape[1], w_attn.shape[2]
    local_heads = head_cols // HEAD_DIM
    block_count = w_ffn.shape[2]
    per = seq_total // C
    hidden_cols = block_count * head_cols
    units = UNITS_ATTN + 3 * block_count
    parts = C * F // units
    ring = [(i, (i + 1) % C) for i in range(C)]
    out_pairs = [
        (zi * F + fi, (fi // per) * F + (fi % per) * C + zi) for zi in range(C) for fi in range(F)
    ]
    back_pairs = [(b, a) for a, b in out_pairs]

    def cyc(a):
        blocks = [
            lax.dynamic_slice_in_dim(a, lax.rem(z - k + C, C) * dz, dz, a.ndim - 1) for k in range(C)
        ]
        return jnp.concatenate(blocks, axis=-1)

    def to_layer(a):
        return cyc(lax.ppermute(a, BOTH, out_pairs))

    def from_layer(a):
        return lax.ppermute(cyc(a), BOTH, back_pairs)

    def ring_gather(shard):
        held = [shard]
        for _ in range(C - 1):
            held.append(lax.ppermute(held[-1], "ctx", ring))
        return jnp.concatenate(held, axis=0), held[-1]

    def after(a, b):
        return lax.optimization_barrier((a, b))[0]

    def ring_scatter(lhs, rhs):
        def part(k):
            return dot(lhs[:, k * dz : (k + 1) * dz], rhs, 0, 0)

        run = part(1).astype(bf16)
        for k in range(2, C + 1):
            got = lax.ppermute(run, "ctx", ring)
            total = got.astype(f32) + part(k % C)
            run = total.astype(bf16)
        return total

    own_input = to_layer(layer_input.reshape(local_rows, width))
    input_all = token_rows(own_input)
    wq = jnp.concatenate([w_attn[0], w_attn[1], w_attn[2]], axis=1)
    w_qkv, last = ring_gather(wq)
    w_out, last = ring_gather(after(w_attn[3], last))
    ffn_flat = w_ffn.reshape(3, dz, hidden_cols)
    w_gate, last = ring_gather(after(ffn_flat[0], last))
    w_up, last = ring_gather(after(ffn_flat[1], last))
    w_down, last = ring_gather(after(ffn_flat[2], last))
    own_grad = to_layer(after(cotangent.reshape(local_rows, width), last))

    gain_rows = cyc(gains[2:4])
    gain_attn, gain_mlp = gain_rows[0], gain_rows[1]
    gain_query = lax.dynamic_slice_in_dim(gains[0], f * head_cols, head_cols)
    gain_key = lax.dynamic_slice_in_dim(gains[1], f * head_cols, head_cols)
    pos = lax.dynamic_slice_in_dim(positions, z * per, per, 0)
    cosine_table, sine_table = rotary_tables(pos)

    projected = dot(input_all, w_qkv, 1, 0)
    query_raw = projected[:, :head_cols]
    key_raw = projected[:, head_cols : 2 * head_cols]
    value_raw = projected[:, 2 * head_cols :]
    query_total, key_total = norm_stats(
        jnp.sum(query_raw * query_raw, axis=-1), jnp.sum(key_raw * key_raw, axis=-1)
    )
    query_scale = lax.rsqrt(query_total / width + epsilon)[..., None]
    key_scale = lax.rsqrt(key_total / width + epsilon)[..., None]
    query_hat = query_raw * query_scale
    key_hat = key_raw * key_scale
    head_shape = (per, seq_length, local_heads, HEAD_DIM)
    query_rows = (
        rotate((query_hat * gain_query).reshape(head_shape), cosine_table, sine_table)
        * HEAD_DIM ** (-0.5)
    ).astype(bf16)
    key_rows = rotate((key_hat * gain_key).reshape(head_shape), cosine_table, sine_table).astype(bf16)
    value_rows = value_raw.astype(bf16).reshape(head_shape)
    attn_mixed, log_total = attend(query_rows, key_rows, value_rows, pos)
    attn_mixed = attn_mixed.reshape(per * seq_length, head_cols)
    attn_out = token_sums(dot(attn_mixed, w_out, 1, 1))
    attn_scale = lax.rsqrt(jnp.mean(attn_out * attn_out, axis=-1, keepdims=True) + epsilon)
    attn_hat = attn_out * attn_scale
    hidden_in = own_input.astype(f32) + attn_hat * gain_attn
    mlp_all = token_rows(hidden_in.astype(bf16))
    gate_value = dot(mlp_all, w_gate, 1, 0)
    up_value = dot(mlp_all, w_up, 1, 0)
    gate_sigmoid = jax.nn.sigmoid(gate_value)
    gate_act = gate_value * gate_sigmoid
    hidden = (gate_act * up_value).astype(bf16)
    mlp_out = token_sums(dot(hidden, w_down, 1, 1))
    mlp_scale = lax.rsqrt(jnp.mean(mlp_out * mlp_out, axis=-1, keepdims=True) + epsilon)
    mlp_hat = mlp_out * mlp_scale
    result = from_layer((hidden_in + mlp_hat * gain_mlp).astype(bf16))

    grad_out = own_grad.astype(f32)
    grad_mlp_gain = jnp.sum(grad_out * mlp_hat, axis=0)
    grad_mlp = rms_back(grad_out * gain_mlp, mlp_hat, mlp_scale).astype(bf16)
    grad_mlp_all = token_rows(grad_mlp)
    grad_hidden = dot(grad_mlp_all, w_down, 1, 0)
    grad_up = (grad_hidden * gate_act).astype(bf16)
    grad_gate = (
        grad_hidden * up_value * gate_sigmoid * (1.0 + gate_value * (1.0 - gate_sigmoid))
    ).astype(bf16)
    back_part = dot(grad_gate, w_gate, 1, 1) + dot(grad_up, w_up, 1, 1)
    g_down = ring_scatter(grad_mlp_all, hidden)
    g_gate = ring_scatter(mlp_all, grad_gate)
    g_up = ring_scatter(mlp_all, grad_up)
    grad_resid = grad_out + token_sums(back_part)
    grad_attn_gain = jnp.sum(grad_resid * attn_hat, axis=0)
    grad_attn_out = rms_back(grad_resid * gain_attn, attn_hat, attn_scale).astype(bf16)
    grad_attn_all = token_rows(grad_attn_out)
    grad_mixed = dot(grad_attn_all, w_out, 1, 0).astype(bf16)
    g_out = ring_scatter(grad_attn_all, attn_mixed)
    grad_query, grad_key, grad_value = attend_back(
        query_rows, key_rows, value_rows, pos, grad_mixed.reshape(head_shape), log_total
    )
    flat = (per * seq_length, head_cols)
    grad_query_norm = unrotate(grad_query * HEAD_DIM ** (-0.5), cosine_table, sine_table).reshape(flat)
    grad_key_norm = unrotate(grad_key, cosine_table, sine_table).reshape(flat)
    query_gain_cols = jnp.sum(grad_query_norm * query_hat, axis=0)
    key_gain_cols = jnp.sum(grad_key_norm * key_hat, axis=0)
    query_weighted = grad_query_norm * gain_query
    key_weighted = grad_key_norm * gain_key
    query_inner, key_inner = norm_stats(
        jnp.sum(query_weighted * query_hat, axis=-1), jnp.sum(key_weighted * key_hat, axis=-1)
    )
    grad_query_raw = query_scale * (query_weighted - query_hat * (query_inner / width)[..., None])
    grad_key_raw = key_scale * (key_weighted - key_hat * (key_inner / width)[..., None])
    grad_projected = jnp.concatenate(
        [grad_query_raw.astype(bf16), grad_key_raw.astype(bf16), grad_value.reshape(flat).astype(bf16)],
        axis=1,
    )
    g_qkv = ring_scatter(input_all, grad_projected)
    grad_input = grad_resid + token_sums(dot(grad_projected, w_qkv, 1, 1))
    grad_input = from_layer(grad_input.astype(bf16)).astype(f32)

    zero = jnp.zeros((width,), f32)
    natural = cyc(jnp.stack([grad_attn_gain, grad_mlp_gain]))
    gain_local = jnp.stack(
        [
            lax.dynamic_update_slice(zero, query_gain_cols, (f * head_cols,)),
            lax.dynamic_update_slice(zero, key_gain_cols, (f * head_cols,)),
            natural[0],
            natural[1],
        ]
    )
    gain_total = jnp.sum(lax.all_gather(gain_local, BOTH, axis=0, tiled=False), axis=0)

    grad_attn = jnp.stack(
        [g_qkv[:, :head_cols], g_qkv[:, head_cols : 2 * head_cols], g_qkv[:, 2 * head_cols :], g_out]
    )
    grad_ffn = jnp.stack([g_gate, g_up, g_down]).reshape(3, dz, block_count, head_cols)
    new_attn = momentum * mom_attn + grad_attn
    new_ffn = momentum * mom_ffn + grad_ffn
    send = jnp.concatenate(
        [
            new_attn.astype(bf16),
            jnp.transpose(new_ffn.astype(bf16), (0, 2, 1, 3)).reshape(3 * block_count, dz, head_cols),
        ],
        axis=0,
    ).reshape(C * F, dz // parts, head_cols)
    got = lax.all_to_all(send, BOTH, split_axis=0, concat_axis=0, tiled=True)
    own = jnp.transpose(got.reshape(C, F, dz // parts, head_cols), (0, 2, 1, 3)).reshape(
        C * dz // parts, F * head_cols
    )

    def peers(a):
        out = [a]
        for s in range(1, parts):
            pairs = [(i, i - i % parts + (i + parts - s) % parts) for i in range(C * F)]
            out.append(lax.ppermute(a, BOTH, pairs))
        return out

    own32 = own.astype(f32)
    square = jnp.sum(own32 * own32)
    total = sum(peers(square.reshape(1, 1)))
    inv = 1.0 / (jnp.sqrt(total) + 1e-07)
    for iteration in range(NS_STEPS):
        factor = inv if iteration == 0 else 1.0
        every = peers(own)
        gram = [(dot(own, b, 1, 1) * (factor * factor)).astype(bf16) for b in every]
        product = sum(dot(g, b, 1, 0) for g, b in zip(gram, every)) * factor
        product_all = peers(product.astype(bf16))
        product_two = sum(dot(g, b, 1, 0) for g, b in zip(gram, product_all))
        own = (
            quintic_one * factor * own.astype(f32) + quintic_two * product + quintic_three * product_two
        ).astype(bf16)
    home = jnp.transpose(own.reshape(C, dz // parts, F, head_cols), (0, 2, 1, 3)).reshape(
        C * F, dz // parts, head_cols
    )
    steps = lax.all_to_all(home, BOTH, split_axis=0, concat_axis=0, tiled=True)
    steps = -muon_rate * steps.astype(f32).reshape(units, dz, head_cols)
    step_attn = steps[:UNITS_ATTN]
    step_ffn = jnp.transpose(
        steps[UNITS_ATTN:].reshape(3, block_count, dz, head_cols), (0, 2, 1, 3)
    )
    new_gain_mom = momentum * gain_mom + gain_total
    return (
        result.reshape(layer_input.shape),
        grad_input.reshape(layer_input.shape),
        grad_attn,
        grad_ffn,
        gain_total,
        new_attn,
        new_ffn,
        new_gain_mom,
        step_attn,
        step_ffn,
        -gain_rate * new_gain_mom,
    )


def solution(mesh):
    tokens = P("fsdp", "ctx", None)
    attn = P(None, "ctx", "fsdp")
    ffn = P(None, "ctx", None, "fsdp")
    in_specs = (tokens, tokens, P(), attn, ffn, P(), attn, ffn, P())
    out_specs = (tokens, tokens, attn, ffn, P(), attn, ffn, P(), attn, ffn, P())
    body = functools.partial(shards, mesh.shape["ctx"], mesh.shape["fsdp"])
    return jax.shard_map(body, mesh=mesh, in_specs=in_specs, out_specs=out_specs, check_vma=False)
```

```python
import functools
import jax
import jax.numpy as jnp
from jax import lax
from jax.experimental import pallas as pl
from jax.experimental.pallas import tpu as pltpu
from jax.sharding import PartitionSpec as P

NS_STEPS = 3
HEAD_DIM = 128
UNITS_ATTN = 4

epsilon = 1e-06
rope_theta = 500000.0
quintic_one = 3.4445
quintic_two = -4.775
quintic_three = 2.0315
momentum = 0.95
muon_rate = 1.0
gain_rate = 0.0005
BOTH = ("ctx", "fsdp")
bf16 = jnp.bfloat16
f32 = jnp.float32


def dot(a, b, ca, cb):
    return lax.dot_general(a, b, (((ca,), (cb,)), ((), ())), preferred_element_type=f32)


def token_rows(operand):
    return lax.all_gather(operand, "fsdp", axis=0, tiled=True)


def token_sums(operand):
    return lax.psum_scatter(operand.astype(bf16), "fsdp", scatter_dimension=0, tiled=True).astype(f32)


def norm_stats(first_sum, second_sum):
    got = lax.all_gather(jnp.stack([first_sum, second_sum]), "fsdp", axis=0, tiled=False)
    total = jnp.sum(got, axis=0)
    return total[0], total[1]


def rms_back(upstream, normed, inv_scale):
    return inv_scale * (upstream - normed * jnp.mean(upstream * normed, axis=-1, keepdims=True))


def rotary_tables(slot_order):
    half_dim = HEAD_DIM // 2
    inverse = rope_theta ** (-(jnp.arange(half_dim, dtype=f32) * 2.0) / HEAD_DIM)
    angles = slot_order.astype(f32)[..., None] * inverse
    angles = jnp.concatenate([angles, angles], axis=-1)
    return (jnp.cos(angles)[..., None, :], jnp.sin(angles)[..., None, :])


def rotate(operand, cosine_table, sine_table):
    half_dim = operand.shape[-1] // 2
    flipped = jnp.concatenate([-operand[..., half_dim:], operand[..., :half_dim]], axis=-1)
    return operand * cosine_table + flipped * sine_table


def unrotate(upstream, cosine_table, sine_table):
    half_dim = upstream.shape[-1] // 2
    shifted = upstream * sine_table
    flipped = jnp.concatenate([shifted[..., half_dim:], -shifted[..., :half_dim]], axis=-1)
    return upstream * cosine_table + flipped


def masked_scores(query_rows, key_rows, pos):
    scores = jnp.einsum("gqhe,gkhe->ghqk", query_rows, key_rows, preferred_element_type=f32)
    causal = pos[:, None, :, None] >= pos[:, None, None, :]
    return jnp.where(causal, scores, -1e30)


def attend(query_rows, key_rows, value_rows, pos):
    scores = masked_scores(query_rows, key_rows, pos)
    row_max = jnp.max(scores, axis=-1, keepdims=True)
    weights = jnp.exp(scores - row_max)
    row_total = jnp.sum(weights, axis=-1, keepdims=True)
    probabilities = (weights / row_total).astype(bf16)
    attn_mixed = jnp.einsum("ghqk,gkhe->gqhe", probabilities, value_rows, preferred_element_type=f32)
    return attn_mixed.astype(bf16), row_max + jnp.log(row_total)


def attend_back(query_rows, key_rows, value_rows, pos, grad_mixed, log_total):
    scores = masked_scores(query_rows, key_rows, pos)
    probabilities = jnp.exp(scores - log_total)
    grad_probs = jnp.einsum("gqhe,gkhe->ghqk", grad_mixed, value_rows, preferred_element_type=f32)
    grad_value = jnp.einsum(
        "ghqk,gqhe->gkhe", probabilities.astype(bf16), grad_mixed, preferred_element_type=f32
    )
    inner_sum = jnp.sum(grad_probs * probabilities, axis=-1, keepdims=True)
    grad_scores = (probabilities * (grad_probs - inner_sum)).astype(bf16)
    grad_query = jnp.einsum("ghqk,gkhe->gqhe", grad_scores, key_rows, preferred_element_type=f32)
    grad_key = jnp.einsum("ghqk,gqhe->gkhe", grad_scores, query_rows, preferred_element_type=f32)
    return grad_query, grad_key, grad_value


MESH = pl.DeviceIdType.MESH
VMEM_LIMIT = 60 * 1024 * 1024
ANY = pl.BlockSpec(memory_space=pl.ANY)


class Plane:
    def __init__(self):
        f = lax.axis_index("fsdp")
        self.f, self.c, self.chip = f, f % 2, f // 2
        x, y = self.chip % 2, self.chip // 2
        self.qx = self.chip + 1 - 2 * x
        self.qy = self.chip + 2 - 4 * y
        self.qd = self.qx + 2 - 4 * y
        self.fc = f + 1 - 2 * self.c
        self.fx = 2 * self.qx + self.c
        self.fy = 2 * self.qy + self.c
        self.fd = 2 * self.qd + self.c
        self.other = 1 - self.c

    def greet(self):
        barrier = pltpu.get_barrier_semaphore()
        for to in (self.fc, self.fx, self.fy):
            pl.semaphore_signal(barrier, inc=1, device_id={"fsdp": to}, device_id_type=MESH)
        pl.semaphore_wait(barrier, 3)


def remote(src, dst, send, recv, i, to, axis="fsdp"):
    return pltpu.make_async_remote_copy(
        src_ref=src, dst_ref=dst, send_sem=send.at[i], recv_sem=recv.at[i],
        device_id={axis: to}, device_id_type=MESH,
    )


def local(src, dst, sems, i):
    copy = pltpu.make_async_copy(src, dst, sems.at[i])
    copy.start()
    return copy


def nn(a, b):
    return lax.dot_general(a, b, (((1,), (0,)), ((), ())), preferred_element_type=f32)


def nt(a, b):
    return lax.dot_general(a, b, (((1,), (1,)), ((), ())), preferred_element_type=f32)


def gather_phase(at, rows, send, recv, base, on_rows):
    half = rows.shape[1] // 2
    A, B = pl.ds(0, half), pl.ds(half, half)

    def cp(i, slot, part, to):
        ref = rows.at[slot] if part is None else rows.at[slot, part]
        return remote(ref, ref, send, recv, base + i, to)

    fcx, fcy, fcd = 2 * at.qx + at.other, 2 * at.qy + at.other, 2 * at.qd + at.other
    sent = []

    def go(*a):
        c = cp(*a)
        c.start()
        sent.append(c)

    def arrived(i, slot, part, frm):
        cp(i, slot, part, frm).wait_recv()

    go(0, at.f, None, at.fc)
    go(1, at.f, A, at.fx)
    go(3, at.f, B, at.fy)
    go(2, at.f, B, at.fx)
    go(4, at.f, A, at.fy)
    arrived(0, at.fc, None, at.fc)
    on_rows(2 * at.chip, 2)
    arrived(1, at.fx, A, at.fx)
    go(5, at.fx, A, at.fy)
    go(7, at.fx, A, at.fc)
    arrived(3, at.fy, B, at.fy)
    go(6, at.fy, B, at.fx)
    go(8, at.fy, B, at.fc)
    arrived(2, at.fx, B, at.fx)
    go(9, at.fx, B, at.fc)
    arrived(4, at.fy, A, at.fy)
    go(10, at.fy, A, at.fc)
    arrived(7, fcx, A, at.fc)
    arrived(9, fcx, B, at.fc)
    on_rows(2 * at.qx, 2)
    arrived(8, fcy, B, at.fc)
    arrived(10, fcy, A, at.fc)
    on_rows(2 * at.qy, 2)
    arrived(5, at.fd, A, at.fy)
    go(11, at.fd, A, at.fc)
    arrived(6, at.fd, B, at.fx)
    go(12, at.fd, B, at.fc)
    on_rows(at.fd, 1)
    arrived(11, fcd, A, at.fc)
    arrived(12, fcd, B, at.fc)
    on_rows(fcd, 1)
    for c in sent:
        c.wait_send()


GATHER_COPIES = 13
SCATTER_COPIES = 10


def scatter_scratch(R, D):
    return [
        pltpu.VMEM((4, R, D), bf16),
        pltpu.VMEM((4, R, D), bf16),
        pltpu.VMEM((2, R, D), f32),
        pltpu.VMEM((3, R, D), bf16),
        pltpu.VMEM((3, R, D), bf16),
    ]


def scatter_phase(at, partial, bufs, send, recv, base):
    to_core, from_core, mine, out, inc = bufs
    R, D = to_core.shape[1], to_core.shape[2]
    half = R // 2
    A, B = pl.ds(0, half), pl.ds(half, half)
    tile = 512
    step = 16
    sent = []

    def go(i, src, dst, to):
        c = remote(src, dst, send, recv, base + i, to)
        c.start()
        sent.append(c)

    def arrived(i, dst, frm):
        remote(dst, dst, send, recv, base + i, frm).wait_recv()

    def compute(order, chip, slot):
        @pl.loop(0, D // tile)
        def _(n):
            cols = pl.ds(pl.multiple_of(n * tile, tile), tile)
            got = partial(chip, cols)
            lo, hi = got[:R], got[R:]
            first = at.c == 0
            mine[slot, :, cols] = jnp.where(first, lo, hi)
            to_core[order, :, cols] = jnp.where(first, hi, lo).astype(bf16)

        go(order, to_core.at[order], from_core.at[order], at.fc)

    def chip_sum(order, slot):
        arrived(order, from_core.at[order], at.fc)

        @pl.loop(0, R // step)
        def _(r):
            rows = pl.ds(pl.multiple_of(r * step, step), step)
            out[order, rows, :] = (mine[slot, rows, :] + from_core[order, rows, :].astype(f32)).astype(bf16)

    def relay(order, start, src):
        @pl.loop(0, half // step)
        def _(r):
            rows = pl.ds(pl.multiple_of(start + r * step, step), step)
            out[order, rows, :] = (out[order, rows, :].astype(f32) + inc[src, rows, :].astype(f32)).astype(bf16)

    compute(0, at.qd, 0)
    compute(1, at.qx, 1)
    chip_sum(0, 0)
    go(4, out.at[0, A], inc.at[0, A], at.fx)
    go(5, out.at[0, B], inc.at[0, B], at.fy)
    compute(2, at.qy, 0)
    chip_sum(1, 1)
    go(6, out.at[1, A], inc.at[1, A], at.fx)
    compute(3, at.chip, 1)
    chip_sum(2, 0)
    go(8, out.at[2, B], inc.at[2, B], at.fy)
    arrived(5, inc.at[0, B], at.fy)
    relay(1, half, 0)
    go(7, out.at[1, B], inc.at[1, B], at.fx)
    arrived(4, inc.at[0, A], at.fx)
    relay(2, 0, 0)
    go(9, out.at[2, A], inc.at[2, A], at.fy)
    arrived(3, from_core.at[3], at.fc)
    arrived(6, inc.at[1, A], at.fx)
    arrived(8, inc.at[2, B], at.fy)
    arrived(7, inc.at[1, B], at.fx)
    arrived(9, inc.at[2, A], at.fy)
    for c in sent:
        c.wait_send()

    def total(rows):
        return (
            mine[1, rows, :]
            + from_core[3, rows, :].astype(f32)
            + inc[1, rows, :].astype(f32)
            + inc[2, rows, :].astype(f32)
        )

    return total


def rms(v):
    return lax.rsqrt(jnp.mean(v * v, axis=-1, keepdims=True) + epsilon)


def back(weighted, normed, scale):
    return scale * (weighted - normed * jnp.mean(weighted * normed, axis=-1, keepdims=True))


def row_loop(R, body, step=16):
    @pl.loop(0, R // step)
    def _(r):
        body(pl.ds(pl.multiple_of(r * step, step), step))


def pair_loop(rows, w_cols, total_cols, body):
    @pl.loop(0, total_cols // w_cols)
    def _(t):
        body(pl.ds(pl.multiple_of(t * w_cols, w_cols), w_cols))


class Stores:
    def __init__(self, sems):
        self.sems, self.steps, self.n = sems, [], 0

    def slot(self):
        if len(self.steps) >= 2:
            for c in self.steps[-2]:
                c.wait()
            self.steps[-2] = []
        return len(self.steps) % 2

    def put(self, pairs):
        done = []
        for src, dst in pairs:
            done.append(local(src, dst, self.sems, self.n))
            self.n += 1
        self.steps.append(done)

    def finish(self):
        for step in self.steps:
            for c in step:
                c.wait()


def enter_kernel(C, x_ref, g_ref, own_ref, gown_ref, all_ref, stage, mine, rows, gown, lsem, osem, send, recv, tsend, trecv):
    at = Plane()
    z = lax.axis_index("ctx")
    F, R = rows.shape[0], rows.shape[1]
    piece = R // C
    barrier = pltpu.get_barrier_semaphore()
    for k in range(1, C):
        pl.semaphore_signal(barrier, inc=1, device_id={"ctx": (z + k) % C}, device_id_type=MESH)
        pl.semaphore_signal(
            barrier, inc=1, device_id={"fsdp": 2 * ((at.chip + k) % C) + at.c}, device_id_type=MESH
        )
    pl.semaphore_signal(barrier, inc=1, device_id={"fsdp": at.fc}, device_id_type=MESH)
    loads = [local(x_ref, mine.at[0], lsem, 0), local(g_ref, mine.at[1], lsem, 1)]
    pl.semaphore_wait(barrier, 2 * (C - 1) + 1)
    sent = []
    keep = []
    for a in range(2):
        loads[a].wait()
        for k in range(1, C):
            j = (at.chip + k) % C
            c = remote(
                mine.at[a, pl.ds(j * piece, piece)], stage.at[a, at.chip], tsend, trecv, 2 * C * a + k, 2 * j + at.c
            )
            c.start()
            sent.append(c)
        keep.append(local(mine.at[a, pl.ds(at.chip * piece, piece)], stage.at[a, at.chip], lsem, 2 + a))

    def landing(a, layer):
        r = pl.ds(layer * piece, piece)
        return rows.at[at.f, r] if a == 0 else gown.at[r]

    for a in range(2):
        keep[a].wait()
        for k in range(1, C):
            frm = (at.chip - k + C) % C
            remote(stage.at[a, frm], stage.at[a, frm], tsend, trecv, 2 * C * a + k, 2 * frm + at.c).wait_recv()
        for k in range(1, C):
            to = (z + k) % C
            c = remote(stage.at[a, to], landing(a, z), tsend, trecv, 2 * C * a + C + k, to, "ctx")
            c.start()
            sent.append(c)
        keep[a] = local(stage.at[a, z], landing(a, z), lsem, 4 + a)

    def arrive(a):
        keep[a].wait()
        for k in range(1, C):
            frm = (z - k + C) % C
            remote(landing(a, frm), landing(a, frm), tsend, trecv, 2 * C * a + C + k, frm, "ctx").wait_recv()

    arrive(0)
    save = local(rows.at[at.f], own_ref, lsem, 6)
    stores = []

    def on_rows(first, count):
        stores.append(local(rows.at[pl.ds(first, count)], all_ref.at[pl.ds(first, count)], osem, len(stores)))

    gather_phase(at, rows, send, recv, 0, on_rows)
    arrive(1)
    local(gown, gown_ref, lsem, 7).wait()
    for c in sent:
        c.wait_send()
    save.wait()
    for c in stores:
        c.wait()


def enter_call(C, F, x, g):
    R, D = x.shape
    one = jax.ShapeDtypeStruct((R, D), bf16)
    return pl.pallas_call(
        functools.partial(enter_kernel, C),
        out_shape=[one, one, jax.ShapeDtypeStruct((F, R, D), bf16)],
        in_specs=[ANY] * 2,
        out_specs=[ANY] * 3,
        scratch_shapes=[
            pltpu.VMEM((2, C, R // C, D), bf16),
            pltpu.VMEM((2, R, D), bf16),
            pltpu.VMEM((F, R, D), bf16),
            pltpu.VMEM((R, D), bf16),
            dma(8), dma(5), dma(GATHER_COPIES), dma(GATHER_COPIES), dma(4 * C), dma(4 * C),
        ],
        compiler_params=params(1),
        cost_estimate=cost(75),
    )(x, g)


def qkv_kernel(all_ref, w_ref, proj_ref, st_ref, rows, w, acc, st, lsem, osem, ssend, srecv):
    at = Plane()
    F, R = rows.shape[0], rows.shape[1]
    e = w.shape[1] // 3
    m = 2 * R
    loads = [local(w_ref, w, lsem, 0)] + [
        local(all_ref.at[pl.ds(2 * p, 2)], rows.at[pl.ds(2 * p, 2)], lsem, 1 + p) for p in range(F // 2)
    ]
    barrier = pltpu.get_barrier_semaphore()
    for k in range(1, F):
        pl.semaphore_signal(barrier, inc=1, device_id={"fsdp": (at.f + k) % F}, device_id_type=MESH)
    pl.semaphore_wait(barrier, F - 1)
    loads[0].wait()
    stores = Stores(osem)
    for p in range(F // 2):
        loads[1 + p].wait()
        s = stores.slot()

        def tile(c):
            acc[s, :, c] = nn(rows[pl.ds(2 * p, 2)].reshape(m, rows.shape[2]), w[:, c])

        pair_loop(m, 256, w.shape[1], tile)
        q, k = acc[s, :, :e], acc[s, :, e : 2 * e]
        st[at.f, :, pl.ds(p * m, m)] = row_sums(q * q, k * k)
        stores.put([(acc.at[s], proj_ref.at[pl.ds(p * m, m)])])
    share_stats(at, F, st, ssend, srecv, 0)
    local(st, st_ref, lsem, 1 + F // 2).wait()
    stores.finish()


def params(number):
    return pltpu.CompilerParams(
        collective_id=number, has_side_effects=True, vmem_limit_bytes=VMEM_LIMIT
    )


def cost(us):
    return pl.CostEstimate(flops=int(us * 1e9), bytes_accessed=2**20, transcendentals=0)


def dma(n):
    return pltpu.SemaphoreType.DMA((n,))


def qkv_call(F, rows, w):
    _, R, D = rows.shape
    n = w.shape[1]
    return pl.pallas_call(
        qkv_kernel,
        out_shape=[
            jax.ShapeDtypeStruct((F * R, n), f32),
            jax.ShapeDtypeStruct((F, 8, F * R), f32),
        ],
        in_specs=[ANY] * 2,
        out_specs=[ANY] * 2,
        scratch_shapes=[
            pltpu.VMEM((F, R, D), bf16),
            pltpu.VMEM((D, n), bf16),
            pltpu.VMEM((2, 2 * R, n), f32),
            pltpu.VMEM((F, 8, F * R), f32),
            dma(6), dma(4), dma(F), dma(F),
        ],
        compiler_params=params(7),
        cost_estimate=cost(22),
    )(rows, w)


def out_kernel(
    mixed_ref, wo_ref, x_ref, gain_ref, hid_ref, ao_ref, in_ref,
    mixed, wo, x, gain, hid, ao, inp, b0, b1, b2, b3, b4, lsem, send, recv,
):
    at = Plane()
    pairs = [(mixed_ref, mixed), (wo_ref, wo), (x_ref, x), (gain_ref, gain)]
    loads = [local(s, d, lsem, i) for i, (s, d) in enumerate(pairs)]
    at.greet()
    R = x.shape[0]
    loads[0].wait()
    loads[1].wait()

    def partial(chip, cols):
        return nt(mixed[pl.ds(pl.multiple_of(chip * 2 * R, 2 * R), 2 * R), :], wo[cols, :])

    total = scatter_phase(at, partial, (b0, b1, b2, b3, b4), send, recv, 0)
    loads[2].wait()
    loads[3].wait()

    def finish(r):
        out = total(r)
        ao[r, :] = out
        hidden_in = x[r, :].astype(f32) + out * rms(out) * gain[...]
        hid[r, :] = hidden_in
        inp[r, :] = hidden_in.astype(bf16)

    row_loop(R, finish)
    for c in [local(ao, ao_ref, lsem, 4), local(hid, hid_ref, lsem, 5), local(inp, in_ref, lsem, 6)]:
        c.wait()


def out_call(F, mixed, wo, x, gain):
    R, D = x.shape
    e = wo.shape[1]
    return pl.pallas_call(
        out_kernel,
        out_shape=[
            jax.ShapeDtypeStruct((R, D), f32),
            jax.ShapeDtypeStruct((R, D), f32),
            jax.ShapeDtypeStruct((R, D), bf16),
        ],
        in_specs=[ANY] * 4,
        out_specs=[ANY] * 3,
        scratch_shapes=[
            pltpu.VMEM((F * R, e), bf16),
            pltpu.VMEM((D, e), bf16),
            pltpu.VMEM((R, D), bf16),
            pltpu.VMEM((1, D), f32),
            pltpu.VMEM((R, D), f32),
            pltpu.VMEM((R, D), f32),
            pltpu.VMEM((R, D), bf16),
        ]
        + scatter_scratch(R, D)
        + [dma(7), dma(SCATTER_COPIES), dma(SCATTER_COPIES)],
        compiler_params=params(8),
        cost_estimate=cost(46),
    )(mixed, wo, x, gain)


def up_kernel(
    in_ref, wg_ref, wu_ref, all_ref, act_ref, der_ref, h_ref,
    wg, wu, rows, act, der, h, lsem, osem, send, recv,
):
    at = Plane()
    own = local(in_ref, rows.at[at.f], lsem, 0)
    loads = [local(wg_ref, wg, lsem, 1), local(wu_ref, wu, lsem, 2)]
    at.greet()
    R = rows.shape[1]
    own.wait()
    waited = []
    stores = Stores(osem)

    def on_rows(first, count):
        s = stores.slot()
        m = count * R
        if not waited:
            for c in loads:
                c.wait()
            waited.append(1)

        def tile(c):
            lhs = rows[pl.ds(first, count)].reshape(m, rows.shape[2])
            g = nn(lhs, wg[:, c])
            u = nn(lhs, wu[:, c])
            sig = jax.nn.sigmoid(g)
            a = g * sig
            act[s, pl.ds(0, m), c] = a.astype(bf16)
            der[s, pl.ds(0, m), c] = (u * (sig * (1.0 + g * (1.0 - sig)))).astype(bf16)
            h[s, pl.ds(0, m), c] = (a * u).astype(bf16)

        pair_loop(m, 256, wg.shape[1], tile)
        start = pl.multiple_of(first * R, R)
        stores.put(
            [
                (act.at[s, pl.ds(0, m)], act_ref.at[pl.ds(start, m)]),
                (der.at[s, pl.ds(0, m)], der_ref.at[pl.ds(start, m)]),
                (h.at[s, pl.ds(0, m)], h_ref.at[pl.ds(start, m)]),
                (rows.at[pl.ds(first, count)], all_ref.at[pl.ds(first, count)]),
            ]
        )

    gather_phase(at, rows, send, recv, 0, on_rows)
    stores.finish()


def up_call(F, inp, wg, wu):
    R, D = inp.shape
    n = wg.shape[1]
    T = F * R
    wide = jax.ShapeDtypeStruct((T, n), bf16)
    return pl.pallas_call(
        up_kernel,
        out_shape=[jax.ShapeDtypeStruct((F, R, D), bf16), wide, wide, wide],
        in_specs=[ANY] * 3,
        out_specs=[ANY] * 4,
        scratch_shapes=[
            pltpu.VMEM((D, n), bf16),
            pltpu.VMEM((D, n), bf16),
            pltpu.VMEM((F, R, D), bf16),
            pltpu.VMEM((2, 2 * R, n), bf16),
            pltpu.VMEM((2, 2 * R, n), bf16),
            pltpu.VMEM((2, 2 * R, n), bf16),
        ]
        + [dma(3), dma(20), dma(GATHER_COPIES), dma(GATHER_COPIES)],
        compiler_params=params(2),
        cost_estimate=cost(46),
    )(inp, wg, wu)


def down_kernel(
    h_ref, wd_ref, hid_ref, cot_ref, gain_ref, act_ref, der_ref,
    res_ref, gg_ref, all_ref, gate_ref, up_ref,
    h, wd, hid, cot, gain, act, der, res, gacc, rows, ggate, gup, b0, b1, b2, b3, b4,
    lsem, osem, asem, send, recv,
):
    at = Plane()
    loads = [
        local(s, d, lsem, i)
        for i, (s, d) in enumerate(
            [(h_ref, h), (wd_ref, wd), (hid_ref, hid), (cot_ref, cot), (gain_ref, gain)]
        )
    ]
    at.greet()
    R = rows.shape[1]
    loads[0].wait()
    loads[1].wait()

    def partial(chip, cols):
        return nt(h[pl.ds(pl.multiple_of(chip * 2 * R, 2 * R), 2 * R), :], wd[cols, :])

    total = scatter_phase(at, partial, (b0, b1, b2, b3, b4), send, recv, 0)
    for c in loads[2:]:
        c.wait()
    gacc[...] = jnp.zeros_like(gacc)

    def finish(r):
        out = total(r)
        scale = rms(out)
        hat = out * scale
        res[r, :] = (hid[r, :] + hat * gain[...]).astype(bf16)
        g = cot[r, :].astype(f32)
        gacc[...] += jnp.sum(g * hat, axis=0, keepdims=True)
        rows[at.f, r, :] = back(g * gain[...], hat, scale).astype(bf16)

    row_loop(R, finish)
    saves = [local(res, res_ref, lsem, 5), local(gacc, gg_ref, lsem, 6)]
    stores = Stores(osem)

    def on_rows(first, count):
        s = stores.slot()
        m = count * R
        start = pl.multiple_of(first * R, R)
        k = len(stores.steps)
        la = local(act_ref.at[pl.ds(start, m)], act.at[s, pl.ds(0, m)], asem, 2 * k)
        ld = local(der_ref.at[pl.ds(start, m)], der.at[s, pl.ds(0, m)], asem, 2 * k + 1)
        la.wait()
        ld.wait()

        def tile(c):
            gh = nn(rows[pl.ds(first, count)].reshape(m, rows.shape[2]), wd[:, c])
            gup[s, pl.ds(0, m), c] = (gh * act[s, pl.ds(0, m), c].astype(f32)).astype(bf16)
            ggate[s, pl.ds(0, m), c] = (gh * der[s, pl.ds(0, m), c].astype(f32)).astype(bf16)

        pair_loop(m, 256, wd.shape[1], tile)
        stores.put(
            [
                (ggate.at[s, pl.ds(0, m)], gate_ref.at[pl.ds(start, m)]),
                (gup.at[s, pl.ds(0, m)], up_ref.at[pl.ds(start, m)]),
                (rows.at[pl.ds(first, count)], all_ref.at[pl.ds(first, count)]),
            ]
        )

    gather_phase(at, rows, send, recv, SCATTER_COPIES, on_rows)
    for s in saves:
        s.wait()
    stores.finish()


def down_call(F, h, wd, hid, cot, gain, act, der):
    R, D = hid.shape
    n = wd.shape[1]
    T = F * R
    copies = SCATTER_COPIES + GATHER_COPIES
    return pl.pallas_call(
        down_kernel,
        out_shape=[
            jax.ShapeDtypeStruct((R, D), bf16),
            jax.ShapeDtypeStruct((1, D), f32),
            jax.ShapeDtypeStruct((F, R, D), bf16),
            jax.ShapeDtypeStruct((T, n), bf16),
            jax.ShapeDtypeStruct((T, n), bf16),
        ],
        in_specs=[ANY] * 7,
        out_specs=[ANY] * 5,
        scratch_shapes=[
            pltpu.VMEM((T, n), bf16),
            pltpu.VMEM((D, n), bf16),
            pltpu.VMEM((R, D), f32),
            pltpu.VMEM((R, D), bf16),
            pltpu.VMEM((1, D), f32),
            pltpu.VMEM((2, 2 * R, n), bf16),
            pltpu.VMEM((2, 2 * R, n), bf16),
            pltpu.VMEM((R, D), bf16),
            pltpu.VMEM((1, D), f32),
            pltpu.VMEM((F, R, D), bf16),
            pltpu.VMEM((2, 2 * R, n), bf16),
            pltpu.VMEM((2, 2 * R, n), bf16),
        ]
        + scatter_scratch(R, D)
        + [dma(7), dma(15), dma(10), dma(copies), dma(copies)],
        compiler_params=params(3),
        cost_estimate=cost(92),
    )(h, wd, hid, cot, gain, act, der)


def mid_kernel(
    gate_ref, up_ref, wg_ref, wu_ref, cot_ref, ao_ref, gain_ref, wo_ref,
    res_ref, gg_ref, all_ref, gm_ref,
    ggate, gup, wg, wu, cot, ao, gain, wo, res, gacc, rows, gm, b0, b1, b2, b3, b4,
    lsem, osem, send, recv,
):
    at = Plane()
    pairs = [
        (gate_ref, ggate), (up_ref, gup), (wg_ref, wg), (wu_ref, wu),
        (cot_ref, cot), (ao_ref, ao), (gain_ref, gain), (wo_ref, wo),
    ]
    loads = [local(s, d, lsem, i) for i, (s, d) in enumerate(pairs)]
    at.greet()
    R = rows.shape[1]
    for c in loads[:4]:
        c.wait()

    def partial(chip, cols):
        r = pl.ds(pl.multiple_of(chip * 2 * R, 2 * R), 2 * R)
        return nt(ggate[r, :], wg[cols, :]) + nt(gup[r, :], wu[cols, :])

    total = scatter_phase(at, partial, (b0, b1, b2, b3, b4), send, recv, 0)
    for c in loads[4:]:
        c.wait()
    gacc[...] = jnp.zeros_like(gacc)

    def finish(r):
        resid = cot[r, :].astype(f32) + total(r)
        res[r, :] = resid
        out = ao[r, :]
        scale = rms(out)
        hat = out * scale
        gacc[...] += jnp.sum(resid * hat, axis=0, keepdims=True)
        rows[at.f, r, :] = back(resid * gain[...], hat, scale).astype(bf16)

    row_loop(R, finish)
    saves = [local(res, res_ref, lsem, 8), local(gacc, gg_ref, lsem, 9)]
    stores = Stores(osem)

    def on_rows(first, count):
        s = stores.slot()
        m = count * R
        start = pl.multiple_of(first * R, R)
        lhs = rows[pl.ds(first, count)].reshape(m, rows.shape[2])
        gm[s, pl.ds(0, m), :] = nn(lhs, wo[...]).astype(bf16)
        stores.put(
            [
                (gm.at[s, pl.ds(0, m)], gm_ref.at[pl.ds(start, m)]),
                (rows.at[pl.ds(first, count)], all_ref.at[pl.ds(first, count)]),
            ]
        )

    gather_phase(at, rows, send, recv, SCATTER_COPIES, on_rows)
    for s in saves:
        s.wait()
    stores.finish()


def mid_call(F, gate, up, wg, wu, cot, ao, gain, wo):
    R, D = cot.shape
    n, e = wg.shape[1], wo.shape[1]
    T = F * R
    copies = SCATTER_COPIES + GATHER_COPIES
    return pl.pallas_call(
        mid_kernel,
        out_shape=[
            jax.ShapeDtypeStruct((R, D), f32),
            jax.ShapeDtypeStruct((1, D), f32),
            jax.ShapeDtypeStruct((F, R, D), bf16),
            jax.ShapeDtypeStruct((T, e), bf16),
        ],
        in_specs=[ANY] * 8,
        out_specs=[ANY] * 4,
        scratch_shapes=[
            pltpu.VMEM((T, n), bf16),
            pltpu.VMEM((T, n), bf16),
            pltpu.VMEM((D, n), bf16),
            pltpu.VMEM((D, n), bf16),
            pltpu.VMEM((R, D), bf16),
            pltpu.VMEM((R, D), f32),
            pltpu.VMEM((1, D), f32),
            pltpu.VMEM((D, e), bf16),
            pltpu.VMEM((R, D), f32),
            pltpu.VMEM((1, D), f32),
            pltpu.VMEM((F, R, D), bf16),
            pltpu.VMEM((2, 2 * R, e), bf16),
        ]
        + scatter_scratch(R, D)
        + [dma(10), dma(10), dma(copies), dma(copies)],
        compiler_params=params(4),
        cost_estimate=cost(92),
    )(gate, up, wg, wu, cot, ao, gain, wo)


def last_kernel(
    width, q_ref, k_ref, v_ref, proj_ref, st_ref, in_ref, w_ref, res_ref, gain_ref,
    out_ref, gp_ref, gsum_ref,
    q, k, proj, st, ins, gains, gsum, gp, w, res, out, b0, b1, b2, b3, b4,
    lsem, send, recv, ssend, srecv, gsend, grecv,
):
    at = Plane()
    F, T = st.shape[0], st.shape[2]
    e = q.shape[1]
    R = res.shape[0]
    pairs = [
        (in_ref, ins.at[at.f]), (st_ref, st), (q_ref, q), (k_ref, k),
        (v_ref, gp.at[:, pl.ds(2 * e, e)]), (proj_ref.at[:, pl.ds(0, 2 * e)], proj), (w_ref, w), (res_ref, res),
        (gain_ref, gains.at[at.f]),
    ]
    loads = [local(s, d, lsem, i) for i, (s, d) in enumerate(pairs)]
    barrier = pltpu.get_barrier_semaphore()
    for s in range(1, F):
        pl.semaphore_signal(barrier, inc=1, device_id={"fsdp": (at.f + s) % F}, device_id_type=MESH)
    pl.semaphore_wait(barrier, F - 1)
    loads[0].wait()
    share_stats(at, F, ins, ssend, srecv, 0)
    for c in loads[1:6]:
        c.wait()
    step = 256

    @pl.loop(0, T // step)
    def _(t):
        r = pl.ds(pl.multiple_of(t * step, step), step)
        sums = jnp.sum(st[:, :, r], axis=0)
        inner = jnp.sum(ins[:, :, r], axis=0) / width
        for row, grad in ((0, q), (1, k)):
            scale = lax.rsqrt(column(sums[row : row + 1], HEAD_DIM) / width + epsilon)
            mean = column(inner[row : row + 1], HEAD_DIM)
            for h in range(e // HEAD_DIM):
                hat = proj[r, row * e + h * HEAD_DIM : row * e + (h + 1) * HEAD_DIM] * scale
                got = scale * (grad[r, h * HEAD_DIM : (h + 1) * HEAD_DIM] - hat * mean)
                gp[r, row * e + h * HEAD_DIM : row * e + (h + 1) * HEAD_DIM] = got.astype(bf16)

    save = local(gp, gp_ref, lsem, 9)
    loads[6].wait()

    def partial(chip, cols):
        return nt(gp[pl.ds(pl.multiple_of(chip * 2 * R, 2 * R), 2 * R), :], w[cols, :])

    total = scatter_phase(at, partial, (b0, b1, b2, b3, b4), send, recv, 0)
    loads[7].wait()

    def finish(r):
        out[r, :] = (res[r, :] + total(r)).astype(bf16)

    row_loop(R, finish)
    store = local(out, out_ref, lsem, 10)
    loads[8].wait()
    share_stats(at, F, gains, gsend, grecv, 0)
    gsum[...] = jnp.sum(gains[...], axis=0)
    local(gsum, gsum_ref, lsem, 11).wait()
    store.wait()
    save.wait()


def last_call(F, wq, wk, gv, proj, st, ins, w, res, gains):
    R, D = res.shape
    n = w.shape[1]
    T, e = F * R, n // 3
    return pl.pallas_call(
        functools.partial(last_kernel, D),
        out_shape=[
            jax.ShapeDtypeStruct((R, D), bf16),
            jax.ShapeDtypeStruct((T, n), bf16),
            jax.ShapeDtypeStruct((8, D), f32),
        ],
        in_specs=[ANY] * 9,
        out_specs=[ANY] * 3,
        scratch_shapes=[
            pltpu.VMEM((T, e), f32),
            pltpu.VMEM((T, e), f32),
            pltpu.VMEM((T, 2 * e), f32),
            pltpu.VMEM((F, 8, T), f32),
            pltpu.VMEM((F, 8, T), f32),
            pltpu.VMEM((F, 8, D), f32),
            pltpu.VMEM((8, D), f32),
            pltpu.VMEM((T, n), bf16),
            pltpu.VMEM((D, n), bf16),
            pltpu.VMEM((R, D), f32),
            pltpu.VMEM((R, D), bf16),
        ]
        + scatter_scratch(R, D)
        + [dma(12), dma(SCATTER_COPIES), dma(SCATTER_COPIES), dma(F), dma(F), dma(F), dma(F)],
        compiler_params=params(5),
        cost_estimate=cost(55),
    )(wq, wk, gv, proj, st, ins, w, res, gains)


def share_stats(at, F, st, send, recv, base):
    sent = []
    for k in range(1, F):
        to = (at.f + k) % F
        c = remote(st.at[at.f], st.at[at.f], send, recv, base + k, to)
        c.start()
        sent.append(c)
    for k in range(1, F):
        frm = (at.f - k + F) % F
        remote(st.at[frm], st.at[frm], send, recv, base + k, frm).wait_recv()
    for c in sent:
        c.wait_send()


def row_sums(a, b):
    r = lax.broadcasted_iota(jnp.int32, (8, a.shape[1]), 0)
    one, two = (r == 0).astype(f32), (r == 1).astype(f32)

    def half(sel, v):
        return lax.dot_general(
            sel, v, (((1,), (1,)), ((), ())), preferred_element_type=f32, precision=lax.Precision.HIGHEST
        )

    return half(one, a) + half(two, b)


def column(row, lanes):
    return jnp.broadcast_to(row, (lanes, row.shape[1])).T


def turn(v, cos, sin):
    return v * cos + pltpu.roll(v, HEAD_DIM // 2, 1) * sin


def seq_columns(st, c, chips, R):
    return jnp.concatenate([st[:, pl.ds(pl.multiple_of((2 * j + c) * R, R), R)] for j in range(chips)], axis=1)


def attend_kernel(width, q_ref, k_ref, v_ref, st_ref, gq_ref, gk_ref, cos_ref, sin_ref, pos_ref, posc_ref, mix_ref, qr_ref, kr_ref, lse_ref):
    c = pl.program_id(0)
    chips, R = q_ref.shape[0], q_ref.shape[2]
    L = chips * R
    sums = jnp.sum(seq_columns_all(st_ref, c, chips, R), axis=0)
    cos, sin = cos_ref[0], sin_ref[0]

    def norm_turn(ref, row, gain):
        scale = lax.rsqrt(column(sums[row : row + 1], HEAD_DIM) / width + epsilon)
        return turn(ref[...].reshape(L, HEAD_DIM) * scale * gain[...], cos, sin)

    qr = (norm_turn(q_ref, 0, gq_ref) * HEAD_DIM ** (-0.5)).astype(bf16)
    kr = norm_turn(k_ref, 1, gk_ref).astype(bf16)
    v = v_ref[...].reshape(L, HEAD_DIM).astype(bf16)
    qr_ref[...] = qr.reshape(qr_ref.shape)
    kr_ref[...] = kr.reshape(kr_ref.shape)
    pos = pos_ref[0]
    for t in range(chips):
        rows = slice(t * R, (t + 1) * R)
        s = nt(qr[rows], kr)
        s = jnp.where(posc_ref[0, rows, :1] >= pos, s, -1e30)
        top = jnp.max(s, axis=-1, keepdims=True)
        e = jnp.exp(s - top)
        total = jnp.sum(e, axis=-1, keepdims=True)
        p = (e * (1.0 / total)).astype(bf16)
        mix_ref[t, 0] = nn(p, v).astype(bf16)
        lse_ref[0, 0, rows, :] = jnp.broadcast_to(top + jnp.log(total), (R, HEAD_DIM))


def seq_columns_all(st_ref, c, chips, R):
    return jnp.concatenate(
        [st_ref[:, :, pl.ds(pl.multiple_of((2 * j + c) * R, R), R)] for j in range(chips)], axis=2
    )


def attend_specs(chips, R, heads, F, L):
    def at(offset):
        return pl.BlockSpec((chips, 1, R, HEAD_DIM), lambda c, h: (0, c, 0, offset + h))

    gain = pl.BlockSpec((1, HEAD_DIM), lambda c, h: (0, h))
    table = pl.BlockSpec((1, L, HEAD_DIM), lambda c, h: (c, 0, 0))
    stats = pl.BlockSpec((F, 8, F * R), lambda c, h: (0, 0, 0))
    posr = pl.BlockSpec((1, 1, L), lambda c, h: (c, 0, 0))
    lse = pl.BlockSpec((1, 1, L, HEAD_DIM), lambda c, h: (c, h, 0, 0))
    return at, gain, table, stats, posr, lse


def attend_call(F, proj, st, gq, gk, cos, sin, pos, posc):
    R = proj.shape[0] // F
    e = proj.shape[1] // 3
    heads, chips = e // HEAD_DIM, F // 2
    L = chips * R
    at, gain, table, stats, posr, lse = attend_specs(chips, R, heads, F, L)
    view = proj.reshape(chips, 2, R, 3 * e)
    flat = jax.ShapeDtypeStruct((chips, 2, R, e), bf16)
    out = pl.pallas_call(
        functools.partial(attend_kernel, heads * HEAD_DIM * F),
        out_shape=[flat, flat, flat, jax.ShapeDtypeStruct((2, heads, L, HEAD_DIM), f32)],
        grid=(2, heads),
        in_specs=[at(0), at(heads), at(2 * heads), stats, gain, gain, table, table, posr, table],
        out_specs=[at(0), at(0), at(0), lse],
        compiler_params=pltpu.CompilerParams(vmem_limit_bytes=VMEM_LIMIT),
        cost_estimate=cost(15),
    )(view, view, view, st, gq, gk, cos, sin, pos, posc)
    return out


def attend_back_kernel(
    width, q_ref, k_ref, v_ref, qr_ref, kr_ref, gm_ref, lse_ref, st_ref, gq_ref, gk_ref, cos_ref, sin_ref, pos_ref, posc_ref,
    wq_ref, wk_ref, gv_ref, in_ref, gg_ref, dk, dv, dq,
):
    c = pl.program_id(0)
    chips, R = q_ref.shape[0], q_ref.shape[2]
    L = chips * R
    kr = kr_ref[...].reshape(L, HEAD_DIM)
    v = v_ref[...].reshape(L, HEAD_DIM).astype(bf16)
    pos = pos_ref[0]
    dk[...] = jnp.zeros_like(dk)
    dv[...] = jnp.zeros_like(dv)
    for t in range(chips):
        rows = slice(t * R, (t + 1) * R)
        qt, gm = qr_ref[t, 0], gm_ref[t, 0]
        s = nt(qt, kr)
        s = jnp.where(posc_ref[0, rows, :1] >= pos, s, -1e30)
        p = jnp.exp(s - lse_ref[0, 0, rows, :1])
        dp = nt(gm, v)
        dv[...] += lax.dot_general(p.astype(bf16), gm, (((0,), (0,)), ((), ())), preferred_element_type=f32)
        inner = jnp.sum(dp * p, axis=-1, keepdims=True)
        ds = (p * (dp - inner)).astype(bf16)
        dq[rows, :] = nn(ds, kr)
        dk[...] += lax.dot_general(ds, qt, (((0,), (0,)), ((), ())), preferred_element_type=f32)
    gv_ref[...] = dv[...].astype(bf16).reshape(gv_ref.shape)
    sums = jnp.sum(seq_columns_all(st_ref, c, chips, R), axis=0)
    cos, sin = cos_ref[0], sin_ref[0]

    def finish(grad, ref, row, gain, out):
        norm = turn(grad, cos, -sin)
        hat = ref[...].reshape(L, HEAD_DIM) * lax.rsqrt(column(sums[row : row + 1], HEAD_DIM) / width + epsilon)
        gg_ref[0, 0, row : row + 1, :] = jnp.sum(norm * hat, axis=0, keepdims=True)
        weighted = norm * gain[...]
        out[...] = weighted.reshape(out.shape)
        return weighted * hat

    gg_ref[...] = jnp.zeros_like(gg_ref)
    in_ref[0, 0] = row_sums(
        finish(dq[...] * HEAD_DIM ** (-0.5), q_ref, 0, gq_ref, wq_ref), finish(dk[...], k_ref, 1, gk_ref, wk_ref)
    )


def attend_back_call(F, proj, qr, kr, gm, lse_in, st, gq, gk, cos, sin, pos, posc):
    R = proj.shape[0] // F
    e = proj.shape[1] // 3
    heads, chips = e // HEAD_DIM, F // 2
    L = chips * R
    at, gain, table, stats, posr, lse = attend_specs(chips, R, heads, F, L)
    view = proj.reshape(chips, 2, R, 3 * e)
    flat = (chips, 2, R, e)
    small = pl.BlockSpec((1, 1, 8, L), lambda c, h: (c, h, 0, 0))
    tiny = pl.BlockSpec((1, 1, 8, HEAD_DIM), lambda c, h: (c, h, 0, 0))
    wide = jax.ShapeDtypeStruct(flat, f32)
    return pl.pallas_call(
        functools.partial(attend_back_kernel, heads * HEAD_DIM * F),
        out_shape=[
            wide, wide, jax.ShapeDtypeStruct(flat, bf16),
            jax.ShapeDtypeStruct((2, heads, 8, L), f32),
            jax.ShapeDtypeStruct((2, heads, 8, HEAD_DIM), f32),
        ],
        grid=(2, heads),
        in_specs=[
            at(0), at(heads), at(2 * heads), at(0), at(0), at(0), lse, stats, gain, gain, table, table, posr, table,
        ],
        out_specs=[at(0), at(0), at(0), small, tiny],
        scratch_shapes=[pltpu.VMEM((L, HEAD_DIM), f32)] * 3,
        compiler_params=pltpu.CompilerParams(vmem_limit_bytes=VMEM_LIMIT),
        cost_estimate=cost(35),
    )(view, view, view, qr, kr, gm.reshape(flat), lse_in, st, gq, gk, cos, sin, pos, posc)


def newton_kernel(
    C, x_ref, rows_ref, gain_ref, out_ref, home_ref, gsum_ref,
    v, gram, y, yf, stat, stage, gains, gsum,
    lsem, osem, vsend, vrecv, ysend, yrecv, ssend, srecv, tsend, trecv, gsend, grecv,
):
    me = lax.axis_index("fsdp")
    z = lax.axis_index("ctx")
    core, chip = me % 2, me // 2
    peer = me + 1 - 2 * core
    load = local(x_ref, v.at[0], lsem, 0)
    gload = local(gain_ref, gains.at[z], lsem, 1)
    barrier = pltpu.get_barrier_semaphore()
    pl.semaphore_signal(barrier, inc=1, device_id={"fsdp": peer}, device_id_type=MESH)
    for k in range(1, C):
        pl.semaphore_signal(barrier, inc=1, device_id={"ctx": (z + k) % C}, device_id_type=MESH)
        pl.semaphore_signal(
            barrier, inc=1, device_id={"fsdp": 2 * ((chip + k) % C) + core}, device_id_type=MESH
        )
    pl.semaphore_wait(barrier, 2 * (C - 1) + 1)
    piece = rows_ref.shape[1] // C

    def part(j):
        return pl.ds(j * piece, piece)

    sent, keep = [], []
    for a in range(2):
        for k in range(1, C):
            to = (z + k) % C
            c = remote(rows_ref.at[a, part(to)], stage.at[a, z], tsend, trecv, 2 * C * a + k, to, "ctx")
            c.start()
            sent.append(c)
        keep.append(local(rows_ref.at[a, part(z)], stage.at[a, z], lsem, 2 + a))
    gload.wait()
    for k in range(1, C):
        c = remote(gains.at[z], gains.at[z], gsend, grecv, k, (z + k) % C, "ctx")
        c.start()
        sent.append(c)

    def leave_layer():
        for a in range(2):
            for k in range(1, C):
                frm = (z - k + C) % C
                remote(stage.at[a, frm], stage.at[a, frm], tsend, trecv, 2 * C * a + k, frm, "ctx").wait_recv()
            keep[a].wait()
            for k in range(1, C):
                to = (chip + k) % C
                c = remote(
                    stage.at[a, to], home_ref.at[a, part(chip)], tsend, trecv, 2 * C * a + C + k, 2 * to + core
                )
                c.start()
                sent.append(c)
            keep[a] = local(stage.at[a, chip], home_ref.at[a, part(chip)], lsem, 4 + a)

    def arrived_home():
        for a in range(2):
            keep[a].wait()
            for k in range(1, C):
                frm = (chip - k + C) % C
                dst = home_ref.at[a, part(frm)]
                remote(dst, dst, tsend, trecv, 2 * C * a + C + k, 2 * frm + core).wait_recv()
        for k in range(1, C):
            frm = (z - k + C) % C
            remote(gains.at[frm], gains.at[frm], gsend, grecv, k, frm, "ctx").wait_recv()
        gsum[...] = jnp.sum(gains[...], axis=0)
        local(gsum, gsum_ref, lsem, 6).wait()
        for c in sent:
            c.wait_send()

    load.wait()
    M, D = v.shape[1], v.shape[2]
    tile, col = 256, 512
    tiles = M // tile

    def block(i):
        return pl.ds(i * tile, tile)

    def swap(buf, i, sends, recvs):
        return remote(buf.at[0, block(i)], buf.at[1, block(i)], sends, recvs, i, peer)

    pending = [swap(v, i, vsend, vrecv) for i in range(tiles)]
    for c in pending:
        c.start()
    stat[0] = jnp.zeros_like(stat[0])

    def add(r):
        part = v[0, r, :].astype(f32)
        stat[0] += jnp.sum((part * part).reshape(-1, 8, D // 128, 128), axis=(0, 2))

    row_loop(M, add)
    share = remote(stat.at[0], stat.at[1], ssend, srecv, 0, peer)
    share.start()
    share.wait()
    inv = 1.0 / (jnp.sqrt(jnp.sum(stat[0] + stat[1])) + 1e-07)

    for iteration in range(NS_STEPS):
        factor = inv if iteration == 0 else 1.0

        def grams(h, n):
            rhs = pl.ds(pl.multiple_of(n * col, col), col)
            cols = pl.ds(pl.multiple_of(h * M + n * col, col), col)

            @pl.loop(0, tiles)
            def _(i):
                rows = pl.ds(pl.multiple_of(i * tile, tile), tile)
                got = nt(v[0, rows, :], v[h, rhs, :])
                if iteration == 0:
                    got = got * (factor * factor)
                gram[rows, cols] = got.astype(bf16)

        @pl.loop(0, M // col)
        def _(n):
            grams(0, n)

        for c in pending:
            c.wait()

        @pl.loop(0, M // col)
        def _(n):
            grams(1, n)

        def times(src, i, n):
            rows = block(i)
            cols = pl.ds(pl.multiple_of(n * col, col), col)
            return cols, nn(gram[rows, :M], src[0, :, cols]) + nn(gram[rows, M:], src[1, :, cols])

        pending = []
        for i in range(tiles):

            @pl.loop(0, D // col)
            def _(n):
                cols, got = times(v, i, n)
                if iteration == 0:
                    got = got * factor
                yf[block(i), cols] = got
                y[0, block(i), cols] = got.astype(bf16)

            c = swap(y, i, ysend, yrecv)
            c.start()
            pending.append(c)
        for c in pending:
            c.wait()
        if iteration == 0:
            leave_layer()
        pending = []
        for i in range(tiles):

            @pl.loop(0, D // col)
            def _(n):
                cols, got = times(y, i, n)
                old = v[0, block(i), cols].astype(f32)
                if iteration == 0:
                    old = old * factor
                v[0, block(i), cols] = (
                    quintic_one * old + quintic_two * yf[block(i), cols] + quintic_three * got
                ).astype(bf16)

            if iteration < NS_STEPS - 1:
                c = swap(v, i, vsend, vrecv)
            else:
                c = pltpu.make_async_copy(v.at[0, block(i)], out_ref.at[block(i)], osem.at[i])
            c.start()
            pending.append(c)
    arrived_home()
    for c in pending:
        c.wait()


def newton_call(C, x, rows, gains):
    M, D = x.shape
    _, R, _ = rows.shape
    n = M // 256
    return pl.pallas_call(
        functools.partial(newton_kernel, C),
        out_shape=[
            jax.ShapeDtypeStruct((M, D), bf16),
            jax.ShapeDtypeStruct((2, R, D), bf16),
            jax.ShapeDtypeStruct((8, D), f32),
        ],
        in_specs=[ANY] * 3,
        out_specs=[ANY] * 3,
        scratch_shapes=[
            pltpu.VMEM((2, M, D), bf16),
            pltpu.VMEM((M, 2 * M), bf16),
            pltpu.VMEM((2, M, D), bf16),
            pltpu.VMEM((M, D), f32),
            pltpu.VMEM((2, 8, 128), f32),
            pltpu.VMEM((2, C, R // C, D), bf16),
            pltpu.VMEM((C, 8, D), f32),
            pltpu.VMEM((8, D), f32),
            dma(7), dma(n), dma(n), dma(n), dma(n), dma(n), dma(1), dma(1),
            dma(4 * C), dma(4 * C), dma(C), dma(C),
        ],
        compiler_params=params(6),
        cost_estimate=cost(95),
    )(x, rows, gains)


def project(C, F, x, w):
    own = to_layer(C, F, x)
    rows = token_rows(own)
    return own, rows, dot(rows, w, 1, 0)


def attn_out_and_up(C, F, mixed, wo, x, gain, wg, wu):
    if kernels_fit(C, F):
        hidden_in, out, inp = out_call(F, mixed, wo, x, gain)
        return (hidden_in, out, *up_call(F, inp, wg, wu))
    out = token_sums(dot(mixed, wo, 1, 1))
    hidden_in = x.astype(f32) + out * rms(out) * gain
    rows = token_rows(hidden_in.astype(bf16))
    g, u = dot(rows, wg, 1, 0), dot(rows, wu, 1, 0)
    sig = jax.nn.sigmoid(g)
    der = u * (sig * (1.0 + g * (1.0 - sig)))
    act = g * sig
    return hidden_in, out, rows, act.astype(bf16), der.astype(bf16), (act * u).astype(bf16)


def down_and_back(C, F, h, wd, hidden_in, cot, gain, act, der):
    if kernels_fit(C, F):
        return down_call(F, h, wd, hidden_in, cot, gain, act, der)
    out = token_sums(dot(h, wd, 1, 1))
    scale = rms(out)
    hat = out * scale
    g = cot.astype(f32)
    rows = token_rows(back(g * gain, hat, scale).astype(bf16))
    gh = dot(rows, wd, 1, 0)
    return (
        (hidden_in + hat * gain).astype(bf16),
        jnp.sum(g * hat, axis=0, keepdims=True),
        rows,
        (gh * der.astype(f32)).astype(bf16),
        (gh * act.astype(f32)).astype(bf16),
    )


def back_to_attn(C, F, grad_gate, grad_up, wg, wu, cot, out, gain, wo):
    if kernels_fit(C, F):
        return mid_call(F, grad_gate, grad_up, wg, wu, cot, out, gain, wo)
    resid = cot.astype(f32) + token_sums(dot(grad_gate, wg, 1, 1) + dot(grad_up, wu, 1, 1))
    scale = rms(out)
    hat = out * scale
    rows = token_rows(back(resid * gain, hat, scale).astype(bf16))
    return resid, jnp.sum(resid * hat, axis=0, keepdims=True), rows, dot(rows, wo, 1, 0).astype(bf16)


def back_to_input(C, F, grad_projected, w, resid):
    return (resid + token_sums(dot(grad_projected, w, 1, 1))).astype(bf16)


def kernels_fit(C, F):
    return C == 4 and F == 8 and UNITS_ATTN * 4 * 2 == C * F


def to_layer(C, F, x):
    z, chip = lax.axis_index("ctx"), lax.axis_index("fsdp") // 2
    x = x.reshape(C, x.shape[0] // C, x.shape[1])
    got = []
    for k in range(C):
        pairs = [
            (s * F + f, (f // 2) * F + 2 * ((s + k) % C) + f % 2) for s in range(C) for f in range(F)
        ]
        block = lax.dynamic_index_in_dim(x, (z + k) % C, 0, keepdims=False)
        got.append(lax.ppermute(block, BOTH, pairs))
    got = jnp.stack(got)
    got = [lax.dynamic_index_in_dim(got, (chip - s + C) % C, 0, keepdims=False) for s in range(C)]
    return jnp.concatenate(got, axis=0)


def from_layer(C, F, x):
    z, chip = lax.axis_index("ctx"), lax.axis_index("fsdp") // 2
    x = x.reshape(C, x.shape[0] // C, x.shape[1])
    got = []
    for k in range(C):
        pairs = [
            ((f // 2) * F + 2 * ((s + k) % C) + f % 2, s * F + f) for s in range(C) for f in range(F)
        ]
        block = lax.dynamic_index_in_dim(x, (chip - k + C) % C, 0, keepdims=False)
        got.append(lax.ppermute(block, BOTH, pairs))
    got = jnp.stack(got)
    got = [lax.dynamic_index_in_dim(got, (j - z + C) % C, 0, keepdims=False) for j in range(C)]
    return jnp.concatenate(got, axis=0)


def shards(C, F, layer_input, cotangent, positions, w_attn, w_ffn, gains, mom_attn, mom_ffn, gain_mom):
    z = lax.axis_index("ctx")
    f = lax.axis_index("fsdp")
    local_rows, width = layer_input.shape[1], layer_input.shape[2]
    seq_total, seq_length = positions.shape
    dz, head_cols = w_attn.shape[1], w_attn.shape[2]
    local_heads = head_cols // HEAD_DIM
    block_count = w_ffn.shape[2]
    per = seq_total // C
    piece = local_rows // C
    chips = F // per
    tokens = F * local_rows
    hidden_cols = block_count * head_cols
    units = UNITS_ATTN + 3 * block_count
    parts = C * F // units

    def after(a, b):
        return lax.optimization_barrier((a, b))[0]

    def rows_gather(shard):
        return lax.all_gather(shard, "ctx", axis=0, tiled=True)

    def rows_product(lhs, rhs):
        return dot(lhs.reshape(tokens, width), rhs, 0, 0).astype(bf16)

    def rows_scatter(grad):
        return lax.psum_scatter(grad, "ctx", scatter_dimension=0, tiled=True)

    w_qkv = rows_gather(jnp.concatenate([w_attn[0], w_attn[1], w_attn[2]], axis=1))
    w_out = rows_gather(w_attn[3])
    ffn_flat = w_ffn.reshape(3, dz, hidden_cols)
    w_gate = rows_gather(ffn_flat[0])
    w_up = rows_gather(ffn_flat[1])
    w_down = rows_gather(ffn_flat[2])
    gain_query = lax.dynamic_slice_in_dim(gains[0], f * head_cols, head_cols)
    gain_key = lax.dynamic_slice_in_dim(gains[1], f * head_cols, head_cols)
    pos = lax.dynamic_slice_in_dim(positions, z * per, per, 0)
    pos = jnp.transpose(pos.reshape(per, C, chips, piece), (0, 2, 1, 3)).reshape(per, seq_length)
    cosine_table, sine_table = rotary_tables(pos)
    kernels = kernels_fit(C, F)

    def heads(a):
        return jnp.transpose(
            a.reshape(chips, per, local_rows, local_heads, HEAD_DIM), (1, 0, 2, 3, 4)
        ).reshape(per, seq_length, local_heads, HEAD_DIM)

    def unheads(a):
        return jnp.transpose(
            a.reshape(per, chips, local_rows, local_heads, HEAD_DIM), (1, 0, 2, 3, 4)
        ).reshape(tokens, head_cols)

    if kernels:
        sign = jnp.where(jnp.arange(HEAD_DIM) < HEAD_DIM // 2, -1.0, 1.0)
        tables = (
            gain_query[None],
            gain_key[None],
            jnp.broadcast_to(cosine_table[:, :, 0], (per, seq_length, HEAD_DIM)),
            sine_table[:, :, 0] * sign,
            pos.astype(f32)[:, None, :],
            jnp.broadcast_to(pos.astype(f32)[..., None], (per, seq_length, HEAD_DIM)),
        )
        own_input, own_grad, input_all = enter_call(
            C, F, layer_input.reshape(local_rows, width), cotangent.reshape(local_rows, width)
        )
        projected, stats = qkv_call(F, input_all, w_qkv)
        attn_mixed, query_rows, key_rows, log_total = attend_call(F, projected, stats, *tables)
        attn_mixed = attn_mixed.reshape(tokens, head_cols)
    else:
        own_input, input_all, projected = project(C, F, layer_input.reshape(local_rows, width), w_qkv)
        own_grad = to_layer(C, F, after(cotangent.reshape(local_rows, width), own_input))
        query_raw = projected[:, :head_cols]
        key_raw = projected[:, head_cols : 2 * head_cols]
        value_raw = projected[:, 2 * head_cols :]
        query_total, key_total = norm_stats(
            jnp.sum(query_raw * query_raw, axis=-1), jnp.sum(key_raw * key_raw, axis=-1)
        )
        query_scale = lax.rsqrt(query_total / width + epsilon)[..., None]
        key_scale = lax.rsqrt(key_total / width + epsilon)[..., None]
        query_hat = query_raw * query_scale
        key_hat = key_raw * key_scale
        query_rows = (
            rotate(heads(query_hat * gain_query), cosine_table, sine_table) * HEAD_DIM ** (-0.5)
        ).astype(bf16)
        key_rows = rotate(heads(key_hat * gain_key), cosine_table, sine_table).astype(bf16)
        value_rows = heads(value_raw.astype(bf16))
        attn_mixed, log_total = attend(query_rows, key_rows, value_rows, pos)
        attn_mixed = unheads(attn_mixed)
    hidden_in, attn_out, mlp_all, act, der, hidden = attn_out_and_up(
        C, F, attn_mixed, w_out, own_input, gains[2:3], w_gate, w_up
    )
    result, mlp_gain, grad_mlp_all, grad_gate, grad_up = down_and_back(
        C, F, hidden, w_down, hidden_in, own_grad, gains[3:4], act, der
    )
    p_down = rows_product(grad_mlp_all, hidden)
    p_gate = rows_product(mlp_all, grad_gate)
    p_up = rows_product(mlp_all, grad_up)
    g_down = rows_scatter(p_down)
    g_gate = rows_scatter(p_gate)
    g_up = rows_scatter(p_up)
    grad_gate, grad_up, p_down, p_gate, p_up = lax.optimization_barrier(
        (grad_gate, grad_up, p_down, p_gate, p_up)
    )
    grad_resid, attn_gain, grad_attn_all, grad_mixed = back_to_attn(
        C, F, grad_gate, grad_up, w_gate, w_up, own_grad, attn_out, gains[2:3], w_out
    )
    p_out = rows_product(grad_attn_all, attn_mixed)
    grad_mixed, p_out, g_down = lax.optimization_barrier((grad_mixed, p_out, g_down))
    g_out = rows_scatter(p_out)
    if kernels:
        weighted_q, weighted_k, grad_value, inner, gain_cols = attend_back_call(
            F, projected, query_rows, key_rows, grad_mixed, log_total, stats, *tables
        )
        inner = jnp.transpose(
            jnp.sum(inner, axis=1).reshape(per, 8, chips, local_rows), (1, 2, 0, 3)
        ).reshape(8, tokens)
        gain_cols = jnp.sum(gain_cols, axis=0)
        query_gain_cols = gain_cols[:, 0].reshape(head_cols)
        key_gain_cols = gain_cols[:, 1].reshape(head_cols)
        flat = (tokens, head_cols)
        zero = jnp.zeros((width,), f32)
        gain_local = jnp.stack(
            [
                lax.dynamic_update_slice(zero, query_gain_cols, (f * head_cols,)),
                lax.dynamic_update_slice(zero, key_gain_cols, (f * head_cols,)),
                attn_gain[0],
                mlp_gain[0],
                *[zero] * 4,
            ]
        )
        grad_rows, grad_projected, gain_layer = last_call(
            F, weighted_q.reshape(flat), weighted_k.reshape(flat), grad_value.reshape(flat),
            projected, stats, inner, w_qkv, grad_resid, gain_local,
        )
    else:
        grad_query, grad_key, grad_value = attend_back(
            query_rows, key_rows, value_rows, pos, heads(grad_mixed), log_total
        )
        grad_query_norm = unheads(unrotate(grad_query * HEAD_DIM ** (-0.5), cosine_table, sine_table))
        grad_key_norm = unheads(unrotate(grad_key, cosine_table, sine_table))
        query_gain_cols = jnp.sum(grad_query_norm * query_hat, axis=0)
        key_gain_cols = jnp.sum(grad_key_norm * key_hat, axis=0)
        query_weighted = grad_query_norm * gain_query
        key_weighted = grad_key_norm * gain_key
        query_inner, key_inner = norm_stats(
            jnp.sum(query_weighted * query_hat, axis=-1), jnp.sum(key_weighted * key_hat, axis=-1)
        )
        grad_query_raw = query_scale * (query_weighted - query_hat * (query_inner / width)[..., None])
        grad_key_raw = key_scale * (key_weighted - key_hat * (key_inner / width)[..., None])
        grad_projected = jnp.concatenate(
            [grad_query_raw.astype(bf16), grad_key_raw.astype(bf16), unheads(grad_value).astype(bf16)],
            axis=1,
        )
        grad_rows = back_to_input(C, F, grad_projected, w_qkv, grad_resid)
    p_qkv = rows_product(input_all, grad_projected)
    g_qkv = rows_scatter(p_qkv)
    if not kernels:
        grad_input = from_layer(C, F, grad_rows)
        result = from_layer(C, F, result)
        zero = jnp.zeros((width,), f32)
        gain_local = jnp.stack(
            [
                lax.dynamic_update_slice(zero, query_gain_cols, (f * head_cols,)),
                lax.dynamic_update_slice(zero, key_gain_cols, (f * head_cols,)),
                attn_gain[0],
                mlp_gain[0],
            ]
        )
        gain_total = jnp.sum(lax.all_gather(gain_local, BOTH, axis=0, tiled=False), axis=0)

    g_qkv, g_out, g_gate, g_up, g_down, _ = lax.optimization_barrier(
        (g_qkv, g_out, g_gate, g_up, g_down, grad_rows)
    )
    g_qkv, g_out, g_gate, g_up, g_down = (g.astype(f32) for g in (g_qkv, g_out, g_gate, g_up, g_down))
    grad_attn = jnp.stack(
        [g_qkv[:, :head_cols], g_qkv[:, head_cols : 2 * head_cols], g_qkv[:, 2 * head_cols :], g_out]
    )
    grad_ffn = jnp.stack([g_gate, g_up, g_down]).reshape(3, dz, block_count, head_cols)
    new_attn = momentum * mom_attn + grad_attn
    new_ffn = momentum * mom_ffn + grad_ffn
    send = jnp.concatenate(
        [
            new_attn.astype(bf16),
            jnp.transpose(new_ffn.astype(bf16), (0, 2, 1, 3)).reshape(3 * block_count, dz, head_cols),
        ],
        axis=0,
    ).reshape(C * F, dz // parts, head_cols)
    got = lax.all_to_all(send, BOTH, split_axis=0, concat_axis=0, tiled=True)
    own = jnp.transpose(got.reshape(C, F, dz // parts, head_cols), (0, 2, 1, 3)).reshape(
        C * dz // parts, F * head_cols
    )

    def peers(a):
        out = [a]
        for s in range(1, parts):
            pairs = [(i, i - i % parts + (i + parts - s) % parts) for i in range(C * F)]
            out.append(lax.ppermute(a, BOTH, pairs))
        return out

    if kernels:
        own, back_rows, gain_total = newton_call(C, own, jnp.stack([result, grad_rows]), gain_layer)
        result, grad_input, gain_total = back_rows[0], back_rows[1], gain_total[:4]
    else:
        own32 = own.astype(f32)
        square = jnp.sum(own32 * own32)
        total = sum(peers(square.reshape(1, 1)))
        inv = 1.0 / (jnp.sqrt(total) + 1e-07)
        for iteration in range(NS_STEPS):
            factor = inv if iteration == 0 else 1.0
            every = peers(own)
            gram = [(dot(own, b, 1, 1) * (factor * factor)).astype(bf16) for b in every]
            product = sum(dot(g, b, 1, 0) for g, b in zip(gram, every)) * factor
            product_all = peers(product.astype(bf16))
            product_two = sum(dot(g, b, 1, 0) for g, b in zip(gram, product_all))
            own = (
                quintic_one * factor * own.astype(f32) + quintic_two * product + quintic_three * product_two
            ).astype(bf16)
    own, result, grad_input = lax.optimization_barrier((own, result, grad_input))
    home = jnp.transpose(own.reshape(C, dz // parts, F, head_cols), (0, 2, 1, 3)).reshape(
        C * F, dz // parts, head_cols
    )
    steps = lax.all_to_all(home, BOTH, split_axis=0, concat_axis=0, tiled=True)
    steps = -muon_rate * steps.astype(f32).reshape(units, dz, head_cols)
    step_attn = steps[:UNITS_ATTN]
    step_ffn = jnp.transpose(
        steps[UNITS_ATTN:].reshape(3, block_count, dz, head_cols), (0, 2, 1, 3)
    )
    new_gain_mom = momentum * gain_mom + gain_total
    return (
        result.reshape(layer_input.shape),
        grad_input.astype(f32).reshape(layer_input.shape),
        grad_attn,
        grad_ffn,
        gain_total,
        new_attn,
        new_ffn,
        new_gain_mom,
        step_attn,
        step_ffn,
        -gain_rate * new_gain_mom,
    )


def solution(mesh):
    tokens = P("fsdp", "ctx", None)
    attn = P(None, "ctx", "fsdp")
    ffn = P(None, "ctx", None, "fsdp")
    in_specs = (tokens, tokens, P(), attn, ffn, P(), attn, ffn, P())
    out_specs = (tokens, tokens, attn, ffn, P(), attn, ffn, P(), attn, ffn, P())
    body = functools.partial(shards, mesh.shape["ctx"], mesh.shape["fsdp"])
    return jax.shard_map(body, mesh=mesh, in_specs=in_specs, out_specs=out_specs, check_vma=False)
```

```python
import functools
import jax
import jax.numpy as jnp
from jax import lax
from jax.experimental import pallas as pl
from jax.experimental.pallas import tpu as pltpu
from jax.sharding import PartitionSpec as P

NS_STEPS = 3
HEAD_DIM = 128
UNITS_ATTN = 4

epsilon = 1e-06
rope_theta = 500000.0
quintic_one = 3.4445
quintic_two = -4.775
quintic_three = 2.0315
momentum = 0.95
muon_rate = 1.0
gain_rate = 0.0005
BOTH = ("ctx", "fsdp")
bf16 = jnp.bfloat16
f32 = jnp.float32


def dot(a, b, ca, cb):
    return lax.dot_general(a, b, (((ca,), (cb,)), ((), ())), preferred_element_type=f32)


def token_rows(operand):
    return lax.all_gather(operand, "fsdp", axis=0, tiled=True)


def token_sums(operand):
    return lax.psum_scatter(operand.astype(bf16), "fsdp", scatter_dimension=0, tiled=True).astype(f32)


def norm_stats(first_sum, second_sum):
    got = lax.all_gather(jnp.stack([first_sum, second_sum]), "fsdp", axis=0, tiled=False)
    total = jnp.sum(got, axis=0)
    return total[0], total[1]


def rms_back(upstream, normed, inv_scale):
    return inv_scale * (upstream - normed * jnp.mean(upstream * normed, axis=-1, keepdims=True))


def rotary_tables(slot_order):
    half_dim = HEAD_DIM // 2
    inverse = rope_theta ** (-(jnp.arange(half_dim, dtype=f32) * 2.0) / HEAD_DIM)
    angles = slot_order.astype(f32)[..., None] * inverse
    angles = jnp.concatenate([angles, angles], axis=-1)
    return (jnp.cos(angles)[..., None, :], jnp.sin(angles)[..., None, :])


def rotate(operand, cosine_table, sine_table):
    half_dim = operand.shape[-1] // 2
    flipped = jnp.concatenate([-operand[..., half_dim:], operand[..., :half_dim]], axis=-1)
    return operand * cosine_table + flipped * sine_table


def unrotate(upstream, cosine_table, sine_table):
    half_dim = upstream.shape[-1] // 2
    shifted = upstream * sine_table
    flipped = jnp.concatenate([shifted[..., half_dim:], -shifted[..., :half_dim]], axis=-1)
    return upstream * cosine_table + flipped


def masked_scores(query_rows, key_rows, pos):
    scores = jnp.einsum("gqhe,gkhe->ghqk", query_rows, key_rows, preferred_element_type=f32)
    causal = pos[:, None, :, None] >= pos[:, None, None, :]
    return jnp.where(causal, scores, -1e30)


def attend(query_rows, key_rows, value_rows, pos):
    scores = masked_scores(query_rows, key_rows, pos)
    row_max = jnp.max(scores, axis=-1, keepdims=True)
    weights = jnp.exp(scores - row_max)
    row_total = jnp.sum(weights, axis=-1, keepdims=True)
    probabilities = (weights / row_total).astype(bf16)
    attn_mixed = jnp.einsum("ghqk,gkhe->gqhe", probabilities, value_rows, preferred_element_type=f32)
    return attn_mixed.astype(bf16), row_max + jnp.log(row_total)


def attend_back(query_rows, key_rows, value_rows, pos, grad_mixed, log_total):
    scores = masked_scores(query_rows, key_rows, pos)
    probabilities = jnp.exp(scores - log_total)
    grad_probs = jnp.einsum("gqhe,gkhe->ghqk", grad_mixed, value_rows, preferred_element_type=f32)
    grad_value = jnp.einsum(
        "ghqk,gqhe->gkhe", probabilities.astype(bf16), grad_mixed, preferred_element_type=f32
    )
    inner_sum = jnp.sum(grad_probs * probabilities, axis=-1, keepdims=True)
    grad_scores = (probabilities * (grad_probs - inner_sum)).astype(bf16)
    grad_query = jnp.einsum("ghqk,gkhe->gqhe", grad_scores, key_rows, preferred_element_type=f32)
    grad_key = jnp.einsum("ghqk,gqhe->gkhe", grad_scores, query_rows, preferred_element_type=f32)
    return grad_query, grad_key, grad_value


MESH = pl.DeviceIdType.MESH
VMEM_LIMIT = 60 * 1024 * 1024
ANY = pl.BlockSpec(memory_space=pl.ANY)


class Plane:
    def __init__(self):
        f = lax.axis_index("fsdp")
        self.f, self.c, self.chip = f, f % 2, f // 2
        x, y = self.chip % 2, self.chip // 2
        self.qx = self.chip + 1 - 2 * x
        self.qy = self.chip + 2 - 4 * y
        self.qd = self.qx + 2 - 4 * y
        self.fc = f + 1 - 2 * self.c
        self.fx = 2 * self.qx + self.c
        self.fy = 2 * self.qy + self.c
        self.fd = 2 * self.qd + self.c
        self.other = 1 - self.c

    def greet(self):
        barrier = pltpu.get_barrier_semaphore()
        for to in (self.fc, self.fx, self.fy):
            pl.semaphore_signal(barrier, inc=1, device_id={"fsdp": to}, device_id_type=MESH)
        pl.semaphore_wait(barrier, 3)


def remote(src, dst, send, recv, i, to, axis="fsdp"):
    return pltpu.make_async_remote_copy(
        src_ref=src, dst_ref=dst, send_sem=send.at[i], recv_sem=recv.at[i],
        device_id={axis: to}, device_id_type=MESH,
    )


def local(src, dst, sems, i):
    copy = pltpu.make_async_copy(src, dst, sems.at[i])
    copy.start()
    return copy


def nn(a, b):
    return lax.dot_general(a, b, (((1,), (0,)), ((), ())), preferred_element_type=f32)


def nt(a, b):
    return lax.dot_general(a, b, (((1,), (1,)), ((), ())), preferred_element_type=f32)


def gather_phase(at, rows, send, recv, base, on_rows):
    half = rows.shape[1] // 2
    A, B = pl.ds(0, half), pl.ds(half, half)

    def cp(i, slot, part, to):
        ref = rows.at[slot] if part is None else rows.at[slot, part]
        return remote(ref, ref, send, recv, base + i, to)

    fcx, fcy, fcd = 2 * at.qx + at.other, 2 * at.qy + at.other, 2 * at.qd + at.other
    sent = []

    def go(*a):
        c = cp(*a)
        c.start()
        sent.append(c)

    def arrived(i, slot, part, frm):
        cp(i, slot, part, frm).wait_recv()

    go(0, at.f, None, at.fc)
    go(1, at.f, A, at.fx)
    go(3, at.f, B, at.fy)
    go(2, at.f, B, at.fx)
    go(4, at.f, A, at.fy)
    arrived(0, at.fc, None, at.fc)
    on_rows(2 * at.chip, 2)
    arrived(1, at.fx, A, at.fx)
    go(5, at.fx, A, at.fy)
    go(7, at.fx, A, at.fc)
    arrived(3, at.fy, B, at.fy)
    go(6, at.fy, B, at.fx)
    go(8, at.fy, B, at.fc)
    arrived(2, at.fx, B, at.fx)
    go(9, at.fx, B, at.fc)
    arrived(4, at.fy, A, at.fy)
    go(10, at.fy, A, at.fc)
    arrived(7, fcx, A, at.fc)
    arrived(9, fcx, B, at.fc)
    on_rows(2 * at.qx, 2)
    arrived(8, fcy, B, at.fc)
    arrived(10, fcy, A, at.fc)
    on_rows(2 * at.qy, 2)
    arrived(5, at.fd, A, at.fy)
    go(11, at.fd, A, at.fc)
    arrived(6, at.fd, B, at.fx)
    go(12, at.fd, B, at.fc)
    on_rows(at.fd, 1)
    arrived(11, fcd, A, at.fc)
    arrived(12, fcd, B, at.fc)
    on_rows(fcd, 1)
    for c in sent:
        c.wait_send()


GATHER_COPIES = 13
SCATTER_COPIES = 10


def scatter_scratch(R, D):
    return [
        pltpu.VMEM((4, R, D), bf16),
        pltpu.VMEM((4, R, D), bf16),
        pltpu.VMEM((2, R, D), f32),
        pltpu.VMEM((3, R, D), bf16),
        pltpu.VMEM((3, R, D), bf16),
    ]


def scatter_phase(at, partial, bufs, send, recv, base, between=None):
    to_core, from_core, mine, out, inc = bufs
    R, D = to_core.shape[1], to_core.shape[2]
    half = R // 2
    A, B = pl.ds(0, half), pl.ds(half, half)
    tile = 512
    step = 16
    sent = []

    def go(i, src, dst, to):
        c = remote(src, dst, send, recv, base + i, to)
        c.start()
        sent.append(c)

    def arrived(i, dst, frm):
        remote(dst, dst, send, recv, base + i, frm).wait_recv()

    def compute(order, chip, slot):
        @pl.loop(0, D // tile)
        def _(n):
            cols = pl.ds(pl.multiple_of(n * tile, tile), tile)
            got = partial(chip, cols)
            lo, hi = got[:R], got[R:]
            first = at.c == 0
            mine[slot, :, cols] = jnp.where(first, lo, hi)
            to_core[order, :, cols] = jnp.where(first, hi, lo).astype(bf16)

        go(order, to_core.at[order], from_core.at[order], at.fc)

    def chip_sum(order, slot):
        arrived(order, from_core.at[order], at.fc)

        @pl.loop(0, R // step)
        def _(r):
            rows = pl.ds(pl.multiple_of(r * step, step), step)
            out[order, rows, :] = (mine[slot, rows, :] + from_core[order, rows, :].astype(f32)).astype(bf16)

    def relay(order, start, src):
        @pl.loop(0, half // step)
        def _(r):
            rows = pl.ds(pl.multiple_of(start + r * step, step), step)
            out[order, rows, :] = (out[order, rows, :].astype(f32) + inc[src, rows, :].astype(f32)).astype(bf16)

    compute(0, at.qd, 0)
    compute(1, at.qx, 1)
    if between is not None:
        between()
    chip_sum(0, 0)
    go(4, out.at[0, A], inc.at[0, A], at.fx)
    go(5, out.at[0, B], inc.at[0, B], at.fy)
    compute(2, at.qy, 0)
    chip_sum(1, 1)
    go(6, out.at[1, A], inc.at[1, A], at.fx)
    compute(3, at.chip, 1)
    chip_sum(2, 0)
    go(8, out.at[2, B], inc.at[2, B], at.fy)
    arrived(5, inc.at[0, B], at.fy)
    relay(1, half, 0)
    go(7, out.at[1, B], inc.at[1, B], at.fx)
    arrived(4, inc.at[0, A], at.fx)
    relay(2, 0, 0)
    go(9, out.at[2, A], inc.at[2, A], at.fy)
    arrived(3, from_core.at[3], at.fc)
    arrived(6, inc.at[1, A], at.fx)
    arrived(8, inc.at[2, B], at.fy)
    arrived(7, inc.at[1, B], at.fx)
    arrived(9, inc.at[2, A], at.fy)
    for c in sent:
        c.wait_send()

    def total(rows):
        return (
            mine[1, rows, :]
            + from_core[3, rows, :].astype(f32)
            + inc[1, rows, :].astype(f32)
            + inc[2, rows, :].astype(f32)
        )

    return total


def rms(v):
    return lax.rsqrt(jnp.mean(v * v, axis=-1, keepdims=True) + epsilon)


def back(weighted, normed, scale):
    return scale * (weighted - normed * jnp.mean(weighted * normed, axis=-1, keepdims=True))


def row_loop(R, body, step=16):
    @pl.loop(0, R // step)
    def _(r):
        body(pl.ds(pl.multiple_of(r * step, step), step))


def pair_loop(rows, w_cols, total_cols, body):
    @pl.loop(0, total_cols // w_cols)
    def _(t):
        body(pl.ds(pl.multiple_of(t * w_cols, w_cols), w_cols))


class Stores:
    def __init__(self, sems):
        self.sems, self.steps, self.n = sems, [], 0

    def slot(self):
        if len(self.steps) >= 2:
            for c in self.steps[-2]:
                c.wait()
            self.steps[-2] = []
        return len(self.steps) % 2

    def put(self, pairs):
        done = []
        for src, dst in pairs:
            done.append(local(src, dst, self.sems, self.n))
            self.n += 1
        self.steps.append(done)

    def finish(self):
        for step in self.steps:
            for c in step:
                c.wait()


class Moving:
    def __init__(self, at, C, mine, stage, landing, lsem, base, send, recv):
        self.at, self.C, self.mine, self.stage, self.landing = at, C, mine, stage, landing
        self.lsem, self.base, self.send, self.recv = lsem, base, send, recv
        self.z = lax.axis_index("ctx")
        self.piece = mine.shape[0] // C
        self.sent = []

    def greet(self, barrier):
        at, C = self.at, self.C
        for k in range(1, C):
            pl.semaphore_signal(barrier, inc=1, device_id={"ctx": (self.z + k) % C}, device_id_type=MESH)
            pl.semaphore_signal(
                barrier, inc=1, device_id={"fsdp": 2 * ((at.chip + k) % C) + at.c}, device_id_type=MESH
            )

    def first(self):
        at, C, piece = self.at, self.C, self.piece
        for k in range(1, C):
            j = (at.chip + k) % C
            src = self.mine.at[pl.ds(j * piece, piece)]
            c = remote(src, self.stage.at[at.chip], self.send, self.recv, k, 2 * j + at.c)
            c.start()
            self.sent.append(c)
        src = self.mine.at[pl.ds(at.chip * piece, piece)]
        self.keep = local(src, self.stage.at[at.chip], self.lsem, self.base)

    def land(self, layer):
        return self.landing.at[pl.ds(layer * self.piece, self.piece)]

    def second(self):
        at, C, z = self.at, self.C, self.z
        self.keep.wait()
        for k in range(1, C):
            frm = (at.chip - k + C) % C
            remote(self.stage.at[frm], self.stage.at[frm], self.send, self.recv, k, 2 * frm + at.c).wait_recv()
        for k in range(1, C):
            to = (z + k) % C
            c = remote(self.stage.at[to], self.land(z), self.send, self.recv, C + k, to, "ctx")
            c.start()
            self.sent.append(c)
        self.keep = local(self.stage.at[z], self.land(z), self.lsem, self.base + 1)

    def finish(self):
        C, z = self.C, self.z
        self.keep.wait()
        for k in range(1, C):
            frm = (z - k + C) % C
            remote(self.land(frm), self.land(frm), self.send, self.recv, C + k, frm, "ctx").wait_recv()
        for c in self.sent:
            c.wait_send()


def enter_kernel(C, x_ref, own_ref, all_ref, stage, mine, rows, lsem, osem, send, recv, tsend, trecv):
    at = Plane()
    load = local(x_ref, mine, lsem, 0)
    moving = Moving(at, C, mine, stage, rows.at[at.f], lsem, 1, tsend, trecv)
    barrier = pltpu.get_barrier_semaphore()
    moving.greet(barrier)
    pl.semaphore_signal(barrier, inc=1, device_id={"fsdp": at.fc}, device_id_type=MESH)
    pl.semaphore_wait(barrier, 2 * (C - 1) + 1)
    load.wait()
    moving.first()
    moving.second()
    moving.finish()
    save = local(rows.at[at.f], own_ref, lsem, 3)
    stores = []

    def on_rows(first, count):
        stores.append(local(rows.at[pl.ds(first, count)], all_ref.at[pl.ds(first, count)], osem, len(stores)))

    gather_phase(at, rows, send, recv, 0, on_rows)
    save.wait()
    for c in stores:
        c.wait()


def enter_call(C, F, x):
    R, D = x.shape
    return pl.pallas_call(
        functools.partial(enter_kernel, C),
        out_shape=[jax.ShapeDtypeStruct((R, D), bf16), jax.ShapeDtypeStruct((F, R, D), bf16)],
        in_specs=[ANY],
        out_specs=[ANY] * 2,
        scratch_shapes=[
            pltpu.VMEM((C, R // C, D), bf16),
            pltpu.VMEM((R, D), bf16),
            pltpu.VMEM((F, R, D), bf16),
            dma(4), dma(5), dma(GATHER_COPIES), dma(GATHER_COPIES), dma(2 * C), dma(2 * C),
        ],
        compiler_params=params(1),
        cost_estimate=cost(70),
    )(x)


def qkv_kernel(all_ref, w_ref, proj_ref, st_ref, rows, w, acc, st, lsem, osem, ssend, srecv):
    at = Plane()
    F, R = rows.shape[0], rows.shape[1]
    e = w.shape[1] // 3
    m = 2 * R
    loads = [local(w_ref, w, lsem, 0)] + [
        local(all_ref.at[pl.ds(2 * p, 2)], rows.at[pl.ds(2 * p, 2)], lsem, 1 + p) for p in range(F // 2)
    ]
    barrier = pltpu.get_barrier_semaphore()
    for k in range(1, F):
        pl.semaphore_signal(barrier, inc=1, device_id={"fsdp": (at.f + k) % F}, device_id_type=MESH)
    pl.semaphore_wait(barrier, F - 1)
    loads[0].wait()
    stores = Stores(osem)
    for p in range(F // 2):
        loads[1 + p].wait()
        s = stores.slot()

        def tile(c):
            acc[s, :, c] = nn(rows[pl.ds(2 * p, 2)].reshape(m, rows.shape[2]), w[:, c])

        pair_loop(m, 256, w.shape[1], tile)
        q, k = acc[s, :, :e], acc[s, :, e : 2 * e]
        st[at.f, :, pl.ds(p * m, m)] = row_sums(q * q, k * k)
        stores.put([(acc.at[s], proj_ref.at[pl.ds(p * m, m)])])
    share_stats(at, F, st, ssend, srecv, 0)
    local(st, st_ref, lsem, 1 + F // 2).wait()
    stores.finish()


def params(number):
    return pltpu.CompilerParams(
        collective_id=number, has_side_effects=True, vmem_limit_bytes=VMEM_LIMIT
    )


def cost(us):
    return pl.CostEstimate(flops=int(us * 1e9), bytes_accessed=2**20, transcendentals=0)


def dma(n):
    return pltpu.SemaphoreType.DMA((n,))


def qkv_call(F, rows, w):
    _, R, D = rows.shape
    n = w.shape[1]
    return pl.pallas_call(
        qkv_kernel,
        out_shape=[
            jax.ShapeDtypeStruct((F * R, n), f32),
            jax.ShapeDtypeStruct((F, 8, F * R), f32),
        ],
        in_specs=[ANY] * 2,
        out_specs=[ANY] * 2,
        scratch_shapes=[
            pltpu.VMEM((F, R, D), bf16),
            pltpu.VMEM((D, n), bf16),
            pltpu.VMEM((2, 2 * R, n), f32),
            pltpu.VMEM((F, 8, F * R), f32),
            dma(6), dma(4), dma(F), dma(F),
        ],
        compiler_params=params(7),
        cost_estimate=cost(22),
    )(rows, w)


def out_kernel(
    mixed_ref, wo_ref, x_ref, gain_ref, hid_ref, ao_ref, in_ref,
    mixed, wo, x, gain, hid, ao, inp, b0, b1, b2, b3, b4, lsem, send, recv,
):
    at = Plane()
    pairs = [(mixed_ref, mixed), (wo_ref, wo), (x_ref, x), (gain_ref, gain)]
    loads = [local(s, d, lsem, i) for i, (s, d) in enumerate(pairs)]
    at.greet()
    R = x.shape[0]
    loads[0].wait()
    loads[1].wait()

    def partial(chip, cols):
        return nt(mixed[pl.ds(pl.multiple_of(chip * 2 * R, 2 * R), 2 * R), :], wo[cols, :])

    total = scatter_phase(at, partial, (b0, b1, b2, b3, b4), send, recv, 0)
    loads[2].wait()
    loads[3].wait()

    def finish(r):
        out = total(r)
        ao[r, :] = out
        hidden_in = x[r, :].astype(f32) + out * rms(out) * gain[...]
        hid[r, :] = hidden_in
        inp[r, :] = hidden_in.astype(bf16)

    row_loop(R, finish)
    for c in [local(ao, ao_ref, lsem, 4), local(hid, hid_ref, lsem, 5), local(inp, in_ref, lsem, 6)]:
        c.wait()


def out_call(F, mixed, wo, x, gain):
    R, D = x.shape
    e = wo.shape[1]
    return pl.pallas_call(
        out_kernel,
        out_shape=[
            jax.ShapeDtypeStruct((R, D), f32),
            jax.ShapeDtypeStruct((R, D), f32),
            jax.ShapeDtypeStruct((R, D), bf16),
        ],
        in_specs=[ANY] * 4,
        out_specs=[ANY] * 3,
        scratch_shapes=[
            pltpu.VMEM((F * R, e), bf16),
            pltpu.VMEM((D, e), bf16),
            pltpu.VMEM((R, D), bf16),
            pltpu.VMEM((1, D), f32),
            pltpu.VMEM((R, D), f32),
            pltpu.VMEM((R, D), f32),
            pltpu.VMEM((R, D), bf16),
        ]
        + scatter_scratch(R, D)
        + [dma(7), dma(SCATTER_COPIES), dma(SCATTER_COPIES)],
        compiler_params=params(8),
        cost_estimate=cost(46),
    )(mixed, wo, x, gain)


def up_kernel(
    in_ref, wg_ref, wu_ref, all_ref, act_ref, der_ref, h_ref,
    w, rows, act, der, h, lsem, osem, send, recv,
):
    at = Plane()
    own = local(in_ref, rows.at[at.f], lsem, 0)
    n = act.shape[2]
    loads = [local(wg_ref, w.at[:, pl.ds(0, n)], lsem, 1), local(wu_ref, w.at[:, pl.ds(n, n)], lsem, 2)]
    width = 256
    at.greet()
    R = rows.shape[1]
    own.wait()
    waited = []
    stores = Stores(osem)

    def on_rows(first, count):
        s = stores.slot()
        m = count * R
        if not waited:
            for c in loads:
                c.wait()
            waited.append(1)

        @pl.loop(0, n // width)
        def _(t):
            c = pl.ds(pl.multiple_of(t * width, width), width)
            lhs = rows[pl.ds(first, count)].reshape(m, rows.shape[2])
            g = nn(lhs, w[:, c])
            u = nn(lhs, w[:, pl.ds(pl.multiple_of(n + t * width, width), width)])
            sig = jax.nn.sigmoid(g)
            a = g * sig
            act[s, pl.ds(0, m), c] = a.astype(bf16)
            der[s, pl.ds(0, m), c] = (u * (sig * (1.0 + g * (1.0 - sig)))).astype(bf16)
            h[s, pl.ds(0, m), c] = (a * u).astype(bf16)

        start = pl.multiple_of(first * R, R)
        stores.put(
            [
                (act.at[s, pl.ds(0, m)], act_ref.at[pl.ds(start, m)]),
                (der.at[s, pl.ds(0, m)], der_ref.at[pl.ds(start, m)]),
                (h.at[s, pl.ds(0, m)], h_ref.at[pl.ds(start, m)]),
                (rows.at[pl.ds(first, count)], all_ref.at[pl.ds(first, count)]),
            ]
        )

    gather_phase(at, rows, send, recv, 0, on_rows)
    stores.finish()


def up_call(F, inp, wg, wu):
    R, D = inp.shape
    n = wg.shape[1]
    T = F * R
    wide = jax.ShapeDtypeStruct((T, n), bf16)
    return pl.pallas_call(
        up_kernel,
        out_shape=[jax.ShapeDtypeStruct((F, R, D), bf16), wide, wide, wide],
        in_specs=[ANY] * 3,
        out_specs=[ANY] * 4,
        scratch_shapes=[
            pltpu.VMEM((D, 2 * n), bf16),
            pltpu.VMEM((F, R, D), bf16),
            pltpu.VMEM((2, 2 * R, n), bf16),
            pltpu.VMEM((2, 2 * R, n), bf16),
            pltpu.VMEM((2, 2 * R, n), bf16),
        ]
        + [dma(3), dma(20), dma(GATHER_COPIES), dma(GATHER_COPIES)],
        compiler_params=params(2),
        cost_estimate=cost(46),
    )(inp, wg, wu)


def down_kernel(
    C, h_ref, wd_ref, hid_ref, cot_ref, gain_ref, act_ref, der_ref,
    res_ref, gg_ref, all_ref, grad_ref, own_ref,
    h, wd, hid, mine, gain, act, der, res, gacc, rows, grad, cot, stage, b0, b1, b2, b3, b4,
    lsem, osem, asem, send, recv, tsend, trecv,
):
    at = Plane()
    loads = [
        local(s, d, lsem, i)
        for i, (s, d) in enumerate(
            [(cot_ref, mine), (h_ref, h), (wd_ref, wd), (hid_ref, hid), (gain_ref, gain)]
        )
    ]
    moving = Moving(at, C, mine, stage, cot, lsem, 5, tsend, trecv)
    barrier = pltpu.get_barrier_semaphore()
    moving.greet(barrier)
    pl.semaphore_signal(barrier, inc=1, device_id={"fsdp": at.fc}, device_id_type=MESH)
    pl.semaphore_wait(barrier, 2 * (C - 1) + 1)
    R = rows.shape[1]
    n = wd.shape[1]
    loads[0].wait()
    moving.first()
    loads[1].wait()
    loads[2].wait()

    def partial(chip, cols):
        return nt(h[pl.ds(pl.multiple_of(chip * 2 * R, 2 * R), 2 * R), :], wd[cols, :])

    total = scatter_phase(at, partial, (b0, b1, b2, b3, b4), send, recv, 0, moving.second)
    for c in loads[3:]:
        c.wait()
    moving.finish()
    gacc[...] = jnp.zeros_like(gacc)

    def finish(r):
        out = total(r)
        scale = rms(out)
        hat = out * scale
        res[r, :] = (hid[r, :] + hat * gain[...]).astype(bf16)
        g = cot[r, :].astype(f32)
        gacc[...] += jnp.sum(g * hat, axis=0, keepdims=True)
        rows[at.f, r, :] = back(g * gain[...], hat, scale).astype(bf16)

    row_loop(R, finish)
    saves = [local(res, res_ref, lsem, 7), local(gacc, gg_ref, lsem, 8), local(cot, own_ref, lsem, 9)]
    stores = Stores(osem)

    def on_rows(first, count):
        s = stores.slot()
        m = count * R
        start = pl.multiple_of(first * R, R)
        k = len(stores.steps)
        la = local(act_ref.at[pl.ds(start, m)], act.at[s, pl.ds(0, m)], asem, 2 * k)
        ld = local(der_ref.at[pl.ds(start, m)], der.at[s, pl.ds(0, m)], asem, 2 * k + 1)
        la.wait()
        ld.wait()

        width = 512

        @pl.loop(0, n // width)
        def _(t):
            c = pl.ds(pl.multiple_of(t * width, width), width)
            up = pl.ds(pl.multiple_of(n + t * width, width), width)
            gh = nn(rows[pl.ds(first, count)].reshape(m, rows.shape[2]), wd[:, c])
            grad[s, pl.ds(0, m), up] = (gh * act[s, pl.ds(0, m), c].astype(f32)).astype(bf16)
            grad[s, pl.ds(0, m), c] = (gh * der[s, pl.ds(0, m), c].astype(f32)).astype(bf16)

        stores.put(
            [
                (grad.at[s, pl.ds(0, m)], grad_ref.at[pl.ds(start, m)]),
                (rows.at[pl.ds(first, count)], all_ref.at[pl.ds(first, count)]),
            ]
        )

    gather_phase(at, rows, send, recv, SCATTER_COPIES, on_rows)
    for s in saves:
        s.wait()
    stores.finish()


def down_call(C, F, h, wd, hid, cot, gain, act, der):
    R, D = hid.shape
    n = wd.shape[1]
    T = F * R
    copies = SCATTER_COPIES + GATHER_COPIES
    one = jax.ShapeDtypeStruct((R, D), bf16)
    return pl.pallas_call(
        functools.partial(down_kernel, C),
        out_shape=[
            one,
            jax.ShapeDtypeStruct((1, D), f32),
            jax.ShapeDtypeStruct((F, R, D), bf16),
            jax.ShapeDtypeStruct((T, 2 * n), bf16),
            one,
        ],
        in_specs=[ANY] * 7,
        out_specs=[ANY] * 5,
        scratch_shapes=[
            pltpu.VMEM((T, n), bf16),
            pltpu.VMEM((D, n), bf16),
            pltpu.VMEM((R, D), f32),
            pltpu.VMEM((R, D), bf16),
            pltpu.VMEM((1, D), f32),
            pltpu.VMEM((2, 2 * R, n), bf16),
            pltpu.VMEM((2, 2 * R, n), bf16),
            pltpu.VMEM((R, D), bf16),
            pltpu.VMEM((1, D), f32),
            pltpu.VMEM((F, R, D), bf16),
            pltpu.VMEM((2, 2 * R, 2 * n), bf16),
            pltpu.VMEM((R, D), bf16),
            pltpu.VMEM((C, R // C, D), bf16),
        ]
        + scatter_scratch(R, D)
        + [dma(10), dma(15), dma(10), dma(copies), dma(copies), dma(2 * C), dma(2 * C)],
        compiler_params=params(3),
        cost_estimate=cost(95),
    )(h, wd, hid, cot, gain, act, der)


def mid_kernel(
    grad_ref, wg_ref, wu_ref, cot_ref, ao_ref, gain_ref, wo_ref,
    res_ref, gg_ref, all_ref, gm_ref,
    grad, w, cot, ao, gain, wo, res, gacc, rows, gm, b0, b1, b2, b3, b4,
    lsem, osem, send, recv,
):
    at = Plane()
    n = w.shape[1] // 2
    pairs = [
        (grad_ref, grad), (wg_ref, w.at[:, pl.ds(0, n)]), (wu_ref, w.at[:, pl.ds(n, n)]),
        (cot_ref, cot), (ao_ref, ao), (gain_ref, gain), (wo_ref, wo),
    ]
    loads = [local(s, d, lsem, i) for i, (s, d) in enumerate(pairs)]
    at.greet()
    R = rows.shape[1]
    for c in loads[:3]:
        c.wait()

    def partial(chip, cols):
        return nt(grad[pl.ds(pl.multiple_of(chip * 2 * R, 2 * R), 2 * R), :], w[cols, :])

    total = scatter_phase(at, partial, (b0, b1, b2, b3, b4), send, recv, 0)
    for c in loads[3:]:
        c.wait()
    gacc[...] = jnp.zeros_like(gacc)

    def finish(r):
        resid = cot[r, :].astype(f32) + total(r)
        res[r, :] = resid
        out = ao[r, :]
        scale = rms(out)
        hat = out * scale
        gacc[...] += jnp.sum(resid * hat, axis=0, keepdims=True)
        rows[at.f, r, :] = back(resid * gain[...], hat, scale).astype(bf16)

    row_loop(R, finish)
    saves = [local(res, res_ref, lsem, 8), local(gacc, gg_ref, lsem, 9)]
    stores = Stores(osem)

    def on_rows(first, count):
        s = stores.slot()
        m = count * R
        start = pl.multiple_of(first * R, R)
        lhs = rows[pl.ds(first, count)].reshape(m, rows.shape[2])
        gm[s, pl.ds(0, m), :] = nn(lhs, wo[...]).astype(bf16)
        stores.put(
            [
                (gm.at[s, pl.ds(0, m)], gm_ref.at[pl.ds(start, m)]),
                (rows.at[pl.ds(first, count)], all_ref.at[pl.ds(first, count)]),
            ]
        )

    gather_phase(at, rows, send, recv, SCATTER_COPIES, on_rows)
    for s in saves:
        s.wait()
    stores.finish()


def mid_call(F, grad, wg, wu, cot, ao, gain, wo):
    R, D = cot.shape
    n, e = 2 * wg.shape[1], wo.shape[1]
    T = F * R
    copies = SCATTER_COPIES + GATHER_COPIES
    return pl.pallas_call(
        mid_kernel,
        out_shape=[
            jax.ShapeDtypeStruct((R, D), f32),
            jax.ShapeDtypeStruct((1, D), f32),
            jax.ShapeDtypeStruct((F, R, D), bf16),
            jax.ShapeDtypeStruct((T, e), bf16),
        ],
        in_specs=[ANY] * 7,
        out_specs=[ANY] * 4,
        scratch_shapes=[
            pltpu.VMEM((T, n), bf16),
            pltpu.VMEM((D, n), bf16),
            pltpu.VMEM((R, D), bf16),
            pltpu.VMEM((R, D), f32),
            pltpu.VMEM((1, D), f32),
            pltpu.VMEM((D, e), bf16),
            pltpu.VMEM((R, D), f32),
            pltpu.VMEM((1, D), f32),
            pltpu.VMEM((F, R, D), bf16),
            pltpu.VMEM((2, 2 * R, e), bf16),
        ]
        + scatter_scratch(R, D)
        + [dma(10), dma(10), dma(copies), dma(copies)],
        compiler_params=params(4),
        cost_estimate=cost(92),
    )(grad, wg, wu, cot, ao, gain, wo)


def last_kernel(
    width, q_ref, k_ref, v_ref, proj_ref, st_ref, in_ref, w_ref, res_ref, gain_ref,
    out_ref, gp_ref, gsum_ref,
    q, k, proj, st, ins, gains, gsum, gp, w, res, out, b0, b1, b2, b3, b4,
    lsem, send, recv, ssend, srecv, gsend, grecv,
):
    at = Plane()
    F, T = st.shape[0], st.shape[2]
    e = q.shape[1]
    R = res.shape[0]
    pairs = [
        (in_ref, ins.at[at.f]), (st_ref, st), (q_ref, q), (k_ref, k),
        (v_ref, gp.at[:, pl.ds(2 * e, e)]), (proj_ref.at[:, pl.ds(0, 2 * e)], proj), (w_ref, w), (res_ref, res),
        (gain_ref, gains.at[at.f]),
    ]
    loads = [local(s, d, lsem, i) for i, (s, d) in enumerate(pairs)]
    barrier = pltpu.get_barrier_semaphore()
    for s in range(1, F):
        pl.semaphore_signal(barrier, inc=1, device_id={"fsdp": (at.f + s) % F}, device_id_type=MESH)
    pl.semaphore_wait(barrier, F - 1)
    loads[0].wait()
    share_stats(at, F, ins, ssend, srecv, 0)
    for c in loads[1:6]:
        c.wait()
    step = 256

    @pl.loop(0, T // step)
    def _(t):
        r = pl.ds(pl.multiple_of(t * step, step), step)
        sums = jnp.sum(st[:, :, r], axis=0)
        inner = jnp.sum(ins[:, :, r], axis=0) / width
        for row, grad in ((0, q), (1, k)):
            scale = lax.rsqrt(column(sums[row : row + 1], HEAD_DIM) / width + epsilon)
            mean = column(inner[row : row + 1], HEAD_DIM)
            for h in range(e // HEAD_DIM):
                hat = proj[r, row * e + h * HEAD_DIM : row * e + (h + 1) * HEAD_DIM] * scale
                got = scale * (grad[r, h * HEAD_DIM : (h + 1) * HEAD_DIM] - hat * mean)
                gp[r, row * e + h * HEAD_DIM : row * e + (h + 1) * HEAD_DIM] = got.astype(bf16)

    save = local(gp, gp_ref, lsem, 9)
    loads[6].wait()

    def partial(chip, cols):
        return nt(gp[pl.ds(pl.multiple_of(chip * 2 * R, 2 * R), 2 * R), :], w[cols, :])

    total = scatter_phase(at, partial, (b0, b1, b2, b3, b4), send, recv, 0)
    loads[7].wait()

    def finish(r):
        out[r, :] = (res[r, :] + total(r)).astype(bf16)

    row_loop(R, finish)
    store = local(out, out_ref, lsem, 10)
    loads[8].wait()
    share_stats(at, F, gains, gsend, grecv, 0)
    gsum[...] = jnp.sum(gains[...], axis=0)
    local(gsum, gsum_ref, lsem, 11).wait()
    store.wait()
    save.wait()


def last_call(F, wq, wk, gv, proj, st, ins, w, res, gains):
    R, D = res.shape
    n = w.shape[1]
    T, e = F * R, n // 3
    return pl.pallas_call(
        functools.partial(last_kernel, D),
        out_shape=[
            jax.ShapeDtypeStruct((R, D), bf16),
            jax.ShapeDtypeStruct((T, n), bf16),
            jax.ShapeDtypeStruct((8, D), f32),
        ],
        in_specs=[ANY] * 9,
        out_specs=[ANY] * 3,
        scratch_shapes=[
            pltpu.VMEM((T, e), f32),
            pltpu.VMEM((T, e), f32),
            pltpu.VMEM((T, 2 * e), f32),
            pltpu.VMEM((F, 8, T), f32),
            pltpu.VMEM((F, 8, T), f32),
            pltpu.VMEM((F, 8, D), f32),
            pltpu.VMEM((8, D), f32),
            pltpu.VMEM((T, n), bf16),
            pltpu.VMEM((D, n), bf16),
            pltpu.VMEM((R, D), f32),
            pltpu.VMEM((R, D), bf16),
        ]
        + scatter_scratch(R, D)
        + [dma(12), dma(SCATTER_COPIES), dma(SCATTER_COPIES), dma(F), dma(F), dma(F), dma(F)],
        compiler_params=params(5),
        cost_estimate=cost(55),
    )(wq, wk, gv, proj, st, ins, w, res, gains)


def tn(a, b):
    return lax.dot_general(a, b, (((0,), (0,)), ((), ())), preferred_element_type=f32)


def grad_kernel(*refs):
    out = refs[-1]
    start = 0
    for x_ref, dy_ref in zip(refs[:-1:2], refs[1:-1:2]):
        got = tn(x_ref[...], dy_ref[...]).astype(bf16)
        units = dy_ref.shape[1] // out.shape[-1]
        for b in range(units):
            out[(start + b,) + (0,) * (len(out.shape) - 3)] = got[:, b * out.shape[-1] : (b + 1) * out.shape[-1]]
        start += units


def grad_call(pairs, units, cols, groups):
    T, D = pairs[0][0].shape
    tile = 512
    specs, args = [], []
    for x, dy in pairs:
        specs += [
            pl.BlockSpec((T, tile), lambda g, d: (0, d)),
            pl.BlockSpec((T, dy.shape[1] // groups), lambda g, d: (0, g)),
        ]
        args += [x, dy]
    return pl.pallas_call(
        grad_kernel,
        out_shape=jax.ShapeDtypeStruct((units, groups, D, cols), bf16),
        grid=(groups, D // tile),
        in_specs=specs,
        out_specs=pl.BlockSpec((units, 1, tile, cols), lambda g, d: (0, g, d, 0)),
        compiler_params=pltpu.CompilerParams(vmem_limit_bytes=VMEM_LIMIT),
        cost_estimate=cost(12 * groups),
    )(*args)


def share_stats(at, F, st, send, recv, base):
    sent = []
    for k in range(1, F):
        to = (at.f + k) % F
        c = remote(st.at[at.f], st.at[at.f], send, recv, base + k, to)
        c.start()
        sent.append(c)
    for k in range(1, F):
        frm = (at.f - k + F) % F
        remote(st.at[frm], st.at[frm], send, recv, base + k, frm).wait_recv()
    for c in sent:
        c.wait_send()


def row_sums(a, b):
    r = lax.broadcasted_iota(jnp.int32, (8, a.shape[1]), 0)
    one, two = (r == 0).astype(f32), (r == 1).astype(f32)

    def half(sel, v):
        return lax.dot_general(
            sel, v, (((1,), (1,)), ((), ())), preferred_element_type=f32, precision=lax.Precision.HIGHEST
        )

    return half(one, a) + half(two, b)


def column(row, lanes):
    return jnp.broadcast_to(row, (lanes, row.shape[1])).T


def turn(v, cos, sin):
    return v * cos + pltpu.roll(v, HEAD_DIM // 2, 1) * sin


def seq_columns(st, c, chips, R):
    return jnp.concatenate([st[:, pl.ds(pl.multiple_of((2 * j + c) * R, R), R)] for j in range(chips)], axis=1)


def attend_kernel(width, q_ref, k_ref, v_ref, st_ref, gq_ref, gk_ref, cos_ref, sin_ref, pos_ref, posc_ref, mix_ref, qr_ref, kr_ref, lse_ref):
    c = pl.program_id(0)
    chips, R = q_ref.shape[0], q_ref.shape[2]
    L = chips * R
    sums = jnp.sum(seq_columns_all(st_ref, c, chips, R), axis=0)
    cos, sin = cos_ref[0], sin_ref[0]

    def norm_turn(ref, row, gain):
        scale = lax.rsqrt(column(sums[row : row + 1], HEAD_DIM) / width + epsilon)
        return turn(ref[...].reshape(L, HEAD_DIM) * scale * gain[...], cos, sin)

    qr = (norm_turn(q_ref, 0, gq_ref) * HEAD_DIM ** (-0.5)).astype(bf16)
    kr = norm_turn(k_ref, 1, gk_ref).astype(bf16)
    v = v_ref[...].reshape(L, HEAD_DIM).astype(bf16)
    qr_ref[...] = qr.reshape(qr_ref.shape)
    kr_ref[...] = kr.reshape(kr_ref.shape)
    pos = pos_ref[0]
    for t in range(chips):
        rows = slice(t * R, (t + 1) * R)
        s = nt(qr[rows], kr)
        s = jnp.where(posc_ref[0, rows, :1] >= pos, s, -1e30)
        top = jnp.max(s, axis=-1, keepdims=True)
        e = jnp.exp(s - top)
        total = jnp.sum(e, axis=-1, keepdims=True)
        p = (e * (1.0 / total)).astype(bf16)
        mix_ref[t, 0] = nn(p, v).astype(bf16)
        lse_ref[0, 0, rows, :] = jnp.broadcast_to(top + jnp.log(total), (R, HEAD_DIM))


def seq_columns_all(st_ref, c, chips, R):
    return jnp.concatenate(
        [st_ref[:, :, pl.ds(pl.multiple_of((2 * j + c) * R, R), R)] for j in range(chips)], axis=2
    )


def attend_specs(chips, R, heads, F, L):
    def at(offset):
        return pl.BlockSpec((chips, 1, R, HEAD_DIM), lambda c, h: (0, c, 0, offset + h))

    gain = pl.BlockSpec((1, HEAD_DIM), lambda c, h: (0, h))
    table = pl.BlockSpec((1, L, HEAD_DIM), lambda c, h: (c, 0, 0))
    stats = pl.BlockSpec((F, 8, F * R), lambda c, h: (0, 0, 0))
    posr = pl.BlockSpec((1, 1, L), lambda c, h: (c, 0, 0))
    lse = pl.BlockSpec((1, 1, L, HEAD_DIM), lambda c, h: (c, h, 0, 0))
    return at, gain, table, stats, posr, lse


def attend_call(F, proj, st, gq, gk, cos, sin, pos, posc):
    R = proj.shape[0] // F
    e = proj.shape[1] // 3
    heads, chips = e // HEAD_DIM, F // 2
    L = chips * R
    at, gain, table, stats, posr, lse = attend_specs(chips, R, heads, F, L)
    view = proj.reshape(chips, 2, R, 3 * e)
    flat = jax.ShapeDtypeStruct((chips, 2, R, e), bf16)
    out = pl.pallas_call(
        functools.partial(attend_kernel, heads * HEAD_DIM * F),
        out_shape=[flat, flat, flat, jax.ShapeDtypeStruct((2, heads, L, HEAD_DIM), f32)],
        grid=(2, heads),
        in_specs=[at(0), at(heads), at(2 * heads), stats, gain, gain, table, table, posr, table],
        out_specs=[at(0), at(0), at(0), lse],
        compiler_params=pltpu.CompilerParams(vmem_limit_bytes=VMEM_LIMIT),
        cost_estimate=cost(15),
    )(view, view, view, st, gq, gk, cos, sin, pos, posc)
    return out


def attend_back_kernel(
    width, q_ref, k_ref, v_ref, qr_ref, kr_ref, gm_ref, lse_ref, st_ref, gq_ref, gk_ref, cos_ref, sin_ref, pos_ref, posc_ref,
    wq_ref, wk_ref, gv_ref, in_ref, gg_ref, dk, dv, dq,
):
    c = pl.program_id(0)
    chips, R = q_ref.shape[0], q_ref.shape[2]
    L = chips * R
    kr = kr_ref[...].reshape(L, HEAD_DIM)
    v = v_ref[...].reshape(L, HEAD_DIM).astype(bf16)
    pos = pos_ref[0]
    dk[...] = jnp.zeros_like(dk)
    dv[...] = jnp.zeros_like(dv)
    for t in range(chips):
        rows = slice(t * R, (t + 1) * R)
        qt, gm = qr_ref[t, 0], gm_ref[t, 0]
        s = nt(qt, kr)
        s = jnp.where(posc_ref[0, rows, :1] >= pos, s, -1e30)
        p = jnp.exp(s - lse_ref[0, 0, rows, :1])
        dp = nt(gm, v)
        dv[...] += lax.dot_general(p.astype(bf16), gm, (((0,), (0,)), ((), ())), preferred_element_type=f32)
        inner = jnp.sum(dp * p, axis=-1, keepdims=True)
        ds = (p * (dp - inner)).astype(bf16)
        dq[rows, :] = nn(ds, kr)
        dk[...] += lax.dot_general(ds, qt, (((0,), (0,)), ((), ())), preferred_element_type=f32)
    gv_ref[...] = dv[...].astype(bf16).reshape(gv_ref.shape)
    sums = jnp.sum(seq_columns_all(st_ref, c, chips, R), axis=0)
    cos, sin = cos_ref[0], sin_ref[0]

    def finish(grad, ref, row, gain, out):
        norm = turn(grad, cos, -sin)
        hat = ref[...].reshape(L, HEAD_DIM) * lax.rsqrt(column(sums[row : row + 1], HEAD_DIM) / width + epsilon)
        gg_ref[0, 0, row : row + 1, :] = jnp.sum(norm * hat, axis=0, keepdims=True)
        weighted = norm * gain[...]
        out[...] = weighted.reshape(out.shape)
        return weighted * hat

    gg_ref[...] = jnp.zeros_like(gg_ref)
    in_ref[0, 0] = row_sums(
        finish(dq[...] * HEAD_DIM ** (-0.5), q_ref, 0, gq_ref, wq_ref), finish(dk[...], k_ref, 1, gk_ref, wk_ref)
    )


def attend_back_call(F, proj, qr, kr, gm, lse_in, st, gq, gk, cos, sin, pos, posc):
    R = proj.shape[0] // F
    e = proj.shape[1] // 3
    heads, chips = e // HEAD_DIM, F // 2
    L = chips * R
    at, gain, table, stats, posr, lse = attend_specs(chips, R, heads, F, L)
    view = proj.reshape(chips, 2, R, 3 * e)
    flat = (chips, 2, R, e)
    small = pl.BlockSpec((1, 1, 8, L), lambda c, h: (c, h, 0, 0))
    tiny = pl.BlockSpec((1, 1, 8, HEAD_DIM), lambda c, h: (c, h, 0, 0))
    wide = jax.ShapeDtypeStruct(flat, f32)
    return pl.pallas_call(
        functools.partial(attend_back_kernel, heads * HEAD_DIM * F),
        out_shape=[
            wide, wide, jax.ShapeDtypeStruct(flat, bf16),
            jax.ShapeDtypeStruct((2, heads, 8, L), f32),
            jax.ShapeDtypeStruct((2, heads, 8, HEAD_DIM), f32),
        ],
        grid=(2, heads),
        in_specs=[
            at(0), at(heads), at(2 * heads), at(0), at(0), at(0), lse, stats, gain, gain, table, table, posr, table,
        ],
        out_specs=[at(0), at(0), at(0), small, tiny],
        scratch_shapes=[pltpu.VMEM((L, HEAD_DIM), f32)] * 3,
        compiler_params=pltpu.CompilerParams(vmem_limit_bytes=VMEM_LIMIT),
        cost_estimate=cost(35),
    )(view, view, view, qr, kr, gm.reshape(flat), lse_in, st, gq, gk, cos, sin, pos, posc)


def newton_kernel(
    C, m_ref, rows_ref, gain_ref, out_ref, home_ref, gsum_ref,
    v, gram, y, yf, stat, stage, gains, gsum,
    lsem, osem, vsend, vrecv, ysend, yrecv, ssend, srecv, tsend, trecv, gsend, grecv, usend, urecv, usem,
):
    me = lax.axis_index("fsdp")
    z = lax.axis_index("ctx")
    core, chip = me % 2, me // 2
    peer = me + 1 - 2 * core
    F = 2 * C
    cols = m_ref.shape[2]
    gload = local(gain_ref, gains.at[z], lsem, 1)
    barrier = pltpu.get_barrier_semaphore()
    for k in range(1, C):
        pl.semaphore_signal(barrier, inc=1, device_id={"ctx": (z + k) % C}, device_id_type=MESH)
    for k in range(1, F):
        pl.semaphore_signal(barrier, inc=1, device_id={"fsdp": (me + k) % F}, device_id_type=MESH)
    pl.semaphore_wait(barrier, C + F - 2)
    rows_in = v.shape[1] // C
    units_sent, units_kept = [], []
    for k in range(F):
        to = (me + k) % F
        for b in range(C):
            src = m_ref.at[to // 2, pl.ds((2 * b + to % 2) * rows_in, rows_in)]
            dst = v.at[0, pl.ds(b * rows_in, rows_in), pl.ds(me * cols, cols)]
            if k == 0:
                units_kept.append(local(src, dst, usem, b))
            else:
                c = remote(src, dst, usend, urecv, k * C + b, to)
                c.start()
                units_sent.append(c)
    piece = rows_ref.shape[1] // C

    def part(j):
        return pl.ds(j * piece, piece)

    sent, keep = [], []
    for a in range(2):
        for k in range(1, C):
            to = (z + k) % C
            c = remote(rows_ref.at[a, part(to)], stage.at[a, z], tsend, trecv, 2 * C * a + k, to, "ctx")
            c.start()
            sent.append(c)
        keep.append(local(rows_ref.at[a, part(z)], stage.at[a, z], lsem, 2 + a))
    gload.wait()
    for k in range(1, C):
        c = remote(gains.at[z], gains.at[z], gsend, grecv, k, (z + k) % C, "ctx")
        c.start()
        sent.append(c)

    def leave_layer():
        for a in range(2):
            for k in range(1, C):
                frm = (z - k + C) % C
                remote(stage.at[a, frm], stage.at[a, frm], tsend, trecv, 2 * C * a + k, frm, "ctx").wait_recv()
            keep[a].wait()
            for k in range(1, C):
                to = (chip + k) % C
                c = remote(
                    stage.at[a, to], home_ref.at[a, part(chip)], tsend, trecv, 2 * C * a + C + k, 2 * to + core
                )
                c.start()
                sent.append(c)
            keep[a] = local(stage.at[a, chip], home_ref.at[a, part(chip)], lsem, 4 + a)

    def arrived_home():
        for a in range(2):
            keep[a].wait()
            for k in range(1, C):
                frm = (chip - k + C) % C
                dst = home_ref.at[a, part(frm)]
                remote(dst, dst, tsend, trecv, 2 * C * a + C + k, 2 * frm + core).wait_recv()
        for k in range(1, C):
            frm = (z - k + C) % C
            remote(gains.at[frm], gains.at[frm], gsend, grecv, k, frm, "ctx").wait_recv()
        gsum[...] = jnp.sum(gains[...], axis=0)
        local(gsum, gsum_ref, lsem, 6).wait()
        for c in sent:
            c.wait_send()

    for k in range(1, F):
        frm = (me - k + F) % F
        for b in range(C):
            dst = v.at[0, pl.ds(b * rows_in, rows_in), pl.ds(frm * cols, cols)]
            remote(dst, dst, usend, urecv, k * C + b, frm).wait_recv()
    for c in units_sent:
        c.wait_send()
    for c in units_kept:
        c.wait()
    M, D = v.shape[1], v.shape[2]
    tile, col = 512, 1024
    tiles = M // tile

    def block(i):
        return pl.ds(i * tile, tile)

    def swap(buf, i, sends, recvs):
        return remote(buf.at[0, block(i)], buf.at[1, block(i)], sends, recvs, i, peer)

    pending = [swap(v, i, vsend, vrecv) for i in range(tiles)]
    for c in pending:
        c.start()
    stat[0] = jnp.zeros_like(stat[0])

    def add(r):
        part = v[0, r, :].astype(f32)
        stat[0] += jnp.sum((part * part).reshape(-1, 8, D // 128, 128), axis=(0, 2))

    row_loop(M, add)
    share = remote(stat.at[0], stat.at[1], ssend, srecv, 0, peer)
    share.start()
    share.wait()
    inv = 1.0 / (jnp.sqrt(jnp.sum(stat[0] + stat[1])) + 1e-07)

    for iteration in range(NS_STEPS):
        factor = inv if iteration == 0 else 1.0

        def grams(h, n):
            rhs = pl.ds(pl.multiple_of(n * col, col), col)
            cols = pl.ds(pl.multiple_of(h * M + n * col, col), col)

            @pl.loop(0, tiles)
            def _(i):
                rows = pl.ds(pl.multiple_of(i * tile, tile), tile)
                got = nt(v[0, rows, :], v[h, rhs, :])
                if iteration == 0:
                    got = got * (factor * factor)
                gram[rows, cols] = got.astype(bf16)

        @pl.loop(0, M // col)
        def _(n):
            grams(0, n)

        for c in pending:
            c.wait()

        @pl.loop(0, M // col)
        def _(n):
            grams(1, n)

        def times(src, i, n):
            rows = block(i)
            cols = pl.ds(pl.multiple_of(n * col, col), col)
            return cols, nn(gram[rows, :M], src[0, :, cols]) + nn(gram[rows, M:], src[1, :, cols])

        pending = []
        for i in range(tiles):

            @pl.loop(0, D // col)
            def _(n):
                cols, got = times(v, i, n)
                if iteration == 0:
                    got = got * factor
                yf[block(i), cols] = got
                y[0, block(i), cols] = got.astype(bf16)

            c = swap(y, i, ysend, yrecv)
            c.start()
            pending.append(c)
        for c in pending:
            c.wait()
        if iteration == 0:
            leave_layer()
        pending = []
        for i in range(tiles):

            @pl.loop(0, D // col)
            def _(n):
                cols, got = times(y, i, n)
                old = v[0, block(i), cols].astype(f32)
                if iteration == 0:
                    old = old * factor
                v[0, block(i), cols] = (
                    quintic_one * old + quintic_two * yf[block(i), cols] + quintic_three * got
                ).astype(bf16)

            if iteration < NS_STEPS - 1:
                c = swap(v, i, vsend, vrecv)
            else:
                c = pltpu.make_async_copy(v.at[0, block(i)], out_ref.at[block(i)], osem.at[i])
            c.start()
            pending.append(c)
    arrived_home()
    for c in pending:
        c.wait()


def newton_call(C, x, rows, gains):
    _, D, cols = x.shape
    M = D // 2
    _, R, _ = rows.shape
    n = M // 512
    return pl.pallas_call(
        functools.partial(newton_kernel, C),
        out_shape=[
            jax.ShapeDtypeStruct((M, D), bf16),
            jax.ShapeDtypeStruct((2, R, D), bf16),
            jax.ShapeDtypeStruct((8, D), f32),
        ],
        in_specs=[ANY] * 3,
        out_specs=[ANY] * 3,
        scratch_shapes=[
            pltpu.VMEM((2, M, D), bf16),
            pltpu.VMEM((M, 2 * M), bf16),
            pltpu.VMEM((2, M, D), bf16),
            pltpu.VMEM((M, D), f32),
            pltpu.VMEM((2, 8, 128), f32),
            pltpu.VMEM((2, C, R // C, D), bf16),
            pltpu.VMEM((C, 8, D), f32),
            pltpu.VMEM((8, D), f32),
            dma(7), dma(n), dma(n), dma(n), dma(n), dma(n), dma(1), dma(1),
            dma(4 * C), dma(4 * C), dma(C), dma(C), dma(2 * C * C), dma(2 * C * C), dma(C),
        ],
        compiler_params=params(6),
        cost_estimate=cost(95),
    )(x, rows, gains)


def project(C, F, x, w):
    own = to_layer(C, F, x)
    rows = token_rows(own)
    return own, rows, dot(rows, w, 1, 0)


def attn_out_and_up(C, F, mixed, wo, x, gain, wg, wu):
    if kernels_fit(C, F):
        hidden_in, out, inp = out_call(F, mixed, wo, x, gain)
        return (hidden_in, out, *up_call(F, inp, wg, wu))
    out = token_sums(dot(mixed, wo, 1, 1))
    hidden_in = x.astype(f32) + out * rms(out) * gain
    rows = token_rows(hidden_in.astype(bf16))
    g, u = dot(rows, wg, 1, 0), dot(rows, wu, 1, 0)
    sig = jax.nn.sigmoid(g)
    der = u * (sig * (1.0 + g * (1.0 - sig)))
    act = g * sig
    return hidden_in, out, rows, act.astype(bf16), der.astype(bf16), (act * u).astype(bf16)


def down_and_back(C, F, h, wd, hidden_in, cot, gain, act, der):
    if kernels_fit(C, F):
        return down_call(C, F, h, wd, hidden_in, cot, gain, act, der)
    cot = to_layer(C, F, cot)
    out = token_sums(dot(h, wd, 1, 1))
    scale = rms(out)
    hat = out * scale
    g = cot.astype(f32)
    rows = token_rows(back(g * gain, hat, scale).astype(bf16))
    gh = dot(rows, wd, 1, 0)
    return (
        (hidden_in + hat * gain).astype(bf16),
        jnp.sum(g * hat, axis=0, keepdims=True),
        rows,
        jnp.concatenate([(gh * der.astype(f32)).astype(bf16), (gh * act.astype(f32)).astype(bf16)], axis=1),
        cot,
    )


def back_to_attn(C, F, grad, wg, wu, cot, out, gain, wo):
    if kernels_fit(C, F):
        return mid_call(F, grad, wg, wu, cot, out, gain, wo)
    resid = cot.astype(f32) + token_sums(dot(grad, jnp.concatenate([wg, wu], axis=1), 1, 1))
    scale = rms(out)
    hat = out * scale
    rows = token_rows(back(resid * gain, hat, scale).astype(bf16))
    return resid, jnp.sum(resid * hat, axis=0, keepdims=True), rows, dot(rows, wo, 1, 0).astype(bf16)


def back_to_input(C, F, grad_projected, w, resid):
    return (resid + token_sums(dot(grad_projected, w, 1, 1))).astype(bf16)


def kernels_fit(C, F):
    return C == 4 and F == 8 and UNITS_ATTN * 4 * 2 == C * F


def to_layer(C, F, x):
    z, chip = lax.axis_index("ctx"), lax.axis_index("fsdp") // 2
    x = x.reshape(C, x.shape[0] // C, x.shape[1])
    got = []
    for k in range(C):
        pairs = [
            (s * F + f, (f // 2) * F + 2 * ((s + k) % C) + f % 2) for s in range(C) for f in range(F)
        ]
        block = lax.dynamic_index_in_dim(x, (z + k) % C, 0, keepdims=False)
        got.append(lax.ppermute(block, BOTH, pairs))
    got = jnp.stack(got)
    got = [lax.dynamic_index_in_dim(got, (chip - s + C) % C, 0, keepdims=False) for s in range(C)]
    return jnp.concatenate(got, axis=0)


def from_layer(C, F, x):
    z, chip = lax.axis_index("ctx"), lax.axis_index("fsdp") // 2
    x = x.reshape(C, x.shape[0] // C, x.shape[1])
    got = []
    for k in range(C):
        pairs = [
            ((f // 2) * F + 2 * ((s + k) % C) + f % 2, s * F + f) for s in range(C) for f in range(F)
        ]
        block = lax.dynamic_index_in_dim(x, (chip - k + C) % C, 0, keepdims=False)
        got.append(lax.ppermute(block, BOTH, pairs))
    got = jnp.stack(got)
    got = [lax.dynamic_index_in_dim(got, (j - z + C) % C, 0, keepdims=False) for j in range(C)]
    return jnp.concatenate(got, axis=0)


def shards(C, F, layer_input, cotangent, positions, w_attn, w_ffn, gains, mom_attn, mom_ffn, gain_mom):
    z = lax.axis_index("ctx")
    f = lax.axis_index("fsdp")
    local_rows, width = layer_input.shape[1], layer_input.shape[2]
    seq_total, seq_length = positions.shape
    dz, head_cols = w_attn.shape[1], w_attn.shape[2]
    local_heads = head_cols // HEAD_DIM
    block_count = w_ffn.shape[2]
    per = seq_total // C
    piece = local_rows // C
    chips = F // per
    tokens = F * local_rows
    hidden_cols = block_count * head_cols
    units = UNITS_ATTN + 3 * block_count
    parts = C * F // units

    def after(a, b):
        return lax.optimization_barrier((a, b))[0]

    def rows_gather(shard):
        return lax.all_gather(shard, "ctx", axis=0, tiled=True)

    def product(units, groups, *pairs):
        pairs = [(x.reshape(tokens, width), dy) for x, dy in pairs]
        if kernels:
            return grad_call(pairs, units, head_cols, groups)
        grad = jnp.concatenate([dot(x, dy, 0, 0).astype(bf16) for x, dy in pairs], axis=1)
        return jnp.transpose(grad.reshape(width, groups, units, head_cols), (2, 1, 0, 3))

    def scatter(grad):
        if kernels:
            return lax.psum_scatter(grad, "ctx", scatter_dimension=0, tiled=True)[0]
        return lax.psum_scatter(grad, "ctx", scatter_dimension=2, tiled=True)

    kernels = kernels_fit(C, F)
    w_qkv = rows_gather(jnp.concatenate([w_attn[0], w_attn[1], w_attn[2]], axis=1))
    w_out = rows_gather(w_attn[3])
    ffn_flat = w_ffn.reshape(3, dz, hidden_cols)
    w_gate = rows_gather(ffn_flat[0])
    w_up = rows_gather(ffn_flat[1])
    w_down = rows_gather(ffn_flat[2])

    gain_query = lax.dynamic_slice_in_dim(gains[0], f * head_cols, head_cols)
    gain_key = lax.dynamic_slice_in_dim(gains[1], f * head_cols, head_cols)
    pos = lax.dynamic_slice_in_dim(positions, z * per, per, 0)
    pos = jnp.transpose(pos.reshape(per, C, chips, piece), (0, 2, 1, 3)).reshape(per, seq_length)
    cosine_table, sine_table = rotary_tables(pos)

    def heads(a):
        return jnp.transpose(
            a.reshape(chips, per, local_rows, local_heads, HEAD_DIM), (1, 0, 2, 3, 4)
        ).reshape(per, seq_length, local_heads, HEAD_DIM)

    def unheads(a):
        return jnp.transpose(
            a.reshape(per, chips, local_rows, local_heads, HEAD_DIM), (1, 0, 2, 3, 4)
        ).reshape(tokens, head_cols)

    if kernels:
        sign = jnp.where(jnp.arange(HEAD_DIM) < HEAD_DIM // 2, -1.0, 1.0)
        tables = (
            gain_query[None],
            gain_key[None],
            jnp.broadcast_to(cosine_table[:, :, 0], (per, seq_length, HEAD_DIM)),
            sine_table[:, :, 0] * sign,
            pos.astype(f32)[:, None, :],
            jnp.broadcast_to(pos.astype(f32)[..., None], (per, seq_length, HEAD_DIM)),
        )
        own_input, input_all = enter_call(C, F, layer_input.reshape(local_rows, width))
        projected, stats = qkv_call(F, input_all, w_qkv)
        attn_mixed, query_rows, key_rows, log_total = attend_call(F, projected, stats, *tables)
        attn_mixed = attn_mixed.reshape(tokens, head_cols)
    else:
        own_input, input_all, projected = project(C, F, layer_input.reshape(local_rows, width), w_qkv)
        query_raw = projected[:, :head_cols]
        key_raw = projected[:, head_cols : 2 * head_cols]
        value_raw = projected[:, 2 * head_cols :]
        query_total, key_total = norm_stats(
            jnp.sum(query_raw * query_raw, axis=-1), jnp.sum(key_raw * key_raw, axis=-1)
        )
        query_scale = lax.rsqrt(query_total / width + epsilon)[..., None]
        key_scale = lax.rsqrt(key_total / width + epsilon)[..., None]
        query_hat = query_raw * query_scale
        key_hat = key_raw * key_scale
        query_rows = (
            rotate(heads(query_hat * gain_query), cosine_table, sine_table) * HEAD_DIM ** (-0.5)
        ).astype(bf16)
        key_rows = rotate(heads(key_hat * gain_key), cosine_table, sine_table).astype(bf16)
        value_rows = heads(value_raw.astype(bf16))
        attn_mixed, log_total = attend(query_rows, key_rows, value_rows, pos)
        attn_mixed = unheads(attn_mixed)
    hidden_in, attn_out, mlp_all, act, der, hidden = attn_out_and_up(
        C, F, attn_mixed, w_out, own_input, gains[2:3], w_gate, w_up
    )
    result, mlp_gain, grad_mlp_all, grad_ffn_in, own_grad = down_and_back(
        C, F, hidden, w_down, hidden_in, cotangent.reshape(local_rows, width), gains[3:4], act, der
    )
    if kernels:
        units_in = jnp.concatenate(
            [mom_attn[:, None].astype(bf16), jnp.transpose(mom_ffn.astype(bf16), (2, 0, 1, 3))], axis=1
        )
        units_in = after(units_in, w_down)
        mom_own = jnp.swapaxes(lax.all_to_all(units_in, "ctx", split_axis=0, concat_axis=0, tiled=True), 0, 1)
        grad_mlp_all, mom_own = lax.optimization_barrier((grad_mlp_all, mom_own))
    p_down = product(block_count, 1, (grad_mlp_all, hidden))
    g_down = scatter(p_down)
    p_gate_up = product(block_count, 2, (mlp_all, grad_ffn_in))
    if kernels:
        grad_ffn_in, p_gate_up = lax.optimization_barrier((grad_ffn_in, p_gate_up))
    g_gate_up = scatter(p_gate_up)
    grad_resid, attn_gain, grad_attn_all, grad_mixed = back_to_attn(
        C, F, grad_ffn_in, w_gate, w_up, own_grad, attn_out, gains[2:3], w_out
    )
    if kernels:
        grad_mixed = after(grad_mixed, g_down)
        weighted_q, weighted_k, grad_value, inner, gain_cols = attend_back_call(
            F, projected, query_rows, key_rows, grad_mixed, log_total, stats, *tables
        )
        inner = jnp.transpose(
            jnp.sum(inner, axis=1).reshape(per, 8, chips, local_rows), (1, 2, 0, 3)
        ).reshape(8, tokens)
        gain_cols = jnp.sum(gain_cols, axis=0)
        query_gain_cols = gain_cols[:, 0].reshape(head_cols)
        key_gain_cols = gain_cols[:, 1].reshape(head_cols)
        flat = (tokens, head_cols)
        zero = jnp.zeros((width,), f32)
        gain_local = jnp.stack(
            [
                lax.dynamic_update_slice(zero, query_gain_cols, (f * head_cols,)),
                lax.dynamic_update_slice(zero, key_gain_cols, (f * head_cols,)),
                attn_gain[0],
                mlp_gain[0],
                *[zero] * 4,
            ]
        )
        grad_rows, grad_projected, gain_layer = last_call(
            F, weighted_q.reshape(flat), weighted_k.reshape(flat), grad_value.reshape(flat),
            projected, stats, inner, w_qkv, grad_resid, gain_local,
        )
    else:
        grad_query, grad_key, grad_value = attend_back(
            query_rows, key_rows, value_rows, pos, heads(grad_mixed), log_total
        )
        grad_query_norm = unheads(unrotate(grad_query * HEAD_DIM ** (-0.5), cosine_table, sine_table))
        grad_key_norm = unheads(unrotate(grad_key, cosine_table, sine_table))
        query_gain_cols = jnp.sum(grad_query_norm * query_hat, axis=0)
        key_gain_cols = jnp.sum(grad_key_norm * key_hat, axis=0)
        query_weighted = grad_query_norm * gain_query
        key_weighted = grad_key_norm * gain_key
        query_inner, key_inner = norm_stats(
            jnp.sum(query_weighted * query_hat, axis=-1), jnp.sum(key_weighted * key_hat, axis=-1)
        )
        grad_query_raw = query_scale * (query_weighted - query_hat * (query_inner / width)[..., None])
        grad_key_raw = key_scale * (key_weighted - key_hat * (key_inner / width)[..., None])
        grad_projected = jnp.concatenate(
            [grad_query_raw.astype(bf16), grad_key_raw.astype(bf16), unheads(grad_value).astype(bf16)],
            axis=1,
        )
        grad_rows = back_to_input(C, F, grad_projected, w_qkv, grad_resid)
    g_attn = scatter(
        product(UNITS_ATTN, 1, (input_all, grad_projected), (grad_attn_all, attn_mixed))
    )
    if not kernels:
        grad_input = from_layer(C, F, grad_rows)
        result = from_layer(C, F, result)
        zero = jnp.zeros((width,), f32)
        gain_local = jnp.stack(
            [
                lax.dynamic_update_slice(zero, query_gain_cols, (f * head_cols,)),
                lax.dynamic_update_slice(zero, key_gain_cols, (f * head_cols,)),
                attn_gain[0],
                mlp_gain[0],
            ]
        )
        gain_total = jnp.sum(lax.all_gather(gain_local, BOTH, axis=0, tiled=False), axis=0)

    if kernels:
        got = jnp.stack([g_attn[0], g_gate_up[0], g_gate_up[1], g_down[0]])
        mom = mom_own.reshape(got.shape).astype(f32)
        owned = (momentum * mom + got.astype(f32)).astype(bf16)
        sent_back = got.reshape(UNITS_ATTN, C, dz, head_cols)
        sent_back = lax.all_to_all(sent_back, "ctx", split_axis=1, concat_axis=0, tiled=False)
        sent_back = sent_back.reshape(C, UNITS_ATTN, dz, head_cols).astype(f32)
        grad_attn = sent_back[:, 0]
        grad_ffn = jnp.transpose(sent_back[:, 1:], (1, 2, 0, 3))
        own, back_rows, gain_total = newton_call(C, owned, jnp.stack([result, grad_rows]), gain_layer)
        result, grad_input, gain_total = back_rows[0], back_rows[1], gain_total[:4]
    else:
        grad_attn = g_attn[:, 0].astype(f32)
        grad_ffn = jnp.transpose(
            jnp.concatenate([g_gate_up, g_down], axis=1).astype(f32), (1, 2, 0, 3)
        )
    new_attn = momentum * mom_attn + grad_attn
    new_ffn = momentum * mom_ffn + grad_ffn
    if not kernels:
        send = jnp.concatenate(
            [
                new_attn.astype(bf16),
                jnp.transpose(new_ffn.astype(bf16), (0, 2, 1, 3)).reshape(3 * block_count, dz, head_cols),
            ],
            axis=0,
        ).reshape(C * F, dz // parts, head_cols)
        own = lax.all_to_all(send, BOTH, split_axis=0, concat_axis=0, tiled=True)
        own = jnp.transpose(own.reshape(C, F, dz // parts, head_cols), (0, 2, 1, 3)).reshape(
            C * dz // parts, F * head_cols
        )

        def peers(a):
            out = [a]
            for s in range(1, parts):
                pairs = [(i, i - i % parts + (i + parts - s) % parts) for i in range(C * F)]
                out.append(lax.ppermute(a, BOTH, pairs))
            return out

        own32 = own.astype(f32)
        square = jnp.sum(own32 * own32)
        total = sum(peers(square.reshape(1, 1)))
        inv = 1.0 / (jnp.sqrt(total) + 1e-07)
        for iteration in range(NS_STEPS):
            factor = inv if iteration == 0 else 1.0
            every = peers(own)
            gram = [(dot(own, b, 1, 1) * (factor * factor)).astype(bf16) for b in every]
            product = sum(dot(g, b, 1, 0) for g, b in zip(gram, every)) * factor
            product_all = peers(product.astype(bf16))
            product_two = sum(dot(g, b, 1, 0) for g, b in zip(gram, product_all))
            own = (
                quintic_one * factor * own.astype(f32) + quintic_two * product + quintic_three * product_two
            ).astype(bf16)
    home = jnp.transpose(own.reshape(C, dz // parts, F, head_cols), (0, 2, 1, 3)).reshape(
        C * F, dz // parts, head_cols
    )
    steps = lax.all_to_all(home, BOTH, split_axis=0, concat_axis=0, tiled=True)
    steps = -muon_rate * steps.astype(f32)
    if kernels:
        steps = steps.reshape(C, UNITS_ATTN, dz, head_cols)
        step_attn = steps[:, 0]
        step_ffn = jnp.transpose(steps[:, 1:], (1, 2, 0, 3))
    else:
        steps = steps.reshape(units, dz, head_cols)
        step_attn = steps[:UNITS_ATTN]
        step_ffn = jnp.transpose(
            steps[UNITS_ATTN:].reshape(3, block_count, dz, head_cols), (0, 2, 1, 3)
        )
    new_gain_mom = momentum * gain_mom + gain_total
    return (
        result.reshape(layer_input.shape),
        grad_input.astype(f32).reshape(layer_input.shape),
        grad_attn,
        grad_ffn,
        gain_total,
        new_attn,
        new_ffn,
        new_gain_mom,
        step_attn,
        step_ffn,
        -gain_rate * new_gain_mom,
    )


def solution(mesh):
    tokens = P("fsdp", "ctx", None)
    attn = P(None, "ctx", "fsdp")
    ffn = P(None, "ctx", None, "fsdp")
    in_specs = (tokens, tokens, P(), attn, ffn, P(), attn, ffn, P())
    out_specs = (tokens, tokens, attn, ffn, P(), attn, ffn, P(), attn, ffn, P())
    body = functools.partial(shards, mesh.shape["ctx"], mesh.shape["fsdp"])
    return jax.shard_map(body, mesh=mesh, in_specs=in_specs, out_specs=out_specs, check_vma=False)
```

```python
import functools
import jax
import jax.numpy as jnp
from jax import lax
from jax.experimental import pallas as pl
from jax.experimental.pallas import tpu as pltpu
from jax.sharding import PartitionSpec as P

NS_STEPS = 3
HEAD_DIM = 128
UNITS_ATTN = 4

epsilon = 1e-06
rope_theta = 500000.0
quintic_one = 3.4445
quintic_two = -4.775
quintic_three = 2.0315
momentum = 0.95
muon_rate = 1.0
gain_rate = 0.0005
BOTH = ("ctx", "fsdp")
bf16 = jnp.bfloat16
f32 = jnp.float32


def dot(a, b, ca, cb):
    return lax.dot_general(a, b, (((ca,), (cb,)), ((), ())), preferred_element_type=f32)


def token_rows(operand):
    return lax.all_gather(operand, "fsdp", axis=0, tiled=True)


def token_sums(operand):
    return lax.psum_scatter(operand.astype(bf16), "fsdp", scatter_dimension=0, tiled=True).astype(f32)


def norm_stats(first_sum, second_sum):
    got = lax.all_gather(jnp.stack([first_sum, second_sum]), "fsdp", axis=0, tiled=False)
    total = jnp.sum(got, axis=0)
    return total[0], total[1]


def rms_back(upstream, normed, inv_scale):
    return inv_scale * (upstream - normed * jnp.mean(upstream * normed, axis=-1, keepdims=True))


def rotary_tables(slot_order):
    half_dim = HEAD_DIM // 2
    inverse = rope_theta ** (-(jnp.arange(half_dim, dtype=f32) * 2.0) / HEAD_DIM)
    angles = slot_order.astype(f32)[..., None] * inverse
    angles = jnp.concatenate([angles, angles], axis=-1)
    return (jnp.cos(angles)[..., None, :], jnp.sin(angles)[..., None, :])


def rotate(operand, cosine_table, sine_table):
    half_dim = operand.shape[-1] // 2
    flipped = jnp.concatenate([-operand[..., half_dim:], operand[..., :half_dim]], axis=-1)
    return operand * cosine_table + flipped * sine_table


def unrotate(upstream, cosine_table, sine_table):
    half_dim = upstream.shape[-1] // 2
    shifted = upstream * sine_table
    flipped = jnp.concatenate([shifted[..., half_dim:], -shifted[..., :half_dim]], axis=-1)
    return upstream * cosine_table + flipped


def masked_scores(query_rows, key_rows, pos):
    scores = jnp.einsum("gqhe,gkhe->ghqk", query_rows, key_rows, preferred_element_type=f32)
    causal = pos[:, None, :, None] >= pos[:, None, None, :]
    return jnp.where(causal, scores, -1e30)


def attend(query_rows, key_rows, value_rows, pos):
    scores = masked_scores(query_rows, key_rows, pos)
    row_max = jnp.max(scores, axis=-1, keepdims=True)
    weights = jnp.exp(scores - row_max)
    row_total = jnp.sum(weights, axis=-1, keepdims=True)
    probabilities = (weights / row_total).astype(bf16)
    attn_mixed = jnp.einsum("ghqk,gkhe->gqhe", probabilities, value_rows, preferred_element_type=f32)
    return attn_mixed.astype(bf16), row_max + jnp.log(row_total)


def attend_back(query_rows, key_rows, value_rows, pos, grad_mixed, log_total):
    scores = masked_scores(query_rows, key_rows, pos)
    probabilities = jnp.exp(scores - log_total)
    grad_probs = jnp.einsum("gqhe,gkhe->ghqk", grad_mixed, value_rows, preferred_element_type=f32)
    grad_value = jnp.einsum(
        "ghqk,gqhe->gkhe", probabilities.astype(bf16), grad_mixed, preferred_element_type=f32
    )
    inner_sum = jnp.sum(grad_probs * probabilities, axis=-1, keepdims=True)
    grad_scores = (probabilities * (grad_probs - inner_sum)).astype(bf16)
    grad_query = jnp.einsum("ghqk,gkhe->gqhe", grad_scores, key_rows, preferred_element_type=f32)
    grad_key = jnp.einsum("ghqk,gqhe->gkhe", grad_scores, query_rows, preferred_element_type=f32)
    return grad_query, grad_key, grad_value


MESH = pl.DeviceIdType.MESH
VMEM_LIMIT = 60 * 1024 * 1024
ANY = pl.BlockSpec(memory_space=pl.ANY)


class Plane:
    def __init__(self):
        f = lax.axis_index("fsdp")
        self.f, self.c, self.chip = f, f % 2, f // 2
        x, y = self.chip % 2, self.chip // 2
        self.qx = self.chip + 1 - 2 * x
        self.qy = self.chip + 2 - 4 * y
        self.qd = self.qx + 2 - 4 * y
        self.fc = f + 1 - 2 * self.c
        self.fx = 2 * self.qx + self.c
        self.fy = 2 * self.qy + self.c
        self.fd = 2 * self.qd + self.c
        self.other = 1 - self.c

    def greet(self):
        barrier = pltpu.get_barrier_semaphore()
        for to in (self.fc, self.fx, self.fy):
            pl.semaphore_signal(barrier, inc=1, device_id={"fsdp": to}, device_id_type=MESH)
        pl.semaphore_wait(barrier, 3)


def remote(src, dst, send, recv, i, to, axis="fsdp"):
    return pltpu.make_async_remote_copy(
        src_ref=src, dst_ref=dst, send_sem=send.at[i], recv_sem=recv.at[i],
        device_id={axis: to}, device_id_type=MESH,
    )


def local(src, dst, sems, i):
    copy = pltpu.make_async_copy(src, dst, sems.at[i])
    copy.start()
    return copy


def nn(a, b):
    return lax.dot_general(a, b, (((1,), (0,)), ((), ())), preferred_element_type=f32)


def nt(a, b):
    return lax.dot_general(a, b, (((1,), (1,)), ((), ())), preferred_element_type=f32)


def gather_phase(at, rows, send, recv, base, on_rows):
    half = rows.shape[1] // 2
    A, B = pl.ds(0, half), pl.ds(half, half)

    def cp(i, slot, part, to):
        ref = rows.at[slot] if part is None else rows.at[slot, part]
        return remote(ref, ref, send, recv, base + i, to)

    fcx, fcy, fcd = 2 * at.qx + at.other, 2 * at.qy + at.other, 2 * at.qd + at.other
    sent = []

    def go(*a):
        c = cp(*a)
        c.start()
        sent.append(c)

    def arrived(i, slot, part, frm):
        cp(i, slot, part, frm).wait_recv()

    go(0, at.f, None, at.fc)
    go(1, at.f, A, at.fx)
    go(3, at.f, B, at.fy)
    go(2, at.f, B, at.fx)
    go(4, at.f, A, at.fy)
    arrived(0, at.fc, None, at.fc)
    on_rows(2 * at.chip, 2)
    arrived(1, at.fx, A, at.fx)
    go(5, at.fx, A, at.fy)
    go(7, at.fx, A, at.fc)
    arrived(3, at.fy, B, at.fy)
    go(6, at.fy, B, at.fx)
    go(8, at.fy, B, at.fc)
    arrived(2, at.fx, B, at.fx)
    go(9, at.fx, B, at.fc)
    arrived(4, at.fy, A, at.fy)
    go(10, at.fy, A, at.fc)
    arrived(7, fcx, A, at.fc)
    arrived(9, fcx, B, at.fc)
    on_rows(2 * at.qx, 2)
    arrived(8, fcy, B, at.fc)
    arrived(10, fcy, A, at.fc)
    on_rows(2 * at.qy, 2)
    arrived(5, at.fd, A, at.fy)
    go(11, at.fd, A, at.fc)
    arrived(6, at.fd, B, at.fx)
    go(12, at.fd, B, at.fc)
    on_rows(at.fd, 1)
    arrived(11, fcd, A, at.fc)
    arrived(12, fcd, B, at.fc)
    on_rows(fcd, 1)
    for c in sent:
        c.wait_send()


GATHER_COPIES = 13
SCATTER_COPIES = 10


def scatter_scratch(R, D):
    return [
        pltpu.VMEM((4, R, D), bf16),
        pltpu.VMEM((4, R, D), bf16),
        pltpu.VMEM((2, R, D), f32),
        pltpu.VMEM((3, R, D), bf16),
        pltpu.VMEM((3, R, D), bf16),
    ]


def scatter_phase(at, partial, bufs, send, recv, base, between=None):
    to_core, from_core, mine, out, inc = bufs
    R, D = to_core.shape[1], to_core.shape[2]
    half = R // 2
    A, B = pl.ds(0, half), pl.ds(half, half)
    tile = 512
    step = 16
    sent = []

    def go(i, src, dst, to):
        c = remote(src, dst, send, recv, base + i, to)
        c.start()
        sent.append(c)

    def arrived(i, dst, frm):
        remote(dst, dst, send, recv, base + i, frm).wait_recv()

    def compute(order, chip, slot):
        @pl.loop(0, D // tile)
        def _(n):
            cols = pl.ds(pl.multiple_of(n * tile, tile), tile)
            got = partial(chip, cols)
            lo, hi = got[:R], got[R:]
            first = at.c == 0
            mine[slot, :, cols] = jnp.where(first, lo, hi)
            to_core[order, :, cols] = jnp.where(first, hi, lo).astype(bf16)

        go(order, to_core.at[order], from_core.at[order], at.fc)

    def chip_sum(order, slot):
        arrived(order, from_core.at[order], at.fc)

        @pl.loop(0, R // step)
        def _(r):
            rows = pl.ds(pl.multiple_of(r * step, step), step)
            out[order, rows, :] = (mine[slot, rows, :] + from_core[order, rows, :].astype(f32)).astype(bf16)

    def relay(order, start, src):
        @pl.loop(0, half // step)
        def _(r):
            rows = pl.ds(pl.multiple_of(start + r * step, step), step)
            out[order, rows, :] = (out[order, rows, :].astype(f32) + inc[src, rows, :].astype(f32)).astype(bf16)

    compute(0, at.qd, 0)
    compute(1, at.qx, 1)
    if between is not None:
        between()
    chip_sum(0, 0)
    go(4, out.at[0, A], inc.at[0, A], at.fx)
    go(5, out.at[0, B], inc.at[0, B], at.fy)
    compute(2, at.qy, 0)
    chip_sum(1, 1)
    go(6, out.at[1, A], inc.at[1, A], at.fx)
    compute(3, at.chip, 1)
    chip_sum(2, 0)
    go(8, out.at[2, B], inc.at[2, B], at.fy)
    arrived(5, inc.at[0, B], at.fy)
    relay(1, half, 0)
    go(7, out.at[1, B], inc.at[1, B], at.fx)
    arrived(4, inc.at[0, A], at.fx)
    relay(2, 0, 0)
    go(9, out.at[2, A], inc.at[2, A], at.fy)
    arrived(3, from_core.at[3], at.fc)
    arrived(6, inc.at[1, A], at.fx)
    arrived(8, inc.at[2, B], at.fy)
    arrived(7, inc.at[1, B], at.fx)
    arrived(9, inc.at[2, A], at.fy)
    for c in sent:
        c.wait_send()

    def total(rows):
        return (
            mine[1, rows, :]
            + from_core[3, rows, :].astype(f32)
            + inc[1, rows, :].astype(f32)
            + inc[2, rows, :].astype(f32)
        )

    return total


def rms(v):
    return lax.rsqrt(jnp.mean(v * v, axis=-1, keepdims=True) + epsilon)


def back(weighted, normed, scale):
    return scale * (weighted - normed * jnp.mean(weighted * normed, axis=-1, keepdims=True))


def row_loop(R, body, step=16):
    @pl.loop(0, R // step)
    def _(r):
        body(pl.ds(pl.multiple_of(r * step, step), step))


def pair_loop(rows, w_cols, total_cols, body):
    @pl.loop(0, total_cols // w_cols)
    def _(t):
        body(pl.ds(pl.multiple_of(t * w_cols, w_cols), w_cols))


class Stores:
    def __init__(self, sems):
        self.sems, self.steps, self.n = sems, [], 0

    def slot(self):
        if len(self.steps) >= 2:
            for c in self.steps[-2]:
                c.wait()
            self.steps[-2] = []
        return len(self.steps) % 2

    def put(self, pairs):
        done = []
        for src, dst in pairs:
            done.append(local(src, dst, self.sems, self.n))
            self.n += 1
        self.steps.append(done)

    def finish(self):
        for step in self.steps:
            for c in step:
                c.wait()


class Moving:
    def __init__(self, at, C, mine, stage, landing, lsem, base, send, recv):
        self.at, self.C, self.mine, self.stage, self.landing = at, C, mine, stage, landing
        self.lsem, self.base, self.send, self.recv = lsem, base, send, recv
        self.z = lax.axis_index("ctx")
        self.piece = mine.shape[0] // C
        self.sent = []

    def greet(self, barrier):
        at, C = self.at, self.C
        for k in range(1, C):
            pl.semaphore_signal(barrier, inc=1, device_id={"ctx": (self.z + k) % C}, device_id_type=MESH)
            pl.semaphore_signal(
                barrier, inc=1, device_id={"fsdp": 2 * ((at.chip + k) % C) + at.c}, device_id_type=MESH
            )

    def first(self):
        at, C, piece = self.at, self.C, self.piece
        for k in range(1, C):
            j = (at.chip + k) % C
            src = self.mine.at[pl.ds(j * piece, piece)]
            c = remote(src, self.stage.at[at.chip], self.send, self.recv, k, 2 * j + at.c)
            c.start()
            self.sent.append(c)
        src = self.mine.at[pl.ds(at.chip * piece, piece)]
        self.keep = local(src, self.stage.at[at.chip], self.lsem, self.base)

    def land(self, layer):
        return self.landing.at[pl.ds(layer * self.piece, self.piece)]

    def second(self):
        at, C, z = self.at, self.C, self.z
        self.keep.wait()
        for k in range(1, C):
            frm = (at.chip - k + C) % C
            remote(self.stage.at[frm], self.stage.at[frm], self.send, self.recv, k, 2 * frm + at.c).wait_recv()
        for k in range(1, C):
            to = (z + k) % C
            c = remote(self.stage.at[to], self.land(z), self.send, self.recv, C + k, to, "ctx")
            c.start()
            self.sent.append(c)
        self.keep = local(self.stage.at[z], self.land(z), self.lsem, self.base + 1)

    def finish(self):
        C, z = self.C, self.z
        self.keep.wait()
        for k in range(1, C):
            frm = (z - k + C) % C
            remote(self.land(frm), self.land(frm), self.send, self.recv, C + k, frm, "ctx").wait_recv()
        for c in self.sent:
            c.wait_send()


def enter_kernel(C, x_ref, own_ref, all_ref, stage, mine, rows, lsem, osem, send, recv, tsend, trecv):
    at = Plane()
    load = local(x_ref, mine, lsem, 0)
    moving = Moving(at, C, mine, stage, rows.at[at.f], lsem, 1, tsend, trecv)
    barrier = pltpu.get_barrier_semaphore()
    moving.greet(barrier)
    pl.semaphore_signal(barrier, inc=1, device_id={"fsdp": at.fc}, device_id_type=MESH)
    pl.semaphore_wait(barrier, 2 * (C - 1) + 1)
    load.wait()
    moving.first()
    moving.second()
    moving.finish()
    save = local(rows.at[at.f], own_ref, lsem, 3)
    stores = []

    def on_rows(first, count):
        stores.append(local(rows.at[pl.ds(first, count)], all_ref.at[pl.ds(first, count)], osem, len(stores)))

    gather_phase(at, rows, send, recv, 0, on_rows)
    save.wait()
    for c in stores:
        c.wait()


def enter_call(C, F, x):
    R, D = x.shape
    return pl.pallas_call(
        functools.partial(enter_kernel, C),
        out_shape=[jax.ShapeDtypeStruct((R, D), bf16), jax.ShapeDtypeStruct((F, R, D), bf16)],
        in_specs=[ANY],
        out_specs=[ANY] * 2,
        scratch_shapes=[
            pltpu.VMEM((C, R // C, D), bf16),
            pltpu.VMEM((R, D), bf16),
            pltpu.VMEM((F, R, D), bf16),
            dma(4), dma(5), dma(GATHER_COPIES), dma(GATHER_COPIES), dma(2 * C), dma(2 * C),
        ],
        compiler_params=params(1),
        cost_estimate=cost(70),
    )(x)


def qkv_kernel(all_ref, w_ref, proj_ref, st_ref, rows, w, acc, st, lsem, osem, ssend, srecv):
    at = Plane()
    F, R = rows.shape[0], rows.shape[1]
    e = w.shape[1] // 3
    m = 2 * R
    loads = [local(w_ref.at[:, pl.ds(0, 3 * e)], w, lsem, 0)] + [
        local(all_ref.at[pl.ds(2 * p, 2)], rows.at[pl.ds(2 * p, 2)], lsem, 1 + p) for p in range(F // 2)
    ]
    barrier = pltpu.get_barrier_semaphore()
    for k in range(1, F):
        pl.semaphore_signal(barrier, inc=1, device_id={"fsdp": (at.f + k) % F}, device_id_type=MESH)
    pl.semaphore_wait(barrier, F - 1)
    loads[0].wait()
    stores = Stores(osem)
    for p in range(F // 2):
        loads[1 + p].wait()
        s = stores.slot()

        def tile(c):
            acc[s, :, c] = nn(rows[pl.ds(2 * p, 2)].reshape(m, rows.shape[2]), w[:, c])

        pair_loop(m, 256, w.shape[1], tile)
        q, k = acc[s, :, :e], acc[s, :, e : 2 * e]
        st[at.f, :, pl.ds(p * m, m)] = row_sums(q * q, k * k)
        stores.put([(acc.at[s], proj_ref.at[pl.ds(p * m, m)])])
    share_stats(at, F, st, ssend, srecv, 0)
    local(st, st_ref, lsem, 1 + F // 2).wait()
    stores.finish()


def params(number):
    return pltpu.CompilerParams(
        collective_id=number, has_side_effects=True, vmem_limit_bytes=VMEM_LIMIT
    )


def cost(us):
    return pl.CostEstimate(flops=int(us * 1e9), bytes_accessed=2**20, transcendentals=0)


def dma(n):
    return pltpu.SemaphoreType.DMA((n,))


def qkv_call(F, rows, w):
    _, R, D = rows.shape
    n = w.shape[1] // 4 * 3
    return pl.pallas_call(
        qkv_kernel,
        out_shape=[
            jax.ShapeDtypeStruct((F * R, n), f32),
            jax.ShapeDtypeStruct((F, 8, F * R), f32),
        ],
        in_specs=[ANY] * 2,
        out_specs=[ANY] * 2,
        scratch_shapes=[
            pltpu.VMEM((F, R, D), bf16),
            pltpu.VMEM((D, n), bf16),
            pltpu.VMEM((2, 2 * R, n), f32),
            pltpu.VMEM((F, 8, F * R), f32),
            dma(6), dma(4), dma(F), dma(F),
        ],
        compiler_params=params(7),
        cost_estimate=cost(22),
    )(rows, w)


def out_kernel(
    mixed_ref, wo_ref, x_ref, gain_ref, hid_ref, ao_ref, in_ref,
    mixed, wo, x, gain, hid, ao, inp, b0, b1, b2, b3, b4, lsem, send, recv,
):
    at = Plane()
    e = wo.shape[1]
    pairs = [(mixed_ref, mixed), (wo_ref.at[:, pl.ds(3 * e, e)], wo), (x_ref, x), (gain_ref, gain)]
    loads = [local(s, d, lsem, i) for i, (s, d) in enumerate(pairs)]
    at.greet()
    R = x.shape[0]
    loads[0].wait()
    loads[1].wait()

    def partial(chip, cols):
        return nt(mixed[pl.ds(pl.multiple_of(chip * 2 * R, 2 * R), 2 * R), :], wo[cols, :])

    total = scatter_phase(at, partial, (b0, b1, b2, b3, b4), send, recv, 0)
    loads[2].wait()
    loads[3].wait()

    def finish(r):
        out = total(r)
        ao[r, :] = out
        hidden_in = x[r, :].astype(f32) + out * rms(out) * gain[...]
        hid[r, :] = hidden_in
        inp[r, :] = hidden_in.astype(bf16)

    row_loop(R, finish)
    for c in [local(ao, ao_ref, lsem, 4), local(hid, hid_ref, lsem, 5), local(inp, in_ref, lsem, 6)]:
        c.wait()


def out_call(F, mixed, wo, x, gain):
    R, D = x.shape
    e = wo.shape[1] // 4
    return pl.pallas_call(
        out_kernel,
        out_shape=[
            jax.ShapeDtypeStruct((R, D), f32),
            jax.ShapeDtypeStruct((R, D), f32),
            jax.ShapeDtypeStruct((R, D), bf16),
        ],
        in_specs=[ANY] * 4,
        out_specs=[ANY] * 3,
        scratch_shapes=[
            pltpu.VMEM((F * R, e), bf16),
            pltpu.VMEM((D, e), bf16),
            pltpu.VMEM((R, D), bf16),
            pltpu.VMEM((1, D), f32),
            pltpu.VMEM((R, D), f32),
            pltpu.VMEM((R, D), f32),
            pltpu.VMEM((R, D), bf16),
        ]
        + scatter_scratch(R, D)
        + [dma(7), dma(SCATTER_COPIES), dma(SCATTER_COPIES)],
        compiler_params=params(8),
        cost_estimate=cost(46),
    )(mixed, wo, x, gain)


def up_kernel(
    in_ref, wg_ref, wu_ref, all_ref, act_ref, der_ref, h_ref,
    w, rows, act, der, h, lsem, osem, send, recv,
):
    at = Plane()
    own = local(in_ref, rows.at[at.f], lsem, 0)
    n = act.shape[2]
    loads = [local(wg_ref, w.at[:, pl.ds(0, n)], lsem, 1), local(wu_ref, w.at[:, pl.ds(n, n)], lsem, 2)]
    width = 256
    at.greet()
    R = rows.shape[1]
    own.wait()
    waited = []
    stores = Stores(osem)

    def on_rows(first, count):
        s = stores.slot()
        m = count * R
        if not waited:
            for c in loads:
                c.wait()
            waited.append(1)

        @pl.loop(0, n // width)
        def _(t):
            c = pl.ds(pl.multiple_of(t * width, width), width)
            lhs = rows[pl.ds(first, count)].reshape(m, rows.shape[2])
            g = nn(lhs, w[:, c])
            u = nn(lhs, w[:, pl.ds(pl.multiple_of(n + t * width, width), width)])
            sig = jax.nn.sigmoid(g)
            a = g * sig
            act[s, pl.ds(0, m), c] = a.astype(bf16)
            der[s, pl.ds(0, m), c] = (u * (sig * (1.0 + g * (1.0 - sig)))).astype(bf16)
            h[s, pl.ds(0, m), c] = (a * u).astype(bf16)

        start = pl.multiple_of(first * R, R)
        stores.put(
            [
                (act.at[s, pl.ds(0, m)], act_ref.at[pl.ds(start, m)]),
                (der.at[s, pl.ds(0, m)], der_ref.at[pl.ds(start, m)]),
                (h.at[s, pl.ds(0, m)], h_ref.at[pl.ds(start, m)]),
                (rows.at[pl.ds(first, count)], all_ref.at[pl.ds(first, count)]),
            ]
        )

    gather_phase(at, rows, send, recv, 0, on_rows)
    stores.finish()


def up_call(F, inp, wg, wu):
    R, D = inp.shape
    n = wg.shape[1]
    T = F * R
    wide = jax.ShapeDtypeStruct((T, n), bf16)
    return pl.pallas_call(
        up_kernel,
        out_shape=[jax.ShapeDtypeStruct((F, R, D), bf16), wide, wide, wide],
        in_specs=[ANY] * 3,
        out_specs=[ANY] * 4,
        scratch_shapes=[
            pltpu.VMEM((D, 2 * n), bf16),
            pltpu.VMEM((F, R, D), bf16),
            pltpu.VMEM((2, 2 * R, n), bf16),
            pltpu.VMEM((2, 2 * R, n), bf16),
            pltpu.VMEM((2, 2 * R, n), bf16),
        ]
        + [dma(3), dma(20), dma(GATHER_COPIES), dma(GATHER_COPIES)],
        compiler_params=params(2),
        cost_estimate=cost(46),
    )(inp, wg, wu)


def down_kernel(
    C, h_ref, wd_ref, hid_ref, cot_ref, gain_ref, act_ref, der_ref, unit_ref,
    res_ref, gg_ref, all_ref, grad_ref, own_ref, mom_ref, p_ref,
    h, wd, hid, mine, gain, act, der, res, gacc, rows, grad, cot, stage, prod, b0, b1, b2, b3, b4,
    lsem, osem, asem, psem, send, recv, tsend, trecv, usend, urecv,
):
    at = Plane()
    loads = [
        local(s, d, lsem, i)
        for i, (s, d) in enumerate(
            [(cot_ref, mine), (h_ref, h), (wd_ref, wd), (hid_ref, hid), (gain_ref, gain)]
        )
    ]
    moving = Moving(at, C, mine, stage, cot, lsem, 5, tsend, trecv)
    barrier = pltpu.get_barrier_semaphore()
    moving.greet(barrier)
    pl.semaphore_signal(barrier, inc=1, device_id={"fsdp": at.fc}, device_id_type=MESH)
    pl.semaphore_wait(barrier, 2 * (C - 1) + 1)
    R = rows.shape[1]
    n = wd.shape[1]
    loads[0].wait()
    moving.first()
    loads[1].wait()
    loads[2].wait()

    def partial(chip, cols):
        return nt(h[pl.ds(pl.multiple_of(chip * 2 * R, 2 * R), 2 * R), :], wd[cols, :])

    z = moving.z
    units = []

    def between():
        moving.second()
        for k in range(1, C):
            to = (z + k) % C
            c = remote(unit_ref.at[to], mom_ref.at[z], usend, urecv, k, to, "ctx")
            c.start()
            units.append(c)
        units.append(local(unit_ref.at[z], mom_ref.at[z], lsem, 10))

    total = scatter_phase(at, partial, (b0, b1, b2, b3, b4), send, recv, 0, between)
    for c in loads[3:]:
        c.wait()
    moving.finish()
    gacc[...] = jnp.zeros_like(gacc)

    def finish(r):
        out = total(r)
        scale = rms(out)
        hat = out * scale
        res[r, :] = (hid[r, :] + hat * gain[...]).astype(bf16)
        g = cot[r, :].astype(f32)
        gacc[...] += jnp.sum(g * hat, axis=0, keepdims=True)
        rows[at.f, r, :] = back(g * gain[...], hat, scale).astype(bf16)

    row_loop(R, finish)
    saves = [local(res, res_ref, lsem, 7), local(gacc, gg_ref, lsem, 8), local(cot, own_ref, lsem, 9)]
    stores = Stores(osem)

    def on_rows(first, count):
        s = stores.slot()
        m = count * R
        start = pl.multiple_of(first * R, R)
        k = len(stores.steps)
        la = local(act_ref.at[pl.ds(start, m)], act.at[s, pl.ds(0, m)], asem, 2 * k)
        ld = local(der_ref.at[pl.ds(start, m)], der.at[s, pl.ds(0, m)], asem, 2 * k + 1)
        la.wait()
        ld.wait()

        width = 512

        @pl.loop(0, n // width)
        def _(t):
            c = pl.ds(pl.multiple_of(t * width, width), width)
            up = pl.ds(pl.multiple_of(n + t * width, width), width)
            gh = nn(rows[pl.ds(first, count)].reshape(m, rows.shape[2]), wd[:, c])
            grad[s, pl.ds(0, m), up] = (gh * act[s, pl.ds(0, m), c].astype(f32)).astype(bf16)
            grad[s, pl.ds(0, m), c] = (gh * der[s, pl.ds(0, m), c].astype(f32)).astype(bf16)

        stores.put(
            [
                (grad.at[s, pl.ds(0, m)], grad_ref.at[pl.ds(start, m)]),
                (rows.at[pl.ds(first, count)], all_ref.at[pl.ds(first, count)]),
            ]
        )

    gather_phase(at, rows, send, recv, SCATTER_COPIES, on_rows)
    F, D = rows.shape[0], rows.shape[2]
    tile, cols = prod.shape[1], p_ref.shape[3]
    puts = []
    for t in range(D // tile):
        if t >= 2:
            for c in puts[t - 2]:
                c.wait()
        rhs = rows[:, :, t * tile : (t + 1) * tile].reshape(F * R, tile)
        prod[t % 2] = lax.dot_general(
            rhs, h[...], (((0,), (0,)), ((), ())), preferred_element_type=f32
        ).astype(bf16)
        puts.append(
            [
                local(
                    prod.at[t % 2, :, pl.ds(b * cols, cols)],
                    p_ref.at[b, 0, pl.ds(t * tile, tile)],
                    psem,
                    t * (n // cols) + b,
                )
                for b in range(n // cols)
            ]
        )
    for step in puts[-2:]:
        for c in step:
            c.wait()
    for k in range(1, C):
        frm = (z - k + C) % C
        remote(mom_ref.at[frm], mom_ref.at[frm], usend, urecv, k, frm, "ctx").wait_recv()
    for c in units[:-1]:
        c.wait_send()
    units[-1].wait()
    for s in saves:
        s.wait()
    stores.finish()


def down_call(C, F, h, wd, hid, cot, gain, act, der, units):
    R, D = hid.shape
    n = wd.shape[1]
    T = F * R
    copies = SCATTER_COPIES + GATHER_COPIES
    one = jax.ShapeDtypeStruct((R, D), bf16)
    return pl.pallas_call(
        functools.partial(down_kernel, C),
        out_shape=[
            one,
            jax.ShapeDtypeStruct((1, D), f32),
            jax.ShapeDtypeStruct((F, R, D), bf16),
            jax.ShapeDtypeStruct((T, 2 * n), bf16),
            one,
            jax.ShapeDtypeStruct(units.shape, bf16),
            jax.ShapeDtypeStruct((units.shape[1], 1, D, units.shape[3]), bf16),
        ],
        in_specs=[ANY] * 8,
        out_specs=[ANY] * 7,
        scratch_shapes=[
            pltpu.VMEM((T, n), bf16),
            pltpu.VMEM((D, n), bf16),
            pltpu.VMEM((R, D), f32),
            pltpu.VMEM((R, D), bf16),
            pltpu.VMEM((1, D), f32),
            pltpu.VMEM((2, 2 * R, n), bf16),
            pltpu.VMEM((2, 2 * R, n), bf16),
            pltpu.VMEM((R, D), bf16),
            pltpu.VMEM((1, D), f32),
            pltpu.VMEM((F, R, D), bf16),
            pltpu.VMEM((2, 2 * R, 2 * n), bf16),
            pltpu.VMEM((R, D), bf16),
            pltpu.VMEM((C, R // C, D), bf16),
            pltpu.VMEM((2, 512, n), bf16),
        ]
        + scatter_scratch(R, D)
        + [dma(11), dma(15), dma(10), dma(16), dma(copies), dma(copies), dma(2 * C), dma(2 * C), dma(C), dma(C)],
        compiler_params=params(3),
        cost_estimate=cost(115),
    )(h, wd, hid, cot, gain, act, der, units)


def mid_kernel(
    grad_ref, wg_ref, wu_ref, cot_ref, ao_ref, gain_ref, wo_ref,
    res_ref, gg_ref, all_ref, gm_ref,
    grad, w, cot, ao, gain, wo, res, gacc, rows, gm, b0, b1, b2, b3, b4,
    lsem, osem, send, recv,
):
    at = Plane()
    n, e = w.shape[1] // 2, wo.shape[1]
    pairs = [
        (grad_ref, grad), (wg_ref, w.at[:, pl.ds(0, n)]), (wu_ref, w.at[:, pl.ds(n, n)]),
        (cot_ref, cot), (ao_ref, ao), (gain_ref, gain), (wo_ref.at[:, pl.ds(3 * e, e)], wo),
    ]
    loads = [local(s, d, lsem, i) for i, (s, d) in enumerate(pairs)]
    at.greet()
    R = rows.shape[1]
    for c in loads[:3]:
        c.wait()

    def partial(chip, cols):
        return nt(grad[pl.ds(pl.multiple_of(chip * 2 * R, 2 * R), 2 * R), :], w[cols, :])

    total = scatter_phase(at, partial, (b0, b1, b2, b3, b4), send, recv, 0)
    for c in loads[3:]:
        c.wait()
    gacc[...] = jnp.zeros_like(gacc)

    def finish(r):
        resid = cot[r, :].astype(f32) + total(r)
        res[r, :] = resid
        out = ao[r, :]
        scale = rms(out)
        hat = out * scale
        gacc[...] += jnp.sum(resid * hat, axis=0, keepdims=True)
        rows[at.f, r, :] = back(resid * gain[...], hat, scale).astype(bf16)

    row_loop(R, finish)
    saves = [local(res, res_ref, lsem, 8), local(gacc, gg_ref, lsem, 9)]
    stores = Stores(osem)

    def on_rows(first, count):
        s = stores.slot()
        m = count * R
        start = pl.multiple_of(first * R, R)
        lhs = rows[pl.ds(first, count)].reshape(m, rows.shape[2])
        gm[s, pl.ds(0, m), :] = nn(lhs, wo[...]).astype(bf16)
        stores.put(
            [
                (gm.at[s, pl.ds(0, m)], gm_ref.at[pl.ds(start, m)]),
                (rows.at[pl.ds(first, count)], all_ref.at[pl.ds(first, count)]),
            ]
        )

    gather_phase(at, rows, send, recv, SCATTER_COPIES, on_rows)
    for s in saves:
        s.wait()
    stores.finish()


def mid_call(F, grad, wg, wu, cot, ao, gain, wo):
    R, D = cot.shape
    n, e = 2 * wg.shape[1], wo.shape[1] // 4
    T = F * R
    copies = SCATTER_COPIES + GATHER_COPIES
    return pl.pallas_call(
        mid_kernel,
        out_shape=[
            jax.ShapeDtypeStruct((R, D), f32),
            jax.ShapeDtypeStruct((1, D), f32),
            jax.ShapeDtypeStruct((F, R, D), bf16),
            jax.ShapeDtypeStruct((T, e), bf16),
        ],
        in_specs=[ANY] * 7,
        out_specs=[ANY] * 4,
        scratch_shapes=[
            pltpu.VMEM((T, n), bf16),
            pltpu.VMEM((D, n), bf16),
            pltpu.VMEM((R, D), bf16),
            pltpu.VMEM((R, D), f32),
            pltpu.VMEM((1, D), f32),
            pltpu.VMEM((D, e), bf16),
            pltpu.VMEM((R, D), f32),
            pltpu.VMEM((1, D), f32),
            pltpu.VMEM((F, R, D), bf16),
            pltpu.VMEM((2, 2 * R, e), bf16),
        ]
        + scatter_scratch(R, D)
        + [dma(10), dma(10), dma(copies), dma(copies)],
        compiler_params=params(4),
        cost_estimate=cost(92),
    )(grad, wg, wu, cot, ao, gain, wo)


def last_kernel(
    width, q_ref, k_ref, v_ref, proj_ref, st_ref, in_ref, w_ref, res_ref, gain_ref,
    out_ref, gp_ref, gsum_ref,
    q, k, proj, st, ins, gains, gsum, gp, w, res, out, b0, b1, b2, b3, b4,
    lsem, send, recv, ssend, srecv, gsend, grecv,
):
    at = Plane()
    F, T = st.shape[0], st.shape[2]
    e = q.shape[1]
    R = res.shape[0]
    pairs = [
        (in_ref, ins.at[at.f]), (st_ref, st), (q_ref, q), (k_ref, k),
        (v_ref, gp.at[:, pl.ds(2 * e, e)]), (proj_ref.at[:, pl.ds(0, 2 * e)], proj), (w_ref.at[:, pl.ds(0, 3 * e)], w), (res_ref, res),
        (gain_ref, gains.at[at.f]),
    ]
    loads = [local(s, d, lsem, i) for i, (s, d) in enumerate(pairs)]
    barrier = pltpu.get_barrier_semaphore()
    for s in range(1, F):
        pl.semaphore_signal(barrier, inc=1, device_id={"fsdp": (at.f + s) % F}, device_id_type=MESH)
    pl.semaphore_wait(barrier, F - 1)
    loads[0].wait()
    share_stats(at, F, ins, ssend, srecv, 0)
    for c in loads[1:6]:
        c.wait()
    step = 256

    @pl.loop(0, T // step)
    def _(t):
        r = pl.ds(pl.multiple_of(t * step, step), step)
        sums = jnp.sum(st[:, :, r], axis=0)
        inner = jnp.sum(ins[:, :, r], axis=0) / width
        for row, grad in ((0, q), (1, k)):
            scale = lax.rsqrt(column(sums[row : row + 1], HEAD_DIM) / width + epsilon)
            mean = column(inner[row : row + 1], HEAD_DIM)
            for h in range(e // HEAD_DIM):
                hat = proj[r, row * e + h * HEAD_DIM : row * e + (h + 1) * HEAD_DIM] * scale
                got = scale * (grad[r, h * HEAD_DIM : (h + 1) * HEAD_DIM] - hat * mean)
                gp[r, row * e + h * HEAD_DIM : row * e + (h + 1) * HEAD_DIM] = got.astype(bf16)

    save = local(gp, gp_ref, lsem, 9)
    loads[6].wait()

    def partial(chip, cols):
        return nt(gp[pl.ds(pl.multiple_of(chip * 2 * R, 2 * R), 2 * R), :], w[cols, :])

    total = scatter_phase(at, partial, (b0, b1, b2, b3, b4), send, recv, 0)
    loads[7].wait()

    def finish(r):
        out[r, :] = (res[r, :] + total(r)).astype(bf16)

    row_loop(R, finish)
    store = local(out, out_ref, lsem, 10)
    loads[8].wait()
    share_stats(at, F, gains, gsend, grecv, 0)
    gsum[...] = jnp.sum(gains[...], axis=0)
    local(gsum, gsum_ref, lsem, 11).wait()
    store.wait()
    save.wait()


def last_call(F, wq, wk, gv, proj, st, ins, w, res, gains):
    R, D = res.shape
    n = w.shape[1] // 4 * 3
    T, e = F * R, n // 3
    return pl.pallas_call(
        functools.partial(last_kernel, D),
        out_shape=[
            jax.ShapeDtypeStruct((R, D), bf16),
            jax.ShapeDtypeStruct((T, n), bf16),
            jax.ShapeDtypeStruct((8, D), f32),
        ],
        in_specs=[ANY] * 9,
        out_specs=[ANY] * 3,
        scratch_shapes=[
            pltpu.VMEM((T, e), f32),
            pltpu.VMEM((T, e), f32),
            pltpu.VMEM((T, 2 * e), f32),
            pltpu.VMEM((F, 8, T), f32),
            pltpu.VMEM((F, 8, T), f32),
            pltpu.VMEM((F, 8, D), f32),
            pltpu.VMEM((8, D), f32),
            pltpu.VMEM((T, n), bf16),
            pltpu.VMEM((D, n), bf16),
            pltpu.VMEM((R, D), f32),
            pltpu.VMEM((R, D), bf16),
        ]
        + scatter_scratch(R, D)
        + [dma(12), dma(SCATTER_COPIES), dma(SCATTER_COPIES), dma(F), dma(F), dma(F), dma(F)],
        compiler_params=params(5),
        cost_estimate=cost(55),
    )(wq, wk, gv, proj, st, ins, w, res, gains)


def tn(a, b):
    return lax.dot_general(a, b, (((0,), (0,)), ((), ())), preferred_element_type=f32)


def grad_kernel(*refs):
    out = refs[-1]
    start = 0
    for x_ref, dy_ref in zip(refs[:-1:2], refs[1:-1:2]):
        got = tn(x_ref[...], dy_ref[...]).astype(bf16)
        units = dy_ref.shape[1] // out.shape[-1]
        for b in range(units):
            out[(start + b,) + (0,) * (len(out.shape) - 3)] = got[:, b * out.shape[-1] : (b + 1) * out.shape[-1]]
        start += units


def grad_call(pairs, units, cols, groups):
    T, D = pairs[0][0].shape
    tile = 512
    specs, args = [], []
    for x, dy in pairs:
        specs += [
            pl.BlockSpec((T, tile), lambda g, d: (0, d)),
            pl.BlockSpec((T, dy.shape[1] // groups), lambda g, d: (0, g)),
        ]
        args += [x, dy]
    return pl.pallas_call(
        grad_kernel,
        out_shape=jax.ShapeDtypeStruct((units, groups, D, cols), bf16),
        grid=(groups, D // tile),
        in_specs=specs,
        out_specs=pl.BlockSpec((units, 1, tile, cols), lambda g, d: (0, g, d, 0)),
        compiler_params=pltpu.CompilerParams(vmem_limit_bytes=VMEM_LIMIT),
        cost_estimate=cost(12 * groups),
    )(*args)


def share_stats(at, F, st, send, recv, base):
    sent = []
    for k in range(1, F):
        to = (at.f + k) % F
        c = remote(st.at[at.f], st.at[at.f], send, recv, base + k, to)
        c.start()
        sent.append(c)
    for k in range(1, F):
        frm = (at.f - k + F) % F
        remote(st.at[frm], st.at[frm], send, recv, base + k, frm).wait_recv()
    for c in sent:
        c.wait_send()


def row_sums(a, b):
    r = lax.broadcasted_iota(jnp.int32, (8, a.shape[1]), 0)
    one, two = (r == 0).astype(f32), (r == 1).astype(f32)

    def half(sel, v):
        return lax.dot_general(
            sel, v, (((1,), (1,)), ((), ())), preferred_element_type=f32, precision=lax.Precision.HIGHEST
        )

    return half(one, a) + half(two, b)


def column(row, lanes):
    return jnp.broadcast_to(row, (lanes, row.shape[1])).T


def turn(v, cos, sin):
    return v * cos + pltpu.roll(v, HEAD_DIM // 2, 1) * sin


def seq_columns(st, c, chips, R):
    return jnp.concatenate([st[:, pl.ds(pl.multiple_of((2 * j + c) * R, R), R)] for j in range(chips)], axis=1)


def attend_kernel(width, q_ref, k_ref, v_ref, st_ref, gq_ref, gk_ref, cos_ref, sin_ref, pos_ref, posc_ref, mix_ref, qr_ref, kr_ref, lse_ref):
    c = pl.program_id(0)
    chips, R = q_ref.shape[0], q_ref.shape[2]
    L = chips * R
    sums = jnp.sum(seq_columns_all(st_ref, c, chips, R), axis=0)
    cos, sin = cos_ref[0], sin_ref[0]

    def norm_turn(ref, row, gain):
        scale = lax.rsqrt(column(sums[row : row + 1], HEAD_DIM) / width + epsilon)
        return turn(ref[...].reshape(L, HEAD_DIM) * scale * gain[...], cos, sin)

    qr = (norm_turn(q_ref, 0, gq_ref) * HEAD_DIM ** (-0.5)).astype(bf16)
    kr = norm_turn(k_ref, 1, gk_ref).astype(bf16)
    v = v_ref[...].reshape(L, HEAD_DIM).astype(bf16)
    qr_ref[...] = qr.reshape(qr_ref.shape)
    kr_ref[...] = kr.reshape(kr_ref.shape)
    pos = pos_ref[0]
    for t in range(chips):
        rows = slice(t * R, (t + 1) * R)
        s = nt(qr[rows], kr)
        s = jnp.where(posc_ref[0, rows, :1] >= pos, s, -1e30)
        top = jnp.max(s, axis=-1, keepdims=True)
        e = jnp.exp(s - top)
        total = jnp.sum(e, axis=-1, keepdims=True)
        p = (e * (1.0 / total)).astype(bf16)
        mix_ref[t, 0] = nn(p, v).astype(bf16)
        lse_ref[0, 0, rows, :] = jnp.broadcast_to(top + jnp.log(total), (R, HEAD_DIM))


def seq_columns_all(st_ref, c, chips, R):
    return jnp.concatenate(
        [st_ref[:, :, pl.ds(pl.multiple_of((2 * j + c) * R, R), R)] for j in range(chips)], axis=2
    )


def attend_specs(chips, R, heads, F, L):
    def at(offset):
        return pl.BlockSpec((chips, 1, R, HEAD_DIM), lambda c, h: (0, c, 0, offset + h))

    gain = pl.BlockSpec((1, HEAD_DIM), lambda c, h: (0, h))
    table = pl.BlockSpec((1, L, HEAD_DIM), lambda c, h: (c, 0, 0))
    stats = pl.BlockSpec((F, 8, F * R), lambda c, h: (0, 0, 0))
    posr = pl.BlockSpec((1, 1, L), lambda c, h: (c, 0, 0))
    lse = pl.BlockSpec((1, 1, L, HEAD_DIM), lambda c, h: (c, h, 0, 0))
    return at, gain, table, stats, posr, lse


def attend_call(F, proj, st, gq, gk, cos, sin, pos, posc):
    R = proj.shape[0] // F
    e = proj.shape[1] // 3
    heads, chips = e // HEAD_DIM, F // 2
    L = chips * R
    at, gain, table, stats, posr, lse = attend_specs(chips, R, heads, F, L)
    view = proj.reshape(chips, 2, R, 3 * e)
    flat = jax.ShapeDtypeStruct((chips, 2, R, e), bf16)
    out = pl.pallas_call(
        functools.partial(attend_kernel, heads * HEAD_DIM * F),
        out_shape=[flat, flat, flat, jax.ShapeDtypeStruct((2, heads, L, HEAD_DIM), f32)],
        grid=(2, heads),
        in_specs=[at(0), at(heads), at(2 * heads), stats, gain, gain, table, table, posr, table],
        out_specs=[at(0), at(0), at(0), lse],
        compiler_params=pltpu.CompilerParams(vmem_limit_bytes=VMEM_LIMIT),
        cost_estimate=cost(15),
    )(view, view, view, st, gq, gk, cos, sin, pos, posc)
    return out


def attend_back_kernel(
    width, q_ref, k_ref, v_ref, qr_ref, kr_ref, gm_ref, lse_ref, st_ref, gq_ref, gk_ref, cos_ref, sin_ref, pos_ref, posc_ref,
    wq_ref, wk_ref, gv_ref, in_ref, gg_ref, dk, dv, dq,
):
    c = pl.program_id(0)
    chips, R = q_ref.shape[0], q_ref.shape[2]
    L = chips * R
    kr = kr_ref[...].reshape(L, HEAD_DIM)
    v = v_ref[...].reshape(L, HEAD_DIM).astype(bf16)
    pos = pos_ref[0]
    dk[...] = jnp.zeros_like(dk)
    dv[...] = jnp.zeros_like(dv)
    for t in range(chips):
        rows = slice(t * R, (t + 1) * R)
        qt, gm = qr_ref[t, 0], gm_ref[t, 0]
        s = nt(qt, kr)
        s = jnp.where(posc_ref[0, rows, :1] >= pos, s, -1e30)
        p = jnp.exp(s - lse_ref[0, 0, rows, :1])
        dp = nt(gm, v)
        dv[...] += lax.dot_general(p.astype(bf16), gm, (((0,), (0,)), ((), ())), preferred_element_type=f32)
        inner = jnp.sum(dp * p, axis=-1, keepdims=True)
        ds = (p * (dp - inner)).astype(bf16)
        dq[rows, :] = nn(ds, kr)
        dk[...] += lax.dot_general(ds, qt, (((0,), (0,)), ((), ())), preferred_element_type=f32)
    gv_ref[...] = dv[...].astype(bf16).reshape(gv_ref.shape)
    sums = jnp.sum(seq_columns_all(st_ref, c, chips, R), axis=0)
    cos, sin = cos_ref[0], sin_ref[0]

    def finish(grad, ref, row, gain, out):
        norm = turn(grad, cos, -sin)
        hat = ref[...].reshape(L, HEAD_DIM) * lax.rsqrt(column(sums[row : row + 1], HEAD_DIM) / width + epsilon)
        gg_ref[0, 0, row : row + 1, :] = jnp.sum(norm * hat, axis=0, keepdims=True)
        weighted = norm * gain[...]
        out[...] = weighted.reshape(out.shape)
        return weighted * hat

    gg_ref[...] = jnp.zeros_like(gg_ref)
    in_ref[0, 0] = row_sums(
        finish(dq[...] * HEAD_DIM ** (-0.5), q_ref, 0, gq_ref, wq_ref), finish(dk[...], k_ref, 1, gk_ref, wk_ref)
    )


def attend_back_call(F, proj, qr, kr, gm, lse_in, st, gq, gk, cos, sin, pos, posc):
    R = proj.shape[0] // F
    e = proj.shape[1] // 3
    heads, chips = e // HEAD_DIM, F // 2
    L = chips * R
    at, gain, table, stats, posr, lse = attend_specs(chips, R, heads, F, L)
    view = proj.reshape(chips, 2, R, 3 * e)
    flat = (chips, 2, R, e)
    small = pl.BlockSpec((1, 1, 8, L), lambda c, h: (c, h, 0, 0))
    tiny = pl.BlockSpec((1, 1, 8, HEAD_DIM), lambda c, h: (c, h, 0, 0))
    wide = jax.ShapeDtypeStruct(flat, f32)
    return pl.pallas_call(
        functools.partial(attend_back_kernel, heads * HEAD_DIM * F),
        out_shape=[
            wide, wide, jax.ShapeDtypeStruct(flat, bf16),
            jax.ShapeDtypeStruct((2, heads, 8, L), f32),
            jax.ShapeDtypeStruct((2, heads, 8, HEAD_DIM), f32),
        ],
        grid=(2, heads),
        in_specs=[
            at(0), at(heads), at(2 * heads), at(0), at(0), at(0), lse, stats, gain, gain, table, table, posr, table,
        ],
        out_specs=[at(0), at(0), at(0), small, tiny],
        scratch_shapes=[pltpu.VMEM((L, HEAD_DIM), f32)] * 3,
        compiler_params=pltpu.CompilerParams(vmem_limit_bytes=VMEM_LIMIT),
        cost_estimate=cost(35),
    )(view, view, view, qr, kr, gm.reshape(flat), lse_in, st, gq, gk, cos, sin, pos, posc)


def newton_kernel(
    C, m_ref, rows_ref, gain_ref, out_ref, home_ref, gsum_ref,
    v, gram, y, yf, stat, stage, gains, gsum,
    lsem, osem, vsend, vrecv, ysend, yrecv, ssend, srecv, tsend, trecv, gsend, grecv, usend, urecv, usem,
):
    me = lax.axis_index("fsdp")
    z = lax.axis_index("ctx")
    core, chip = me % 2, me // 2
    peer = me + 1 - 2 * core
    F = 2 * C
    cols = m_ref.shape[2]
    gload = local(gain_ref, gains.at[z], lsem, 1)
    barrier = pltpu.get_barrier_semaphore()
    for k in range(1, C):
        pl.semaphore_signal(barrier, inc=1, device_id={"ctx": (z + k) % C}, device_id_type=MESH)
    for k in range(1, F):
        pl.semaphore_signal(barrier, inc=1, device_id={"fsdp": (me + k) % F}, device_id_type=MESH)
    pl.semaphore_wait(barrier, C + F - 2)
    rows_in = v.shape[1] // C
    units_sent, units_kept = [], []
    for k in range(F):
        to = (me + k) % F
        for b in range(C):
            src = m_ref.at[to // 2, pl.ds((2 * b + to % 2) * rows_in, rows_in)]
            dst = v.at[0, pl.ds(b * rows_in, rows_in), pl.ds(me * cols, cols)]
            if k == 0:
                units_kept.append(local(src, dst, usem, b))
            else:
                c = remote(src, dst, usend, urecv, k * C + b, to)
                c.start()
                units_sent.append(c)
    piece = rows_ref.shape[1] // C

    def part(j):
        return pl.ds(j * piece, piece)

    sent, keep = [], []
    for a in range(2):
        for k in range(1, C):
            to = (z + k) % C
            c = remote(rows_ref.at[a, part(to)], stage.at[a, z], tsend, trecv, 2 * C * a + k, to, "ctx")
            c.start()
            sent.append(c)
        keep.append(local(rows_ref.at[a, part(z)], stage.at[a, z], lsem, 2 + a))
    gload.wait()
    for k in range(1, C):
        c = remote(gains.at[z], gains.at[z], gsend, grecv, k, (z + k) % C, "ctx")
        c.start()
        sent.append(c)

    def leave_layer():
        for a in range(2):
            for k in range(1, C):
                frm = (z - k + C) % C
                remote(stage.at[a, frm], stage.at[a, frm], tsend, trecv, 2 * C * a + k, frm, "ctx").wait_recv()
            keep[a].wait()
            for k in range(1, C):
                to = (chip + k) % C
                c = remote(
                    stage.at[a, to], home_ref.at[a, part(chip)], tsend, trecv, 2 * C * a + C + k, 2 * to + core
                )
                c.start()
                sent.append(c)
            keep[a] = local(stage.at[a, chip], home_ref.at[a, part(chip)], lsem, 4 + a)

    def arrived_home():
        for a in range(2):
            keep[a].wait()
            for k in range(1, C):
                frm = (chip - k + C) % C
                dst = home_ref.at[a, part(frm)]
                remote(dst, dst, tsend, trecv, 2 * C * a + C + k, 2 * frm + core).wait_recv()
        for k in range(1, C):
            frm = (z - k + C) % C
            remote(gains.at[frm], gains.at[frm], gsend, grecv, k, frm, "ctx").wait_recv()
        gsum[...] = jnp.sum(gains[...], axis=0)
        local(gsum, gsum_ref, lsem, 6).wait()
        for c in sent:
            c.wait_send()

    for k in range(1, F):
        frm = (me - k + F) % F
        for b in range(C):
            dst = v.at[0, pl.ds(b * rows_in, rows_in), pl.ds(frm * cols, cols)]
            remote(dst, dst, usend, urecv, k * C + b, frm).wait_recv()
    for c in units_sent:
        c.wait_send()
    for c in units_kept:
        c.wait()
    M, D = v.shape[1], v.shape[2]
    tile, col = 512, 1024
    tiles = M // tile

    def block(i):
        return pl.ds(i * tile, tile)

    def swap(buf, i, sends, recvs):
        return remote(buf.at[0, block(i)], buf.at[1, block(i)], sends, recvs, i, peer)

    pending = [swap(v, i, vsend, vrecv) for i in range(tiles)]
    for c in pending:
        c.start()
    stat[0] = jnp.zeros_like(stat[0])

    def add(r):
        part = v[0, r, :].astype(f32)
        stat[0] += jnp.sum((part * part).reshape(-1, 8, D // 128, 128), axis=(0, 2))

    row_loop(M, add)
    share = remote(stat.at[0], stat.at[1], ssend, srecv, 0, peer)
    share.start()
    share.wait()
    inv = 1.0 / (jnp.sqrt(jnp.sum(stat[0] + stat[1])) + 1e-07)

    for iteration in range(NS_STEPS):
        factor = inv if iteration == 0 else 1.0

        def grams(h, n):
            rhs = pl.ds(pl.multiple_of(n * col, col), col)
            cols = pl.ds(pl.multiple_of(h * M + n * col, col), col)

            @pl.loop(0, tiles)
            def _(i):
                rows = pl.ds(pl.multiple_of(i * tile, tile), tile)
                got = nt(v[0, rows, :], v[h, rhs, :])
                if iteration == 0:
                    got = got * (factor * factor)
                gram[rows, cols] = got.astype(bf16)

        @pl.loop(0, M // col)
        def _(n):
            grams(0, n)

        for c in pending:
            c.wait()

        @pl.loop(0, M // col)
        def _(n):
            grams(1, n)

        def times(src, i, n):
            rows = block(i)
            cols = pl.ds(pl.multiple_of(n * col, col), col)
            return cols, nn(gram[rows, :M], src[0, :, cols]) + nn(gram[rows, M:], src[1, :, cols])

        pending = []
        for i in range(tiles):

            @pl.loop(0, D // col)
            def _(n):
                cols, got = times(v, i, n)
                if iteration == 0:
                    got = got * factor
                yf[block(i), cols] = got
                y[0, block(i), cols] = got.astype(bf16)

            c = swap(y, i, ysend, yrecv)
            c.start()
            pending.append(c)
        for c in pending:
            c.wait()
        if iteration == NS_STEPS - 1:
            leave_layer()
        pending = []
        for i in range(tiles):

            @pl.loop(0, D // col)
            def _(n):
                cols, got = times(y, i, n)
                old = v[0, block(i), cols].astype(f32)
                if iteration == 0:
                    old = old * factor
                v[0, block(i), cols] = (
                    quintic_one * old + quintic_two * yf[block(i), cols] + quintic_three * got
                ).astype(bf16)

            if iteration < NS_STEPS - 1:
                c = swap(v, i, vsend, vrecv)
            else:
                c = pltpu.make_async_copy(v.at[0, block(i)], out_ref.at[block(i)], osem.at[i])
            c.start()
            pending.append(c)
    arrived_home()
    for c in pending:
        c.wait()


def newton_call(C, x, rows, gains):
    _, D, cols = x.shape
    M = D // 2
    _, R, _ = rows.shape
    n = M // 512
    return pl.pallas_call(
        functools.partial(newton_kernel, C),
        out_shape=[
            jax.ShapeDtypeStruct((M, D), bf16),
            jax.ShapeDtypeStruct((2, R, D), bf16),
            jax.ShapeDtypeStruct((8, D), f32),
        ],
        in_specs=[ANY] * 3,
        out_specs=[ANY] * 3,
        scratch_shapes=[
            pltpu.VMEM((2, M, D), bf16),
            pltpu.VMEM((M, 2 * M), bf16),
            pltpu.VMEM((2, M, D), bf16),
            pltpu.VMEM((M, D), f32),
            pltpu.VMEM((2, 8, 128), f32),
            pltpu.VMEM((2, C, R // C, D), bf16),
            pltpu.VMEM((C, 8, D), f32),
            pltpu.VMEM((8, D), f32),
            dma(7), dma(n), dma(n), dma(n), dma(n), dma(n), dma(1), dma(1),
            dma(4 * C), dma(4 * C), dma(C), dma(C), dma(2 * C * C), dma(2 * C * C), dma(C),
        ],
        compiler_params=params(6),
        cost_estimate=cost(95),
    )(x, rows, gains)


def project(C, F, x, w):
    own = to_layer(C, F, x)
    rows = token_rows(own)
    return own, rows, dot(rows, w, 1, 0)


def attn_out_and_up(C, F, mixed, wo, x, gain, wg, wu):
    if kernels_fit(C, F):
        hidden_in, out, inp = out_call(F, mixed, wo, x, gain)
        return (hidden_in, out, *up_call(F, inp, wg, wu))
    out = token_sums(dot(mixed, wo, 1, 1))
    hidden_in = x.astype(f32) + out * rms(out) * gain
    rows = token_rows(hidden_in.astype(bf16))
    g, u = dot(rows, wg, 1, 0), dot(rows, wu, 1, 0)
    sig = jax.nn.sigmoid(g)
    der = u * (sig * (1.0 + g * (1.0 - sig)))
    act = g * sig
    return hidden_in, out, rows, act.astype(bf16), der.astype(bf16), (act * u).astype(bf16)


def down_and_back(C, F, h, wd, hidden_in, cot, gain, act, der, units):
    if kernels_fit(C, F):
        return down_call(C, F, h, wd, hidden_in, cot, gain, act, der, units)
    cot = to_layer(C, F, cot)
    out = token_sums(dot(h, wd, 1, 1))
    scale = rms(out)
    hat = out * scale
    g = cot.astype(f32)
    rows = token_rows(back(g * gain, hat, scale).astype(bf16))
    gh = dot(rows, wd, 1, 0)
    return (
        (hidden_in + hat * gain).astype(bf16),
        jnp.sum(g * hat, axis=0, keepdims=True),
        rows,
        jnp.concatenate([(gh * der.astype(f32)).astype(bf16), (gh * act.astype(f32)).astype(bf16)], axis=1),
        cot,
        None,
        None,
    )


def back_to_attn(C, F, grad, wg, wu, cot, out, gain, wo):
    if kernels_fit(C, F):
        return mid_call(F, grad, wg, wu, cot, out, gain, wo)
    resid = cot.astype(f32) + token_sums(dot(grad, jnp.concatenate([wg, wu], axis=1), 1, 1))
    scale = rms(out)
    hat = out * scale
    rows = token_rows(back(resid * gain, hat, scale).astype(bf16))
    return resid, jnp.sum(resid * hat, axis=0, keepdims=True), rows, dot(rows, wo, 1, 0).astype(bf16)


def back_to_input(C, F, grad_projected, w, resid):
    return (resid + token_sums(dot(grad_projected, w, 1, 1))).astype(bf16)


def kernels_fit(C, F):
    return C == 4 and F == 8 and UNITS_ATTN * 4 * 2 == C * F


def to_layer(C, F, x):
    z, chip = lax.axis_index("ctx"), lax.axis_index("fsdp") // 2
    x = x.reshape(C, x.shape[0] // C, x.shape[1])
    got = []
    for k in range(C):
        pairs = [
            (s * F + f, (f // 2) * F + 2 * ((s + k) % C) + f % 2) for s in range(C) for f in range(F)
        ]
        block = lax.dynamic_index_in_dim(x, (z + k) % C, 0, keepdims=False)
        got.append(lax.ppermute(block, BOTH, pairs))
    got = jnp.stack(got)
    got = [lax.dynamic_index_in_dim(got, (chip - s + C) % C, 0, keepdims=False) for s in range(C)]
    return jnp.concatenate(got, axis=0)


def from_layer(C, F, x):
    z, chip = lax.axis_index("ctx"), lax.axis_index("fsdp") // 2
    x = x.reshape(C, x.shape[0] // C, x.shape[1])
    got = []
    for k in range(C):
        pairs = [
            ((f // 2) * F + 2 * ((s + k) % C) + f % 2, s * F + f) for s in range(C) for f in range(F)
        ]
        block = lax.dynamic_index_in_dim(x, (chip - k + C) % C, 0, keepdims=False)
        got.append(lax.ppermute(block, BOTH, pairs))
    got = jnp.stack(got)
    got = [lax.dynamic_index_in_dim(got, (j - z + C) % C, 0, keepdims=False) for j in range(C)]
    return jnp.concatenate(got, axis=0)


def shards(C, F, layer_input, cotangent, positions, w_attn, w_ffn, gains, mom_attn, mom_ffn, gain_mom):
    z = lax.axis_index("ctx")
    f = lax.axis_index("fsdp")
    local_rows, width = layer_input.shape[1], layer_input.shape[2]
    seq_total, seq_length = positions.shape
    dz, head_cols = w_attn.shape[1], w_attn.shape[2]
    local_heads = head_cols // HEAD_DIM
    block_count = w_ffn.shape[2]
    per = seq_total // C
    piece = local_rows // C
    chips = F // per
    tokens = F * local_rows
    hidden_cols = block_count * head_cols
    units = UNITS_ATTN + 3 * block_count
    parts = C * F // units

    def after(a, b):
        return lax.optimization_barrier((a, b))[0]

    def rows_gather(shard):
        return lax.all_gather(shard, "ctx", axis=0, tiled=True)

    def product(units, groups, *pairs):
        pairs = [(x.reshape(tokens, width), dy) for x, dy in pairs]
        if kernels:
            return grad_call(pairs, units, head_cols, groups)
        grad = jnp.concatenate([dot(x, dy, 0, 0).astype(bf16) for x, dy in pairs], axis=1)
        return jnp.transpose(grad.reshape(width, groups, units, head_cols), (2, 1, 0, 3))

    def scatter(grad):
        if kernels:
            return lax.psum_scatter(grad, "ctx", scatter_dimension=0, tiled=True)[0]
        return lax.psum_scatter(grad, "ctx", scatter_dimension=2, tiled=True)

    kernels = kernels_fit(C, F)
    w_heads = rows_gather(jnp.concatenate([w_attn[i] for i in range(UNITS_ATTN)], axis=1))
    w_qkv, w_out = (w_heads, w_heads) if kernels else (w_heads[:, : 3 * head_cols], w_heads[:, 3 * head_cols :])
    ffn_flat = w_ffn.reshape(3, dz, hidden_cols)
    w_gate = rows_gather(ffn_flat[0])
    w_up = rows_gather(ffn_flat[1])
    w_down = rows_gather(ffn_flat[2])

    gain_query = lax.dynamic_slice_in_dim(gains[0], f * head_cols, head_cols)
    gain_key = lax.dynamic_slice_in_dim(gains[1], f * head_cols, head_cols)
    pos = lax.dynamic_slice_in_dim(positions, z * per, per, 0)
    pos = jnp.transpose(pos.reshape(per, C, chips, piece), (0, 2, 1, 3)).reshape(per, seq_length)
    cosine_table, sine_table = rotary_tables(pos)

    def heads(a):
        return jnp.transpose(
            a.reshape(chips, per, local_rows, local_heads, HEAD_DIM), (1, 0, 2, 3, 4)
        ).reshape(per, seq_length, local_heads, HEAD_DIM)

    def unheads(a):
        return jnp.transpose(
            a.reshape(per, chips, local_rows, local_heads, HEAD_DIM), (1, 0, 2, 3, 4)
        ).reshape(tokens, head_cols)

    if kernels:
        sign = jnp.where(jnp.arange(HEAD_DIM) < HEAD_DIM // 2, -1.0, 1.0)
        tables = (
            gain_query[None],
            gain_key[None],
            jnp.broadcast_to(cosine_table[:, :, 0], (per, seq_length, HEAD_DIM)),
            sine_table[:, :, 0] * sign,
            pos.astype(f32)[:, None, :],
            jnp.broadcast_to(pos.astype(f32)[..., None], (per, seq_length, HEAD_DIM)),
        )
        own_input, input_all = enter_call(C, F, layer_input.reshape(local_rows, width))
        projected, stats = qkv_call(F, input_all, w_qkv)
        attn_mixed, query_rows, key_rows, log_total = attend_call(F, projected, stats, *tables)
        attn_mixed = attn_mixed.reshape(tokens, head_cols)
    else:
        own_input, input_all, projected = project(C, F, layer_input.reshape(local_rows, width), w_qkv)
        query_raw = projected[:, :head_cols]
        key_raw = projected[:, head_cols : 2 * head_cols]
        value_raw = projected[:, 2 * head_cols :]
        query_total, key_total = norm_stats(
            jnp.sum(query_raw * query_raw, axis=-1), jnp.sum(key_raw * key_raw, axis=-1)
        )
        query_scale = lax.rsqrt(query_total / width + epsilon)[..., None]
        key_scale = lax.rsqrt(key_total / width + epsilon)[..., None]
        query_hat = query_raw * query_scale
        key_hat = key_raw * key_scale
        query_rows = (
            rotate(heads(query_hat * gain_query), cosine_table, sine_table) * HEAD_DIM ** (-0.5)
        ).astype(bf16)
        key_rows = rotate(heads(key_hat * gain_key), cosine_table, sine_table).astype(bf16)
        value_rows = heads(value_raw.astype(bf16))
        attn_mixed, log_total = attend(query_rows, key_rows, value_rows, pos)
        attn_mixed = unheads(attn_mixed)
    hidden_in, attn_out, mlp_all, act, der, hidden = attn_out_and_up(
        C, F, attn_mixed, w_out, own_input, gains[2:3], w_gate, w_up
    )
    by_layer = None
    if kernels:
        by_layer = jnp.concatenate(
            [mom_attn[:, None].astype(bf16), jnp.transpose(mom_ffn.astype(bf16), (2, 0, 1, 3))], axis=1
        )
    result, mlp_gain, grad_mlp_all, grad_ffn_in, own_grad, mom_own, p_down = down_and_back(
        C, F, hidden, w_down, hidden_in, cotangent.reshape(local_rows, width), gains[3:4], act, der, by_layer
    )
    if kernels:
        mom_own = jnp.swapaxes(mom_own, 0, 1)
    else:
        p_down = product(block_count, 1, (grad_mlp_all, hidden))
    g_down = scatter(p_down)
    p_gate_up = product(block_count, 2, (mlp_all, grad_ffn_in))
    if kernels:
        grad_ffn_in, p_gate_up = lax.optimization_barrier((grad_ffn_in, p_gate_up))
    g_gate_up = scatter(p_gate_up)
    grad_resid, attn_gain, grad_attn_all, grad_mixed = back_to_attn(
        C, F, grad_ffn_in, w_gate, w_up, own_grad, attn_out, gains[2:3], w_out
    )
    if kernels:
        grad_mixed = after(grad_mixed, g_down)
        weighted_q, weighted_k, grad_value, inner, gain_cols = attend_back_call(
            F, projected, query_rows, key_rows, grad_mixed, log_total, stats, *tables
        )
        inner = jnp.transpose(
            jnp.sum(inner, axis=1).reshape(per, 8, chips, local_rows), (1, 2, 0, 3)
        ).reshape(8, tokens)
        gain_cols = jnp.sum(gain_cols, axis=0)
        query_gain_cols = gain_cols[:, 0].reshape(head_cols)
        key_gain_cols = gain_cols[:, 1].reshape(head_cols)
        flat = (tokens, head_cols)
        zero = jnp.zeros((width,), f32)
        gain_local = jnp.stack(
            [
                lax.dynamic_update_slice(zero, query_gain_cols, (f * head_cols,)),
                lax.dynamic_update_slice(zero, key_gain_cols, (f * head_cols,)),
                attn_gain[0],
                mlp_gain[0],
                *[zero] * 4,
            ]
        )
        grad_rows, grad_projected, gain_layer = last_call(
            F, weighted_q.reshape(flat), weighted_k.reshape(flat), grad_value.reshape(flat),
            projected, stats, inner, w_qkv, grad_resid, gain_local,
        )
    else:
        grad_query, grad_key, grad_value = attend_back(
            query_rows, key_rows, value_rows, pos, heads(grad_mixed), log_total
        )
        grad_query_norm = unheads(unrotate(grad_query * HEAD_DIM ** (-0.5), cosine_table, sine_table))
        grad_key_norm = unheads(unrotate(grad_key, cosine_table, sine_table))
        query_gain_cols = jnp.sum(grad_query_norm * query_hat, axis=0)
        key_gain_cols = jnp.sum(grad_key_norm * key_hat, axis=0)
        query_weighted = grad_query_norm * gain_query
        key_weighted = grad_key_norm * gain_key
        query_inner, key_inner = norm_stats(
            jnp.sum(query_weighted * query_hat, axis=-1), jnp.sum(key_weighted * key_hat, axis=-1)
        )
        grad_query_raw = query_scale * (query_weighted - query_hat * (query_inner / width)[..., None])
        grad_key_raw = key_scale * (key_weighted - key_hat * (key_inner / width)[..., None])
        grad_projected = jnp.concatenate(
            [grad_query_raw.astype(bf16), grad_key_raw.astype(bf16), unheads(grad_value).astype(bf16)],
            axis=1,
        )
        grad_rows = back_to_input(C, F, grad_projected, w_qkv, grad_resid)
    g_attn = scatter(
        product(UNITS_ATTN, 1, (input_all, grad_projected), (grad_attn_all, attn_mixed))
    )
    if not kernels:
        grad_input = from_layer(C, F, grad_rows)
        result = from_layer(C, F, result)
        zero = jnp.zeros((width,), f32)
        gain_local = jnp.stack(
            [
                lax.dynamic_update_slice(zero, query_gain_cols, (f * head_cols,)),
                lax.dynamic_update_slice(zero, key_gain_cols, (f * head_cols,)),
                attn_gain[0],
                mlp_gain[0],
            ]
        )
        gain_total = jnp.sum(lax.all_gather(gain_local, BOTH, axis=0, tiled=False), axis=0)

    if kernels:
        got = jnp.stack([g_attn[0], g_gate_up[0], g_gate_up[1], g_down[0]])
        mom = mom_own.reshape(got.shape).astype(f32)
        owned = (momentum * mom + got.astype(f32)).astype(bf16)
        sent_back = got.reshape(UNITS_ATTN, C, dz, head_cols)
        sent_back = lax.all_to_all(sent_back, "ctx", split_axis=1, concat_axis=0, tiled=False)
        sent_back = sent_back.reshape(C, UNITS_ATTN, dz, head_cols).astype(f32)
        grad_attn = sent_back[:, 0]
        grad_ffn = jnp.transpose(sent_back[:, 1:], (1, 2, 0, 3))
        own, back_rows, gain_total = newton_call(C, owned, jnp.stack([result, grad_rows]), gain_layer)
        result, grad_input, gain_total = back_rows[0], back_rows[1], gain_total[:4]
    else:
        grad_attn = g_attn[:, 0].astype(f32)
        grad_ffn = jnp.transpose(
            jnp.concatenate([g_gate_up, g_down], axis=1).astype(f32), (1, 2, 0, 3)
        )
    new_attn = momentum * mom_attn + grad_attn
    new_ffn = momentum * mom_ffn + grad_ffn
    if not kernels:
        send = jnp.concatenate(
            [
                new_attn.astype(bf16),
                jnp.transpose(new_ffn.astype(bf16), (0, 2, 1, 3)).reshape(3 * block_count, dz, head_cols),
            ],
            axis=0,
        ).reshape(C * F, dz // parts, head_cols)
        own = lax.all_to_all(send, BOTH, split_axis=0, concat_axis=0, tiled=True)
        own = jnp.transpose(own.reshape(C, F, dz // parts, head_cols), (0, 2, 1, 3)).reshape(
            C * dz // parts, F * head_cols
        )

        def peers(a):
            out = [a]
            for s in range(1, parts):
                pairs = [(i, i - i % parts + (i + parts - s) % parts) for i in range(C * F)]
                out.append(lax.ppermute(a, BOTH, pairs))
            return out

        own32 = own.astype(f32)
        square = jnp.sum(own32 * own32)
        total = sum(peers(square.reshape(1, 1)))
        inv = 1.0 / (jnp.sqrt(total) + 1e-07)
        for iteration in range(NS_STEPS):
            factor = inv if iteration == 0 else 1.0
            every = peers(own)
            gram = [(dot(own, b, 1, 1) * (factor * factor)).astype(bf16) for b in every]
            product = sum(dot(g, b, 1, 0) for g, b in zip(gram, every)) * factor
            product_all = peers(product.astype(bf16))
            product_two = sum(dot(g, b, 1, 0) for g, b in zip(gram, product_all))
            own = (
                quintic_one * factor * own.astype(f32) + quintic_two * product + quintic_three * product_two
            ).astype(bf16)
    home = jnp.transpose(own.reshape(C, dz // parts, F, head_cols), (0, 2, 1, 3)).reshape(
        C * F, dz // parts, head_cols
    )
    steps = lax.all_to_all(home, BOTH, split_axis=0, concat_axis=0, tiled=True)
    steps = -muon_rate * steps.astype(f32)
    if kernels:
        steps = steps.reshape(C, UNITS_ATTN, dz, head_cols)
        step_attn = steps[:, 0]
        step_ffn = jnp.transpose(steps[:, 1:], (1, 2, 0, 3))
    else:
        steps = steps.reshape(units, dz, head_cols)
        step_attn = steps[:UNITS_ATTN]
        step_ffn = jnp.transpose(
            steps[UNITS_ATTN:].reshape(3, block_count, dz, head_cols), (0, 2, 1, 3)
        )
    new_gain_mom = momentum * gain_mom + gain_total
    return (
        result.reshape(layer_input.shape),
        grad_input.astype(f32).reshape(layer_input.shape),
        grad_attn,
        grad_ffn,
        gain_total,
        new_attn,
        new_ffn,
        new_gain_mom,
        step_attn,
        step_ffn,
        -gain_rate * new_gain_mom,
    )


def solution(mesh):
    tokens = P("fsdp", "ctx", None)
    attn = P(None, "ctx", "fsdp")
    ffn = P(None, "ctx", None, "fsdp")
    in_specs = (tokens, tokens, P(), attn, ffn, P(), attn, ffn, P())
    out_specs = (tokens, tokens, attn, ffn, P(), attn, ffn, P(), attn, ffn, P())
    body = functools.partial(shards, mesh.shape["ctx"], mesh.shape["fsdp"])
    return jax.shard_map(body, mesh=mesh, in_specs=in_specs, out_specs=out_specs, check_vma=False)
```

```python
import functools
import jax
import jax.numpy as jnp
from jax import lax
from jax.experimental import pallas as pl
from jax.experimental.pallas import tpu as pltpu
from jax.sharding import PartitionSpec as P

NS_STEPS = 3
HEAD_DIM = 128
UNITS_ATTN = 4

epsilon = 1e-06
rope_theta = 500000.0
quintic_one = 3.4445
quintic_two = -4.775
quintic_three = 2.0315
momentum = 0.95
muon_rate = 1.0
gain_rate = 0.0005
BOTH = ("ctx", "fsdp")
bf16 = jnp.bfloat16
f32 = jnp.float32


def dot(a, b, ca, cb):
    return lax.dot_general(a, b, (((ca,), (cb,)), ((), ())), preferred_element_type=f32)


def token_rows(operand):
    return lax.all_gather(operand, "fsdp", axis=0, tiled=True)


def token_sums(operand):
    return lax.psum_scatter(operand.astype(bf16), "fsdp", scatter_dimension=0, tiled=True).astype(f32)


def norm_stats(first_sum, second_sum):
    got = lax.all_gather(jnp.stack([first_sum, second_sum]), "fsdp", axis=0, tiled=False)
    total = jnp.sum(got, axis=0)
    return total[0], total[1]


def rms_back(upstream, normed, inv_scale):
    return inv_scale * (upstream - normed * jnp.mean(upstream * normed, axis=-1, keepdims=True))


def rotary_tables(slot_order):
    half_dim = HEAD_DIM // 2
    inverse = rope_theta ** (-(jnp.arange(half_dim, dtype=f32) * 2.0) / HEAD_DIM)
    angles = slot_order.astype(f32)[..., None] * inverse
    angles = jnp.concatenate([angles, angles], axis=-1)
    return (jnp.cos(angles)[..., None, :], jnp.sin(angles)[..., None, :])


def rotate(operand, cosine_table, sine_table):
    half_dim = operand.shape[-1] // 2
    flipped = jnp.concatenate([-operand[..., half_dim:], operand[..., :half_dim]], axis=-1)
    return operand * cosine_table + flipped * sine_table


def unrotate(upstream, cosine_table, sine_table):
    half_dim = upstream.shape[-1] // 2
    shifted = upstream * sine_table
    flipped = jnp.concatenate([shifted[..., half_dim:], -shifted[..., :half_dim]], axis=-1)
    return upstream * cosine_table + flipped


def masked_scores(query_rows, key_rows, pos):
    scores = jnp.einsum("gqhe,gkhe->ghqk", query_rows, key_rows, preferred_element_type=f32)
    causal = pos[:, None, :, None] >= pos[:, None, None, :]
    return jnp.where(causal, scores, -1e30)


def attend(query_rows, key_rows, value_rows, pos):
    scores = masked_scores(query_rows, key_rows, pos)
    row_max = jnp.max(scores, axis=-1, keepdims=True)
    weights = jnp.exp(scores - row_max)
    row_total = jnp.sum(weights, axis=-1, keepdims=True)
    probabilities = (weights / row_total).astype(bf16)
    attn_mixed = jnp.einsum("ghqk,gkhe->gqhe", probabilities, value_rows, preferred_element_type=f32)
    return attn_mixed.astype(bf16), row_max + jnp.log(row_total)


def attend_back(query_rows, key_rows, value_rows, pos, grad_mixed, log_total):
    scores = masked_scores(query_rows, key_rows, pos)
    probabilities = jnp.exp(scores - log_total)
    grad_probs = jnp.einsum("gqhe,gkhe->ghqk", grad_mixed, value_rows, preferred_element_type=f32)
    grad_value = jnp.einsum(
        "ghqk,gqhe->gkhe", probabilities.astype(bf16), grad_mixed, preferred_element_type=f32
    )
    inner_sum = jnp.sum(grad_probs * probabilities, axis=-1, keepdims=True)
    grad_scores = (probabilities * (grad_probs - inner_sum)).astype(bf16)
    grad_query = jnp.einsum("ghqk,gkhe->gqhe", grad_scores, key_rows, preferred_element_type=f32)
    grad_key = jnp.einsum("ghqk,gqhe->gkhe", grad_scores, query_rows, preferred_element_type=f32)
    return grad_query, grad_key, grad_value


MESH = pl.DeviceIdType.MESH
VMEM_LIMIT = 60 * 1024 * 1024
ANY = pl.BlockSpec(memory_space=pl.ANY)


class Plane:
    def __init__(self):
        f = lax.axis_index("fsdp")
        self.f, self.c, self.chip = f, f % 2, f // 2
        x, y = self.chip % 2, self.chip // 2
        self.qx = self.chip + 1 - 2 * x
        self.qy = self.chip + 2 - 4 * y
        self.qd = self.qx + 2 - 4 * y
        self.fc = f + 1 - 2 * self.c
        self.fx = 2 * self.qx + self.c
        self.fy = 2 * self.qy + self.c
        self.fd = 2 * self.qd + self.c
        self.other = 1 - self.c

    def greet(self):
        barrier = pltpu.get_barrier_semaphore()
        for to in (self.fc, self.fx, self.fy):
            pl.semaphore_signal(barrier, inc=1, device_id={"fsdp": to}, device_id_type=MESH)
        pl.semaphore_wait(barrier, 3)


def remote(src, dst, send, recv, i, to, axis="fsdp"):
    return pltpu.make_async_remote_copy(
        src_ref=src, dst_ref=dst, send_sem=send.at[i], recv_sem=recv.at[i],
        device_id={axis: to}, device_id_type=MESH,
    )


def local(src, dst, sems, i):
    copy = pltpu.make_async_copy(src, dst, sems.at[i])
    copy.start()
    return copy


def nn(a, b):
    return lax.dot_general(a, b, (((1,), (0,)), ((), ())), preferred_element_type=f32)


def nt(a, b):
    return lax.dot_general(a, b, (((1,), (1,)), ((), ())), preferred_element_type=f32)


def gather_phase(at, rows, send, recv, base, on_rows):
    half = rows.shape[1] // 2
    A, B = pl.ds(0, half), pl.ds(half, half)

    def cp(i, slot, part, to):
        ref = rows.at[slot] if part is None else rows.at[slot, part]
        return remote(ref, ref, send, recv, base + i, to)

    fcx, fcy, fcd = 2 * at.qx + at.other, 2 * at.qy + at.other, 2 * at.qd + at.other
    sent = []

    def go(*a):
        c = cp(*a)
        c.start()
        sent.append(c)

    def arrived(i, slot, part, frm):
        cp(i, slot, part, frm).wait_recv()

    go(0, at.f, None, at.fc)
    go(1, at.f, A, at.fx)
    go(3, at.f, B, at.fy)
    go(2, at.f, B, at.fx)
    go(4, at.f, A, at.fy)
    arrived(0, at.fc, None, at.fc)
    on_rows(2 * at.chip, 2)
    arrived(1, at.fx, A, at.fx)
    go(5, at.fx, A, at.fy)
    go(7, at.fx, A, at.fc)
    arrived(3, at.fy, B, at.fy)
    go(6, at.fy, B, at.fx)
    go(8, at.fy, B, at.fc)
    arrived(2, at.fx, B, at.fx)
    go(9, at.fx, B, at.fc)
    arrived(4, at.fy, A, at.fy)
    go(10, at.fy, A, at.fc)
    arrived(7, fcx, A, at.fc)
    arrived(9, fcx, B, at.fc)
    on_rows(2 * at.qx, 2)
    arrived(8, fcy, B, at.fc)
    arrived(10, fcy, A, at.fc)
    on_rows(2 * at.qy, 2)
    arrived(5, at.fd, A, at.fy)
    go(11, at.fd, A, at.fc)
    arrived(6, at.fd, B, at.fx)
    go(12, at.fd, B, at.fc)
    on_rows(at.fd, 1)
    arrived(11, fcd, A, at.fc)
    arrived(12, fcd, B, at.fc)
    on_rows(fcd, 1)
    for c in sent:
        c.wait_send()


GATHER_COPIES = 13
SCATTER_COPIES = 10


def scatter_scratch(R, D):
    return [
        pltpu.VMEM((4, R, D), bf16),
        pltpu.VMEM((4, R, D), bf16),
        pltpu.VMEM((2, R, D), f32),
        pltpu.VMEM((3, R, D), bf16),
        pltpu.VMEM((3, R, D), bf16),
    ]


def scatter_phase(at, partial, bufs, send, recv, base, between=None):
    to_core, from_core, mine, out, inc = bufs
    R, D = to_core.shape[1], to_core.shape[2]
    half = R // 2
    A, B = pl.ds(0, half), pl.ds(half, half)
    tile = 512
    step = 16
    sent = []

    def go(i, src, dst, to):
        c = remote(src, dst, send, recv, base + i, to)
        c.start()
        sent.append(c)

    def arrived(i, dst, frm):
        remote(dst, dst, send, recv, base + i, frm).wait_recv()

    def compute(order, chip, slot):
        @pl.loop(0, D // tile)
        def _(n):
            cols = pl.ds(pl.multiple_of(n * tile, tile), tile)
            got = partial(chip, cols)
            lo, hi = got[:R], got[R:]
            first = at.c == 0
            mine[slot, :, cols] = jnp.where(first, lo, hi)
            to_core[order, :, cols] = jnp.where(first, hi, lo).astype(bf16)

        go(order, to_core.at[order], from_core.at[order], at.fc)

    def chip_sum(order, slot):
        arrived(order, from_core.at[order], at.fc)

        @pl.loop(0, R // step)
        def _(r):
            rows = pl.ds(pl.multiple_of(r * step, step), step)
            out[order, rows, :] = (mine[slot, rows, :] + from_core[order, rows, :].astype(f32)).astype(bf16)

    def relay(order, start, src):
        @pl.loop(0, half // step)
        def _(r):
            rows = pl.ds(pl.multiple_of(start + r * step, step), step)
            out[order, rows, :] = (out[order, rows, :].astype(f32) + inc[src, rows, :].astype(f32)).astype(bf16)

    compute(0, at.qd, 0)
    compute(1, at.qx, 1)
    if between is not None:
        between()
    chip_sum(0, 0)
    go(4, out.at[0, A], inc.at[0, A], at.fx)
    go(5, out.at[0, B], inc.at[0, B], at.fy)
    compute(2, at.qy, 0)
    chip_sum(1, 1)
    go(6, out.at[1, A], inc.at[1, A], at.fx)
    compute(3, at.chip, 1)
    chip_sum(2, 0)
    go(8, out.at[2, B], inc.at[2, B], at.fy)
    arrived(5, inc.at[0, B], at.fy)
    relay(1, half, 0)
    go(7, out.at[1, B], inc.at[1, B], at.fx)
    arrived(4, inc.at[0, A], at.fx)
    relay(2, 0, 0)
    go(9, out.at[2, A], inc.at[2, A], at.fy)
    arrived(3, from_core.at[3], at.fc)
    arrived(6, inc.at[1, A], at.fx)
    arrived(8, inc.at[2, B], at.fy)
    arrived(7, inc.at[1, B], at.fx)
    arrived(9, inc.at[2, A], at.fy)
    for c in sent:
        c.wait_send()

    def total(rows):
        return (
            mine[1, rows, :]
            + from_core[3, rows, :].astype(f32)
            + inc[1, rows, :].astype(f32)
            + inc[2, rows, :].astype(f32)
        )

    return total


def rms(v):
    return lax.rsqrt(jnp.mean(v * v, axis=-1, keepdims=True) + epsilon)


def back(weighted, normed, scale):
    return scale * (weighted - normed * jnp.mean(weighted * normed, axis=-1, keepdims=True))


def row_loop(R, body, step=16):
    @pl.loop(0, R // step)
    def _(r):
        body(pl.ds(pl.multiple_of(r * step, step), step))


def pair_loop(rows, w_cols, total_cols, body):
    @pl.loop(0, total_cols // w_cols)
    def _(t):
        body(pl.ds(pl.multiple_of(t * w_cols, w_cols), w_cols))


class Stores:
    def __init__(self, sems):
        self.sems, self.steps, self.n = sems, [], 0

    def slot(self):
        if len(self.steps) >= 2:
            for c in self.steps[-2]:
                c.wait()
            self.steps[-2] = []
        return len(self.steps) % 2

    def put(self, pairs):
        done = []
        for src, dst in pairs:
            done.append(local(src, dst, self.sems, self.n))
            self.n += 1
        self.steps.append(done)

    def finish(self):
        for step in self.steps:
            for c in step:
                c.wait()


class Moving:
    def __init__(self, at, C, mine, stage, landing, lsem, base, send, recv):
        self.at, self.C, self.mine, self.stage, self.landing = at, C, mine, stage, landing
        self.lsem, self.base, self.send, self.recv = lsem, base, send, recv
        self.z = lax.axis_index("ctx")
        self.piece = mine.shape[0] // C
        self.sent = []

    def greet(self, barrier):
        at, C = self.at, self.C
        for k in range(1, C):
            pl.semaphore_signal(barrier, inc=1, device_id={"ctx": (self.z + k) % C}, device_id_type=MESH)
            pl.semaphore_signal(
                barrier, inc=1, device_id={"fsdp": 2 * ((at.chip + k) % C) + at.c}, device_id_type=MESH
            )

    def first(self):
        at, C, piece = self.at, self.C, self.piece
        for k in range(1, C):
            j = (at.chip + k) % C
            src = self.mine.at[pl.ds(j * piece, piece)]
            c = remote(src, self.stage.at[at.chip], self.send, self.recv, k, 2 * j + at.c)
            c.start()
            self.sent.append(c)
        src = self.mine.at[pl.ds(at.chip * piece, piece)]
        self.keep = local(src, self.stage.at[at.chip], self.lsem, self.base)

    def land(self, layer):
        return self.landing.at[pl.ds(layer * self.piece, self.piece)]

    def second(self):
        at, C, z = self.at, self.C, self.z
        self.keep.wait()
        for k in range(1, C):
            frm = (at.chip - k + C) % C
            remote(self.stage.at[frm], self.stage.at[frm], self.send, self.recv, k, 2 * frm + at.c).wait_recv()
        for k in range(1, C):
            to = (z + k) % C
            c = remote(self.stage.at[to], self.land(z), self.send, self.recv, C + k, to, "ctx")
            c.start()
            self.sent.append(c)
        self.keep = local(self.stage.at[z], self.land(z), self.lsem, self.base + 1)

    def finish(self):
        C, z = self.C, self.z
        self.keep.wait()
        for k in range(1, C):
            frm = (z - k + C) % C
            remote(self.land(frm), self.land(frm), self.send, self.recv, C + k, frm, "ctx").wait_recv()
        for c in self.sent:
            c.wait_send()


def enter_kernel(C, x_ref, own_ref, all_ref, stage, mine, rows, lsem, osem, send, recv, tsend, trecv):
    at = Plane()
    load = local(x_ref, mine, lsem, 0)
    moving = Moving(at, C, mine, stage, rows.at[at.f], lsem, 1, tsend, trecv)
    barrier = pltpu.get_barrier_semaphore()
    moving.greet(barrier)
    pl.semaphore_signal(barrier, inc=1, device_id={"fsdp": at.fc}, device_id_type=MESH)
    pl.semaphore_wait(barrier, 2 * (C - 1) + 1)
    load.wait()
    moving.first()
    moving.second()
    moving.finish()
    save = local(rows.at[at.f], own_ref, lsem, 3)
    stores = []

    def on_rows(first, count):
        stores.append(local(rows.at[pl.ds(first, count)], all_ref.at[pl.ds(first, count)], osem, len(stores)))

    gather_phase(at, rows, send, recv, 0, on_rows)
    save.wait()
    for c in stores:
        c.wait()


def enter_call(C, F, x):
    R, D = x.shape
    return pl.pallas_call(
        functools.partial(enter_kernel, C),
        out_shape=[jax.ShapeDtypeStruct((R, D), bf16), jax.ShapeDtypeStruct((F, R, D), bf16)],
        in_specs=[ANY],
        out_specs=[ANY] * 2,
        scratch_shapes=[
            pltpu.VMEM((C, R // C, D), bf16),
            pltpu.VMEM((R, D), bf16),
            pltpu.VMEM((F, R, D), bf16),
            dma(4), dma(5), dma(GATHER_COPIES), dma(GATHER_COPIES), dma(2 * C), dma(2 * C),
        ],
        compiler_params=params(1),
        cost_estimate=cost(70),
    )(x)


def qkv_kernel(all_ref, w_ref, proj_ref, st_ref, rows, w, acc, st, lsem, osem, ssend, srecv):
    at = Plane()
    F, R = rows.shape[0], rows.shape[1]
    e = w.shape[1] // 3
    m = 2 * R
    loads = [local(w_ref.at[:, pl.ds(0, 3 * e)], w, lsem, 0)] + [
        local(all_ref.at[pl.ds(2 * p, 2)], rows.at[pl.ds(2 * p, 2)], lsem, 1 + p) for p in range(F // 2)
    ]
    barrier = pltpu.get_barrier_semaphore()
    for k in range(1, F):
        pl.semaphore_signal(barrier, inc=1, device_id={"fsdp": (at.f + k) % F}, device_id_type=MESH)
    pl.semaphore_wait(barrier, F - 1)
    loads[0].wait()
    stores = Stores(osem)
    for p in range(F // 2):
        loads[1 + p].wait()
        s = stores.slot()

        def tile(c):
            acc[s, :, c] = nn(rows[pl.ds(2 * p, 2)].reshape(m, rows.shape[2]), w[:, c])

        pair_loop(m, 256, w.shape[1], tile)
        q, k = acc[s, :, :e], acc[s, :, e : 2 * e]
        st[at.f, :, pl.ds(p * m, m)] = row_sums(q * q, k * k)
        stores.put([(acc.at[s], proj_ref.at[pl.ds(p * m, m)])])
    share_stats(at, F, st, ssend, srecv, 0)
    local(st, st_ref, lsem, 1 + F // 2).wait()
    stores.finish()


def params(number):
    return pltpu.CompilerParams(
        collective_id=number, has_side_effects=True, vmem_limit_bytes=VMEM_LIMIT
    )


def cost(us):
    return pl.CostEstimate(flops=int(us * 1e9), bytes_accessed=2**20, transcendentals=0)


def dma(n):
    return pltpu.SemaphoreType.DMA((n,))


def qkv_call(F, rows, w):
    _, R, D = rows.shape
    n = w.shape[1] // 4 * 3
    return pl.pallas_call(
        qkv_kernel,
        out_shape=[
            jax.ShapeDtypeStruct((F * R, n), f32),
            jax.ShapeDtypeStruct((F, 8, F * R), f32),
        ],
        in_specs=[ANY] * 2,
        out_specs=[ANY] * 2,
        scratch_shapes=[
            pltpu.VMEM((F, R, D), bf16),
            pltpu.VMEM((D, n), bf16),
            pltpu.VMEM((2, 2 * R, n), f32),
            pltpu.VMEM((F, 8, F * R), f32),
            dma(6), dma(4), dma(F), dma(F),
        ],
        compiler_params=params(7),
        cost_estimate=cost(22),
    )(rows, w)


def out_kernel(
    mixed_ref, wo_ref, x_ref, gain_ref, hid_ref, ao_ref, in_ref,
    mixed, wo, x, gain, hid, ao, inp, b0, b1, b2, b3, b4, lsem, send, recv,
):
    at = Plane()
    e = wo.shape[1]
    pairs = [(mixed_ref, mixed), (wo_ref.at[:, pl.ds(3 * e, e)], wo), (x_ref, x), (gain_ref, gain)]
    loads = [local(s, d, lsem, i) for i, (s, d) in enumerate(pairs)]
    at.greet()
    R = x.shape[0]
    loads[0].wait()
    loads[1].wait()

    def partial(chip, cols):
        return nt(mixed[pl.ds(pl.multiple_of(chip * 2 * R, 2 * R), 2 * R), :], wo[cols, :])

    total = scatter_phase(at, partial, (b0, b1, b2, b3, b4), send, recv, 0)
    loads[2].wait()
    loads[3].wait()

    def finish(r):
        out = total(r)
        ao[r, :] = out
        hidden_in = x[r, :].astype(f32) + out * rms(out) * gain[...]
        hid[r, :] = hidden_in
        inp[r, :] = hidden_in.astype(bf16)

    row_loop(R, finish)
    for c in [local(ao, ao_ref, lsem, 4), local(hid, hid_ref, lsem, 5), local(inp, in_ref, lsem, 6)]:
        c.wait()


def out_call(F, mixed, wo, x, gain):
    R, D = x.shape
    e = wo.shape[1] // 4
    return pl.pallas_call(
        out_kernel,
        out_shape=[
            jax.ShapeDtypeStruct((R, D), f32),
            jax.ShapeDtypeStruct((R, D), f32),
            jax.ShapeDtypeStruct((R, D), bf16),
        ],
        in_specs=[ANY] * 4,
        out_specs=[ANY] * 3,
        scratch_shapes=[
            pltpu.VMEM((F * R, e), bf16),
            pltpu.VMEM((D, e), bf16),
            pltpu.VMEM((R, D), bf16),
            pltpu.VMEM((1, D), f32),
            pltpu.VMEM((R, D), f32),
            pltpu.VMEM((R, D), f32),
            pltpu.VMEM((R, D), bf16),
        ]
        + scatter_scratch(R, D)
        + [dma(7), dma(SCATTER_COPIES), dma(SCATTER_COPIES)],
        compiler_params=params(8),
        cost_estimate=cost(46),
    )(mixed, wo, x, gain)


def up_kernel(
    in_ref, w_ref, all_ref, act_ref, der_ref, h_ref,
    w, rows, act, der, h, lsem, osem, send, recv,
):
    at = Plane()
    own = local(in_ref, rows.at[at.f], lsem, 0)
    n = act.shape[2]
    loads = [local(w_ref, w, lsem, 1)]
    width = 256
    at.greet()
    R = rows.shape[1]
    own.wait()
    waited = []
    stores = Stores(osem)

    def on_rows(first, count):
        s = stores.slot()
        m = count * R
        if not waited:
            for c in loads:
                c.wait()
            waited.append(1)

        @pl.loop(0, n // width)
        def _(t):
            c = pl.ds(pl.multiple_of(t * width, width), width)
            lhs = rows[pl.ds(first, count)].reshape(m, rows.shape[2])
            g = nn(lhs, w[:, c])
            u = nn(lhs, w[:, pl.ds(pl.multiple_of(n + t * width, width), width)])
            sig = jax.nn.sigmoid(g)
            a = g * sig
            act[s, pl.ds(0, m), c] = a.astype(bf16)
            der[s, pl.ds(0, m), c] = (u * (sig * (1.0 + g * (1.0 - sig)))).astype(bf16)
            h[s, pl.ds(0, m), c] = (a * u).astype(bf16)

        start = pl.multiple_of(first * R, R)
        stores.put(
            [
                (act.at[s, pl.ds(0, m)], act_ref.at[pl.ds(start, m)]),
                (der.at[s, pl.ds(0, m)], der_ref.at[pl.ds(start, m)]),
                (h.at[s, pl.ds(0, m)], h_ref.at[pl.ds(start, m)]),
                (rows.at[pl.ds(first, count)], all_ref.at[pl.ds(first, count)]),
            ]
        )

    gather_phase(at, rows, send, recv, 0, on_rows)
    stores.finish()


def up_call(F, inp, w):
    R, D = inp.shape
    n = w.shape[1] // 2
    T = F * R
    wide = jax.ShapeDtypeStruct((T, n), bf16)
    return pl.pallas_call(
        up_kernel,
        out_shape=[jax.ShapeDtypeStruct((F, R, D), bf16), wide, wide, wide],
        in_specs=[ANY] * 2,
        out_specs=[ANY] * 4,
        scratch_shapes=[
            pltpu.VMEM((D, 2 * n), bf16),
            pltpu.VMEM((F, R, D), bf16),
            pltpu.VMEM((2, 2 * R, n), bf16),
            pltpu.VMEM((2, 2 * R, n), bf16),
            pltpu.VMEM((2, 2 * R, n), bf16),
        ]
        + [dma(2), dma(20), dma(GATHER_COPIES), dma(GATHER_COPIES)],
        compiler_params=params(2),
        cost_estimate=cost(46),
    )(inp, w)


def down_kernel(
    C, h_ref, wd_ref, hid_ref, cot_ref, gain_ref, act_ref, der_ref, unit_ref,
    res_ref, gg_ref, all_ref, grad_ref, own_ref, mom_ref, p_ref,
    h, wd, hid, mine, gain, act, der, res, gacc, rows, grad, cot, stage, prod, b0, b1, b2, b3, b4,
    lsem, osem, asem, psem, send, recv, tsend, trecv, usend, urecv,
):
    at = Plane()
    loads = [
        local(s, d, lsem, i)
        for i, (s, d) in enumerate(
            [(cot_ref, mine), (h_ref, h), (wd_ref, wd), (hid_ref, hid), (gain_ref, gain)]
        )
    ]
    moving = Moving(at, C, mine, stage, cot, lsem, 5, tsend, trecv)
    barrier = pltpu.get_barrier_semaphore()
    moving.greet(barrier)
    pl.semaphore_signal(barrier, inc=1, device_id={"fsdp": at.fc}, device_id_type=MESH)
    pl.semaphore_wait(barrier, 2 * (C - 1) + 1)
    R = rows.shape[1]
    n = wd.shape[1]
    z = moving.z
    units = []

    def send_units(k):
        to = (z + k) % C
        c = remote(unit_ref.at[to], mom_ref.at[z], usend, urecv, k, to, "ctx")
        c.start()
        units.append(c)

    send_units(1)
    loads[0].wait()
    moving.first()
    loads[1].wait()
    loads[2].wait()

    def partial(chip, cols):
        return nt(h[pl.ds(pl.multiple_of(chip * 2 * R, 2 * R), 2 * R), :], wd[cols, :])

    def between():
        moving.second()
        for k in range(2, C):
            send_units(k)
        units.append(local(unit_ref.at[z], mom_ref.at[z], lsem, 10))

    total = scatter_phase(at, partial, (b0, b1, b2, b3, b4), send, recv, 0, between)
    for c in loads[3:]:
        c.wait()
    moving.finish()
    gacc[...] = jnp.zeros_like(gacc)

    def finish(r):
        out = total(r)
        scale = rms(out)
        hat = out * scale
        res[r, :] = (hid[r, :] + hat * gain[...]).astype(bf16)
        g = cot[r, :].astype(f32)
        gacc[...] += jnp.sum(g * hat, axis=0, keepdims=True)
        rows[at.f, r, :] = back(g * gain[...], hat, scale).astype(bf16)

    row_loop(R, finish)
    saves = [local(res, res_ref, lsem, 7), local(gacc, gg_ref, lsem, 8), local(cot, own_ref, lsem, 9)]
    stores = Stores(osem)

    def on_rows(first, count):
        s = stores.slot()
        m = count * R
        start = pl.multiple_of(first * R, R)
        k = len(stores.steps)
        la = local(act_ref.at[pl.ds(start, m)], act.at[s, pl.ds(0, m)], asem, 2 * k)
        ld = local(der_ref.at[pl.ds(start, m)], der.at[s, pl.ds(0, m)], asem, 2 * k + 1)
        la.wait()
        ld.wait()

        width = 512

        @pl.loop(0, n // width)
        def _(t):
            c = pl.ds(pl.multiple_of(t * width, width), width)
            up = pl.ds(pl.multiple_of(n + t * width, width), width)
            gh = nn(rows[pl.ds(first, count)].reshape(m, rows.shape[2]), wd[:, c])
            grad[s, pl.ds(0, m), up] = (gh * act[s, pl.ds(0, m), c].astype(f32)).astype(bf16)
            grad[s, pl.ds(0, m), c] = (gh * der[s, pl.ds(0, m), c].astype(f32)).astype(bf16)

        stores.put(
            [
                (grad.at[s, pl.ds(0, m)], grad_ref.at[pl.ds(start, m)]),
                (rows.at[pl.ds(first, count)], all_ref.at[pl.ds(first, count)]),
            ]
        )

    gather_phase(at, rows, send, recv, SCATTER_COPIES, on_rows)
    F, D = rows.shape[0], rows.shape[2]
    tile, cols = prod.shape[1], p_ref.shape[3]
    puts = []
    for t in range(D // tile):
        if t >= 2:
            for c in puts[t - 2]:
                c.wait()
        rhs = rows[:, :, t * tile : (t + 1) * tile].reshape(F * R, tile)
        prod[t % 2] = lax.dot_general(
            rhs, h[...], (((0,), (0,)), ((), ())), preferred_element_type=f32
        ).astype(bf16)
        puts.append(
            [
                local(
                    prod.at[t % 2, :, pl.ds(b * cols, cols)],
                    p_ref.at[b, 0, pl.ds(t * tile, tile)],
                    psem,
                    t * (n // cols) + b,
                )
                for b in range(n // cols)
            ]
        )
    for step in puts[-2:]:
        for c in step:
            c.wait()
    for k in range(1, C):
        frm = (z - k + C) % C
        remote(mom_ref.at[frm], mom_ref.at[frm], usend, urecv, k, frm, "ctx").wait_recv()
    for c in units[:-1]:
        c.wait_send()
    units[-1].wait()
    for s in saves:
        s.wait()
    stores.finish()


def down_call(C, F, h, wd, hid, cot, gain, act, der, units):
    R, D = hid.shape
    n = wd.shape[1]
    T = F * R
    copies = SCATTER_COPIES + GATHER_COPIES
    one = jax.ShapeDtypeStruct((R, D), bf16)
    return pl.pallas_call(
        functools.partial(down_kernel, C),
        out_shape=[
            one,
            jax.ShapeDtypeStruct((1, D), f32),
            jax.ShapeDtypeStruct((F, R, D), bf16),
            jax.ShapeDtypeStruct((T, 2 * n), bf16),
            one,
            jax.ShapeDtypeStruct(units.shape, bf16),
            jax.ShapeDtypeStruct((units.shape[1], 1, D, units.shape[3]), bf16),
        ],
        in_specs=[ANY] * 8,
        out_specs=[ANY] * 7,
        scratch_shapes=[
            pltpu.VMEM((T, n), bf16),
            pltpu.VMEM((D, n), bf16),
            pltpu.VMEM((R, D), f32),
            pltpu.VMEM((R, D), bf16),
            pltpu.VMEM((1, D), f32),
            pltpu.VMEM((2, 2 * R, n), bf16),
            pltpu.VMEM((2, 2 * R, n), bf16),
            pltpu.VMEM((R, D), bf16),
            pltpu.VMEM((1, D), f32),
            pltpu.VMEM((F, R, D), bf16),
            pltpu.VMEM((2, 2 * R, 2 * n), bf16),
            pltpu.VMEM((R, D), bf16),
            pltpu.VMEM((C, R // C, D), bf16),
            pltpu.VMEM((2, 512, n), bf16),
        ]
        + scatter_scratch(R, D)
        + [dma(11), dma(15), dma(10), dma(16), dma(copies), dma(copies), dma(2 * C), dma(2 * C), dma(C), dma(C)],
        compiler_params=params(3),
        cost_estimate=cost(115),
    )(h, wd, hid, cot, gain, act, der, units)


def mid_kernel(
    grad_ref, w_ref, cot_ref, ao_ref, gain_ref, wo_ref,
    res_ref, gg_ref, all_ref, gm_ref,
    grad, w, cot, ao, gain, wo, res, gacc, rows, gm, b0, b1, b2, b3, b4,
    lsem, osem, send, recv,
):
    at = Plane()
    e = wo.shape[1]
    pairs = [
        (grad_ref, grad), (w_ref, w),
        (cot_ref, cot), (ao_ref, ao), (gain_ref, gain), (wo_ref.at[:, pl.ds(3 * e, e)], wo),
    ]
    loads = [local(s, d, lsem, i) for i, (s, d) in enumerate(pairs)]
    at.greet()
    R = rows.shape[1]
    for c in loads[:2]:
        c.wait()

    def partial(chip, cols):
        return nt(grad[pl.ds(pl.multiple_of(chip * 2 * R, 2 * R), 2 * R), :], w[cols, :])

    total = scatter_phase(at, partial, (b0, b1, b2, b3, b4), send, recv, 0)
    for c in loads[2:]:
        c.wait()
    gacc[...] = jnp.zeros_like(gacc)

    def finish(r):
        resid = cot[r, :].astype(f32) + total(r)
        res[r, :] = resid
        out = ao[r, :]
        scale = rms(out)
        hat = out * scale
        gacc[...] += jnp.sum(resid * hat, axis=0, keepdims=True)
        rows[at.f, r, :] = back(resid * gain[...], hat, scale).astype(bf16)

    row_loop(R, finish)
    saves = [local(res, res_ref, lsem, 8), local(gacc, gg_ref, lsem, 9)]
    stores = Stores(osem)

    def on_rows(first, count):
        s = stores.slot()
        m = count * R
        start = pl.multiple_of(first * R, R)
        lhs = rows[pl.ds(first, count)].reshape(m, rows.shape[2])
        gm[s, pl.ds(0, m), :] = nn(lhs, wo[...]).astype(bf16)
        stores.put(
            [
                (gm.at[s, pl.ds(0, m)], gm_ref.at[pl.ds(start, m)]),
                (rows.at[pl.ds(first, count)], all_ref.at[pl.ds(first, count)]),
            ]
        )

    gather_phase(at, rows, send, recv, SCATTER_COPIES, on_rows)
    for s in saves:
        s.wait()
    stores.finish()


def mid_call(F, grad, w, cot, ao, gain, wo):
    R, D = cot.shape
    n, e = w.shape[1], wo.shape[1] // 4
    T = F * R
    copies = SCATTER_COPIES + GATHER_COPIES
    return pl.pallas_call(
        mid_kernel,
        out_shape=[
            jax.ShapeDtypeStruct((R, D), f32),
            jax.ShapeDtypeStruct((1, D), f32),
            jax.ShapeDtypeStruct((F, R, D), bf16),
            jax.ShapeDtypeStruct((T, e), bf16),
        ],
        in_specs=[ANY] * 6,
        out_specs=[ANY] * 4,
        scratch_shapes=[
            pltpu.VMEM((T, n), bf16),
            pltpu.VMEM((D, n), bf16),
            pltpu.VMEM((R, D), bf16),
            pltpu.VMEM((R, D), f32),
            pltpu.VMEM((1, D), f32),
            pltpu.VMEM((D, e), bf16),
            pltpu.VMEM((R, D), f32),
            pltpu.VMEM((1, D), f32),
            pltpu.VMEM((F, R, D), bf16),
            pltpu.VMEM((2, 2 * R, e), bf16),
        ]
        + scatter_scratch(R, D)
        + [dma(10), dma(10), dma(copies), dma(copies)],
        compiler_params=params(4),
        cost_estimate=cost(92),
    )(grad, w, cot, ao, gain, wo)


def last_kernel(
    width, q_ref, k_ref, v_ref, proj_ref, st_ref, in_ref, w_ref, res_ref, gain_ref,
    out_ref, gp_ref, gsum_ref,
    q, k, proj, st, ins, gains, gsum, gp, w, res, out, b0, b1, b2, b3, b4,
    lsem, send, recv, ssend, srecv, gsend, grecv,
):
    at = Plane()
    F, T = st.shape[0], st.shape[2]
    e = q.shape[1]
    R = res.shape[0]
    pairs = [
        (in_ref, ins.at[at.f]), (st_ref, st), (q_ref, q), (k_ref, k),
        (v_ref, gp.at[:, pl.ds(2 * e, e)]), (proj_ref.at[:, pl.ds(0, 2 * e)], proj), (w_ref.at[:, pl.ds(0, 3 * e)], w), (res_ref, res),
        (gain_ref, gains.at[at.f]),
    ]
    loads = [local(s, d, lsem, i) for i, (s, d) in enumerate(pairs)]
    barrier = pltpu.get_barrier_semaphore()
    for s in range(1, F):
        pl.semaphore_signal(barrier, inc=1, device_id={"fsdp": (at.f + s) % F}, device_id_type=MESH)
    pl.semaphore_wait(barrier, F - 1)
    loads[0].wait()
    share_stats(at, F, ins, ssend, srecv, 0)
    for c in loads[1:6]:
        c.wait()
    step = 256

    @pl.loop(0, T // step)
    def _(t):
        r = pl.ds(pl.multiple_of(t * step, step), step)
        sums = jnp.sum(st[:, :, r], axis=0)
        inner = jnp.sum(ins[:, :, r], axis=0) / width
        for row, grad in ((0, q), (1, k)):
            scale = lax.rsqrt(column(sums[row : row + 1], HEAD_DIM) / width + epsilon)
            mean = column(inner[row : row + 1], HEAD_DIM)
            for h in range(e // HEAD_DIM):
                hat = proj[r, row * e + h * HEAD_DIM : row * e + (h + 1) * HEAD_DIM] * scale
                got = scale * (grad[r, h * HEAD_DIM : (h + 1) * HEAD_DIM] - hat * mean)
                gp[r, row * e + h * HEAD_DIM : row * e + (h + 1) * HEAD_DIM] = got.astype(bf16)

    save = local(gp, gp_ref, lsem, 9)
    loads[6].wait()

    def partial(chip, cols):
        return nt(gp[pl.ds(pl.multiple_of(chip * 2 * R, 2 * R), 2 * R), :], w[cols, :])

    total = scatter_phase(at, partial, (b0, b1, b2, b3, b4), send, recv, 0)
    loads[7].wait()

    def finish(r):
        out[r, :] = (res[r, :] + total(r)).astype(bf16)

    row_loop(R, finish)
    store = local(out, out_ref, lsem, 10)
    loads[8].wait()
    share_stats(at, F, gains, gsend, grecv, 0)
    gsum[...] = jnp.sum(gains[...], axis=0)
    local(gsum, gsum_ref, lsem, 11).wait()
    store.wait()
    save.wait()


def last_call(F, wq, wk, gv, proj, st, ins, w, res, gains):
    R, D = res.shape
    n = w.shape[1] // 4 * 3
    T, e = F * R, n // 3
    return pl.pallas_call(
        functools.partial(last_kernel, D),
        out_shape=[
            jax.ShapeDtypeStruct((R, D), bf16),
            jax.ShapeDtypeStruct((T, n), bf16),
            jax.ShapeDtypeStruct((8, D), f32),
        ],
        in_specs=[ANY] * 9,
        out_specs=[ANY] * 3,
        scratch_shapes=[
            pltpu.VMEM((T, e), f32),
            pltpu.VMEM((T, e), f32),
            pltpu.VMEM((T, 2 * e), f32),
            pltpu.VMEM((F, 8, T), f32),
            pltpu.VMEM((F, 8, T), f32),
            pltpu.VMEM((F, 8, D), f32),
            pltpu.VMEM((8, D), f32),
            pltpu.VMEM((T, n), bf16),
            pltpu.VMEM((D, n), bf16),
            pltpu.VMEM((R, D), f32),
            pltpu.VMEM((R, D), bf16),
        ]
        + scatter_scratch(R, D)
        + [dma(12), dma(SCATTER_COPIES), dma(SCATTER_COPIES), dma(F), dma(F), dma(F), dma(F)],
        compiler_params=params(5),
        cost_estimate=cost(55),
    )(wq, wk, gv, proj, st, ins, w, res, gains)


def tn(a, b):
    return lax.dot_general(a, b, (((0,), (0,)), ((), ())), preferred_element_type=f32)


def grad_kernel(*refs):
    out = refs[-1]
    start = 0
    for x_ref, dy_ref in zip(refs[:-1:2], refs[1:-1:2]):
        got = tn(x_ref[...], dy_ref[...]).astype(bf16)
        units = dy_ref.shape[1] // out.shape[-1]
        for b in range(units):
            out[(start + b,) + (0,) * (len(out.shape) - 3)] = got[:, b * out.shape[-1] : (b + 1) * out.shape[-1]]
        start += units


def grad_call(pairs, units, cols, groups):
    T, D = pairs[0][0].shape
    tile = 512
    specs, args = [], []
    for x, dy in pairs:
        specs += [
            pl.BlockSpec((T, tile), lambda g, d: (0, d)),
            pl.BlockSpec((T, dy.shape[1] // groups), lambda g, d: (0, g)),
        ]
        args += [x, dy]
    return pl.pallas_call(
        grad_kernel,
        out_shape=jax.ShapeDtypeStruct((units, groups, D, cols), bf16),
        grid=(groups, D // tile),
        in_specs=specs,
        out_specs=pl.BlockSpec((units, 1, tile, cols), lambda g, d: (0, g, d, 0)),
        compiler_params=pltpu.CompilerParams(vmem_limit_bytes=VMEM_LIMIT),
        cost_estimate=cost(12 * groups),
    )(*args)


def share_stats(at, F, st, send, recv, base):
    sent = []
    for k in range(1, F):
        to = (at.f + k) % F
        c = remote(st.at[at.f], st.at[at.f], send, recv, base + k, to)
        c.start()
        sent.append(c)
    for k in range(1, F):
        frm = (at.f - k + F) % F
        remote(st.at[frm], st.at[frm], send, recv, base + k, frm).wait_recv()
    for c in sent:
        c.wait_send()


def row_sums(a, b):
    r = lax.broadcasted_iota(jnp.int32, (8, a.shape[1]), 0)
    one, two = (r == 0).astype(f32), (r == 1).astype(f32)

    def half(sel, v):
        return lax.dot_general(
            sel, v, (((1,), (1,)), ((), ())), preferred_element_type=f32, precision=lax.Precision.HIGHEST
        )

    return half(one, a) + half(two, b)


def column(row, lanes):
    return jnp.broadcast_to(row, (lanes, row.shape[1])).T


def turn(v, cos, sin):
    return v * cos + pltpu.roll(v, HEAD_DIM // 2, 1) * sin


def seq_columns(st, c, chips, R):
    return jnp.concatenate([st[:, pl.ds(pl.multiple_of((2 * j + c) * R, R), R)] for j in range(chips)], axis=1)


def attend_kernel(width, q_ref, k_ref, v_ref, st_ref, gq_ref, gk_ref, cos_ref, sin_ref, pos_ref, posc_ref, mix_ref, qr_ref, kr_ref, lse_ref):
    c = pl.program_id(0)
    chips, R = q_ref.shape[0], q_ref.shape[2]
    L = chips * R
    sums = jnp.sum(seq_columns_all(st_ref, c, chips, R), axis=0)
    cos, sin = cos_ref[0], sin_ref[0]

    def norm_turn(ref, row, gain):
        scale = lax.rsqrt(column(sums[row : row + 1], HEAD_DIM) / width + epsilon)
        return turn(ref[...].reshape(L, HEAD_DIM) * scale * gain[...], cos, sin)

    qr = (norm_turn(q_ref, 0, gq_ref) * HEAD_DIM ** (-0.5)).astype(bf16)
    kr = norm_turn(k_ref, 1, gk_ref).astype(bf16)
    v = v_ref[...].reshape(L, HEAD_DIM).astype(bf16)
    qr_ref[...] = qr.reshape(qr_ref.shape)
    kr_ref[...] = kr.reshape(kr_ref.shape)
    pos = pos_ref[0]
    for t in range(chips):
        rows = slice(t * R, (t + 1) * R)
        s = nt(qr[rows], kr)
        s = jnp.where(posc_ref[0, rows, :1] >= pos, s, -1e30)
        top = jnp.max(s, axis=-1, keepdims=True)
        e = jnp.exp(s - top)
        total = jnp.sum(e, axis=-1, keepdims=True)
        p = (e * (1.0 / total)).astype(bf16)
        mix_ref[t, 0] = nn(p, v).astype(bf16)
        lse_ref[0, 0, rows, :] = jnp.broadcast_to(top + jnp.log(total), (R, HEAD_DIM))


def seq_columns_all(st_ref, c, chips, R):
    return jnp.concatenate(
        [st_ref[:, :, pl.ds(pl.multiple_of((2 * j + c) * R, R), R)] for j in range(chips)], axis=2
    )


def attend_specs(chips, R, heads, F, L):
    def at(offset):
        return pl.BlockSpec((chips, 1, R, HEAD_DIM), lambda c, h: (0, c, 0, offset + h))

    gain = pl.BlockSpec((1, HEAD_DIM), lambda c, h: (0, h))
    table = pl.BlockSpec((1, L, HEAD_DIM), lambda c, h: (c, 0, 0))
    stats = pl.BlockSpec((F, 8, F * R), lambda c, h: (0, 0, 0))
    posr = pl.BlockSpec((1, 1, L), lambda c, h: (c, 0, 0))
    lse = pl.BlockSpec((1, 1, L, HEAD_DIM), lambda c, h: (c, h, 0, 0))
    return at, gain, table, stats, posr, lse


def attend_call(F, proj, st, gq, gk, cos, sin, pos, posc):
    R = proj.shape[0] // F
    e = proj.shape[1] // 3
    heads, chips = e // HEAD_DIM, F // 2
    L = chips * R
    at, gain, table, stats, posr, lse = attend_specs(chips, R, heads, F, L)
    view = proj.reshape(chips, 2, R, 3 * e)
    flat = jax.ShapeDtypeStruct((chips, 2, R, e), bf16)
    out = pl.pallas_call(
        functools.partial(attend_kernel, heads * HEAD_DIM * F),
        out_shape=[flat, flat, flat, jax.ShapeDtypeStruct((2, heads, L, HEAD_DIM), f32)],
        grid=(2, heads),
        in_specs=[at(0), at(heads), at(2 * heads), stats, gain, gain, table, table, posr, table],
        out_specs=[at(0), at(0), at(0), lse],
        compiler_params=pltpu.CompilerParams(vmem_limit_bytes=VMEM_LIMIT),
        cost_estimate=cost(15),
    )(view, view, view, st, gq, gk, cos, sin, pos, posc)
    return out


def attend_back_kernel(
    width, q_ref, k_ref, v_ref, qr_ref, kr_ref, gm_ref, lse_ref, st_ref, gq_ref, gk_ref, cos_ref, sin_ref, pos_ref, posc_ref,
    wq_ref, wk_ref, gv_ref, in_ref, gg_ref, dk, dv, dq,
):
    c = pl.program_id(0)
    chips, R = q_ref.shape[0], q_ref.shape[2]
    L = chips * R
    kr = kr_ref[...].reshape(L, HEAD_DIM)
    v = v_ref[...].reshape(L, HEAD_DIM).astype(bf16)
    pos = pos_ref[0]
    dk[...] = jnp.zeros_like(dk)
    dv[...] = jnp.zeros_like(dv)
    for t in range(chips):
        rows = slice(t * R, (t + 1) * R)
        qt, gm = qr_ref[t, 0], gm_ref[t, 0]
        s = nt(qt, kr)
        s = jnp.where(posc_ref[0, rows, :1] >= pos, s, -1e30)
        p = jnp.exp(s - lse_ref[0, 0, rows, :1])
        dp = nt(gm, v)
        dv[...] += lax.dot_general(p.astype(bf16), gm, (((0,), (0,)), ((), ())), preferred_element_type=f32)
        inner = jnp.sum(dp * p, axis=-1, keepdims=True)
        ds = (p * (dp - inner)).astype(bf16)
        dq[rows, :] = nn(ds, kr)
        dk[...] += lax.dot_general(ds, qt, (((0,), (0,)), ((), ())), preferred_element_type=f32)
    gv_ref[...] = dv[...].astype(bf16).reshape(gv_ref.shape)
    sums = jnp.sum(seq_columns_all(st_ref, c, chips, R), axis=0)
    cos, sin = cos_ref[0], sin_ref[0]

    def finish(grad, ref, row, gain, out):
        norm = turn(grad, cos, -sin)
        hat = ref[...].reshape(L, HEAD_DIM) * lax.rsqrt(column(sums[row : row + 1], HEAD_DIM) / width + epsilon)
        gg_ref[0, 0, row : row + 1, :] = jnp.sum(norm * hat, axis=0, keepdims=True)
        weighted = norm * gain[...]
        out[...] = weighted.reshape(out.shape)
        return weighted * hat

    gg_ref[...] = jnp.zeros_like(gg_ref)
    in_ref[0, 0] = row_sums(
        finish(dq[...] * HEAD_DIM ** (-0.5), q_ref, 0, gq_ref, wq_ref), finish(dk[...], k_ref, 1, gk_ref, wk_ref)
    )


def attend_back_call(F, proj, qr, kr, gm, lse_in, st, gq, gk, cos, sin, pos, posc):
    R = proj.shape[0] // F
    e = proj.shape[1] // 3
    heads, chips = e // HEAD_DIM, F // 2
    L = chips * R
    at, gain, table, stats, posr, lse = attend_specs(chips, R, heads, F, L)
    view = proj.reshape(chips, 2, R, 3 * e)
    flat = (chips, 2, R, e)
    small = pl.BlockSpec((1, 1, 8, L), lambda c, h: (c, h, 0, 0))
    tiny = pl.BlockSpec((1, 1, 8, HEAD_DIM), lambda c, h: (c, h, 0, 0))
    wide = jax.ShapeDtypeStruct(flat, f32)
    return pl.pallas_call(
        functools.partial(attend_back_kernel, heads * HEAD_DIM * F),
        out_shape=[
            wide, wide, jax.ShapeDtypeStruct(flat, bf16),
            jax.ShapeDtypeStruct((2, heads, 8, L), f32),
            jax.ShapeDtypeStruct((2, heads, 8, HEAD_DIM), f32),
        ],
        grid=(2, heads),
        in_specs=[
            at(0), at(heads), at(2 * heads), at(0), at(0), at(0), lse, stats, gain, gain, table, table, posr, table,
        ],
        out_specs=[at(0), at(0), at(0), small, tiny],
        scratch_shapes=[pltpu.VMEM((L, HEAD_DIM), f32)] * 3,
        compiler_params=pltpu.CompilerParams(vmem_limit_bytes=VMEM_LIMIT),
        cost_estimate=cost(35),
    )(view, view, view, qr, kr, gm.reshape(flat), lse_in, st, gq, gk, cos, sin, pos, posc)


def newton_kernel(
    C, m_ref, rows_ref, gain_ref, out_ref, stage_ref, gsum_ref,
    v, gram, y, yf, stat, gains, gsum,
    lsem, osem, vsend, vrecv, ysend, yrecv, ssend, srecv, tsend, trecv, gsend, grecv, usend, urecv, usem,
):
    me = lax.axis_index("fsdp")
    z = lax.axis_index("ctx")
    core, chip = me % 2, me // 2
    peer = me + 1 - 2 * core
    F = 2 * C
    cols = m_ref.shape[2]
    gload = local(gain_ref, gains.at[z], lsem, 1)
    barrier = pltpu.get_barrier_semaphore()
    for k in range(1, C):
        pl.semaphore_signal(barrier, inc=1, device_id={"ctx": (z + k) % C}, device_id_type=MESH)
    for k in range(1, F):
        pl.semaphore_signal(barrier, inc=1, device_id={"fsdp": (me + k) % F}, device_id_type=MESH)
    pl.semaphore_wait(barrier, C + F - 2)
    rows_in = v.shape[1] // C
    units_sent, units_kept = [], []
    for k in range(F):
        to = (me + k) % F
        for b in range(C):
            src = m_ref.at[to // 2, pl.ds((2 * b + to % 2) * rows_in, rows_in)]
            dst = v.at[0, pl.ds(b * rows_in, rows_in), pl.ds(me * cols, cols)]
            if k == 0:
                units_kept.append(local(src, dst, usem, b))
            else:
                c = remote(src, dst, usend, urecv, k * C + b, to)
                c.start()
                units_sent.append(c)
    piece = rows_ref.shape[1] // C

    def part(j):
        return pl.ds(j * piece, piece)

    sent, keep = [], []
    for a in range(2):
        for k in range(1, C):
            to = (z + k) % C
            c = remote(rows_ref.at[a, part(to)], stage_ref.at[a, z], tsend, trecv, C * a + k, to, "ctx")
            c.start()
            sent.append(c)
        keep.append(local(rows_ref.at[a, part(z)], stage_ref.at[a, z], lsem, 2 + a))
    gload.wait()
    for k in range(1, C):
        c = remote(gains.at[z], gains.at[z], gsend, grecv, k, (z + k) % C, "ctx")
        c.start()
        sent.append(c)

    def rows_arrived():
        for a in range(2):
            keep[a].wait()
            for k in range(1, C):
                dst = stage_ref.at[a, (z - k + C) % C]
                remote(dst, dst, tsend, trecv, C * a + k, (z - k + C) % C, "ctx").wait_recv()
        for k in range(1, C):
            frm = (z - k + C) % C
            remote(gains.at[frm], gains.at[frm], gsend, grecv, k, frm, "ctx").wait_recv()
        gsum[...] = jnp.sum(gains[...], axis=0)
        local(gsum, gsum_ref, lsem, 6).wait()
        for c in sent:
            c.wait_send()

    for k in range(1, F):
        frm = (me - k + F) % F
        for b in range(C):
            dst = v.at[0, pl.ds(b * rows_in, rows_in), pl.ds(frm * cols, cols)]
            remote(dst, dst, usend, urecv, k * C + b, frm).wait_recv()
    for c in units_sent:
        c.wait_send()
    for c in units_kept:
        c.wait()
    M, D = v.shape[1], v.shape[2]
    tile, col = 512, 1024
    tiles = M // tile

    def block(i):
        return pl.ds(i * tile, tile)

    def swap(buf, i, sends, recvs):
        return remote(buf.at[0, block(i)], buf.at[1, block(i)], sends, recvs, i, peer)

    pending = [swap(v, i, vsend, vrecv) for i in range(tiles)]
    for c in pending:
        c.start()
    stat[0] = jnp.zeros_like(stat[0])

    def add(r):
        part = v[0, r, :].astype(f32)
        stat[0] += jnp.sum((part * part).reshape(-1, 8, D // 128, 128), axis=(0, 2))

    row_loop(M, add)
    share = remote(stat.at[0], stat.at[1], ssend, srecv, 0, peer)
    share.start()
    share.wait()
    inv = 1.0 / (jnp.sqrt(jnp.sum(stat[0] + stat[1])) + 1e-07)

    for iteration in range(NS_STEPS):
        factor = inv if iteration == 0 else 1.0

        def grams(h, n):
            rhs = pl.ds(pl.multiple_of(n * col, col), col)
            cols = pl.ds(pl.multiple_of(h * M + n * col, col), col)

            @pl.loop(0, tiles)
            def _(i):
                rows = pl.ds(pl.multiple_of(i * tile, tile), tile)
                got = nt(v[0, rows, :], v[h, rhs, :])
                if iteration == 0:
                    got = got * (factor * factor)
                gram[rows, cols] = got.astype(bf16)

        @pl.loop(0, M // col)
        def _(n):
            grams(0, n)

        for c in pending:
            c.wait()

        @pl.loop(0, M // col)
        def _(n):
            grams(1, n)

        def times(src, i, n):
            rows = block(i)
            cols = pl.ds(pl.multiple_of(n * col, col), col)
            return cols, nn(gram[rows, :M], src[0, :, cols]) + nn(gram[rows, M:], src[1, :, cols])

        pending = []
        for i in range(tiles):

            @pl.loop(0, D // col)
            def _(n):
                cols, got = times(v, i, n)
                if iteration == 0:
                    got = got * factor
                yf[block(i), cols] = got
                y[0, block(i), cols] = got.astype(bf16)

            c = swap(y, i, ysend, yrecv)
            c.start()
            pending.append(c)
        for c in pending:
            c.wait()
        pending = []
        for i in range(tiles):

            @pl.loop(0, D // col)
            def _(n):
                cols, got = times(y, i, n)
                old = v[0, block(i), cols].astype(f32)
                if iteration == 0:
                    old = old * factor
                v[0, block(i), cols] = (
                    quintic_one * old + quintic_two * yf[block(i), cols] + quintic_three * got
                ).astype(bf16)

            if iteration < NS_STEPS - 1:
                c = swap(v, i, vsend, vrecv)
            else:
                c = pltpu.make_async_copy(v.at[0, block(i)], out_ref.at[block(i)], osem.at[i])
            c.start()
            pending.append(c)
    rows_arrived()
    for c in pending:
        c.wait()


def newton_call(C, x, rows, gains):
    _, D, cols = x.shape
    M = D // 2
    _, R, _ = rows.shape
    n = M // 512
    return pl.pallas_call(
        functools.partial(newton_kernel, C),
        out_shape=[
            jax.ShapeDtypeStruct((M, D), bf16),
            jax.ShapeDtypeStruct((2, C, R // C, D), bf16),
            jax.ShapeDtypeStruct((8, D), f32),
        ],
        in_specs=[ANY] * 3,
        out_specs=[ANY] * 3,
        scratch_shapes=[
            pltpu.VMEM((2, M, D), bf16),
            pltpu.VMEM((M, 2 * M), bf16),
            pltpu.VMEM((2, M, D), bf16),
            pltpu.VMEM((M, D), f32),
            pltpu.VMEM((2, 8, 128), f32),
            pltpu.VMEM((C, 8, D), f32),
            pltpu.VMEM((8, D), f32),
            dma(7), dma(n), dma(n), dma(n), dma(n), dma(n), dma(1), dma(1),
            dma(2 * C), dma(2 * C), dma(C), dma(C), dma(2 * C * C), dma(2 * C * C), dma(C),
        ],
        compiler_params=params(6),
        cost_estimate=cost(95),
    )(x, rows, gains)


def leave_kernel(C, stage_ref, home_ref, lsem, send, recv):
    at = Plane()
    piece = stage_ref.shape[2]
    barrier = pltpu.get_barrier_semaphore()
    for k in range(1, C):
        pl.semaphore_signal(
            barrier, inc=1, device_id={"fsdp": 2 * ((at.chip + k) % C) + at.c}, device_id_type=MESH
        )
    pl.semaphore_wait(barrier, C - 1)

    def part(j):
        return pl.ds(j * piece, piece)

    sent, keep = [], []
    for a in range(2):
        for k in range(1, C):
            to = (at.chip + k) % C
            c = remote(stage_ref.at[a, to], home_ref.at[a, part(at.chip)], send, recv, C * a + k, 2 * to + at.c)
            c.start()
            sent.append(c)
        keep.append(local(stage_ref.at[a, at.chip], home_ref.at[a, part(at.chip)], lsem, a))
    for a in range(2):
        keep[a].wait()
        for k in range(1, C):
            frm = (at.chip - k + C) % C
            dst = home_ref.at[a, part(frm)]
            remote(dst, dst, send, recv, C * a + k, 2 * frm + at.c).wait_recv()
    for c in sent:
        c.wait_send()


def leave_call(C, stage):
    return pl.pallas_call(
        functools.partial(leave_kernel, C),
        out_shape=jax.ShapeDtypeStruct((2, C * stage.shape[2], stage.shape[3]), bf16),
        in_specs=[ANY],
        out_specs=ANY,
        scratch_shapes=[dma(2), dma(2 * C), dma(2 * C)],
        compiler_params=params(9),
        cost_estimate=cost(30),
    )(stage)


def project(C, F, x, w):
    own = to_layer(C, F, x)
    rows = token_rows(own)
    return own, rows, dot(rows, w, 1, 0)


def attn_out_and_up(C, F, mixed, wo, x, gain, w):
    if kernels_fit(C, F):
        hidden_in, out, inp = out_call(F, mixed, wo, x, gain)
        return (hidden_in, out, *up_call(F, inp, w))
    out = token_sums(dot(mixed, wo, 1, 1))
    hidden_in = x.astype(f32) + out * rms(out) * gain
    rows = token_rows(hidden_in.astype(bf16))
    g, u = jnp.split(dot(rows, w, 1, 0), 2, axis=1)
    sig = jax.nn.sigmoid(g)
    der = u * (sig * (1.0 + g * (1.0 - sig)))
    act = g * sig
    return hidden_in, out, rows, act.astype(bf16), der.astype(bf16), (act * u).astype(bf16)


def down_and_back(C, F, h, wd, hidden_in, cot, gain, act, der, units):
    if kernels_fit(C, F):
        return down_call(C, F, h, wd, hidden_in, cot, gain, act, der, units)
    cot = to_layer(C, F, cot)
    out = token_sums(dot(h, wd, 1, 1))
    scale = rms(out)
    hat = out * scale
    g = cot.astype(f32)
    rows = token_rows(back(g * gain, hat, scale).astype(bf16))
    gh = dot(rows, wd, 1, 0)
    return (
        (hidden_in + hat * gain).astype(bf16),
        jnp.sum(g * hat, axis=0, keepdims=True),
        rows,
        jnp.concatenate([(gh * der.astype(f32)).astype(bf16), (gh * act.astype(f32)).astype(bf16)], axis=1),
        cot,
        None,
        None,
    )


def back_to_attn(C, F, grad, w, cot, out, gain, wo):
    if kernels_fit(C, F):
        return mid_call(F, grad, w, cot, out, gain, wo)
    resid = cot.astype(f32) + token_sums(dot(grad, w, 1, 1))
    scale = rms(out)
    hat = out * scale
    rows = token_rows(back(resid * gain, hat, scale).astype(bf16))
    return resid, jnp.sum(resid * hat, axis=0, keepdims=True), rows, dot(rows, wo, 1, 0).astype(bf16)


def back_to_input(C, F, grad_projected, w, resid):
    return (resid + token_sums(dot(grad_projected, w, 1, 1))).astype(bf16)


def kernels_fit(C, F):
    return C == 4 and F == 8 and UNITS_ATTN * 4 * 2 == C * F


def to_layer(C, F, x):
    z, chip = lax.axis_index("ctx"), lax.axis_index("fsdp") // 2
    x = x.reshape(C, x.shape[0] // C, x.shape[1])
    got = []
    for k in range(C):
        pairs = [
            (s * F + f, (f // 2) * F + 2 * ((s + k) % C) + f % 2) for s in range(C) for f in range(F)
        ]
        block = lax.dynamic_index_in_dim(x, (z + k) % C, 0, keepdims=False)
        got.append(lax.ppermute(block, BOTH, pairs))
    got = jnp.stack(got)
    got = [lax.dynamic_index_in_dim(got, (chip - s + C) % C, 0, keepdims=False) for s in range(C)]
    return jnp.concatenate(got, axis=0)


def from_layer(C, F, x):
    z, chip = lax.axis_index("ctx"), lax.axis_index("fsdp") // 2
    x = x.reshape(C, x.shape[0] // C, x.shape[1])
    got = []
    for k in range(C):
        pairs = [
            ((f // 2) * F + 2 * ((s + k) % C) + f % 2, s * F + f) for s in range(C) for f in range(F)
        ]
        block = lax.dynamic_index_in_dim(x, (chip - k + C) % C, 0, keepdims=False)
        got.append(lax.ppermute(block, BOTH, pairs))
    got = jnp.stack(got)
    got = [lax.dynamic_index_in_dim(got, (j - z + C) % C, 0, keepdims=False) for j in range(C)]
    return jnp.concatenate(got, axis=0)


def shards(C, F, layer_input, cotangent, positions, w_attn, w_ffn, gains, mom_attn, mom_ffn, gain_mom):
    z = lax.axis_index("ctx")
    f = lax.axis_index("fsdp")
    local_rows, width = layer_input.shape[1], layer_input.shape[2]
    seq_total, seq_length = positions.shape
    dz, head_cols = w_attn.shape[1], w_attn.shape[2]
    local_heads = head_cols // HEAD_DIM
    block_count = w_ffn.shape[2]
    per = seq_total // C
    piece = local_rows // C
    chips = F // per
    tokens = F * local_rows
    hidden_cols = block_count * head_cols
    units = UNITS_ATTN + 3 * block_count
    parts = C * F // units

    def after(a, b):
        return lax.optimization_barrier((a, b))[0]

    def rows_gather(shard):
        return lax.all_gather(shard, "ctx", axis=0, tiled=True)

    def product(units, groups, *pairs):
        pairs = [(x.reshape(tokens, width), dy) for x, dy in pairs]
        if kernels:
            return grad_call(pairs, units, head_cols, groups)
        grad = jnp.concatenate([dot(x, dy, 0, 0).astype(bf16) for x, dy in pairs], axis=1)
        return jnp.transpose(grad.reshape(width, groups, units, head_cols), (2, 1, 0, 3))

    def scatter(grad):
        if kernels:
            return lax.psum_scatter(grad, "ctx", scatter_dimension=0, tiled=True)[0]
        return lax.psum_scatter(grad, "ctx", scatter_dimension=2, tiled=True)

    kernels = kernels_fit(C, F)
    w_heads = rows_gather(jnp.concatenate([w_attn[i] for i in range(UNITS_ATTN)], axis=1))
    w_qkv, w_out = (w_heads, w_heads) if kernels else (w_heads[:, : 3 * head_cols], w_heads[:, 3 * head_cols :])
    ffn_flat = w_ffn.reshape(3, dz, hidden_cols)
    w_gate_up = rows_gather(jnp.concatenate([ffn_flat[0], ffn_flat[1]], axis=1))
    w_down = rows_gather(ffn_flat[2])

    gain_query = lax.dynamic_slice_in_dim(gains[0], f * head_cols, head_cols)
    gain_key = lax.dynamic_slice_in_dim(gains[1], f * head_cols, head_cols)
    pos = lax.dynamic_slice_in_dim(positions, z * per, per, 0)
    pos = jnp.transpose(pos.reshape(per, C, chips, piece), (0, 2, 1, 3)).reshape(per, seq_length)
    cosine_table, sine_table = rotary_tables(pos)

    def heads(a):
        return jnp.transpose(
            a.reshape(chips, per, local_rows, local_heads, HEAD_DIM), (1, 0, 2, 3, 4)
        ).reshape(per, seq_length, local_heads, HEAD_DIM)

    def unheads(a):
        return jnp.transpose(
            a.reshape(per, chips, local_rows, local_heads, HEAD_DIM), (1, 0, 2, 3, 4)
        ).reshape(tokens, head_cols)

    if kernels:
        sign = jnp.where(jnp.arange(HEAD_DIM) < HEAD_DIM // 2, -1.0, 1.0)
        tables = (
            gain_query[None],
            gain_key[None],
            jnp.broadcast_to(cosine_table[:, :, 0], (per, seq_length, HEAD_DIM)),
            sine_table[:, :, 0] * sign,
            pos.astype(f32)[:, None, :],
            jnp.broadcast_to(pos.astype(f32)[..., None], (per, seq_length, HEAD_DIM)),
        )
        own_input, input_all = enter_call(C, F, layer_input.reshape(local_rows, width))
        projected, stats = qkv_call(F, input_all, w_qkv)
        attn_mixed, query_rows, key_rows, log_total = attend_call(F, projected, stats, *tables)
        attn_mixed = attn_mixed.reshape(tokens, head_cols)
    else:
        own_input, input_all, projected = project(C, F, layer_input.reshape(local_rows, width), w_qkv)
        query_raw = projected[:, :head_cols]
        key_raw = projected[:, head_cols : 2 * head_cols]
        value_raw = projected[:, 2 * head_cols :]
        query_total, key_total = norm_stats(
            jnp.sum(query_raw * query_raw, axis=-1), jnp.sum(key_raw * key_raw, axis=-1)
        )
        query_scale = lax.rsqrt(query_total / width + epsilon)[..., None]
        key_scale = lax.rsqrt(key_total / width + epsilon)[..., None]
        query_hat = query_raw * query_scale
        key_hat = key_raw * key_scale
        query_rows = (
            rotate(heads(query_hat * gain_query), cosine_table, sine_table) * HEAD_DIM ** (-0.5)
        ).astype(bf16)
        key_rows = rotate(heads(key_hat * gain_key), cosine_table, sine_table).astype(bf16)
        value_rows = heads(value_raw.astype(bf16))
        attn_mixed, log_total = attend(query_rows, key_rows, value_rows, pos)
        attn_mixed = unheads(attn_mixed)
    hidden_in, attn_out, mlp_all, act, der, hidden = attn_out_and_up(
        C, F, attn_mixed, w_out, own_input, gains[2:3], w_gate_up
    )
    by_layer = None
    if kernels:
        by_layer = jnp.concatenate(
            [mom_attn[:, None].astype(bf16), jnp.transpose(mom_ffn.astype(bf16), (2, 0, 1, 3))], axis=1
        )
    result, mlp_gain, grad_mlp_all, grad_ffn_in, own_grad, mom_own, p_down = down_and_back(
        C, F, hidden, w_down, hidden_in, cotangent.reshape(local_rows, width), gains[3:4], act, der, by_layer
    )
    if kernels:
        mom_own = jnp.swapaxes(mom_own, 0, 1)
    else:
        p_down = product(block_count, 1, (grad_mlp_all, hidden))
    g_down = scatter(p_down)
    p_gate_up = product(block_count, 2, (mlp_all, grad_ffn_in))
    if kernels:
        grad_ffn_in, p_gate_up = lax.optimization_barrier((grad_ffn_in, p_gate_up))
    g_gate_up = scatter(p_gate_up)
    grad_resid, attn_gain, grad_attn_all, grad_mixed = back_to_attn(
        C, F, grad_ffn_in, w_gate_up, own_grad, attn_out, gains[2:3], w_out
    )
    if kernels:
        grad_mixed = after(grad_mixed, g_down)
        weighted_q, weighted_k, grad_value, inner, gain_cols = attend_back_call(
            F, projected, query_rows, key_rows, grad_mixed, log_total, stats, *tables
        )
        inner = jnp.transpose(
            jnp.sum(inner, axis=1).reshape(per, 8, chips, local_rows), (1, 2, 0, 3)
        ).reshape(8, tokens)
        gain_cols = jnp.sum(gain_cols, axis=0)
        query_gain_cols = gain_cols[:, 0].reshape(head_cols)
        key_gain_cols = gain_cols[:, 1].reshape(head_cols)
        flat = (tokens, head_cols)
        zero = jnp.zeros((width,), f32)
        gain_local = jnp.stack(
            [
                lax.dynamic_update_slice(zero, query_gain_cols, (f * head_cols,)),
                lax.dynamic_update_slice(zero, key_gain_cols, (f * head_cols,)),
                attn_gain[0],
                mlp_gain[0],
                *[zero] * 4,
            ]
        )
        grad_rows, grad_projected, gain_layer = last_call(
            F, weighted_q.reshape(flat), weighted_k.reshape(flat), grad_value.reshape(flat),
            projected, stats, inner, w_qkv, grad_resid, gain_local,
        )
    else:
        grad_query, grad_key, grad_value = attend_back(
            query_rows, key_rows, value_rows, pos, heads(grad_mixed), log_total
        )
        grad_query_norm = unheads(unrotate(grad_query * HEAD_DIM ** (-0.5), cosine_table, sine_table))
        grad_key_norm = unheads(unrotate(grad_key, cosine_table, sine_table))
        query_gain_cols = jnp.sum(grad_query_norm * query_hat, axis=0)
        key_gain_cols = jnp.sum(grad_key_norm * key_hat, axis=0)
        query_weighted = grad_query_norm * gain_query
        key_weighted = grad_key_norm * gain_key
        query_inner, key_inner = norm_stats(
            jnp.sum(query_weighted * query_hat, axis=-1), jnp.sum(key_weighted * key_hat, axis=-1)
        )
        grad_query_raw = query_scale * (query_weighted - query_hat * (query_inner / width)[..., None])
        grad_key_raw = key_scale * (key_weighted - key_hat * (key_inner / width)[..., None])
        grad_projected = jnp.concatenate(
            [grad_query_raw.astype(bf16), grad_key_raw.astype(bf16), unheads(grad_value).astype(bf16)],
            axis=1,
        )
        grad_rows = back_to_input(C, F, grad_projected, w_qkv, grad_resid)
    g_attn = scatter(
        product(UNITS_ATTN, 1, (input_all, grad_projected), (grad_attn_all, attn_mixed))
    )
    if not kernels:
        grad_input = from_layer(C, F, grad_rows)
        result = from_layer(C, F, result)
        zero = jnp.zeros((width,), f32)
        gain_local = jnp.stack(
            [
                lax.dynamic_update_slice(zero, query_gain_cols, (f * head_cols,)),
                lax.dynamic_update_slice(zero, key_gain_cols, (f * head_cols,)),
                attn_gain[0],
                mlp_gain[0],
            ]
        )
        gain_total = jnp.sum(lax.all_gather(gain_local, BOTH, axis=0, tiled=False), axis=0)

    if kernels:
        early = jnp.stack([jnp.zeros_like(g_down[0]), g_gate_up[0], g_gate_up[1], g_down[0]])
        mom = momentum * mom_own.reshape(early.shape).astype(f32)
        owned = (mom + early.astype(f32)).astype(bf16)
        mom_first = mom[0]
        early, owned, mom_first, grad_rows = lax.optimization_barrier((early, owned, mom_first, grad_rows))
        late = (mom_first + g_attn[0].astype(f32)).astype(bf16)
        owned = lax.dynamic_update_slice(owned, late[None], (0, 0, 0))
        got = lax.dynamic_update_slice(early, g_attn, (0, 0, 0))
        sent_back = got.reshape(UNITS_ATTN, C, dz, head_cols)
        sent_back = lax.all_to_all(sent_back, "ctx", split_axis=1, concat_axis=0, tiled=False)
        sent_back = sent_back.reshape(C, UNITS_ATTN, dz, head_cols).astype(f32)
        grad_attn = sent_back[:, 0]
        grad_ffn = jnp.transpose(sent_back[:, 1:], (1, 2, 0, 3))
        own, leaving, gain_total = newton_call(C, owned, jnp.stack([result, grad_rows]), gain_layer)
        back_rows = leave_call(C, leaving)
        result, grad_input, gain_total = back_rows[0], back_rows[1], gain_total[:4]
    else:
        grad_attn = g_attn[:, 0].astype(f32)
        grad_ffn = jnp.transpose(
            jnp.concatenate([g_gate_up, g_down], axis=1).astype(f32), (1, 2, 0, 3)
        )
    new_attn = momentum * mom_attn + grad_attn
    new_ffn = momentum * mom_ffn + grad_ffn
    if not kernels:
        send = jnp.concatenate(
            [
                new_attn.astype(bf16),
                jnp.transpose(new_ffn.astype(bf16), (0, 2, 1, 3)).reshape(3 * block_count, dz, head_cols),
            ],
            axis=0,
        ).reshape(C * F, dz // parts, head_cols)
        own = lax.all_to_all(send, BOTH, split_axis=0, concat_axis=0, tiled=True)
        own = jnp.transpose(own.reshape(C, F, dz // parts, head_cols), (0, 2, 1, 3)).reshape(
            C * dz // parts, F * head_cols
        )

        def peers(a):
            out = [a]
            for s in range(1, parts):
                pairs = [(i, i - i % parts + (i + parts - s) % parts) for i in range(C * F)]
                out.append(lax.ppermute(a, BOTH, pairs))
            return out

        own32 = own.astype(f32)
        square = jnp.sum(own32 * own32)
        total = sum(peers(square.reshape(1, 1)))
        inv = 1.0 / (jnp.sqrt(total) + 1e-07)
        for iteration in range(NS_STEPS):
            factor = inv if iteration == 0 else 1.0
            every = peers(own)
            gram = [(dot(own, b, 1, 1) * (factor * factor)).astype(bf16) for b in every]
            product = sum(dot(g, b, 1, 0) for g, b in zip(gram, every)) * factor
            product_all = peers(product.astype(bf16))
            product_two = sum(dot(g, b, 1, 0) for g, b in zip(gram, product_all))
            own = (
                quintic_one * factor * own.astype(f32) + quintic_two * product + quintic_three * product_two
            ).astype(bf16)
    home = jnp.transpose(own.reshape(C, dz // parts, F, head_cols), (0, 2, 1, 3)).reshape(
        C * F, dz // parts, head_cols
    )
    steps = lax.all_to_all(home, BOTH, split_axis=0, concat_axis=0, tiled=True)
    steps = -muon_rate * steps.astype(f32)
    if kernels:
        steps = steps.reshape(C, UNITS_ATTN, dz, head_cols)
        step_attn = steps[:, 0]
        step_ffn = jnp.transpose(steps[:, 1:], (1, 2, 0, 3))
    else:
        steps = steps.reshape(units, dz, head_cols)
        step_attn = steps[:UNITS_ATTN]
        step_ffn = jnp.transpose(
            steps[UNITS_ATTN:].reshape(3, block_count, dz, head_cols), (0, 2, 1, 3)
        )
    new_gain_mom = momentum * gain_mom + gain_total
    return (
        result.reshape(layer_input.shape),
        grad_input.astype(f32).reshape(layer_input.shape),
        grad_attn,
        grad_ffn,
        gain_total,
        new_attn,
        new_ffn,
        new_gain_mom,
        step_attn,
        step_ffn,
        -gain_rate * new_gain_mom,
    )


def solution(mesh):
    tokens = P("fsdp", "ctx", None)
    attn = P(None, "ctx", "fsdp")
    ffn = P(None, "ctx", None, "fsdp")
    in_specs = (tokens, tokens, P(), attn, ffn, P(), attn, ffn, P())
    out_specs = (tokens, tokens, attn, ffn, P(), attn, ffn, P(), attn, ffn, P())
    body = functools.partial(shards, mesh.shape["ctx"], mesh.shape["fsdp"])
    return jax.shard_map(body, mesh=mesh, in_specs=in_specs, out_specs=out_specs, check_vma=False)
```

```python
import functools
import jax
import jax.numpy as jnp
from jax import lax
from jax.experimental import pallas as pl
from jax.experimental.pallas import tpu as pltpu
from jax.sharding import PartitionSpec as P

NS_STEPS = 3
HEAD_DIM = 128
UNITS_ATTN = 4

epsilon = 1e-06
rope_theta = 500000.0
quintic_one = 3.4445
quintic_two = -4.775
quintic_three = 2.0315
momentum = 0.95
muon_rate = 1.0
gain_rate = 0.0005
BOTH = ("ctx", "fsdp")
bf16 = jnp.bfloat16
f32 = jnp.float32


def dot(a, b, ca, cb):
    return lax.dot_general(a, b, (((ca,), (cb,)), ((), ())), preferred_element_type=f32)


def token_rows(operand):
    return lax.all_gather(operand, "fsdp", axis=0, tiled=True)


def token_sums(operand):
    return lax.psum_scatter(operand.astype(bf16), "fsdp", scatter_dimension=0, tiled=True).astype(f32)


def norm_stats(first_sum, second_sum):
    got = lax.all_gather(jnp.stack([first_sum, second_sum]), "fsdp", axis=0, tiled=False)
    total = jnp.sum(got, axis=0)
    return total[0], total[1]


def rms_back(upstream, normed, inv_scale):
    return inv_scale * (upstream - normed * jnp.mean(upstream * normed, axis=-1, keepdims=True))


def rotary_tables(slot_order):
    half_dim = HEAD_DIM // 2
    inverse = rope_theta ** (-(jnp.arange(half_dim, dtype=f32) * 2.0) / HEAD_DIM)
    angles = slot_order.astype(f32)[..., None] * inverse
    angles = jnp.concatenate([angles, angles], axis=-1)
    return (jnp.cos(angles)[..., None, :], jnp.sin(angles)[..., None, :])


def rotate(operand, cosine_table, sine_table):
    half_dim = operand.shape[-1] // 2
    flipped = jnp.concatenate([-operand[..., half_dim:], operand[..., :half_dim]], axis=-1)
    return operand * cosine_table + flipped * sine_table


def unrotate(upstream, cosine_table, sine_table):
    half_dim = upstream.shape[-1] // 2
    shifted = upstream * sine_table
    flipped = jnp.concatenate([shifted[..., half_dim:], -shifted[..., :half_dim]], axis=-1)
    return upstream * cosine_table + flipped


def masked_scores(query_rows, key_rows, pos):
    scores = jnp.einsum("gqhe,gkhe->ghqk", query_rows, key_rows, preferred_element_type=f32)
    causal = pos[:, None, :, None] >= pos[:, None, None, :]
    return jnp.where(causal, scores, -1e30)


def attend(query_rows, key_rows, value_rows, pos):
    scores = masked_scores(query_rows, key_rows, pos)
    row_max = jnp.max(scores, axis=-1, keepdims=True)
    weights = jnp.exp(scores - row_max)
    row_total = jnp.sum(weights, axis=-1, keepdims=True)
    probabilities = (weights / row_total).astype(bf16)
    attn_mixed = jnp.einsum("ghqk,gkhe->gqhe", probabilities, value_rows, preferred_element_type=f32)
    return attn_mixed.astype(bf16), row_max + jnp.log(row_total)


def attend_back(query_rows, key_rows, value_rows, pos, grad_mixed, log_total):
    scores = masked_scores(query_rows, key_rows, pos)
    probabilities = jnp.exp(scores - log_total)
    grad_probs = jnp.einsum("gqhe,gkhe->ghqk", grad_mixed, value_rows, preferred_element_type=f32)
    grad_value = jnp.einsum(
        "ghqk,gqhe->gkhe", probabilities.astype(bf16), grad_mixed, preferred_element_type=f32
    )
    inner_sum = jnp.sum(grad_probs * probabilities, axis=-1, keepdims=True)
    grad_scores = (probabilities * (grad_probs - inner_sum)).astype(bf16)
    grad_query = jnp.einsum("ghqk,gkhe->gqhe", grad_scores, key_rows, preferred_element_type=f32)
    grad_key = jnp.einsum("ghqk,gqhe->gkhe", grad_scores, query_rows, preferred_element_type=f32)
    return grad_query, grad_key, grad_value


MESH = pl.DeviceIdType.MESH
VMEM_LIMIT = 60 * 1024 * 1024
ANY = pl.BlockSpec(memory_space=pl.ANY)


class Plane:
    def __init__(self):
        f = lax.axis_index("fsdp")
        self.f, self.c, self.chip = f, f % 2, f // 2
        x, y = self.chip % 2, self.chip // 2
        self.qx = self.chip + 1 - 2 * x
        self.qy = self.chip + 2 - 4 * y
        self.qd = self.qx + 2 - 4 * y
        self.fc = f + 1 - 2 * self.c
        self.fx = 2 * self.qx + self.c
        self.fy = 2 * self.qy + self.c
        self.fd = 2 * self.qd + self.c
        self.other = 1 - self.c

    def greet(self):
        barrier = pltpu.get_barrier_semaphore()
        for to in (self.fc, self.fx, self.fy):
            pl.semaphore_signal(barrier, inc=1, device_id={"fsdp": to}, device_id_type=MESH)
        pl.semaphore_wait(barrier, 3)


def partner(i, k):
    if k == 3:
        return 3 - i
    if k == 2:
        return (i + 2) % 4
    return i + 1 - 2 * (i % 2)


FAR_FIRST = (3, 2, 1)


def remote(src, dst, send, recv, i, to, axis="fsdp"):
    return pltpu.make_async_remote_copy(
        src_ref=src, dst_ref=dst, send_sem=send.at[i], recv_sem=recv.at[i],
        device_id={axis: to}, device_id_type=MESH,
    )


def local(src, dst, sems, i):
    copy = pltpu.make_async_copy(src, dst, sems.at[i])
    copy.start()
    return copy


def nn(a, b):
    return lax.dot_general(a, b, (((1,), (0,)), ((), ())), preferred_element_type=f32)


def nt(a, b):
    return lax.dot_general(a, b, (((1,), (1,)), ((), ())), preferred_element_type=f32)


def gather_phase(at, rows, send, recv, base, on_rows):
    half = rows.shape[1] // 2
    A, B = pl.ds(0, half), pl.ds(half, half)

    def cp(i, slot, part, to):
        ref = rows.at[slot] if part is None else rows.at[slot, part]
        return remote(ref, ref, send, recv, base + i, to)

    fcx, fcy, fcd = 2 * at.qx + at.other, 2 * at.qy + at.other, 2 * at.qd + at.other
    sent = []

    def go(*a):
        c = cp(*a)
        c.start()
        sent.append(c)

    def arrived(i, slot, part, frm):
        cp(i, slot, part, frm).wait_recv()

    go(0, at.f, None, at.fc)
    go(1, at.f, A, at.fx)
    go(3, at.f, B, at.fy)
    go(2, at.f, B, at.fx)
    go(4, at.f, A, at.fy)
    arrived(0, at.fc, None, at.fc)
    on_rows(2 * at.chip, 2)
    arrived(1, at.fx, A, at.fx)
    go(5, at.fx, A, at.fy)
    go(7, at.fx, A, at.fc)
    arrived(3, at.fy, B, at.fy)
    go(6, at.fy, B, at.fx)
    go(8, at.fy, B, at.fc)
    arrived(2, at.fx, B, at.fx)
    go(9, at.fx, B, at.fc)
    arrived(4, at.fy, A, at.fy)
    go(10, at.fy, A, at.fc)
    arrived(7, fcx, A, at.fc)
    arrived(9, fcx, B, at.fc)
    on_rows(2 * at.qx, 2)
    arrived(8, fcy, B, at.fc)
    arrived(10, fcy, A, at.fc)
    on_rows(2 * at.qy, 2)
    arrived(5, at.fd, A, at.fy)
    go(11, at.fd, A, at.fc)
    arrived(6, at.fd, B, at.fx)
    go(12, at.fd, B, at.fc)
    on_rows(at.fd, 1)
    arrived(11, fcd, A, at.fc)
    arrived(12, fcd, B, at.fc)
    on_rows(fcd, 1)
    for c in sent:
        c.wait_send()


GATHER_COPIES = 13
SCATTER_COPIES = 10


def scatter_scratch(R, D):
    return [
        pltpu.VMEM((4, R, D), bf16),
        pltpu.VMEM((4, R, D), bf16),
        pltpu.VMEM((2, R, D), f32),
        pltpu.VMEM((3, R, D), bf16),
        pltpu.VMEM((3, R, D), bf16),
    ]


def scatter_phase(at, partial, bufs, send, recv, base, between=None):
    to_core, from_core, mine, out, inc = bufs
    R, D = to_core.shape[1], to_core.shape[2]
    half = R // 2
    A, B = pl.ds(0, half), pl.ds(half, half)
    tile = 512
    step = 16
    sent = []

    def go(i, src, dst, to):
        c = remote(src, dst, send, recv, base + i, to)
        c.start()
        sent.append(c)

    def arrived(i, dst, frm):
        remote(dst, dst, send, recv, base + i, frm).wait_recv()

    def compute(order, chip, slot):
        @pl.loop(0, D // tile)
        def _(n):
            cols = pl.ds(pl.multiple_of(n * tile, tile), tile)
            got = partial(chip, cols)
            lo, hi = got[:R], got[R:]
            first = at.c == 0
            mine[slot, :, cols] = jnp.where(first, lo, hi)
            to_core[order, :, cols] = jnp.where(first, hi, lo).astype(bf16)

        go(order, to_core.at[order], from_core.at[order], at.fc)

    def chip_sum(order, slot):
        arrived(order, from_core.at[order], at.fc)

        @pl.loop(0, R // step)
        def _(r):
            rows = pl.ds(pl.multiple_of(r * step, step), step)
            out[order, rows, :] = (mine[slot, rows, :] + from_core[order, rows, :].astype(f32)).astype(bf16)

    def relay(order, start, src):
        @pl.loop(0, half // step)
        def _(r):
            rows = pl.ds(pl.multiple_of(start + r * step, step), step)
            out[order, rows, :] = (out[order, rows, :].astype(f32) + inc[src, rows, :].astype(f32)).astype(bf16)

    compute(0, at.qd, 0)
    compute(1, at.qx, 1)
    if between is not None:
        between()
    chip_sum(0, 0)
    go(4, out.at[0, A], inc.at[0, A], at.fx)
    go(5, out.at[0, B], inc.at[0, B], at.fy)
    compute(2, at.qy, 0)
    chip_sum(1, 1)
    go(6, out.at[1, A], inc.at[1, A], at.fx)
    compute(3, at.chip, 1)
    chip_sum(2, 0)
    go(8, out.at[2, B], inc.at[2, B], at.fy)
    arrived(5, inc.at[0, B], at.fy)
    relay(1, half, 0)
    go(7, out.at[1, B], inc.at[1, B], at.fx)
    arrived(4, inc.at[0, A], at.fx)
    relay(2, 0, 0)
    go(9, out.at[2, A], inc.at[2, A], at.fy)
    arrived(3, from_core.at[3], at.fc)
    arrived(6, inc.at[1, A], at.fx)
    arrived(8, inc.at[2, B], at.fy)
    arrived(7, inc.at[1, B], at.fx)
    arrived(9, inc.at[2, A], at.fy)
    for c in sent:
        c.wait_send()

    def total(rows):
        return (
            mine[1, rows, :]
            + from_core[3, rows, :].astype(f32)
            + inc[1, rows, :].astype(f32)
            + inc[2, rows, :].astype(f32)
        )

    return total


def rms(v):
    return lax.rsqrt(jnp.mean(v * v, axis=-1, keepdims=True) + epsilon)


def back(weighted, normed, scale):
    return scale * (weighted - normed * jnp.mean(weighted * normed, axis=-1, keepdims=True))


def row_loop(R, body, step=16):
    @pl.loop(0, R // step)
    def _(r):
        body(pl.ds(pl.multiple_of(r * step, step), step))


def pair_loop(rows, w_cols, total_cols, body):
    @pl.loop(0, total_cols // w_cols)
    def _(t):
        body(pl.ds(pl.multiple_of(t * w_cols, w_cols), w_cols))


class Stores:
    def __init__(self, sems):
        self.sems, self.steps, self.n = sems, [], 0

    def slot(self):
        if len(self.steps) >= 2:
            for c in self.steps[-2]:
                c.wait()
            self.steps[-2] = []
        return len(self.steps) % 2

    def put(self, pairs):
        done = []
        for src, dst in pairs:
            done.append(local(src, dst, self.sems, self.n))
            self.n += 1
        self.steps.append(done)

    def finish(self):
        for step in self.steps:
            for c in step:
                c.wait()


class Moving:
    def __init__(self, at, C, mine, stage, landing, lsem, base, send, recv):
        self.at, self.C, self.mine, self.stage, self.landing = at, C, mine, stage, landing
        self.lsem, self.base, self.send, self.recv = lsem, base, send, recv
        self.z = lax.axis_index("ctx")
        self.piece = mine.shape[0] // C
        self.sent = []

    def greet(self, barrier):
        at, C = self.at, self.C
        for k in range(1, C):
            pl.semaphore_signal(barrier, inc=1, device_id={"ctx": (self.z + k) % C}, device_id_type=MESH)
            pl.semaphore_signal(
                barrier, inc=1, device_id={"fsdp": 2 * ((at.chip + k) % C) + at.c}, device_id_type=MESH
            )

    def first(self):
        at, C, piece = self.at, self.C, self.piece
        for k in FAR_FIRST:
            j = partner(at.chip, k)
            src = self.mine.at[pl.ds(j * piece, piece)]
            c = remote(src, self.stage.at[at.chip], self.send, self.recv, k, 2 * j + at.c)
            c.start()
            self.sent.append(c)
        src = self.mine.at[pl.ds(at.chip * piece, piece)]
        self.keep = local(src, self.stage.at[at.chip], self.lsem, self.base)

    def land(self, layer):
        return self.landing.at[pl.ds(layer * self.piece, self.piece)]

    def second(self):
        at, C, z = self.at, self.C, self.z
        self.keep.wait()
        for k in FAR_FIRST:
            frm = partner(at.chip, k)
            remote(self.stage.at[frm], self.stage.at[frm], self.send, self.recv, k, 2 * frm + at.c).wait_recv()
        for k in FAR_FIRST:
            to = partner(z, k)
            c = remote(self.stage.at[to], self.land(z), self.send, self.recv, C + k, to, "ctx")
            c.start()
            self.sent.append(c)
        self.keep = local(self.stage.at[z], self.land(z), self.lsem, self.base + 1)

    def finish(self):
        C, z = self.C, self.z
        self.keep.wait()
        for k in FAR_FIRST:
            frm = partner(z, k)
            remote(self.land(frm), self.land(frm), self.send, self.recv, C + k, frm, "ctx").wait_recv()
        for c in self.sent:
            c.wait_send()


def enter_kernel(C, x_ref, own_ref, all_ref, stage, mine, rows, lsem, osem, send, recv, tsend, trecv):
    at = Plane()
    load = local(x_ref, mine, lsem, 0)
    moving = Moving(at, C, mine, stage, rows.at[at.f], lsem, 1, tsend, trecv)
    barrier = pltpu.get_barrier_semaphore()
    moving.greet(barrier)
    pl.semaphore_signal(barrier, inc=1, device_id={"fsdp": at.fc}, device_id_type=MESH)
    pl.semaphore_wait(barrier, 2 * (C - 1) + 1)
    load.wait()
    moving.first()
    moving.second()
    moving.finish()
    save = local(rows.at[at.f], own_ref, lsem, 3)
    stores = []

    def on_rows(first, count):
        stores.append(local(rows.at[pl.ds(first, count)], all_ref.at[pl.ds(first, count)], osem, len(stores)))

    gather_phase(at, rows, send, recv, 0, on_rows)
    save.wait()
    for c in stores:
        c.wait()


def enter_call(C, F, x):
    R, D = x.shape
    return pl.pallas_call(
        functools.partial(enter_kernel, C),
        out_shape=[jax.ShapeDtypeStruct((R, D), bf16), jax.ShapeDtypeStruct((F, R, D), bf16)],
        in_specs=[ANY],
        out_specs=[ANY] * 2,
        scratch_shapes=[
            pltpu.VMEM((C, R // C, D), bf16),
            pltpu.VMEM((R, D), bf16),
            pltpu.VMEM((F, R, D), bf16),
            dma(4), dma(5), dma(GATHER_COPIES), dma(GATHER_COPIES), dma(2 * C), dma(2 * C),
        ],
        compiler_params=params(1),
        cost_estimate=cost(70),
    )(x)


def qkv_kernel(all_ref, w_ref, proj_ref, st_ref, rows, w, acc, st, lsem, osem, ssend, srecv):
    at = Plane()
    F, R = rows.shape[0], rows.shape[1]
    e = w.shape[1] // 3
    m = 2 * R
    loads = [local(w_ref.at[:, pl.ds(0, 3 * e)], w, lsem, 0)] + [
        local(all_ref.at[pl.ds(2 * p, 2)], rows.at[pl.ds(2 * p, 2)], lsem, 1 + p) for p in range(F // 2)
    ]
    barrier = pltpu.get_barrier_semaphore()
    for k in range(1, F):
        pl.semaphore_signal(barrier, inc=1, device_id={"fsdp": (at.f + k) % F}, device_id_type=MESH)
    pl.semaphore_wait(barrier, F - 1)
    loads[0].wait()
    stores = Stores(osem)
    for p in range(F // 2):
        loads[1 + p].wait()
        s = stores.slot()

        def tile(c):
            acc[s, :, c] = nn(rows[pl.ds(2 * p, 2)].reshape(m, rows.shape[2]), w[:, c])

        pair_loop(m, 256, w.shape[1], tile)
        q, k = acc[s, :, :e], acc[s, :, e : 2 * e]
        st[at.f, :, pl.ds(p * m, m)] = row_sums(q * q, k * k)
        stores.put([(acc.at[s], proj_ref.at[pl.ds(p * m, m)])])
    share_stats(at, F, st, ssend, srecv, 0)
    local(st, st_ref, lsem, 1 + F // 2).wait()
    stores.finish()


def params(number):
    return pltpu.CompilerParams(
        collective_id=number, has_side_effects=True, vmem_limit_bytes=VMEM_LIMIT
    )


def cost(us):
    return pl.CostEstimate(flops=int(us * 1e9), bytes_accessed=2**20, transcendentals=0)


def dma(n):
    return pltpu.SemaphoreType.DMA((n,))


def qkv_call(F, rows, w):
    _, R, D = rows.shape
    n = w.shape[1] // 4 * 3
    return pl.pallas_call(
        qkv_kernel,
        out_shape=[
            jax.ShapeDtypeStruct((F * R, n), f32),
            jax.ShapeDtypeStruct((F, 8, F * R), f32),
        ],
        in_specs=[ANY] * 2,
        out_specs=[ANY] * 2,
        scratch_shapes=[
            pltpu.VMEM((F, R, D), bf16),
            pltpu.VMEM((D, n), bf16),
            pltpu.VMEM((2, 2 * R, n), f32),
            pltpu.VMEM((F, 8, F * R), f32),
            dma(6), dma(4), dma(F), dma(F),
        ],
        compiler_params=params(7),
        cost_estimate=cost(22),
    )(rows, w)


def out_kernel(
    mixed_ref, wo_ref, x_ref, gain_ref, hid_ref, ao_ref, in_ref,
    mixed, wo, x, gain, hid, ao, inp, b0, b1, b2, b3, b4, lsem, send, recv,
):
    at = Plane()
    e = wo.shape[1]
    pairs = [(mixed_ref, mixed), (wo_ref.at[:, pl.ds(3 * e, e)], wo), (x_ref, x), (gain_ref, gain)]
    loads = [local(s, d, lsem, i) for i, (s, d) in enumerate(pairs)]
    at.greet()
    R = x.shape[0]
    loads[0].wait()
    loads[1].wait()

    def partial(chip, cols):
        return nt(mixed[pl.ds(pl.multiple_of(chip * 2 * R, 2 * R), 2 * R), :], wo[cols, :])

    total = scatter_phase(at, partial, (b0, b1, b2, b3, b4), send, recv, 0)
    loads[2].wait()
    loads[3].wait()

    def finish(r):
        out = total(r)
        ao[r, :] = out
        hidden_in = x[r, :].astype(f32) + out * rms(out) * gain[...]
        hid[r, :] = hidden_in
        inp[r, :] = hidden_in.astype(bf16)

    row_loop(R, finish)
    for c in [local(ao, ao_ref, lsem, 4), local(hid, hid_ref, lsem, 5), local(inp, in_ref, lsem, 6)]:
        c.wait()


def out_call(F, mixed, wo, x, gain):
    R, D = x.shape
    e = wo.shape[1] // 4
    return pl.pallas_call(
        out_kernel,
        out_shape=[
            jax.ShapeDtypeStruct((R, D), f32),
            jax.ShapeDtypeStruct((R, D), f32),
            jax.ShapeDtypeStruct((R, D), bf16),
        ],
        in_specs=[ANY] * 4,
        out_specs=[ANY] * 3,
        scratch_shapes=[
            pltpu.VMEM((F * R, e), bf16),
            pltpu.VMEM((D, e), bf16),
            pltpu.VMEM((R, D), bf16),
            pltpu.VMEM((1, D), f32),
            pltpu.VMEM((R, D), f32),
            pltpu.VMEM((R, D), f32),
            pltpu.VMEM((R, D), bf16),
        ]
        + scatter_scratch(R, D)
        + [dma(7), dma(SCATTER_COPIES), dma(SCATTER_COPIES)],
        compiler_params=params(8),
        cost_estimate=cost(46),
    )(mixed, wo, x, gain)


def up_kernel(
    in_ref, w_ref, all_ref, act_ref, der_ref, h_ref,
    w, rows, act, der, h, lsem, osem, send, recv,
):
    at = Plane()
    own = local(in_ref, rows.at[at.f], lsem, 0)
    n = act.shape[2]
    loads = [local(w_ref, w, lsem, 1)]
    width = 256
    at.greet()
    R = rows.shape[1]
    own.wait()
    waited = []
    stores = Stores(osem)

    def on_rows(first, count):
        s = stores.slot()
        m = count * R
        if not waited:
            for c in loads:
                c.wait()
            waited.append(1)

        @pl.loop(0, n // width)
        def _(t):
            c = pl.ds(pl.multiple_of(t * width, width), width)
            lhs = rows[pl.ds(first, count)].reshape(m, rows.shape[2])
            g = nn(lhs, w[:, c])
            u = nn(lhs, w[:, pl.ds(pl.multiple_of(n + t * width, width), width)])
            sig = jax.nn.sigmoid(g)
            a = g * sig
            act[s, pl.ds(0, m), c] = a.astype(bf16)
            der[s, pl.ds(0, m), c] = (u * (sig * (1.0 + g * (1.0 - sig)))).astype(bf16)
            h[s, pl.ds(0, m), c] = (a * u).astype(bf16)

        start = pl.multiple_of(first * R, R)
        stores.put(
            [
                (act.at[s, pl.ds(0, m)], act_ref.at[pl.ds(start, m)]),
                (der.at[s, pl.ds(0, m)], der_ref.at[pl.ds(start, m)]),
                (h.at[s, pl.ds(0, m)], h_ref.at[pl.ds(start, m)]),
                (rows.at[pl.ds(first, count)], all_ref.at[pl.ds(first, count)]),
            ]
        )

    gather_phase(at, rows, send, recv, 0, on_rows)
    stores.finish()


def up_call(F, inp, w):
    R, D = inp.shape
    n = w.shape[1] // 2
    T = F * R
    wide = jax.ShapeDtypeStruct((T, n), bf16)
    return pl.pallas_call(
        up_kernel,
        out_shape=[jax.ShapeDtypeStruct((F, R, D), bf16), wide, wide, wide],
        in_specs=[ANY] * 2,
        out_specs=[ANY] * 4,
        scratch_shapes=[
            pltpu.VMEM((D, 2 * n), bf16),
            pltpu.VMEM((F, R, D), bf16),
            pltpu.VMEM((2, 2 * R, n), bf16),
            pltpu.VMEM((2, 2 * R, n), bf16),
            pltpu.VMEM((2, 2 * R, n), bf16),
        ]
        + [dma(2), dma(20), dma(GATHER_COPIES), dma(GATHER_COPIES)],
        compiler_params=params(2),
        cost_estimate=cost(46),
    )(inp, w)


def down_kernel(
    C, h_ref, wd_ref, hid_ref, cot_ref, gain_ref, act_ref, der_ref, unit_ref,
    res_ref, gg_ref, all_ref, grad_ref, own_ref, mom_ref, p_ref,
    h, wd, hid, mine, gain, act, der, res, gacc, rows, grad, cot, stage, prod, b0, b1, b2, b3, b4,
    lsem, osem, asem, psem, send, recv, tsend, trecv, usend, urecv,
):
    at = Plane()
    loads = [
        local(s, d, lsem, i)
        for i, (s, d) in enumerate(
            [(cot_ref, mine), (h_ref, h), (wd_ref, wd), (hid_ref, hid), (gain_ref, gain)]
        )
    ]
    moving = Moving(at, C, mine, stage, cot, lsem, 5, tsend, trecv)
    barrier = pltpu.get_barrier_semaphore()
    moving.greet(barrier)
    pl.semaphore_signal(barrier, inc=1, device_id={"fsdp": at.fc}, device_id_type=MESH)
    pl.semaphore_wait(barrier, 2 * (C - 1) + 1)
    R = rows.shape[1]
    n = wd.shape[1]
    z = moving.z
    units = []

    def send_units(k):
        to = partner(z, k)
        c = remote(unit_ref.at[to], mom_ref.at[z], usend, urecv, k, to, "ctx")
        c.start()
        units.append(c)

    send_units(FAR_FIRST[0])
    loads[0].wait()
    moving.first()
    loads[1].wait()
    loads[2].wait()

    def partial(chip, cols):
        return nt(h[pl.ds(pl.multiple_of(chip * 2 * R, 2 * R), 2 * R), :], wd[cols, :])

    def between():
        moving.second()
        for k in FAR_FIRST[1:]:
            send_units(k)
        units.append(local(unit_ref.at[z], mom_ref.at[z], lsem, 10))

    total = scatter_phase(at, partial, (b0, b1, b2, b3, b4), send, recv, 0, between)
    for c in loads[3:]:
        c.wait()
    moving.finish()
    gacc[...] = jnp.zeros_like(gacc)

    def finish(r):
        out = total(r)
        scale = rms(out)
        hat = out * scale
        res[r, :] = (hid[r, :] + hat * gain[...]).astype(bf16)
        g = cot[r, :].astype(f32)
        gacc[...] += jnp.sum(g * hat, axis=0, keepdims=True)
        rows[at.f, r, :] = back(g * gain[...], hat, scale).astype(bf16)

    row_loop(R, finish)
    saves = [local(res, res_ref, lsem, 7), local(gacc, gg_ref, lsem, 8), local(cot, own_ref, lsem, 9)]
    stores = Stores(osem)

    def on_rows(first, count):
        s = stores.slot()
        m = count * R
        start = pl.multiple_of(first * R, R)
        k = len(stores.steps)
        la = local(act_ref.at[pl.ds(start, m)], act.at[s, pl.ds(0, m)], asem, 2 * k)
        ld = local(der_ref.at[pl.ds(start, m)], der.at[s, pl.ds(0, m)], asem, 2 * k + 1)
        la.wait()
        ld.wait()

        width = 512

        @pl.loop(0, n // width)
        def _(t):
            c = pl.ds(pl.multiple_of(t * width, width), width)
            up = pl.ds(pl.multiple_of(n + t * width, width), width)
            gh = nn(rows[pl.ds(first, count)].reshape(m, rows.shape[2]), wd[:, c])
            grad[s, pl.ds(0, m), up] = (gh * act[s, pl.ds(0, m), c].astype(f32)).astype(bf16)
            grad[s, pl.ds(0, m), c] = (gh * der[s, pl.ds(0, m), c].astype(f32)).astype(bf16)

        stores.put(
            [
                (grad.at[s, pl.ds(0, m)], grad_ref.at[pl.ds(start, m)]),
                (rows.at[pl.ds(first, count)], all_ref.at[pl.ds(first, count)]),
            ]
        )

    gather_phase(at, rows, send, recv, SCATTER_COPIES, on_rows)
    F, D = rows.shape[0], rows.shape[2]
    tile, cols = prod.shape[1], p_ref.shape[3]
    puts = []
    for t in range(D // tile):
        if t >= 2:
            for c in puts[t - 2]:
                c.wait()
        rhs = rows[:, :, t * tile : (t + 1) * tile].reshape(F * R, tile)
        prod[t % 2] = lax.dot_general(
            rhs, h[...], (((0,), (0,)), ((), ())), preferred_element_type=f32
        ).astype(bf16)
        puts.append(
            [
                local(
                    prod.at[t % 2, :, pl.ds(b * cols, cols)],
                    p_ref.at[b, 0, pl.ds(t * tile, tile)],
                    psem,
                    t * (n // cols) + b,
                )
                for b in range(n // cols)
            ]
        )
    for step in puts[-2:]:
        for c in step:
            c.wait()
    for k in FAR_FIRST:
        frm = partner(z, k)
        remote(mom_ref.at[frm], mom_ref.at[frm], usend, urecv, k, frm, "ctx").wait_recv()
    for c in units[:-1]:
        c.wait_send()
    units[-1].wait()
    for s in saves:
        s.wait()
    stores.finish()


def down_call(C, F, h, wd, hid, cot, gain, act, der, units):
    R, D = hid.shape
    n = wd.shape[1]
    T = F * R
    copies = SCATTER_COPIES + GATHER_COPIES
    one = jax.ShapeDtypeStruct((R, D), bf16)
    return pl.pallas_call(
        functools.partial(down_kernel, C),
        out_shape=[
            one,
            jax.ShapeDtypeStruct((1, D), f32),
            jax.ShapeDtypeStruct((F, R, D), bf16),
            jax.ShapeDtypeStruct((T, 2 * n), bf16),
            one,
            jax.ShapeDtypeStruct(units.shape, bf16),
            jax.ShapeDtypeStruct((units.shape[1], 1, D, units.shape[3]), bf16),
        ],
        in_specs=[ANY] * 8,
        out_specs=[ANY] * 7,
        scratch_shapes=[
            pltpu.VMEM((T, n), bf16),
            pltpu.VMEM((D, n), bf16),
            pltpu.VMEM((R, D), f32),
            pltpu.VMEM((R, D), bf16),
            pltpu.VMEM((1, D), f32),
            pltpu.VMEM((2, 2 * R, n), bf16),
            pltpu.VMEM((2, 2 * R, n), bf16),
            pltpu.VMEM((R, D), bf16),
            pltpu.VMEM((1, D), f32),
            pltpu.VMEM((F, R, D), bf16),
            pltpu.VMEM((2, 2 * R, 2 * n), bf16),
            pltpu.VMEM((R, D), bf16),
            pltpu.VMEM((C, R // C, D), bf16),
            pltpu.VMEM((2, 512, n), bf16),
        ]
        + scatter_scratch(R, D)
        + [dma(11), dma(15), dma(10), dma(16), dma(copies), dma(copies), dma(2 * C), dma(2 * C), dma(C), dma(C)],
        compiler_params=params(3),
        cost_estimate=cost(115),
    )(h, wd, hid, cot, gain, act, der, units)


def mid_kernel(
    grad_ref, w_ref, cot_ref, ao_ref, gain_ref, wo_ref,
    res_ref, gg_ref, all_ref, gm_ref,
    grad, w, cot, ao, gain, wo, res, gacc, rows, gm, b0, b1, b2, b3, b4,
    lsem, osem, send, recv,
):
    at = Plane()
    e = wo.shape[1]
    pairs = [
        (grad_ref, grad), (w_ref, w),
        (cot_ref, cot), (ao_ref, ao), (gain_ref, gain), (wo_ref.at[:, pl.ds(3 * e, e)], wo),
    ]
    loads = [local(s, d, lsem, i) for i, (s, d) in enumerate(pairs)]
    at.greet()
    R = rows.shape[1]
    for c in loads[:2]:
        c.wait()

    def partial(chip, cols):
        return nt(grad[pl.ds(pl.multiple_of(chip * 2 * R, 2 * R), 2 * R), :], w[cols, :])

    total = scatter_phase(at, partial, (b0, b1, b2, b3, b4), send, recv, 0)
    for c in loads[2:]:
        c.wait()
    gacc[...] = jnp.zeros_like(gacc)

    def finish(r):
        resid = cot[r, :].astype(f32) + total(r)
        res[r, :] = resid
        out = ao[r, :]
        scale = rms(out)
        hat = out * scale
        gacc[...] += jnp.sum(resid * hat, axis=0, keepdims=True)
        rows[at.f, r, :] = back(resid * gain[...], hat, scale).astype(bf16)

    row_loop(R, finish)
    saves = [local(res, res_ref, lsem, 8), local(gacc, gg_ref, lsem, 9)]
    stores = Stores(osem)

    def on_rows(first, count):
        s = stores.slot()
        m = count * R
        start = pl.multiple_of(first * R, R)
        lhs = rows[pl.ds(first, count)].reshape(m, rows.shape[2])
        gm[s, pl.ds(0, m), :] = nn(lhs, wo[...]).astype(bf16)
        stores.put(
            [
                (gm.at[s, pl.ds(0, m)], gm_ref.at[pl.ds(start, m)]),
                (rows.at[pl.ds(first, count)], all_ref.at[pl.ds(first, count)]),
            ]
        )

    gather_phase(at, rows, send, recv, SCATTER_COPIES, on_rows)
    for s in saves:
        s.wait()
    stores.finish()


def mid_call(F, grad, w, cot, ao, gain, wo):
    R, D = cot.shape
    n, e = w.shape[1], wo.shape[1] // 4
    T = F * R
    copies = SCATTER_COPIES + GATHER_COPIES
    return pl.pallas_call(
        mid_kernel,
        out_shape=[
            jax.ShapeDtypeStruct((R, D), f32),
            jax.ShapeDtypeStruct((1, D), f32),
            jax.ShapeDtypeStruct((F, R, D), bf16),
            jax.ShapeDtypeStruct((T, e), bf16),
        ],
        in_specs=[ANY] * 6,
        out_specs=[ANY] * 4,
        scratch_shapes=[
            pltpu.VMEM((T, n), bf16),
            pltpu.VMEM((D, n), bf16),
            pltpu.VMEM((R, D), bf16),
            pltpu.VMEM((R, D), f32),
            pltpu.VMEM((1, D), f32),
            pltpu.VMEM((D, e), bf16),
            pltpu.VMEM((R, D), f32),
            pltpu.VMEM((1, D), f32),
            pltpu.VMEM((F, R, D), bf16),
            pltpu.VMEM((2, 2 * R, e), bf16),
        ]
        + scatter_scratch(R, D)
        + [dma(10), dma(10), dma(copies), dma(copies)],
        compiler_params=params(4),
        cost_estimate=cost(92),
    )(grad, w, cot, ao, gain, wo)


def last_kernel(
    width, q_ref, k_ref, v_ref, proj_ref, st_ref, in_ref, w_ref, res_ref, gain_ref,
    out_ref, gp_ref, gsum_ref,
    q, k, proj, st, ins, gains, gsum, gp, w, res, out, b0, b1, b2, b3, b4,
    lsem, send, recv, ssend, srecv, gsend, grecv,
):
    at = Plane()
    F, T = st.shape[0], st.shape[2]
    e = q.shape[1]
    R = res.shape[0]
    pairs = [
        (in_ref, ins.at[at.f]), (st_ref, st), (q_ref, q), (k_ref, k),
        (v_ref, gp.at[:, pl.ds(2 * e, e)]), (proj_ref.at[:, pl.ds(0, 2 * e)], proj), (w_ref.at[:, pl.ds(0, 3 * e)], w), (res_ref, res),
        (gain_ref, gains.at[at.f]),
    ]
    loads = [local(s, d, lsem, i) for i, (s, d) in enumerate(pairs)]
    barrier = pltpu.get_barrier_semaphore()
    for s in range(1, F):
        pl.semaphore_signal(barrier, inc=1, device_id={"fsdp": (at.f + s) % F}, device_id_type=MESH)
    pl.semaphore_wait(barrier, F - 1)
    loads[0].wait()
    share_stats(at, F, ins, ssend, srecv, 0)
    for c in loads[1:6]:
        c.wait()
    step = 256

    @pl.loop(0, T // step)
    def _(t):
        r = pl.ds(pl.multiple_of(t * step, step), step)
        sums = jnp.sum(st[:, :, r], axis=0)
        inner = jnp.sum(ins[:, :, r], axis=0) / width
        for row, grad in ((0, q), (1, k)):
            scale = lax.rsqrt(column(sums[row : row + 1], HEAD_DIM) / width + epsilon)
            mean = column(inner[row : row + 1], HEAD_DIM)
            for h in range(e // HEAD_DIM):
                hat = proj[r, row * e + h * HEAD_DIM : row * e + (h + 1) * HEAD_DIM] * scale
                got = scale * (grad[r, h * HEAD_DIM : (h + 1) * HEAD_DIM] - hat * mean)
                gp[r, row * e + h * HEAD_DIM : row * e + (h + 1) * HEAD_DIM] = got.astype(bf16)

    save = local(gp, gp_ref, lsem, 9)
    loads[6].wait()

    def partial(chip, cols):
        return nt(gp[pl.ds(pl.multiple_of(chip * 2 * R, 2 * R), 2 * R), :], w[cols, :])

    total = scatter_phase(at, partial, (b0, b1, b2, b3, b4), send, recv, 0)
    loads[7].wait()

    def finish(r):
        out[r, :] = (res[r, :] + total(r)).astype(bf16)

    row_loop(R, finish)
    store = local(out, out_ref, lsem, 10)
    loads[8].wait()
    share_stats(at, F, gains, gsend, grecv, 0)
    gsum[...] = jnp.sum(gains[...], axis=0)
    local(gsum, gsum_ref, lsem, 11).wait()
    store.wait()
    save.wait()


def last_call(F, wq, wk, gv, proj, st, ins, w, res, gains):
    R, D = res.shape
    n = w.shape[1] // 4 * 3
    T, e = F * R, n // 3
    return pl.pallas_call(
        functools.partial(last_kernel, D),
        out_shape=[
            jax.ShapeDtypeStruct((R, D), bf16),
            jax.ShapeDtypeStruct((T, n), bf16),
            jax.ShapeDtypeStruct((8, D), f32),
        ],
        in_specs=[ANY] * 9,
        out_specs=[ANY] * 3,
        scratch_shapes=[
            pltpu.VMEM((T, e), f32),
            pltpu.VMEM((T, e), f32),
            pltpu.VMEM((T, 2 * e), f32),
            pltpu.VMEM((F, 8, T), f32),
            pltpu.VMEM((F, 8, T), f32),
            pltpu.VMEM((F, 8, D), f32),
            pltpu.VMEM((8, D), f32),
            pltpu.VMEM((T, n), bf16),
            pltpu.VMEM((D, n), bf16),
            pltpu.VMEM((R, D), f32),
            pltpu.VMEM((R, D), bf16),
        ]
        + scatter_scratch(R, D)
        + [dma(12), dma(SCATTER_COPIES), dma(SCATTER_COPIES), dma(F), dma(F), dma(F), dma(F)],
        compiler_params=params(5),
        cost_estimate=cost(55),
    )(wq, wk, gv, proj, st, ins, w, res, gains)


def tn(a, b):
    return lax.dot_general(a, b, (((0,), (0,)), ((), ())), preferred_element_type=f32)


def grad_kernel(*refs):
    out = refs[-1]
    start = 0
    for x_ref, dy_ref in zip(refs[:-1:2], refs[1:-1:2]):
        got = tn(x_ref[...], dy_ref[...]).astype(bf16)
        units = dy_ref.shape[1] // out.shape[-1]
        for b in range(units):
            out[(start + b,) + (0,) * (len(out.shape) - 3)] = got[:, b * out.shape[-1] : (b + 1) * out.shape[-1]]
        start += units


def grad_call(pairs, units, cols, groups):
    T, D = pairs[0][0].shape
    tile = 512
    specs, args = [], []
    for x, dy in pairs:
        specs += [
            pl.BlockSpec((T, tile), lambda g, d: (0, d)),
            pl.BlockSpec((T, dy.shape[1] // groups), lambda g, d: (0, g)),
        ]
        args += [x, dy]
    return pl.pallas_call(
        grad_kernel,
        out_shape=jax.ShapeDtypeStruct((units, groups, D, cols), bf16),
        grid=(groups, D // tile),
        in_specs=specs,
        out_specs=pl.BlockSpec((units, 1, tile, cols), lambda g, d: (0, g, d, 0)),
        compiler_params=pltpu.CompilerParams(vmem_limit_bytes=VMEM_LIMIT),
        cost_estimate=cost(12 * groups),
    )(*args)


def share_stats(at, F, st, send, recv, base):
    sent = []
    for k in range(1, F):
        to = (at.f + k) % F
        c = remote(st.at[at.f], st.at[at.f], send, recv, base + k, to)
        c.start()
        sent.append(c)
    for k in range(1, F):
        frm = (at.f - k + F) % F
        remote(st.at[frm], st.at[frm], send, recv, base + k, frm).wait_recv()
    for c in sent:
        c.wait_send()


def row_sums(a, b):
    r = lax.broadcasted_iota(jnp.int32, (8, a.shape[1]), 0)
    one, two = (r == 0).astype(f32), (r == 1).astype(f32)

    def half(sel, v):
        return lax.dot_general(
            sel, v, (((1,), (1,)), ((), ())), preferred_element_type=f32, precision=lax.Precision.HIGHEST
        )

    return half(one, a) + half(two, b)


def column(row, lanes):
    return jnp.broadcast_to(row, (lanes, row.shape[1])).T


def turn(v, cos, sin):
    return v * cos + pltpu.roll(v, HEAD_DIM // 2, 1) * sin


def seq_columns(st, c, chips, R):
    return jnp.concatenate([st[:, pl.ds(pl.multiple_of((2 * j + c) * R, R), R)] for j in range(chips)], axis=1)


def attend_kernel(width, q_ref, k_ref, v_ref, st_ref, gq_ref, gk_ref, cos_ref, sin_ref, pos_ref, posc_ref, mix_ref, qr_ref, kr_ref, lse_ref):
    c = pl.program_id(0)
    chips, R = q_ref.shape[0], q_ref.shape[2]
    L = chips * R
    sums = jnp.sum(seq_columns_all(st_ref, c, chips, R), axis=0)
    cos, sin = cos_ref[0], sin_ref[0]

    def norm_turn(ref, row, gain):
        scale = lax.rsqrt(column(sums[row : row + 1], HEAD_DIM) / width + epsilon)
        return turn(ref[...].reshape(L, HEAD_DIM) * scale * gain[...], cos, sin)

    qr = (norm_turn(q_ref, 0, gq_ref) * HEAD_DIM ** (-0.5)).astype(bf16)
    kr = norm_turn(k_ref, 1, gk_ref).astype(bf16)
    v = v_ref[...].reshape(L, HEAD_DIM).astype(bf16)
    qr_ref[...] = qr.reshape(qr_ref.shape)
    kr_ref[...] = kr.reshape(kr_ref.shape)
    pos = pos_ref[0]
    for t in range(chips):
        rows = slice(t * R, (t + 1) * R)
        s = nt(qr[rows], kr)
        s = jnp.where(posc_ref[0, rows, :1] >= pos, s, -1e30)
        top = jnp.max(s, axis=-1, keepdims=True)
        e = jnp.exp(s - top)
        total = jnp.sum(e, axis=-1, keepdims=True)
        p = (e * (1.0 / total)).astype(bf16)
        mix_ref[t, 0] = nn(p, v).astype(bf16)
        lse_ref[0, 0, rows, :] = jnp.broadcast_to(top + jnp.log(total), (R, HEAD_DIM))


def seq_columns_all(st_ref, c, chips, R):
    return jnp.concatenate(
        [st_ref[:, :, pl.ds(pl.multiple_of((2 * j + c) * R, R), R)] for j in range(chips)], axis=2
    )


def attend_specs(chips, R, heads, F, L):
    def at(offset):
        return pl.BlockSpec((chips, 1, R, HEAD_DIM), lambda c, h: (0, c, 0, offset + h))

    gain = pl.BlockSpec((1, HEAD_DIM), lambda c, h: (0, h))
    table = pl.BlockSpec((1, L, HEAD_DIM), lambda c, h: (c, 0, 0))
    stats = pl.BlockSpec((F, 8, F * R), lambda c, h: (0, 0, 0))
    posr = pl.BlockSpec((1, 1, L), lambda c, h: (c, 0, 0))
    lse = pl.BlockSpec((1, 1, L, HEAD_DIM), lambda c, h: (c, h, 0, 0))
    return at, gain, table, stats, posr, lse


def attend_call(F, proj, st, gq, gk, cos, sin, pos, posc):
    R = proj.shape[0] // F
    e = proj.shape[1] // 3
    heads, chips = e // HEAD_DIM, F // 2
    L = chips * R
    at, gain, table, stats, posr, lse = attend_specs(chips, R, heads, F, L)
    view = proj.reshape(chips, 2, R, 3 * e)
    flat = jax.ShapeDtypeStruct((chips, 2, R, e), bf16)
    out = pl.pallas_call(
        functools.partial(attend_kernel, heads * HEAD_DIM * F),
        out_shape=[flat, flat, flat, jax.ShapeDtypeStruct((2, heads, L, HEAD_DIM), f32)],
        grid=(2, heads),
        in_specs=[at(0), at(heads), at(2 * heads), stats, gain, gain, table, table, posr, table],
        out_specs=[at(0), at(0), at(0), lse],
        compiler_params=pltpu.CompilerParams(vmem_limit_bytes=VMEM_LIMIT),
        cost_estimate=cost(15),
    )(view, view, view, st, gq, gk, cos, sin, pos, posc)
    return out


def attend_back_kernel(
    width, q_ref, k_ref, v_ref, qr_ref, kr_ref, gm_ref, lse_ref, st_ref, gq_ref, gk_ref, cos_ref, sin_ref, pos_ref, posc_ref,
    wq_ref, wk_ref, gv_ref, in_ref, gg_ref, dk, dv, dq,
):
    c = pl.program_id(0)
    chips, R = q_ref.shape[0], q_ref.shape[2]
    L = chips * R
    kr = kr_ref[...].reshape(L, HEAD_DIM)
    v = v_ref[...].reshape(L, HEAD_DIM).astype(bf16)
    pos = pos_ref[0]
    dk[...] = jnp.zeros_like(dk)
    dv[...] = jnp.zeros_like(dv)
    for t in range(chips):
        rows = slice(t * R, (t + 1) * R)
        qt, gm = qr_ref[t, 0], gm_ref[t, 0]
        s = nt(qt, kr)
        s = jnp.where(posc_ref[0, rows, :1] >= pos, s, -1e30)
        p = jnp.exp(s - lse_ref[0, 0, rows, :1])
        dp = nt(gm, v)
        dv[...] += lax.dot_general(p.astype(bf16), gm, (((0,), (0,)), ((), ())), preferred_element_type=f32)
        inner = jnp.sum(dp * p, axis=-1, keepdims=True)
        ds = (p * (dp - inner)).astype(bf16)
        dq[rows, :] = nn(ds, kr)
        dk[...] += lax.dot_general(ds, qt, (((0,), (0,)), ((), ())), preferred_element_type=f32)
    gv_ref[...] = dv[...].astype(bf16).reshape(gv_ref.shape)
    sums = jnp.sum(seq_columns_all(st_ref, c, chips, R), axis=0)
    cos, sin = cos_ref[0], sin_ref[0]

    def finish(grad, ref, row, gain, out):
        norm = turn(grad, cos, -sin)
        hat = ref[...].reshape(L, HEAD_DIM) * lax.rsqrt(column(sums[row : row + 1], HEAD_DIM) / width + epsilon)
        gg_ref[0, 0, row : row + 1, :] = jnp.sum(norm * hat, axis=0, keepdims=True)
        weighted = norm * gain[...]
        out[...] = weighted.reshape(out.shape)
        return weighted * hat

    gg_ref[...] = jnp.zeros_like(gg_ref)
    in_ref[0, 0] = row_sums(
        finish(dq[...] * HEAD_DIM ** (-0.5), q_ref, 0, gq_ref, wq_ref), finish(dk[...], k_ref, 1, gk_ref, wk_ref)
    )


def attend_back_call(F, proj, qr, kr, gm, lse_in, st, gq, gk, cos, sin, pos, posc):
    R = proj.shape[0] // F
    e = proj.shape[1] // 3
    heads, chips = e // HEAD_DIM, F // 2
    L = chips * R
    at, gain, table, stats, posr, lse = attend_specs(chips, R, heads, F, L)
    view = proj.reshape(chips, 2, R, 3 * e)
    flat = (chips, 2, R, e)
    small = pl.BlockSpec((1, 1, 8, L), lambda c, h: (c, h, 0, 0))
    tiny = pl.BlockSpec((1, 1, 8, HEAD_DIM), lambda c, h: (c, h, 0, 0))
    wide = jax.ShapeDtypeStruct(flat, f32)
    return pl.pallas_call(
        functools.partial(attend_back_kernel, heads * HEAD_DIM * F),
        out_shape=[
            wide, wide, jax.ShapeDtypeStruct(flat, bf16),
            jax.ShapeDtypeStruct((2, heads, 8, L), f32),
            jax.ShapeDtypeStruct((2, heads, 8, HEAD_DIM), f32),
        ],
        grid=(2, heads),
        in_specs=[
            at(0), at(heads), at(2 * heads), at(0), at(0), at(0), lse, stats, gain, gain, table, table, posr, table,
        ],
        out_specs=[at(0), at(0), at(0), small, tiny],
        scratch_shapes=[pltpu.VMEM((L, HEAD_DIM), f32)] * 3,
        compiler_params=pltpu.CompilerParams(vmem_limit_bytes=VMEM_LIMIT),
        cost_estimate=cost(35),
    )(view, view, view, qr, kr, gm.reshape(flat), lse_in, st, gq, gk, cos, sin, pos, posc)


def newton_kernel(
    C, m_ref, rows_ref, gain_ref, out_ref, stage_ref, gsum_ref,
    v, gram, y, yf, stat, gains, gsum,
    lsem, osem, vsend, vrecv, ysend, yrecv, ssend, srecv, tsend, trecv, gsend, grecv, usend, urecv, usem,
):
    me = lax.axis_index("fsdp")
    z = lax.axis_index("ctx")
    core, chip = me % 2, me // 2
    peer = me + 1 - 2 * core
    F = 2 * C
    cols = m_ref.shape[2]
    gload = local(gain_ref, gains.at[z], lsem, 1)
    barrier = pltpu.get_barrier_semaphore()
    for k in range(1, C):
        pl.semaphore_signal(barrier, inc=1, device_id={"ctx": (z + k) % C}, device_id_type=MESH)
    for k in range(1, F):
        pl.semaphore_signal(barrier, inc=1, device_id={"fsdp": (me + k) % F}, device_id_type=MESH)
    pl.semaphore_wait(barrier, C + F - 2)
    rows_in = v.shape[1] // C
    units_sent, units_kept = [], []
    for k in range(F):
        to = (me + k) % F
        for b in range(C):
            src = m_ref.at[to // 2, pl.ds((2 * b + to % 2) * rows_in, rows_in)]
            dst = v.at[0, pl.ds(b * rows_in, rows_in), pl.ds(me * cols, cols)]
            if k == 0:
                units_kept.append(local(src, dst, usem, b))
            else:
                c = remote(src, dst, usend, urecv, k * C + b, to)
                c.start()
                units_sent.append(c)
    piece = rows_ref.shape[1] // C

    def part(j):
        return pl.ds(j * piece, piece)

    sent, keep = [], []
    for a in range(2):
        for k in FAR_FIRST:
            to = partner(z, k)
            c = remote(rows_ref.at[a, part(to)], stage_ref.at[a, z], tsend, trecv, C * a + k, to, "ctx")
            c.start()
            sent.append(c)
        keep.append(local(rows_ref.at[a, part(z)], stage_ref.at[a, z], lsem, 2 + a))
    gload.wait()
    for k in range(1, C):
        c = remote(gains.at[z], gains.at[z], gsend, grecv, k, (z + k) % C, "ctx")
        c.start()
        sent.append(c)

    def rows_arrived():
        for a in range(2):
            keep[a].wait()
            for k in FAR_FIRST:
                dst = stage_ref.at[a, partner(z, k)]
                remote(dst, dst, tsend, trecv, C * a + k, partner(z, k), "ctx").wait_recv()
        for k in range(1, C):
            frm = (z - k + C) % C
            remote(gains.at[frm], gains.at[frm], gsend, grecv, k, frm, "ctx").wait_recv()
        gsum[...] = jnp.sum(gains[...], axis=0)
        local(gsum, gsum_ref, lsem, 6).wait()
        for c in sent:
            c.wait_send()

    for k in range(1, F):
        frm = (me - k + F) % F
        for b in range(C):
            dst = v.at[0, pl.ds(b * rows_in, rows_in), pl.ds(frm * cols, cols)]
            remote(dst, dst, usend, urecv, k * C + b, frm).wait_recv()
    for c in units_sent:
        c.wait_send()
    for c in units_kept:
        c.wait()
    M, D = v.shape[1], v.shape[2]
    tile, col = 512, 1024
    tiles = M // tile

    def block(i):
        return pl.ds(i * tile, tile)

    def swap(buf, i, sends, recvs):
        return remote(buf.at[0, block(i)], buf.at[1, block(i)], sends, recvs, i, peer)

    pending = [swap(v, i, vsend, vrecv) for i in range(tiles)]
    for c in pending:
        c.start()
    stat[0] = jnp.zeros_like(stat[0])

    def add(r):
        part = v[0, r, :].astype(f32)
        stat[0] += jnp.sum((part * part).reshape(-1, 8, D // 128, 128), axis=(0, 2))

    row_loop(M, add)
    share = remote(stat.at[0], stat.at[1], ssend, srecv, 0, peer)
    share.start()
    share.wait()
    inv = 1.0 / (jnp.sqrt(jnp.sum(stat[0] + stat[1])) + 1e-07)

    for iteration in range(NS_STEPS):
        factor = inv if iteration == 0 else 1.0

        def grams(h, n):
            rhs = pl.ds(pl.multiple_of(n * col, col), col)
            cols = pl.ds(pl.multiple_of(h * M + n * col, col), col)

            @pl.loop(0, tiles)
            def _(i):
                rows = pl.ds(pl.multiple_of(i * tile, tile), tile)
                got = nt(v[0, rows, :], v[h, rhs, :])
                if iteration == 0:
                    got = got * (factor * factor)
                gram[rows, cols] = got.astype(bf16)

        @pl.loop(0, M // col)
        def _(n):
            grams(0, n)

        for c in pending:
            c.wait()

        @pl.loop(0, M // col)
        def _(n):
            grams(1, n)

        def times(src, i, n):
            rows = block(i)
            cols = pl.ds(pl.multiple_of(n * col, col), col)
            return cols, nn(gram[rows, :M], src[0, :, cols]) + nn(gram[rows, M:], src[1, :, cols])

        pending = []
        for i in range(tiles):

            @pl.loop(0, D // col)
            def _(n):
                cols, got = times(v, i, n)
                if iteration == 0:
                    got = got * factor
                yf[block(i), cols] = got
                y[0, block(i), cols] = got.astype(bf16)

            c = swap(y, i, ysend, yrecv)
            c.start()
            pending.append(c)
        for c in pending:
            c.wait()
        pending = []
        for i in range(tiles):

            @pl.loop(0, D // col)
            def _(n):
                cols, got = times(y, i, n)
                old = v[0, block(i), cols].astype(f32)
                if iteration == 0:
                    old = old * factor
                v[0, block(i), cols] = (
                    quintic_one * old + quintic_two * yf[block(i), cols] + quintic_three * got
                ).astype(bf16)

            if iteration < NS_STEPS - 1:
                c = swap(v, i, vsend, vrecv)
            else:
                c = pltpu.make_async_copy(v.at[0, block(i)], out_ref.at[block(i)], osem.at[i])
            c.start()
            pending.append(c)
    rows_arrived()
    for c in pending:
        c.wait()


def newton_call(C, x, rows, gains):
    _, D, cols = x.shape
    M = D // 2
    _, R, _ = rows.shape
    n = M // 512
    return pl.pallas_call(
        functools.partial(newton_kernel, C),
        out_shape=[
            jax.ShapeDtypeStruct((M, D), bf16),
            jax.ShapeDtypeStruct((2, C, R // C, D), bf16),
            jax.ShapeDtypeStruct((8, D), f32),
        ],
        in_specs=[ANY] * 3,
        out_specs=[ANY] * 3,
        scratch_shapes=[
            pltpu.VMEM((2, M, D), bf16),
            pltpu.VMEM((M, 2 * M), bf16),
            pltpu.VMEM((2, M, D), bf16),
            pltpu.VMEM((M, D), f32),
            pltpu.VMEM((2, 8, 128), f32),
            pltpu.VMEM((C, 8, D), f32),
            pltpu.VMEM((8, D), f32),
            dma(7), dma(n), dma(n), dma(n), dma(n), dma(n), dma(1), dma(1),
            dma(2 * C), dma(2 * C), dma(C), dma(C), dma(2 * C * C), dma(2 * C * C), dma(C),
        ],
        compiler_params=params(6),
        cost_estimate=cost(95),
    )(x, rows, gains)


def project(C, F, x, w):
    own = to_layer(C, F, x)
    rows = token_rows(own)
    return own, rows, dot(rows, w, 1, 0)


def attn_out_and_up(C, F, mixed, wo, x, gain, w):
    if kernels_fit(C, F):
        hidden_in, out, inp = out_call(F, mixed, wo, x, gain)
        return (hidden_in, out, *up_call(F, inp, w))
    out = token_sums(dot(mixed, wo, 1, 1))
    hidden_in = x.astype(f32) + out * rms(out) * gain
    rows = token_rows(hidden_in.astype(bf16))
    g, u = jnp.split(dot(rows, w, 1, 0), 2, axis=1)
    sig = jax.nn.sigmoid(g)
    der = u * (sig * (1.0 + g * (1.0 - sig)))
    act = g * sig
    return hidden_in, out, rows, act.astype(bf16), der.astype(bf16), (act * u).astype(bf16)


def down_and_back(C, F, h, wd, hidden_in, cot, gain, act, der, units):
    if kernels_fit(C, F):
        return down_call(C, F, h, wd, hidden_in, cot, gain, act, der, units)
    cot = to_layer(C, F, cot)
    out = token_sums(dot(h, wd, 1, 1))
    scale = rms(out)
    hat = out * scale
    g = cot.astype(f32)
    rows = token_rows(back(g * gain, hat, scale).astype(bf16))
    gh = dot(rows, wd, 1, 0)
    return (
        (hidden_in + hat * gain).astype(bf16),
        jnp.sum(g * hat, axis=0, keepdims=True),
        rows,
        jnp.concatenate([(gh * der.astype(f32)).astype(bf16), (gh * act.astype(f32)).astype(bf16)], axis=1),
        cot,
        None,
        None,
    )


def back_to_attn(C, F, grad, w, cot, out, gain, wo):
    if kernels_fit(C, F):
        return mid_call(F, grad, w, cot, out, gain, wo)
    resid = cot.astype(f32) + token_sums(dot(grad, w, 1, 1))
    scale = rms(out)
    hat = out * scale
    rows = token_rows(back(resid * gain, hat, scale).astype(bf16))
    return resid, jnp.sum(resid * hat, axis=0, keepdims=True), rows, dot(rows, wo, 1, 0).astype(bf16)


def back_to_input(C, F, grad_projected, w, resid):
    return (resid + token_sums(dot(grad_projected, w, 1, 1))).astype(bf16)


def kernels_fit(C, F):
    return C == 4 and F == 8 and UNITS_ATTN * 4 * 2 == C * F


def to_layer(C, F, x):
    z, chip = lax.axis_index("ctx"), lax.axis_index("fsdp") // 2
    x = x.reshape(C, x.shape[0] // C, x.shape[1])
    got = []
    for k in range(C):
        pairs = [
            (s * F + f, (f // 2) * F + 2 * ((s + k) % C) + f % 2) for s in range(C) for f in range(F)
        ]
        block = lax.dynamic_index_in_dim(x, (z + k) % C, 0, keepdims=False)
        got.append(lax.ppermute(block, BOTH, pairs))
    got = jnp.stack(got)
    got = [lax.dynamic_index_in_dim(got, (chip - s + C) % C, 0, keepdims=False) for s in range(C)]
    return jnp.concatenate(got, axis=0)


def go_home(C, F, stage):
    chip = lax.axis_index("fsdp") // 2
    got = [lax.dynamic_index_in_dim(stage, chip, 1, keepdims=False)]
    for k in range(1, C):
        pairs = [(f, 2 * ((f // 2 + k) % C) + f % 2) for f in range(F)]
        block = lax.dynamic_index_in_dim(stage, (chip + k) % C, 1, keepdims=False)
        got.append(lax.ppermute(block, "fsdp", pairs))
    return got


def at_home(C, got):
    chip = lax.axis_index("fsdp") // 2
    got = jnp.stack(got)
    got = [lax.dynamic_index_in_dim(got, (chip - j + C) % C, 0, keepdims=False) for j in range(C)]
    return jnp.concatenate(got, axis=1)


def from_layer(C, F, x):
    z, chip = lax.axis_index("ctx"), lax.axis_index("fsdp") // 2
    x = x.reshape(C, x.shape[0] // C, x.shape[1])
    got = []
    for k in range(C):
        pairs = [
            ((f // 2) * F + 2 * ((s + k) % C) + f % 2, s * F + f) for s in range(C) for f in range(F)
        ]
        block = lax.dynamic_index_in_dim(x, (chip - k + C) % C, 0, keepdims=False)
        got.append(lax.ppermute(block, BOTH, pairs))
    got = jnp.stack(got)
    got = [lax.dynamic_index_in_dim(got, (j - z + C) % C, 0, keepdims=False) for j in range(C)]
    return jnp.concatenate(got, axis=0)


def shards(C, F, layer_input, cotangent, positions, w_attn, w_ffn, gains, mom_attn, mom_ffn, gain_mom):
    z = lax.axis_index("ctx")
    f = lax.axis_index("fsdp")
    local_rows, width = layer_input.shape[1], layer_input.shape[2]
    seq_total, seq_length = positions.shape
    dz, head_cols = w_attn.shape[1], w_attn.shape[2]
    local_heads = head_cols // HEAD_DIM
    block_count = w_ffn.shape[2]
    per = seq_total // C
    piece = local_rows // C
    chips = F // per
    tokens = F * local_rows
    hidden_cols = block_count * head_cols
    units = UNITS_ATTN + 3 * block_count
    parts = C * F // units

    def after(a, b):
        return lax.optimization_barrier((a, b))[0]

    def rows_gather(shard):
        return lax.all_gather(shard, "ctx", axis=0, tiled=True)

    def product(units, groups, *pairs):
        pairs = [(x.reshape(tokens, width), dy) for x, dy in pairs]
        if kernels:
            return grad_call(pairs, units, head_cols, groups)
        grad = jnp.concatenate([dot(x, dy, 0, 0).astype(bf16) for x, dy in pairs], axis=1)
        return jnp.transpose(grad.reshape(width, groups, units, head_cols), (2, 1, 0, 3))

    def scatter(grad):
        if kernels:
            return lax.psum_scatter(grad, "ctx", scatter_dimension=0, tiled=True)[0]
        return lax.psum_scatter(grad, "ctx", scatter_dimension=2, tiled=True)

    kernels = kernels_fit(C, F)
    w_heads = rows_gather(jnp.concatenate([w_attn[i] for i in range(UNITS_ATTN)], axis=1))
    w_qkv, w_out = (w_heads, w_heads) if kernels else (w_heads[:, : 3 * head_cols], w_heads[:, 3 * head_cols :])
    ffn_flat = w_ffn.reshape(3, dz, hidden_cols)
    w_gate_up = rows_gather(jnp.concatenate([ffn_flat[0], ffn_flat[1]], axis=1))
    w_down = rows_gather(ffn_flat[2])

    gain_query = lax.dynamic_slice_in_dim(gains[0], f * head_cols, head_cols)
    gain_key = lax.dynamic_slice_in_dim(gains[1], f * head_cols, head_cols)
    pos = lax.dynamic_slice_in_dim(positions, z * per, per, 0)
    pos = jnp.transpose(pos.reshape(per, C, chips, piece), (0, 2, 1, 3)).reshape(per, seq_length)
    cosine_table, sine_table = rotary_tables(pos)

    def heads(a):
        return jnp.transpose(
            a.reshape(chips, per, local_rows, local_heads, HEAD_DIM), (1, 0, 2, 3, 4)
        ).reshape(per, seq_length, local_heads, HEAD_DIM)

    def unheads(a):
        return jnp.transpose(
            a.reshape(per, chips, local_rows, local_heads, HEAD_DIM), (1, 0, 2, 3, 4)
        ).reshape(tokens, head_cols)

    if kernels:
        sign = jnp.where(jnp.arange(HEAD_DIM) < HEAD_DIM // 2, -1.0, 1.0)
        tables = (
            gain_query[None],
            gain_key[None],
            jnp.broadcast_to(cosine_table[:, :, 0], (per, seq_length, HEAD_DIM)),
            sine_table[:, :, 0] * sign,
            pos.astype(f32)[:, None, :],
            jnp.broadcast_to(pos.astype(f32)[..., None], (per, seq_length, HEAD_DIM)),
        )
        own_input, input_all = enter_call(C, F, layer_input.reshape(local_rows, width))
        projected, stats = qkv_call(F, input_all, w_qkv)
        attn_mixed, query_rows, key_rows, log_total = attend_call(F, projected, stats, *tables)
        attn_mixed = attn_mixed.reshape(tokens, head_cols)
    else:
        own_input, input_all, projected = project(C, F, layer_input.reshape(local_rows, width), w_qkv)
        query_raw = projected[:, :head_cols]
        key_raw = projected[:, head_cols : 2 * head_cols]
        value_raw = projected[:, 2 * head_cols :]
        query_total, key_total = norm_stats(
            jnp.sum(query_raw * query_raw, axis=-1), jnp.sum(key_raw * key_raw, axis=-1)
        )
        query_scale = lax.rsqrt(query_total / width + epsilon)[..., None]
        key_scale = lax.rsqrt(key_total / width + epsilon)[..., None]
        query_hat = query_raw * query_scale
        key_hat = key_raw * key_scale
        query_rows = (
            rotate(heads(query_hat * gain_query), cosine_table, sine_table) * HEAD_DIM ** (-0.5)
        ).astype(bf16)
        key_rows = rotate(heads(key_hat * gain_key), cosine_table, sine_table).astype(bf16)
        value_rows = heads(value_raw.astype(bf16))
        attn_mixed, log_total = attend(query_rows, key_rows, value_rows, pos)
        attn_mixed = unheads(attn_mixed)
    hidden_in, attn_out, mlp_all, act, der, hidden = attn_out_and_up(
        C, F, attn_mixed, w_out, own_input, gains[2:3], w_gate_up
    )
    by_layer = None
    if kernels:
        by_layer = jnp.concatenate(
            [mom_attn[:, None].astype(bf16), jnp.transpose(mom_ffn.astype(bf16), (2, 0, 1, 3))], axis=1
        )
    result, mlp_gain, grad_mlp_all, grad_ffn_in, own_grad, mom_own, p_down = down_and_back(
        C, F, hidden, w_down, hidden_in, cotangent.reshape(local_rows, width), gains[3:4], act, der, by_layer
    )
    if kernels:
        mom_own = jnp.swapaxes(mom_own, 0, 1)
    else:
        p_down = product(block_count, 1, (grad_mlp_all, hidden))
    g_down = scatter(p_down)
    p_gate_up = product(block_count, 2, (mlp_all, grad_ffn_in))
    if kernels:
        grad_ffn_in, p_gate_up = lax.optimization_barrier((grad_ffn_in, p_gate_up))
    g_gate_up = scatter(p_gate_up)
    grad_resid, attn_gain, grad_attn_all, grad_mixed = back_to_attn(
        C, F, grad_ffn_in, w_gate_up, own_grad, attn_out, gains[2:3], w_out
    )
    if kernels:
        grad_mixed = after(grad_mixed, g_down)
        weighted_q, weighted_k, grad_value, inner, gain_cols = attend_back_call(
            F, projected, query_rows, key_rows, grad_mixed, log_total, stats, *tables
        )
        inner = jnp.transpose(
            jnp.sum(inner, axis=1).reshape(per, 8, chips, local_rows), (1, 2, 0, 3)
        ).reshape(8, tokens)
        gain_cols = jnp.sum(gain_cols, axis=0)
        query_gain_cols = gain_cols[:, 0].reshape(head_cols)
        key_gain_cols = gain_cols[:, 1].reshape(head_cols)
        flat = (tokens, head_cols)
        zero = jnp.zeros((width,), f32)
        gain_local = jnp.stack(
            [
                lax.dynamic_update_slice(zero, query_gain_cols, (f * head_cols,)),
                lax.dynamic_update_slice(zero, key_gain_cols, (f * head_cols,)),
                attn_gain[0],
                mlp_gain[0],
                *[zero] * 4,
            ]
        )
        grad_rows, grad_projected, gain_layer = last_call(
            F, weighted_q.reshape(flat), weighted_k.reshape(flat), grad_value.reshape(flat),
            projected, stats, inner, w_qkv, grad_resid, gain_local,
        )
    else:
        grad_query, grad_key, grad_value = attend_back(
            query_rows, key_rows, value_rows, pos, heads(grad_mixed), log_total
        )
        grad_query_norm = unheads(unrotate(grad_query * HEAD_DIM ** (-0.5), cosine_table, sine_table))
        grad_key_norm = unheads(unrotate(grad_key, cosine_table, sine_table))
        query_gain_cols = jnp.sum(grad_query_norm * query_hat, axis=0)
        key_gain_cols = jnp.sum(grad_key_norm * key_hat, axis=0)
        query_weighted = grad_query_norm * gain_query
        key_weighted = grad_key_norm * gain_key
        query_inner, key_inner = norm_stats(
            jnp.sum(query_weighted * query_hat, axis=-1), jnp.sum(key_weighted * key_hat, axis=-1)
        )
        grad_query_raw = query_scale * (query_weighted - query_hat * (query_inner / width)[..., None])
        grad_key_raw = key_scale * (key_weighted - key_hat * (key_inner / width)[..., None])
        grad_projected = jnp.concatenate(
            [grad_query_raw.astype(bf16), grad_key_raw.astype(bf16), unheads(grad_value).astype(bf16)],
            axis=1,
        )
        grad_rows = back_to_input(C, F, grad_projected, w_qkv, grad_resid)
    g_attn = scatter(
        product(UNITS_ATTN, 1, (input_all, grad_projected), (grad_attn_all, attn_mixed))
    )
    if not kernels:
        grad_input = from_layer(C, F, grad_rows)
        result = from_layer(C, F, result)
        zero = jnp.zeros((width,), f32)
        gain_local = jnp.stack(
            [
                lax.dynamic_update_slice(zero, query_gain_cols, (f * head_cols,)),
                lax.dynamic_update_slice(zero, key_gain_cols, (f * head_cols,)),
                attn_gain[0],
                mlp_gain[0],
            ]
        )
        gain_total = jnp.sum(lax.all_gather(gain_local, BOTH, axis=0, tiled=False), axis=0)

    if kernels:
        early = jnp.stack([jnp.zeros_like(g_down[0]), g_gate_up[0], g_gate_up[1], g_down[0]])
        mom = momentum * mom_own.reshape(early.shape).astype(f32)
        owned = (mom + early.astype(f32)).astype(bf16)
        mom_first = mom[0]
        early = jnp.swapaxes(early.reshape(UNITS_ATTN, C, dz, head_cols), 0, 1)
        early, owned, mom_first, grad_rows = lax.optimization_barrier((early, owned, mom_first, grad_rows))
        late = (mom_first + g_attn[0].astype(f32)).astype(bf16)
        owned = lax.dynamic_update_slice(owned, late[None], (0, 0, 0))
        got = lax.dynamic_update_slice(early, g_attn.reshape(C, 1, dz, head_cols), (0, 0, 0, 0))
        sent_back = lax.all_to_all(got, "ctx", split_axis=0, concat_axis=0, tiled=True).astype(f32)
        grad_attn = sent_back[:, 0]
        grad_ffn = jnp.transpose(sent_back[:, 1:], (1, 2, 0, 3))
        own, leaving, gain_total = newton_call(C, owned, jnp.stack([result, grad_rows]), gain_layer)
        homing = go_home(C, F, leaving)
        gain_total = gain_total[:4]
    else:
        grad_attn = g_attn[:, 0].astype(f32)
        grad_ffn = jnp.transpose(
            jnp.concatenate([g_gate_up, g_down], axis=1).astype(f32), (1, 2, 0, 3)
        )
    new_attn = momentum * mom_attn + grad_attn
    new_ffn = momentum * mom_ffn + grad_ffn
    if kernels:
        homing, new_attn, new_ffn, grad_attn, grad_ffn = lax.optimization_barrier(
            (homing, new_attn, new_ffn, grad_attn, grad_ffn)
        )
        back_rows = at_home(C, homing)
        result, grad_input = back_rows[0], back_rows[1]
    if not kernels:
        send = jnp.concatenate(
            [
                new_attn.astype(bf16),
                jnp.transpose(new_ffn.astype(bf16), (0, 2, 1, 3)).reshape(3 * block_count, dz, head_cols),
            ],
            axis=0,
        ).reshape(C * F, dz // parts, head_cols)
        own = lax.all_to_all(send, BOTH, split_axis=0, concat_axis=0, tiled=True)
        own = jnp.transpose(own.reshape(C, F, dz // parts, head_cols), (0, 2, 1, 3)).reshape(
            C * dz // parts, F * head_cols
        )

        def peers(a):
            out = [a]
            for s in range(1, parts):
                pairs = [(i, i - i % parts + (i + parts - s) % parts) for i in range(C * F)]
                out.append(lax.ppermute(a, BOTH, pairs))
            return out

        own32 = own.astype(f32)
        square = jnp.sum(own32 * own32)
        total = sum(peers(square.reshape(1, 1)))
        inv = 1.0 / (jnp.sqrt(total) + 1e-07)
        for iteration in range(NS_STEPS):
            factor = inv if iteration == 0 else 1.0
            every = peers(own)
            gram = [(dot(own, b, 1, 1) * (factor * factor)).astype(bf16) for b in every]
            product = sum(dot(g, b, 1, 0) for g, b in zip(gram, every)) * factor
            product_all = peers(product.astype(bf16))
            product_two = sum(dot(g, b, 1, 0) for g, b in zip(gram, product_all))
            own = (
                quintic_one * factor * own.astype(f32) + quintic_two * product + quintic_three * product_two
            ).astype(bf16)
    home = jnp.transpose(own.reshape(C, dz // parts, F, head_cols), (0, 2, 1, 3)).reshape(
        C * F, dz // parts, head_cols
    )
    steps = lax.all_to_all(home, BOTH, split_axis=0, concat_axis=0, tiled=True)
    steps = -muon_rate * steps.astype(f32)
    if kernels:
        steps = steps.reshape(C, UNITS_ATTN, dz, head_cols)
        step_attn = steps[:, 0]
        step_ffn = jnp.transpose(steps[:, 1:], (1, 2, 0, 3))
    else:
        steps = steps.reshape(units, dz, head_cols)
        step_attn = steps[:UNITS_ATTN]
        step_ffn = jnp.transpose(
            steps[UNITS_ATTN:].reshape(3, block_count, dz, head_cols), (0, 2, 1, 3)
        )
    new_gain_mom = momentum * gain_mom + gain_total
    return (
        result.reshape(layer_input.shape),
        grad_input.astype(f32).reshape(layer_input.shape),
        grad_attn,
        grad_ffn,
        gain_total,
        new_attn,
        new_ffn,
        new_gain_mom,
        step_attn,
        step_ffn,
        -gain_rate * new_gain_mom,
    )


def solution(mesh):
    tokens = P("fsdp", "ctx", None)
    attn = P(None, "ctx", "fsdp")
    ffn = P(None, "ctx", None, "fsdp")
    in_specs = (tokens, tokens, P(), attn, ffn, P(), attn, ffn, P())
    out_specs = (tokens, tokens, attn, ffn, P(), attn, ffn, P(), attn, ffn, P())
    body = functools.partial(shards, mesh.shape["ctx"], mesh.shape["fsdp"])
    return jax.shard_map(body, mesh=mesh, in_specs=in_specs, out_specs=out_specs, check_vma=False)
```

```python
import functools
import jax
import jax.numpy as jnp
from jax import lax
from jax.experimental import pallas as pl
from jax.experimental.pallas import tpu as pltpu
from jax.sharding import PartitionSpec as P

NS_STEPS = 3
HEAD_DIM = 128
UNITS_ATTN = 4

epsilon = 1e-06
rope_theta = 500000.0
quintic_one = 3.4445
quintic_two = -4.775
quintic_three = 2.0315
momentum = 0.95
muon_rate = 1.0
gain_rate = 0.0005
BOTH = ("ctx", "fsdp")
bf16 = jnp.bfloat16
f32 = jnp.float32


def dot(a, b, ca, cb):
    return lax.dot_general(a, b, (((ca,), (cb,)), ((), ())), preferred_element_type=f32)


def token_rows(operand):
    return lax.all_gather(operand, "fsdp", axis=0, tiled=True)


def token_sums(operand):
    return lax.psum_scatter(operand.astype(bf16), "fsdp", scatter_dimension=0, tiled=True).astype(f32)


def norm_stats(first_sum, second_sum):
    got = lax.all_gather(jnp.stack([first_sum, second_sum]), "fsdp", axis=0, tiled=False)
    total = jnp.sum(got, axis=0)
    return total[0], total[1]


def rms_back(upstream, normed, inv_scale):
    return inv_scale * (upstream - normed * jnp.mean(upstream * normed, axis=-1, keepdims=True))


def rotary_tables(slot_order):
    half_dim = HEAD_DIM // 2
    inverse = rope_theta ** (-(jnp.arange(half_dim, dtype=f32) * 2.0) / HEAD_DIM)
    angles = slot_order.astype(f32)[..., None] * inverse
    angles = jnp.concatenate([angles, angles], axis=-1)
    return (jnp.cos(angles)[..., None, :], jnp.sin(angles)[..., None, :])


def rotate(operand, cosine_table, sine_table):
    half_dim = operand.shape[-1] // 2
    flipped = jnp.concatenate([-operand[..., half_dim:], operand[..., :half_dim]], axis=-1)
    return operand * cosine_table + flipped * sine_table


def unrotate(upstream, cosine_table, sine_table):
    half_dim = upstream.shape[-1] // 2
    shifted = upstream * sine_table
    flipped = jnp.concatenate([shifted[..., half_dim:], -shifted[..., :half_dim]], axis=-1)
    return upstream * cosine_table + flipped


def masked_scores(query_rows, key_rows, pos):
    scores = jnp.einsum("gqhe,gkhe->ghqk", query_rows, key_rows, preferred_element_type=f32)
    causal = pos[:, None, :, None] >= pos[:, None, None, :]
    return jnp.where(causal, scores, -1e30)


def attend(query_rows, key_rows, value_rows, pos):
    scores = masked_scores(query_rows, key_rows, pos)
    row_max = jnp.max(scores, axis=-1, keepdims=True)
    weights = jnp.exp(scores - row_max)
    row_total = jnp.sum(weights, axis=-1, keepdims=True)
    probabilities = (weights / row_total).astype(bf16)
    attn_mixed = jnp.einsum("ghqk,gkhe->gqhe", probabilities, value_rows, preferred_element_type=f32)
    return attn_mixed.astype(bf16), row_max + jnp.log(row_total)


def attend_back(query_rows, key_rows, value_rows, pos, grad_mixed, log_total):
    scores = masked_scores(query_rows, key_rows, pos)
    probabilities = jnp.exp(scores - log_total)
    grad_probs = jnp.einsum("gqhe,gkhe->ghqk", grad_mixed, value_rows, preferred_element_type=f32)
    grad_value = jnp.einsum(
        "ghqk,gqhe->gkhe", probabilities.astype(bf16), grad_mixed, preferred_element_type=f32
    )
    inner_sum = jnp.sum(grad_probs * probabilities, axis=-1, keepdims=True)
    grad_scores = (probabilities * (grad_probs - inner_sum)).astype(bf16)
    grad_query = jnp.einsum("ghqk,gkhe->gqhe", grad_scores, key_rows, preferred_element_type=f32)
    grad_key = jnp.einsum("ghqk,gqhe->gkhe", grad_scores, query_rows, preferred_element_type=f32)
    return grad_query, grad_key, grad_value


MESH = pl.DeviceIdType.MESH
VMEM_LIMIT = 60 * 1024 * 1024
ANY = pl.BlockSpec(memory_space=pl.ANY)


class Plane:
    def __init__(self):
        f = lax.axis_index("fsdp")
        self.f, self.c, self.chip = f, f % 2, f // 2
        x, y = self.chip % 2, self.chip // 2
        self.qx = self.chip + 1 - 2 * x
        self.qy = self.chip + 2 - 4 * y
        self.qd = self.qx + 2 - 4 * y
        self.fc = f + 1 - 2 * self.c
        self.fx = 2 * self.qx + self.c
        self.fy = 2 * self.qy + self.c
        self.fd = 2 * self.qd + self.c
        self.other = 1 - self.c

    def greet(self):
        barrier = pltpu.get_barrier_semaphore()
        for to in (self.fc, self.fx, self.fy):
            pl.semaphore_signal(barrier, inc=1, device_id={"fsdp": to}, device_id_type=MESH)
        pl.semaphore_wait(barrier, 3)


def partner(i, k):
    if k == 3:
        return 3 - i
    if k == 2:
        return (i + 2) % 4
    return i + 1 - 2 * (i % 2)


FAR_FIRST = (3, 2, 1)


def remote(src, dst, send, recv, i, to, axis="fsdp"):
    return pltpu.make_async_remote_copy(
        src_ref=src, dst_ref=dst, send_sem=send.at[i], recv_sem=recv.at[i],
        device_id={axis: to}, device_id_type=MESH,
    )


def local(src, dst, sems, i):
    copy = pltpu.make_async_copy(src, dst, sems.at[i])
    copy.start()
    return copy


def nn(a, b):
    return lax.dot_general(a, b, (((1,), (0,)), ((), ())), preferred_element_type=f32)


def nt(a, b):
    return lax.dot_general(a, b, (((1,), (1,)), ((), ())), preferred_element_type=f32)


def gather_phase(at, rows, send, recv, base, on_rows):
    half = rows.shape[1] // 2
    A, B = pl.ds(0, half), pl.ds(half, half)

    def cp(i, slot, part, to):
        ref = rows.at[slot] if part is None else rows.at[slot, part]
        return remote(ref, ref, send, recv, base + i, to)

    fcx, fcy, fcd = 2 * at.qx + at.other, 2 * at.qy + at.other, 2 * at.qd + at.other
    sent = []

    def go(*a):
        c = cp(*a)
        c.start()
        sent.append(c)

    def arrived(i, slot, part, frm):
        cp(i, slot, part, frm).wait_recv()

    go(0, at.f, None, at.fc)
    go(1, at.f, A, at.fx)
    go(3, at.f, B, at.fy)
    go(2, at.f, B, at.fx)
    go(4, at.f, A, at.fy)
    arrived(0, at.fc, None, at.fc)
    on_rows(2 * at.chip, 2)
    arrived(1, at.fx, A, at.fx)
    go(5, at.fx, A, at.fy)
    go(7, at.fx, A, at.fc)
    arrived(3, at.fy, B, at.fy)
    go(6, at.fy, B, at.fx)
    go(8, at.fy, B, at.fc)
    arrived(2, at.fx, B, at.fx)
    go(9, at.fx, B, at.fc)
    arrived(4, at.fy, A, at.fy)
    go(10, at.fy, A, at.fc)
    arrived(7, fcx, A, at.fc)
    arrived(9, fcx, B, at.fc)
    on_rows(2 * at.qx, 2)
    arrived(8, fcy, B, at.fc)
    arrived(10, fcy, A, at.fc)
    on_rows(2 * at.qy, 2)
    arrived(5, at.fd, A, at.fy)
    go(11, at.fd, A, at.fc)
    arrived(6, at.fd, B, at.fx)
    go(12, at.fd, B, at.fc)
    on_rows(at.fd, 1)
    arrived(11, fcd, A, at.fc)
    arrived(12, fcd, B, at.fc)
    on_rows(fcd, 1)
    for c in sent:
        c.wait_send()


GATHER_COPIES = 13
SCATTER_COPIES = 10


def scatter_scratch(R, D):
    return [
        pltpu.VMEM((4, R, D), bf16),
        pltpu.VMEM((4, R, D), bf16),
        pltpu.VMEM((2, R, D), f32),
        pltpu.VMEM((3, R, D), bf16),
        pltpu.VMEM((3, R, D), bf16),
    ]


def scatter_phase(at, partial, bufs, send, recv, base, between=None):
    to_core, from_core, mine, out, inc = bufs
    R, D = to_core.shape[1], to_core.shape[2]
    half = R // 2
    A, B = pl.ds(0, half), pl.ds(half, half)
    tile = 512
    step = 16
    sent = []

    def go(i, src, dst, to):
        c = remote(src, dst, send, recv, base + i, to)
        c.start()
        sent.append(c)

    def arrived(i, dst, frm):
        remote(dst, dst, send, recv, base + i, frm).wait_recv()

    def compute(order, chip, slot):
        @pl.loop(0, D // tile)
        def _(n):
            cols = pl.ds(pl.multiple_of(n * tile, tile), tile)
            got = partial(chip, cols)
            lo, hi = got[:R], got[R:]
            first = at.c == 0
            mine[slot, :, cols] = jnp.where(first, lo, hi)
            to_core[order, :, cols] = jnp.where(first, hi, lo).astype(bf16)

        go(order, to_core.at[order], from_core.at[order], at.fc)

    def chip_sum(order, slot):
        arrived(order, from_core.at[order], at.fc)

        @pl.loop(0, R // step)
        def _(r):
            rows = pl.ds(pl.multiple_of(r * step, step), step)
            out[order, rows, :] = (mine[slot, rows, :] + from_core[order, rows, :].astype(f32)).astype(bf16)

    def relay(order, start, src):
        @pl.loop(0, half // step)
        def _(r):
            rows = pl.ds(pl.multiple_of(start + r * step, step), step)
            out[order, rows, :] = (out[order, rows, :].astype(f32) + inc[src, rows, :].astype(f32)).astype(bf16)

    compute(0, at.qd, 0)
    compute(1, at.qx, 1)
    if between is not None:
        between()
    chip_sum(0, 0)
    go(4, out.at[0, A], inc.at[0, A], at.fx)
    go(5, out.at[0, B], inc.at[0, B], at.fy)
    compute(2, at.qy, 0)
    chip_sum(1, 1)
    go(6, out.at[1, A], inc.at[1, A], at.fx)
    compute(3, at.chip, 1)
    chip_sum(2, 0)
    go(8, out.at[2, B], inc.at[2, B], at.fy)
    arrived(5, inc.at[0, B], at.fy)
    relay(1, half, 0)
    go(7, out.at[1, B], inc.at[1, B], at.fx)
    arrived(4, inc.at[0, A], at.fx)
    relay(2, 0, 0)
    go(9, out.at[2, A], inc.at[2, A], at.fy)
    arrived(3, from_core.at[3], at.fc)
    arrived(6, inc.at[1, A], at.fx)
    arrived(8, inc.at[2, B], at.fy)
    arrived(7, inc.at[1, B], at.fx)
    arrived(9, inc.at[2, A], at.fy)
    for c in sent:
        c.wait_send()

    def total(rows):
        return (
            mine[1, rows, :]
            + from_core[3, rows, :].astype(f32)
            + inc[1, rows, :].astype(f32)
            + inc[2, rows, :].astype(f32)
        )

    return total


def rms(v):
    return lax.rsqrt(jnp.mean(v * v, axis=-1, keepdims=True) + epsilon)


def back(weighted, normed, scale):
    return scale * (weighted - normed * jnp.mean(weighted * normed, axis=-1, keepdims=True))


def row_loop(R, body, step=16):
    @pl.loop(0, R // step)
    def _(r):
        body(pl.ds(pl.multiple_of(r * step, step), step))


def pair_loop(rows, w_cols, total_cols, body):
    @pl.loop(0, total_cols // w_cols)
    def _(t):
        body(pl.ds(pl.multiple_of(t * w_cols, w_cols), w_cols))


class Stores:
    def __init__(self, sems):
        self.sems, self.steps, self.n = sems, [], 0

    def slot(self):
        if len(self.steps) >= 2:
            for c in self.steps[-2]:
                c.wait()
            self.steps[-2] = []
        return len(self.steps) % 2

    def put(self, pairs):
        done = []
        for src, dst in pairs:
            done.append(local(src, dst, self.sems, self.n))
            self.n += 1
        self.steps.append(done)

    def finish(self):
        for step in self.steps:
            for c in step:
                c.wait()


class Moving:
    def __init__(self, at, C, mine, stage, landing, lsem, base, send, recv):
        self.at, self.C, self.mine, self.stage, self.landing = at, C, mine, stage, landing
        self.lsem, self.base, self.send, self.recv = lsem, base, send, recv
        self.z = lax.axis_index("ctx")
        self.piece = mine.shape[0] // C
        self.sent = []

    def greet(self, barrier):
        at, C = self.at, self.C
        for k in range(1, C):
            pl.semaphore_signal(barrier, inc=1, device_id={"ctx": (self.z + k) % C}, device_id_type=MESH)
            pl.semaphore_signal(
                barrier, inc=1, device_id={"fsdp": 2 * ((at.chip + k) % C) + at.c}, device_id_type=MESH
            )

    def first(self):
        at, C, piece = self.at, self.C, self.piece
        for k in FAR_FIRST:
            j = partner(at.chip, k)
            src = self.mine.at[pl.ds(j * piece, piece)]
            c = remote(src, self.stage.at[at.chip], self.send, self.recv, k, 2 * j + at.c)
            c.start()
            self.sent.append(c)
        src = self.mine.at[pl.ds(at.chip * piece, piece)]
        self.keep = local(src, self.stage.at[at.chip], self.lsem, self.base)

    def land(self, layer):
        return self.landing.at[pl.ds(layer * self.piece, self.piece)]

    def second(self):
        at, C, z = self.at, self.C, self.z
        self.keep.wait()
        for k in FAR_FIRST:
            frm = partner(at.chip, k)
            remote(self.stage.at[frm], self.stage.at[frm], self.send, self.recv, k, 2 * frm + at.c).wait_recv()
        for k in FAR_FIRST:
            to = partner(z, k)
            c = remote(self.stage.at[to], self.land(z), self.send, self.recv, C + k, to, "ctx")
            c.start()
            self.sent.append(c)
        self.keep = local(self.stage.at[z], self.land(z), self.lsem, self.base + 1)

    def finish(self):
        C, z = self.C, self.z
        self.keep.wait()
        for k in FAR_FIRST:
            frm = partner(z, k)
            remote(self.land(frm), self.land(frm), self.send, self.recv, C + k, frm, "ctx").wait_recv()
        for c in self.sent:
            c.wait_send()


def enter_kernel(C, x_ref, own_ref, all_ref, stage, mine, rows, lsem, osem, send, recv, tsend, trecv):
    at = Plane()
    load = local(x_ref, mine, lsem, 0)
    moving = Moving(at, C, mine, stage, rows.at[at.f], lsem, 1, tsend, trecv)
    barrier = pltpu.get_barrier_semaphore()
    moving.greet(barrier)
    pl.semaphore_signal(barrier, inc=1, device_id={"fsdp": at.fc}, device_id_type=MESH)
    pl.semaphore_wait(barrier, 2 * (C - 1) + 1)
    load.wait()
    moving.first()
    moving.second()
    moving.finish()
    save = local(rows.at[at.f], own_ref, lsem, 3)
    stores = []

    def on_rows(first, count):
        stores.append(local(rows.at[pl.ds(first, count)], all_ref.at[pl.ds(first, count)], osem, len(stores)))

    gather_phase(at, rows, send, recv, 0, on_rows)
    save.wait()
    for c in stores:
        c.wait()


def enter_call(C, F, x):
    R, D = x.shape
    return pl.pallas_call(
        functools.partial(enter_kernel, C),
        out_shape=[jax.ShapeDtypeStruct((R, D), bf16), jax.ShapeDtypeStruct((F, R, D), bf16)],
        in_specs=[ANY],
        out_specs=[ANY] * 2,
        scratch_shapes=[
            pltpu.VMEM((C, R // C, D), bf16),
            pltpu.VMEM((R, D), bf16),
            pltpu.VMEM((F, R, D), bf16),
            dma(4), dma(5), dma(GATHER_COPIES), dma(GATHER_COPIES), dma(2 * C), dma(2 * C),
        ],
        compiler_params=params(1),
        cost_estimate=cost(70),
    )(x)


def move_kernel(C, x_ref, own_ref, stage, mine, own, lsem, send, recv):
    at = Plane()
    load = local(x_ref, mine, lsem, 0)
    moving = Moving(at, C, mine, stage, own, lsem, 1, send, recv)
    barrier = pltpu.get_barrier_semaphore()
    moving.greet(barrier)
    pl.semaphore_wait(barrier, 2 * (C - 1))
    load.wait()
    moving.first()
    moving.second()
    moving.finish()
    local(own, own_ref, lsem, 3).wait()


def move_call(C, x):
    R, D = x.shape
    return pl.pallas_call(
        functools.partial(move_kernel, C),
        out_shape=jax.ShapeDtypeStruct((R, D), bf16),
        in_specs=[ANY],
        out_specs=ANY,
        scratch_shapes=[
            pltpu.VMEM((C, R // C, D), bf16),
            pltpu.VMEM((R, D), bf16),
            pltpu.VMEM((R, D), bf16),
            dma(4), dma(2 * C), dma(2 * C),
        ],
        compiler_params=params(9),
        cost_estimate=cost(50),
    )(x)


def qkv_kernel(all_ref, w_ref, proj_ref, st_ref, rows, w, acc, st, lsem, osem, ssend, srecv):
    at = Plane()
    F, R = rows.shape[0], rows.shape[1]
    e = w.shape[1] // 3
    m = 2 * R
    loads = [local(w_ref.at[:, pl.ds(0, 3 * e)], w, lsem, 0)] + [
        local(all_ref.at[pl.ds(2 * p, 2)], rows.at[pl.ds(2 * p, 2)], lsem, 1 + p) for p in range(F // 2)
    ]
    barrier = pltpu.get_barrier_semaphore()
    for k in range(1, F):
        pl.semaphore_signal(barrier, inc=1, device_id={"fsdp": (at.f + k) % F}, device_id_type=MESH)
    pl.semaphore_wait(barrier, F - 1)
    loads[0].wait()
    stores = Stores(osem)
    for p in range(F // 2):
        loads[1 + p].wait()
        s = stores.slot()

        def tile(c):
            acc[s, :, c] = nn(rows[pl.ds(2 * p, 2)].reshape(m, rows.shape[2]), w[:, c])

        pair_loop(m, 256, w.shape[1], tile)
        q, k = acc[s, :, :e], acc[s, :, e : 2 * e]
        st[at.f, :, pl.ds(p * m, m)] = row_sums(q * q, k * k)
        stores.put([(acc.at[s], proj_ref.at[pl.ds(p * m, m)])])
    share_stats(at, F, st, ssend, srecv, 0)
    local(st, st_ref, lsem, 1 + F // 2).wait()
    stores.finish()


def params(number):
    return pltpu.CompilerParams(
        collective_id=number, has_side_effects=True, vmem_limit_bytes=VMEM_LIMIT
    )


def cost(us):
    return pl.CostEstimate(flops=int(us * 1e9), bytes_accessed=2**20, transcendentals=0)


def dma(n):
    return pltpu.SemaphoreType.DMA((n,))


def qkv_call(F, rows, w):
    _, R, D = rows.shape
    n = w.shape[1] // 4 * 3
    return pl.pallas_call(
        qkv_kernel,
        out_shape=[
            jax.ShapeDtypeStruct((F * R, n), f32),
            jax.ShapeDtypeStruct((F, 8, F * R), f32),
        ],
        in_specs=[ANY] * 2,
        out_specs=[ANY] * 2,
        scratch_shapes=[
            pltpu.VMEM((F, R, D), bf16),
            pltpu.VMEM((D, n), bf16),
            pltpu.VMEM((2, 2 * R, n), f32),
            pltpu.VMEM((F, 8, F * R), f32),
            dma(6), dma(4), dma(F), dma(F),
        ],
        compiler_params=params(7),
        cost_estimate=cost(22),
    )(rows, w)


def out_kernel(
    mixed_ref, wo_ref, x_ref, gain_ref, hid_ref, ao_ref, in_ref,
    mixed, wo, x, gain, hid, ao, inp, b0, b1, b2, b3, b4, lsem, send, recv,
):
    at = Plane()
    e = wo.shape[1]
    pairs = [(mixed_ref, mixed), (wo_ref.at[:, pl.ds(3 * e, e)], wo), (x_ref, x), (gain_ref, gain)]
    loads = [local(s, d, lsem, i) for i, (s, d) in enumerate(pairs)]
    at.greet()
    R = x.shape[0]
    loads[0].wait()
    loads[1].wait()

    def partial(chip, cols):
        return nt(mixed[pl.ds(pl.multiple_of(chip * 2 * R, 2 * R), 2 * R), :], wo[cols, :])

    total = scatter_phase(at, partial, (b0, b1, b2, b3, b4), send, recv, 0)
    loads[2].wait()
    loads[3].wait()

    def finish(r):
        out = total(r)
        ao[r, :] = out
        hidden_in = x[r, :].astype(f32) + out * rms(out) * gain[...]
        hid[r, :] = hidden_in
        inp[r, :] = hidden_in.astype(bf16)

    row_loop(R, finish)
    for c in [local(ao, ao_ref, lsem, 4), local(hid, hid_ref, lsem, 5), local(inp, in_ref, lsem, 6)]:
        c.wait()


def out_call(F, mixed, wo, x, gain):
    R, D = x.shape
    e = wo.shape[1] // 4
    return pl.pallas_call(
        out_kernel,
        out_shape=[
            jax.ShapeDtypeStruct((R, D), f32),
            jax.ShapeDtypeStruct((R, D), f32),
            jax.ShapeDtypeStruct((R, D), bf16),
        ],
        in_specs=[ANY] * 4,
        out_specs=[ANY] * 3,
        scratch_shapes=[
            pltpu.VMEM((F * R, e), bf16),
            pltpu.VMEM((D, e), bf16),
            pltpu.VMEM((R, D), bf16),
            pltpu.VMEM((1, D), f32),
            pltpu.VMEM((R, D), f32),
            pltpu.VMEM((R, D), f32),
            pltpu.VMEM((R, D), bf16),
        ]
        + scatter_scratch(R, D)
        + [dma(7), dma(SCATTER_COPIES), dma(SCATTER_COPIES)],
        compiler_params=params(8),
        cost_estimate=cost(46),
    )(mixed, wo, x, gain)


def up_kernel(
    in_ref, w_ref, all_ref, act_ref, der_ref, h_ref,
    w, rows, act, der, h, lsem, osem, send, recv,
):
    at = Plane()
    own = local(in_ref, rows.at[at.f], lsem, 0)
    n = act.shape[2]
    loads = [local(w_ref, w, lsem, 1)]
    width = 256
    at.greet()
    R = rows.shape[1]
    own.wait()
    waited = []
    stores = Stores(osem)

    def on_rows(first, count):
        s = stores.slot()
        m = count * R
        if not waited:
            for c in loads:
                c.wait()
            waited.append(1)

        @pl.loop(0, n // width)
        def _(t):
            c = pl.ds(pl.multiple_of(t * width, width), width)
            lhs = rows[pl.ds(first, count)].reshape(m, rows.shape[2])
            g = nn(lhs, w[:, c])
            u = nn(lhs, w[:, pl.ds(pl.multiple_of(n + t * width, width), width)])
            sig = jax.nn.sigmoid(g)
            a = g * sig
            act[s, pl.ds(0, m), c] = a.astype(bf16)
            der[s, pl.ds(0, m), c] = (u * (sig * (1.0 + g * (1.0 - sig)))).astype(bf16)
            h[s, pl.ds(0, m), c] = (a * u).astype(bf16)

        start = pl.multiple_of(first * R, R)
        stores.put(
            [
                (act.at[s, pl.ds(0, m)], act_ref.at[pl.ds(start, m)]),
                (der.at[s, pl.ds(0, m)], der_ref.at[pl.ds(start, m)]),
                (h.at[s, pl.ds(0, m)], h_ref.at[pl.ds(start, m)]),
                (rows.at[pl.ds(first, count)], all_ref.at[pl.ds(first, count)]),
            ]
        )

    gather_phase(at, rows, send, recv, 0, on_rows)
    stores.finish()


def up_call(F, inp, w):
    R, D = inp.shape
    n = w.shape[1] // 2
    T = F * R
    wide = jax.ShapeDtypeStruct((T, n), bf16)
    return pl.pallas_call(
        up_kernel,
        out_shape=[jax.ShapeDtypeStruct((F, R, D), bf16), wide, wide, wide],
        in_specs=[ANY] * 2,
        out_specs=[ANY] * 4,
        scratch_shapes=[
            pltpu.VMEM((D, 2 * n), bf16),
            pltpu.VMEM((F, R, D), bf16),
            pltpu.VMEM((2, 2 * R, n), bf16),
            pltpu.VMEM((2, 2 * R, n), bf16),
            pltpu.VMEM((2, 2 * R, n), bf16),
        ]
        + [dma(2), dma(20), dma(GATHER_COPIES), dma(GATHER_COPIES)],
        compiler_params=params(2),
        cost_estimate=cost(46),
    )(inp, w)


def down_kernel(
    C, h_ref, wd_ref, hid_ref, cot_ref, gain_ref, act_ref, der_ref, unit_ref,
    res_ref, gg_ref, all_ref, grad_ref, mom_ref, p_ref,
    h, wd, hid, cot, gain, act, der, res, gacc, rows, grad, prod, b0, b1, b2, b3, b4,
    lsem, osem, asem, psem, send, recv, usend, urecv,
):
    at = Plane()
    loads = [
        local(s, d, lsem, i)
        for i, (s, d) in enumerate(
            [(h_ref, h), (wd_ref, wd), (hid_ref, hid), (gain_ref, gain), (cot_ref, cot)]
        )
    ]
    z = lax.axis_index("ctx")
    barrier = pltpu.get_barrier_semaphore()
    for to in (at.fc, at.fx, at.fy):
        pl.semaphore_signal(barrier, inc=1, device_id={"fsdp": to}, device_id_type=MESH)
    for k in FAR_FIRST:
        pl.semaphore_signal(barrier, inc=1, device_id={"ctx": partner(z, k)}, device_id_type=MESH)
    pl.semaphore_wait(barrier, C + 2)
    R = rows.shape[1]
    n = wd.shape[1]
    units = []

    def send_units(k):
        to = partner(z, k)
        c = remote(unit_ref.at[to], mom_ref.at[z], usend, urecv, k, to, "ctx")
        c.start()
        units.append(c)

    for k in FAR_FIRST:
        send_units(k)
    units.append(local(unit_ref.at[z], mom_ref.at[z], lsem, 5))
    loads[0].wait()
    loads[1].wait()

    def partial(chip, cols):
        return nt(h[pl.ds(pl.multiple_of(chip * 2 * R, 2 * R), 2 * R), :], wd[cols, :])

    total = scatter_phase(at, partial, (b0, b1, b2, b3, b4), send, recv, 0)
    for c in loads[2:]:
        c.wait()
    gacc[...] = jnp.zeros_like(gacc)

    def finish(r):
        out = total(r)
        scale = rms(out)
        hat = out * scale
        res[r, :] = (hid[r, :] + hat * gain[...]).astype(bf16)
        g = cot[r, :].astype(f32)
        gacc[...] += jnp.sum(g * hat, axis=0, keepdims=True)
        rows[at.f, r, :] = back(g * gain[...], hat, scale).astype(bf16)

    row_loop(R, finish)
    saves = [local(res, res_ref, lsem, 6), local(gacc, gg_ref, lsem, 7)]
    stores = Stores(osem)

    def on_rows(first, count):
        s = stores.slot()
        m = count * R
        start = pl.multiple_of(first * R, R)
        k = len(stores.steps)
        la = local(act_ref.at[pl.ds(start, m)], act.at[s, pl.ds(0, m)], asem, 2 * k)
        ld = local(der_ref.at[pl.ds(start, m)], der.at[s, pl.ds(0, m)], asem, 2 * k + 1)
        la.wait()
        ld.wait()

        width = 512

        @pl.loop(0, n // width)
        def _(t):
            c = pl.ds(pl.multiple_of(t * width, width), width)
            up = pl.ds(pl.multiple_of(n + t * width, width), width)
            gh = nn(rows[pl.ds(first, count)].reshape(m, rows.shape[2]), wd[:, c])
            grad[s, pl.ds(0, m), up] = (gh * act[s, pl.ds(0, m), c].astype(f32)).astype(bf16)
            grad[s, pl.ds(0, m), c] = (gh * der[s, pl.ds(0, m), c].astype(f32)).astype(bf16)

        stores.put(
            [
                (grad.at[s, pl.ds(0, m)], grad_ref.at[pl.ds(start, m)]),
                (rows.at[pl.ds(first, count)], all_ref.at[pl.ds(first, count)]),
            ]
        )

    gather_phase(at, rows, send, recv, SCATTER_COPIES, on_rows)
    F, D = rows.shape[0], rows.shape[2]
    tile, cols = prod.shape[1], p_ref.shape[3]
    puts = []
    for t in range(D // tile):
        if t >= 2:
            for c in puts[t - 2]:
                c.wait()
        rhs = rows[:, :, t * tile : (t + 1) * tile].reshape(F * R, tile)
        prod[t % 2] = lax.dot_general(
            rhs, h[...], (((0,), (0,)), ((), ())), preferred_element_type=f32
        ).astype(bf16)
        puts.append(
            [
                local(
                    prod.at[t % 2, :, pl.ds(b * cols, cols)],
                    p_ref.at[b, 0, pl.ds(t * tile, tile)],
                    psem,
                    t * (n // cols) + b,
                )
                for b in range(n // cols)
            ]
        )
    for step in puts[-2:]:
        for c in step:
            c.wait()
    for k in FAR_FIRST:
        frm = partner(z, k)
        remote(mom_ref.at[frm], mom_ref.at[frm], usend, urecv, k, frm, "ctx").wait_recv()
    for c in units[:-1]:
        c.wait_send()
    units[-1].wait()
    for s in saves:
        s.wait()
    stores.finish()


def down_call(C, F, h, wd, hid, cot, gain, act, der, units):
    R, D = hid.shape
    n = wd.shape[1]
    T = F * R
    copies = SCATTER_COPIES + GATHER_COPIES
    one = jax.ShapeDtypeStruct((R, D), bf16)
    return pl.pallas_call(
        functools.partial(down_kernel, C),
        out_shape=[
            one,
            jax.ShapeDtypeStruct((1, D), f32),
            jax.ShapeDtypeStruct((F, R, D), bf16),
            jax.ShapeDtypeStruct((T, 2 * n), bf16),
            jax.ShapeDtypeStruct(units.shape, bf16),
            jax.ShapeDtypeStruct((units.shape[1], 1, D, units.shape[3]), bf16),
        ],
        in_specs=[ANY] * 8,
        out_specs=[ANY] * 6,
        scratch_shapes=[
            pltpu.VMEM((T, n), bf16),
            pltpu.VMEM((D, n), bf16),
            pltpu.VMEM((R, D), f32),
            pltpu.VMEM((R, D), bf16),
            pltpu.VMEM((1, D), f32),
            pltpu.VMEM((2, 2 * R, n), bf16),
            pltpu.VMEM((2, 2 * R, n), bf16),
            pltpu.VMEM((R, D), bf16),
            pltpu.VMEM((1, D), f32),
            pltpu.VMEM((F, R, D), bf16),
            pltpu.VMEM((2, 2 * R, 2 * n), bf16),
            pltpu.VMEM((2, 512, n), bf16),
        ]
        + scatter_scratch(R, D)
        + [dma(8), dma(15), dma(10), dma(16), dma(copies), dma(copies), dma(C), dma(C)],
        compiler_params=params(3),
        cost_estimate=cost(108),
    )(h, wd, hid, cot, gain, act, der, units)


def mid_kernel(
    grad_ref, w_ref, cot_ref, ao_ref, gain_ref, wo_ref,
    res_ref, gg_ref, all_ref, gm_ref,
    grad, w, cot, ao, gain, wo, res, gacc, rows, gm, b0, b1, b2, b3, b4,
    lsem, osem, send, recv,
):
    at = Plane()
    e = wo.shape[1]
    pairs = [
        (grad_ref, grad), (w_ref, w),
        (cot_ref, cot), (ao_ref, ao), (gain_ref, gain), (wo_ref.at[:, pl.ds(3 * e, e)], wo),
    ]
    loads = [local(s, d, lsem, i) for i, (s, d) in enumerate(pairs)]
    at.greet()
    R = rows.shape[1]
    for c in loads[:2]:
        c.wait()

    def partial(chip, cols):
        return nt(grad[pl.ds(pl.multiple_of(chip * 2 * R, 2 * R), 2 * R), :], w[cols, :])

    total = scatter_phase(at, partial, (b0, b1, b2, b3, b4), send, recv, 0)
    for c in loads[2:]:
        c.wait()
    gacc[...] = jnp.zeros_like(gacc)

    def finish(r):
        resid = cot[r, :].astype(f32) + total(r)
        res[r, :] = resid
        out = ao[r, :]
        scale = rms(out)
        hat = out * scale
        gacc[...] += jnp.sum(resid * hat, axis=0, keepdims=True)
        rows[at.f, r, :] = back(resid * gain[...], hat, scale).astype(bf16)

    row_loop(R, finish)
    saves = [local(res, res_ref, lsem, 8), local(gacc, gg_ref, lsem, 9)]
    stores = Stores(osem)

    def on_rows(first, count):
        s = stores.slot()
        m = count * R
        start = pl.multiple_of(first * R, R)
        lhs = rows[pl.ds(first, count)].reshape(m, rows.shape[2])
        gm[s, pl.ds(0, m), :] = nn(lhs, wo[...]).astype(bf16)
        stores.put(
            [
                (gm.at[s, pl.ds(0, m)], gm_ref.at[pl.ds(start, m)]),
                (rows.at[pl.ds(first, count)], all_ref.at[pl.ds(first, count)]),
            ]
        )

    gather_phase(at, rows, send, recv, SCATTER_COPIES, on_rows)
    for s in saves:
        s.wait()
    stores.finish()


def mid_call(F, grad, w, cot, ao, gain, wo):
    R, D = cot.shape
    n, e = w.shape[1], wo.shape[1] // 4
    T = F * R
    copies = SCATTER_COPIES + GATHER_COPIES
    return pl.pallas_call(
        mid_kernel,
        out_shape=[
            jax.ShapeDtypeStruct((R, D), f32),
            jax.ShapeDtypeStruct((1, D), f32),
            jax.ShapeDtypeStruct((F, R, D), bf16),
            jax.ShapeDtypeStruct((T, e), bf16),
        ],
        in_specs=[ANY] * 6,
        out_specs=[ANY] * 4,
        scratch_shapes=[
            pltpu.VMEM((T, n), bf16),
            pltpu.VMEM((D, n), bf16),
            pltpu.VMEM((R, D), bf16),
            pltpu.VMEM((R, D), f32),
            pltpu.VMEM((1, D), f32),
            pltpu.VMEM((D, e), bf16),
            pltpu.VMEM((R, D), f32),
            pltpu.VMEM((1, D), f32),
            pltpu.VMEM((F, R, D), bf16),
            pltpu.VMEM((2, 2 * R, e), bf16),
        ]
        + scatter_scratch(R, D)
        + [dma(10), dma(10), dma(copies), dma(copies)],
        compiler_params=params(4),
        cost_estimate=cost(92),
    )(grad, w, cot, ao, gain, wo)


def last_kernel(
    width, q_ref, k_ref, v_ref, proj_ref, st_ref, in_ref, w_ref, res_ref, gain_ref,
    out_ref, gp_ref, gsum_ref,
    q, k, proj, st, ins, gains, gsum, gp, w, res, out, b0, b1, b2, b3, b4,
    lsem, send, recv, ssend, srecv, gsend, grecv,
):
    at = Plane()
    F, T = st.shape[0], st.shape[2]
    e = q.shape[1]
    R = res.shape[0]
    pairs = [
        (in_ref, ins.at[at.f]), (st_ref, st), (q_ref, q), (k_ref, k),
        (v_ref, gp.at[:, pl.ds(2 * e, e)]), (proj_ref.at[:, pl.ds(0, 2 * e)], proj), (w_ref.at[:, pl.ds(0, 3 * e)], w), (res_ref, res),
        (gain_ref, gains.at[at.f]),
    ]
    loads = [local(s, d, lsem, i) for i, (s, d) in enumerate(pairs)]
    barrier = pltpu.get_barrier_semaphore()
    for s in range(1, F):
        pl.semaphore_signal(barrier, inc=1, device_id={"fsdp": (at.f + s) % F}, device_id_type=MESH)
    pl.semaphore_wait(barrier, F - 1)
    loads[0].wait()
    share_stats(at, F, ins, ssend, srecv, 0)
    for c in loads[1:6]:
        c.wait()
    step = 256

    @pl.loop(0, T // step)
    def _(t):
        r = pl.ds(pl.multiple_of(t * step, step), step)
        sums = jnp.sum(st[:, :, r], axis=0)
        inner = jnp.sum(ins[:, :, r], axis=0) / width
        for row, grad in ((0, q), (1, k)):
            scale = lax.rsqrt(column(sums[row : row + 1], HEAD_DIM) / width + epsilon)
            mean = column(inner[row : row + 1], HEAD_DIM)
            for h in range(e // HEAD_DIM):
                hat = proj[r, row * e + h * HEAD_DIM : row * e + (h + 1) * HEAD_DIM] * scale
                got = scale * (grad[r, h * HEAD_DIM : (h + 1) * HEAD_DIM] - hat * mean)
                gp[r, row * e + h * HEAD_DIM : row * e + (h + 1) * HEAD_DIM] = got.astype(bf16)

    save = local(gp, gp_ref, lsem, 9)
    loads[6].wait()

    def partial(chip, cols):
        return nt(gp[pl.ds(pl.multiple_of(chip * 2 * R, 2 * R), 2 * R), :], w[cols, :])

    total = scatter_phase(at, partial, (b0, b1, b2, b3, b4), send, recv, 0)
    loads[7].wait()

    def finish(r):
        out[r, :] = (res[r, :] + total(r)).astype(bf16)

    row_loop(R, finish)
    store = local(out, out_ref, lsem, 10)
    loads[8].wait()
    share_stats(at, F, gains, gsend, grecv, 0)
    gsum[...] = jnp.sum(gains[...], axis=0)
    local(gsum, gsum_ref, lsem, 11).wait()
    store.wait()
    save.wait()


def last_call(F, wq, wk, gv, proj, st, ins, w, res, gains):
    R, D = res.shape
    n = w.shape[1] // 4 * 3
    T, e = F * R, n // 3
    return pl.pallas_call(
        functools.partial(last_kernel, D),
        out_shape=[
            jax.ShapeDtypeStruct((R, D), bf16),
            jax.ShapeDtypeStruct((T, n), bf16),
            jax.ShapeDtypeStruct((8, D), f32),
        ],
        in_specs=[ANY] * 9,
        out_specs=[ANY] * 3,
        scratch_shapes=[
            pltpu.VMEM((T, e), f32),
            pltpu.VMEM((T, e), f32),
            pltpu.VMEM((T, 2 * e), f32),
            pltpu.VMEM((F, 8, T), f32),
            pltpu.VMEM((F, 8, T), f32),
            pltpu.VMEM((F, 8, D), f32),
            pltpu.VMEM((8, D), f32),
            pltpu.VMEM((T, n), bf16),
            pltpu.VMEM((D, n), bf16),
            pltpu.VMEM((R, D), f32),
            pltpu.VMEM((R, D), bf16),
        ]
        + scatter_scratch(R, D)
        + [dma(12), dma(SCATTER_COPIES), dma(SCATTER_COPIES), dma(F), dma(F), dma(F), dma(F)],
        compiler_params=params(5),
        cost_estimate=cost(55),
    )(wq, wk, gv, proj, st, ins, w, res, gains)


def tn(a, b):
    return lax.dot_general(a, b, (((0,), (0,)), ((), ())), preferred_element_type=f32)


def grad_kernel(*refs):
    out = refs[-1]
    start = 0
    for x_ref, dy_ref in zip(refs[:-1:2], refs[1:-1:2]):
        got = tn(x_ref[...], dy_ref[...]).astype(bf16)
        units = dy_ref.shape[1] // out.shape[-1]
        for b in range(units):
            out[(start + b,) + (0,) * (len(out.shape) - 3)] = got[:, b * out.shape[-1] : (b + 1) * out.shape[-1]]
        start += units


def grad_call(pairs, units, cols, groups):
    T, D = pairs[0][0].shape
    tile = 512
    specs, args = [], []
    for x, dy in pairs:
        specs += [
            pl.BlockSpec((T, tile), lambda g, d: (0, d)),
            pl.BlockSpec((T, dy.shape[1] // groups), lambda g, d: (0, g)),
        ]
        args += [x, dy]
    return pl.pallas_call(
        grad_kernel,
        out_shape=jax.ShapeDtypeStruct((units, groups, D, cols), bf16),
        grid=(groups, D // tile),
        in_specs=specs,
        out_specs=pl.BlockSpec((units, 1, tile, cols), lambda g, d: (0, g, d, 0)),
        compiler_params=pltpu.CompilerParams(vmem_limit_bytes=VMEM_LIMIT),
        cost_estimate=cost(12 * groups),
    )(*args)


def share_stats(at, F, st, send, recv, base):
    sent = []
    for k in range(1, F):
        to = (at.f + k) % F
        c = remote(st.at[at.f], st.at[at.f], send, recv, base + k, to)
        c.start()
        sent.append(c)
    for k in range(1, F):
        frm = (at.f - k + F) % F
        remote(st.at[frm], st.at[frm], send, recv, base + k, frm).wait_recv()
    for c in sent:
        c.wait_send()


def row_sums(a, b):
    r = lax.broadcasted_iota(jnp.int32, (8, a.shape[1]), 0)
    one, two = (r == 0).astype(f32), (r == 1).astype(f32)

    def half(sel, v):
        return lax.dot_general(
            sel, v, (((1,), (1,)), ((), ())), preferred_element_type=f32, precision=lax.Precision.HIGHEST
        )

    return half(one, a) + half(two, b)


def column(row, lanes):
    return jnp.broadcast_to(row, (lanes, row.shape[1])).T


def turn(v, cos, sin):
    return v * cos + pltpu.roll(v, HEAD_DIM // 2, 1) * sin


def seq_columns(st, c, chips, R):
    return jnp.concatenate([st[:, pl.ds(pl.multiple_of((2 * j + c) * R, R), R)] for j in range(chips)], axis=1)


def attend_kernel(width, q_ref, k_ref, v_ref, st_ref, gq_ref, gk_ref, cos_ref, sin_ref, pos_ref, posc_ref, mix_ref, qr_ref, kr_ref, lse_ref):
    c = pl.program_id(0)
    chips, R = q_ref.shape[0], q_ref.shape[2]
    L = chips * R
    sums = jnp.sum(seq_columns_all(st_ref, c, chips, R), axis=0)
    cos, sin = cos_ref[0], sin_ref[0]

    def norm_turn(ref, row, gain):
        scale = lax.rsqrt(column(sums[row : row + 1], HEAD_DIM) / width + epsilon)
        return turn(ref[...].reshape(L, HEAD_DIM) * scale * gain[...], cos, sin)

    qr = (norm_turn(q_ref, 0, gq_ref) * HEAD_DIM ** (-0.5)).astype(bf16)
    kr = norm_turn(k_ref, 1, gk_ref).astype(bf16)
    v = v_ref[...].reshape(L, HEAD_DIM).astype(bf16)
    qr_ref[...] = qr.reshape(qr_ref.shape)
    kr_ref[...] = kr.reshape(kr_ref.shape)
    pos = pos_ref[0]
    for t in range(chips):
        rows = slice(t * R, (t + 1) * R)
        s = nt(qr[rows], kr)
        s = jnp.where(posc_ref[0, rows, :1] >= pos, s, -1e30)
        top = jnp.max(s, axis=-1, keepdims=True)
        e = jnp.exp(s - top)
        total = jnp.sum(e, axis=-1, keepdims=True)
        p = (e * (1.0 / total)).astype(bf16)
        mix_ref[t, 0] = nn(p, v).astype(bf16)
        lse_ref[0, 0, rows, :] = jnp.broadcast_to(top + jnp.log(total), (R, HEAD_DIM))


def seq_columns_all(st_ref, c, chips, R):
    return jnp.concatenate(
        [st_ref[:, :, pl.ds(pl.multiple_of((2 * j + c) * R, R), R)] for j in range(chips)], axis=2
    )


def attend_specs(chips, R, heads, F, L):
    def at(offset):
        return pl.BlockSpec((chips, 1, R, HEAD_DIM), lambda c, h: (0, c, 0, offset + h))

    gain = pl.BlockSpec((1, HEAD_DIM), lambda c, h: (0, h))
    table = pl.BlockSpec((1, L, HEAD_DIM), lambda c, h: (c, 0, 0))
    stats = pl.BlockSpec((F, 8, F * R), lambda c, h: (0, 0, 0))
    posr = pl.BlockSpec((1, 1, L), lambda c, h: (c, 0, 0))
    lse = pl.BlockSpec((1, 1, L, HEAD_DIM), lambda c, h: (c, h, 0, 0))
    return at, gain, table, stats, posr, lse


def attend_call(F, proj, st, gq, gk, cos, sin, pos, posc):
    R = proj.shape[0] // F
    e = proj.shape[1] // 3
    heads, chips = e // HEAD_DIM, F // 2
    L = chips * R
    at, gain, table, stats, posr, lse = attend_specs(chips, R, heads, F, L)
    view = proj.reshape(chips, 2, R, 3 * e)
    flat = jax.ShapeDtypeStruct((chips, 2, R, e), bf16)
    out = pl.pallas_call(
        functools.partial(attend_kernel, heads * HEAD_DIM * F),
        out_shape=[flat, flat, flat, jax.ShapeDtypeStruct((2, heads, L, HEAD_DIM), f32)],
        grid=(2, heads),
        in_specs=[at(0), at(heads), at(2 * heads), stats, gain, gain, table, table, posr, table],
        out_specs=[at(0), at(0), at(0), lse],
        compiler_params=pltpu.CompilerParams(vmem_limit_bytes=VMEM_LIMIT),
        cost_estimate=cost(15),
    )(view, view, view, st, gq, gk, cos, sin, pos, posc)
    return out


def attend_back_kernel(
    width, q_ref, k_ref, v_ref, qr_ref, kr_ref, gm_ref, lse_ref, st_ref, gq_ref, gk_ref, cos_ref, sin_ref, pos_ref, posc_ref,
    wq_ref, wk_ref, gv_ref, in_ref, gg_ref, dk, dv, dq,
):
    c = pl.program_id(0)
    chips, R = q_ref.shape[0], q_ref.shape[2]
    L = chips * R
    kr = kr_ref[...].reshape(L, HEAD_DIM)
    v = v_ref[...].reshape(L, HEAD_DIM).astype(bf16)
    pos = pos_ref[0]
    dk[...] = jnp.zeros_like(dk)
    dv[...] = jnp.zeros_like(dv)
    for t in range(chips):
        rows = slice(t * R, (t + 1) * R)
        qt, gm = qr_ref[t, 0], gm_ref[t, 0]
        s = nt(qt, kr)
        s = jnp.where(posc_ref[0, rows, :1] >= pos, s, -1e30)
        p = jnp.exp(s - lse_ref[0, 0, rows, :1])
        dp = nt(gm, v)
        dv[...] += lax.dot_general(p.astype(bf16), gm, (((0,), (0,)), ((), ())), preferred_element_type=f32)
        inner = jnp.sum(dp * p, axis=-1, keepdims=True)
        ds = (p * (dp - inner)).astype(bf16)
        dq[rows, :] = nn(ds, kr)
        dk[...] += lax.dot_general(ds, qt, (((0,), (0,)), ((), ())), preferred_element_type=f32)
    gv_ref[...] = dv[...].astype(bf16).reshape(gv_ref.shape)
    sums = jnp.sum(seq_columns_all(st_ref, c, chips, R), axis=0)
    cos, sin = cos_ref[0], sin_ref[0]

    def finish(grad, ref, row, gain, out):
        norm = turn(grad, cos, -sin)
        hat = ref[...].reshape(L, HEAD_DIM) * lax.rsqrt(column(sums[row : row + 1], HEAD_DIM) / width + epsilon)
        gg_ref[0, 0, row : row + 1, :] = jnp.sum(norm * hat, axis=0, keepdims=True)
        weighted = norm * gain[...]
        out[...] = weighted.reshape(out.shape)
        return weighted * hat

    gg_ref[...] = jnp.zeros_like(gg_ref)
    in_ref[0, 0] = row_sums(
        finish(dq[...] * HEAD_DIM ** (-0.5), q_ref, 0, gq_ref, wq_ref), finish(dk[...], k_ref, 1, gk_ref, wk_ref)
    )


def attend_back_call(F, proj, qr, kr, gm, lse_in, st, gq, gk, cos, sin, pos, posc):
    R = proj.shape[0] // F
    e = proj.shape[1] // 3
    heads, chips = e // HEAD_DIM, F // 2
    L = chips * R
    at, gain, table, stats, posr, lse = attend_specs(chips, R, heads, F, L)
    view = proj.reshape(chips, 2, R, 3 * e)
    flat = (chips, 2, R, e)
    small = pl.BlockSpec((1, 1, 8, L), lambda c, h: (c, h, 0, 0))
    tiny = pl.BlockSpec((1, 1, 8, HEAD_DIM), lambda c, h: (c, h, 0, 0))
    wide = jax.ShapeDtypeStruct(flat, f32)
    return pl.pallas_call(
        functools.partial(attend_back_kernel, heads * HEAD_DIM * F),
        out_shape=[
            wide, wide, jax.ShapeDtypeStruct(flat, bf16),
            jax.ShapeDtypeStruct((2, heads, 8, L), f32),
            jax.ShapeDtypeStruct((2, heads, 8, HEAD_DIM), f32),
        ],
        grid=(2, heads),
        in_specs=[
            at(0), at(heads), at(2 * heads), at(0), at(0), at(0), lse, stats, gain, gain, table, table, posr, table,
        ],
        out_specs=[at(0), at(0), at(0), small, tiny],
        scratch_shapes=[pltpu.VMEM((L, HEAD_DIM), f32)] * 3,
        compiler_params=pltpu.CompilerParams(vmem_limit_bytes=VMEM_LIMIT),
        cost_estimate=cost(35),
    )(view, view, view, qr, kr, gm.reshape(flat), lse_in, st, gq, gk, cos, sin, pos, posc)


def newton_kernel(
    C, m_ref, rows_ref, gain_ref, out_ref, stage_ref, gsum_ref,
    v, gram, y, yf, stat, gains, gsum,
    lsem, osem, vsend, vrecv, ysend, yrecv, ssend, srecv, tsend, trecv, gsend, grecv, usend, urecv, usem,
):
    me = lax.axis_index("fsdp")
    z = lax.axis_index("ctx")
    core, chip = me % 2, me // 2
    peer = me + 1 - 2 * core
    F = 2 * C
    cols = m_ref.shape[2]
    gload = local(gain_ref, gains.at[z], lsem, 1)
    barrier = pltpu.get_barrier_semaphore()
    for k in range(1, C):
        pl.semaphore_signal(barrier, inc=1, device_id={"ctx": (z + k) % C}, device_id_type=MESH)
    for k in range(1, F):
        pl.semaphore_signal(barrier, inc=1, device_id={"fsdp": (me + k) % F}, device_id_type=MESH)
    pl.semaphore_wait(barrier, C + F - 2)
    rows_in = v.shape[1] // C
    units_sent, units_kept = [], []
    for k in range(F):
        to = (me + k) % F
        for b in range(C):
            src = m_ref.at[to // 2, pl.ds((2 * b + to % 2) * rows_in, rows_in)]
            dst = v.at[0, pl.ds(b * rows_in, rows_in), pl.ds(me * cols, cols)]
            if k == 0:
                units_kept.append(local(src, dst, usem, b))
            else:
                c = remote(src, dst, usend, urecv, k * C + b, to)
                c.start()
                units_sent.append(c)
    piece = rows_ref.shape[1] // C

    def part(j):
        return pl.ds(j * piece, piece)

    sent, keep = [], []
    for a in range(2):
        for k in FAR_FIRST:
            to = partner(z, k)
            c = remote(rows_ref.at[a, part(to)], stage_ref.at[a, z], tsend, trecv, C * a + k, to, "ctx")
            c.start()
            sent.append(c)
        keep.append(local(rows_ref.at[a, part(z)], stage_ref.at[a, z], lsem, 2 + a))
    gload.wait()
    for k in range(1, C):
        c = remote(gains.at[z], gains.at[z], gsend, grecv, k, (z + k) % C, "ctx")
        c.start()
        sent.append(c)

    def rows_arrived():
        for a in range(2):
            keep[a].wait()
            for k in FAR_FIRST:
                dst = stage_ref.at[a, partner(z, k)]
                remote(dst, dst, tsend, trecv, C * a + k, partner(z, k), "ctx").wait_recv()
        for k in range(1, C):
            frm = (z - k + C) % C
            remote(gains.at[frm], gains.at[frm], gsend, grecv, k, frm, "ctx").wait_recv()
        gsum[...] = jnp.sum(gains[...], axis=0)
        local(gsum, gsum_ref, lsem, 6).wait()
        for c in sent:
            c.wait_send()

    for k in range(1, F):
        frm = (me - k + F) % F
        for b in range(C):
            dst = v.at[0, pl.ds(b * rows_in, rows_in), pl.ds(frm * cols, cols)]
            remote(dst, dst, usend, urecv, k * C + b, frm).wait_recv()
    for c in units_sent:
        c.wait_send()
    for c in units_kept:
        c.wait()
    M, D = v.shape[1], v.shape[2]
    tile, col = 512, 1024
    tiles = M // tile

    def block(i):
        return pl.ds(pl.multiple_of(i * tile, tile), tile)

    halves = D // col

    def swap(buf, n, i, sends, recvs):
        part = (block(i), pl.ds(n * col, col))
        return remote(buf.at[(0, *part)], buf.at[(1, *part)], sends, recvs, n * tiles + i, peer)

    pending = [swap(v, n, i, vsend, vrecv) for n in range(halves) for i in range(tiles)]
    for c in pending:
        c.start()
    stat[0] = jnp.zeros_like(stat[0])

    def add(r):
        part = v[0, r, :].astype(f32)
        stat[0] += jnp.sum((part * part).reshape(-1, 8, D // 128, 128), axis=(0, 2))

    row_loop(M, add)
    share = remote(stat.at[0], stat.at[1], ssend, srecv, 0, peer)
    share.start()
    share.wait()
    inv = 1.0 / (jnp.sqrt(jnp.sum(stat[0] + stat[1])) + 1e-07)

    for iteration in range(NS_STEPS):
        factor = inv if iteration == 0 else 1.0

        def grams(h, n):
            rhs = pl.ds(pl.multiple_of(n * col, col), col)
            cols = pl.ds(pl.multiple_of(h * M + n * col, col), col)

            @pl.loop(0, tiles)
            def _(i):
                rows = pl.ds(pl.multiple_of(i * tile, tile), tile)
                got = nt(v[0, rows, :], v[h, rhs, :])
                if iteration == 0:
                    got = got * (factor * factor)
                gram[rows, cols] = got.astype(bf16)

        @pl.loop(0, M // col)
        def _(n):
            grams(0, n)

        for c in pending:
            c.wait()

        @pl.loop(0, M // col)
        def _(n):
            grams(1, n)

        def times(src, i, n):
            rows, c = block(i), pl.ds(n * col, col)
            return nn(gram[rows, :M], src[0, :, c]) + nn(gram[rows, M:], src[1, :, c])

        swaps = []
        for n in range(halves):

            @pl.loop(0, tiles)
            def _(i):
                at = (block(i), pl.ds(n * col, col))
                got = times(v, i, n)
                if iteration == 0:
                    got = got * factor
                yf[at] = got
                y[(0, *at)] = got.astype(bf16)
                swap(y, n, i, ysend, yrecv).start()

            swaps += [swap(y, n, i, ysend, yrecv) for i in range(tiles)]
        pending = []
        for n in range(halves):
            for c in swaps[n * tiles : (n + 1) * tiles]:
                c.wait()

            @pl.loop(0, tiles)
            def _(i):
                at = (block(i), pl.ds(n * col, col))
                got = times(y, i, n)
                old = v[(0, *at)].astype(f32)
                if iteration == 0:
                    old = old * factor
                v[(0, *at)] = (quintic_one * old + quintic_two * yf[at] + quintic_three * got).astype(bf16)
                if iteration < NS_STEPS - 1:
                    swap(v, n, i, vsend, vrecv).start()

            if iteration < NS_STEPS - 1:
                pending += [swap(v, n, i, vsend, vrecv) for i in range(tiles)]
            else:
                for b in range(C):
                    for g in range(n * col // cols, (n + 1) * col // cols):
                        src = v.at[0, pl.ds(b * rows_in, rows_in), pl.ds(g * cols, cols)]
                        pending.append(local(src, out_ref.at[b * F + g], osem, b * F + g))
    rows_arrived()
    for c in pending:
        c.wait()


def newton_call(C, x, rows, gains):
    _, D, cols = x.shape
    M = D // 2
    _, R, _ = rows.shape
    n = 4
    return pl.pallas_call(
        functools.partial(newton_kernel, C),
        out_shape=[
            jax.ShapeDtypeStruct((2 * C * C, M // C, cols), bf16),
            jax.ShapeDtypeStruct((2, C, R // C, D), bf16),
            jax.ShapeDtypeStruct((8, D), f32),
        ],
        in_specs=[ANY] * 3,
        out_specs=[ANY] * 3,
        scratch_shapes=[
            pltpu.VMEM((2, M, D), bf16),
            pltpu.VMEM((M, 2 * M), bf16),
            pltpu.VMEM((2, M, D), bf16),
            pltpu.VMEM((M, D), f32),
            pltpu.VMEM((2, 8, 128), f32),
            pltpu.VMEM((C, 8, D), f32),
            pltpu.VMEM((8, D), f32),
            dma(7), dma(2 * C * C), dma(n), dma(n), dma(n), dma(n), dma(1), dma(1),
            dma(2 * C), dma(2 * C), dma(C), dma(C), dma(2 * C * C), dma(2 * C * C), dma(C),
        ],
        compiler_params=params(6),
        cost_estimate=cost(95),
    )(x, rows, gains)


def project(C, F, x, w):
    own = to_layer(C, F, x)
    rows = token_rows(own)
    return own, rows, dot(rows, w, 1, 0)


def attn_out_and_up(C, F, mixed, wo, x, gain, w, cot):
    if kernels_fit(C, F):
        hidden_in, out, inp = out_call(F, mixed, wo, x, gain)
        cot, inp = lax.optimization_barrier((cot, inp))
        cot, inp = lax.optimization_barrier((move_call(C, cot), inp))
        return (cot, hidden_in, out, *up_call(F, inp, w))
    out = token_sums(dot(mixed, wo, 1, 1))
    hidden_in = x.astype(f32) + out * rms(out) * gain
    rows = token_rows(hidden_in.astype(bf16))
    g, u = jnp.split(dot(rows, w, 1, 0), 2, axis=1)
    sig = jax.nn.sigmoid(g)
    der = u * (sig * (1.0 + g * (1.0 - sig)))
    act = g * sig
    cot = to_layer(C, F, cot)
    return cot, hidden_in, out, rows, act.astype(bf16), der.astype(bf16), (act * u).astype(bf16)


def down_and_back(C, F, h, wd, hidden_in, cot, gain, act, der, units):
    if kernels_fit(C, F):
        return down_call(C, F, h, wd, hidden_in, cot, gain, act, der, units)
    out = token_sums(dot(h, wd, 1, 1))
    scale = rms(out)
    hat = out * scale
    g = cot.astype(f32)
    rows = token_rows(back(g * gain, hat, scale).astype(bf16))
    gh = dot(rows, wd, 1, 0)
    return (
        (hidden_in + hat * gain).astype(bf16),
        jnp.sum(g * hat, axis=0, keepdims=True),
        rows,
        jnp.concatenate([(gh * der.astype(f32)).astype(bf16), (gh * act.astype(f32)).astype(bf16)], axis=1),
        None,
        None,
    )


def back_to_attn(C, F, grad, w, cot, out, gain, wo):
    if kernels_fit(C, F):
        return mid_call(F, grad, w, cot, out, gain, wo)
    resid = cot.astype(f32) + token_sums(dot(grad, w, 1, 1))
    scale = rms(out)
    hat = out * scale
    rows = token_rows(back(resid * gain, hat, scale).astype(bf16))
    return resid, jnp.sum(resid * hat, axis=0, keepdims=True), rows, dot(rows, wo, 1, 0).astype(bf16)


def back_to_input(C, F, grad_projected, w, resid):
    return (resid + token_sums(dot(grad_projected, w, 1, 1))).astype(bf16)


def kernels_fit(C, F):
    return C == 4 and F == 8 and UNITS_ATTN * 4 * 2 == C * F


def to_layer(C, F, x):
    z, chip = lax.axis_index("ctx"), lax.axis_index("fsdp") // 2
    x = x.reshape(C, x.shape[0] // C, x.shape[1])
    got = []
    for k in range(C):
        pairs = [
            (s * F + f, (f // 2) * F + 2 * ((s + k) % C) + f % 2) for s in range(C) for f in range(F)
        ]
        block = lax.dynamic_index_in_dim(x, (z + k) % C, 0, keepdims=False)
        got.append(lax.ppermute(block, BOTH, pairs))
    got = jnp.stack(got)
    got = [lax.dynamic_index_in_dim(got, (chip - s + C) % C, 0, keepdims=False) for s in range(C)]
    return jnp.concatenate(got, axis=0)


def go_home(C, F, stage):
    chip = lax.axis_index("fsdp") // 2
    got = [lax.dynamic_index_in_dim(stage, chip, 1, keepdims=False)]
    for k in range(1, C):
        pairs = [(f, 2 * ((f // 2 + k) % C) + f % 2) for f in range(F)]
        block = lax.dynamic_index_in_dim(stage, (chip + k) % C, 1, keepdims=False)
        got.append(lax.ppermute(block, "fsdp", pairs))
    return got


def at_home(C, got):
    chip = lax.axis_index("fsdp") // 2
    got = jnp.stack(got)
    got = [lax.dynamic_index_in_dim(got, (chip - j + C) % C, 0, keepdims=False) for j in range(C)]
    return jnp.concatenate(got, axis=1)


def from_layer(C, F, x):
    z, chip = lax.axis_index("ctx"), lax.axis_index("fsdp") // 2
    x = x.reshape(C, x.shape[0] // C, x.shape[1])
    got = []
    for k in range(C):
        pairs = [
            ((f // 2) * F + 2 * ((s + k) % C) + f % 2, s * F + f) for s in range(C) for f in range(F)
        ]
        block = lax.dynamic_index_in_dim(x, (chip - k + C) % C, 0, keepdims=False)
        got.append(lax.ppermute(block, BOTH, pairs))
    got = jnp.stack(got)
    got = [lax.dynamic_index_in_dim(got, (j - z + C) % C, 0, keepdims=False) for j in range(C)]
    return jnp.concatenate(got, axis=0)


def shards(C, F, layer_input, cotangent, positions, w_attn, w_ffn, gains, mom_attn, mom_ffn, gain_mom):
    z = lax.axis_index("ctx")
    f = lax.axis_index("fsdp")
    local_rows, width = layer_input.shape[1], layer_input.shape[2]
    seq_total, seq_length = positions.shape
    dz, head_cols = w_attn.shape[1], w_attn.shape[2]
    local_heads = head_cols // HEAD_DIM
    block_count = w_ffn.shape[2]
    per = seq_total // C
    piece = local_rows // C
    chips = F // per
    tokens = F * local_rows
    hidden_cols = block_count * head_cols
    units = UNITS_ATTN + 3 * block_count
    parts = C * F // units

    def after(a, b):
        return lax.optimization_barrier((a, b))[0]

    def rows_gather(shard):
        return lax.all_gather(shard, "ctx", axis=0, tiled=True)

    def product(units, groups, *pairs):
        pairs = [(x.reshape(tokens, width), dy) for x, dy in pairs]
        if kernels:
            return grad_call(pairs, units, head_cols, groups)
        grad = jnp.concatenate([dot(x, dy, 0, 0).astype(bf16) for x, dy in pairs], axis=1)
        return jnp.transpose(grad.reshape(width, groups, units, head_cols), (2, 1, 0, 3))

    def scatter(grad):
        if kernels:
            return lax.psum_scatter(grad, "ctx", scatter_dimension=0, tiled=True)[0]
        return lax.psum_scatter(grad, "ctx", scatter_dimension=2, tiled=True)

    kernels = kernels_fit(C, F)
    w_heads = rows_gather(jnp.concatenate([w_attn[i] for i in range(UNITS_ATTN)], axis=1))
    w_qkv, w_out = (w_heads, w_heads) if kernels else (w_heads[:, : 3 * head_cols], w_heads[:, 3 * head_cols :])
    ffn_flat = w_ffn.reshape(3, dz, hidden_cols)
    w_gate_up = rows_gather(jnp.concatenate([ffn_flat[0], ffn_flat[1]], axis=1))
    w_down = rows_gather(ffn_flat[2])

    gain_query = lax.dynamic_slice_in_dim(gains[0], f * head_cols, head_cols)
    gain_key = lax.dynamic_slice_in_dim(gains[1], f * head_cols, head_cols)
    pos = lax.dynamic_slice_in_dim(positions, z * per, per, 0)
    pos = jnp.transpose(pos.reshape(per, C, chips, piece), (0, 2, 1, 3)).reshape(per, seq_length)
    cosine_table, sine_table = rotary_tables(pos)

    def heads(a):
        return jnp.transpose(
            a.reshape(chips, per, local_rows, local_heads, HEAD_DIM), (1, 0, 2, 3, 4)
        ).reshape(per, seq_length, local_heads, HEAD_DIM)

    def unheads(a):
        return jnp.transpose(
            a.reshape(per, chips, local_rows, local_heads, HEAD_DIM), (1, 0, 2, 3, 4)
        ).reshape(tokens, head_cols)

    if kernels:
        sign = jnp.where(jnp.arange(HEAD_DIM) < HEAD_DIM // 2, -1.0, 1.0)
        tables = (
            gain_query[None],
            gain_key[None],
            jnp.broadcast_to(cosine_table[:, :, 0], (per, seq_length, HEAD_DIM)),
            sine_table[:, :, 0] * sign,
            pos.astype(f32)[:, None, :],
            jnp.broadcast_to(pos.astype(f32)[..., None], (per, seq_length, HEAD_DIM)),
        )
        own_input, input_all = enter_call(C, F, layer_input.reshape(local_rows, width))
        projected, stats = qkv_call(F, input_all, w_qkv)
        attn_mixed, query_rows, key_rows, log_total = attend_call(F, projected, stats, *tables)
        attn_mixed = attn_mixed.reshape(tokens, head_cols)
    else:
        own_input, input_all, projected = project(C, F, layer_input.reshape(local_rows, width), w_qkv)
        query_raw = projected[:, :head_cols]
        key_raw = projected[:, head_cols : 2 * head_cols]
        value_raw = projected[:, 2 * head_cols :]
        query_total, key_total = norm_stats(
            jnp.sum(query_raw * query_raw, axis=-1), jnp.sum(key_raw * key_raw, axis=-1)
        )
        query_scale = lax.rsqrt(query_total / width + epsilon)[..., None]
        key_scale = lax.rsqrt(key_total / width + epsilon)[..., None]
        query_hat = query_raw * query_scale
        key_hat = key_raw * key_scale
        query_rows = (
            rotate(heads(query_hat * gain_query), cosine_table, sine_table) * HEAD_DIM ** (-0.5)
        ).astype(bf16)
        key_rows = rotate(heads(key_hat * gain_key), cosine_table, sine_table).astype(bf16)
        value_rows = heads(value_raw.astype(bf16))
        attn_mixed, log_total = attend(query_rows, key_rows, value_rows, pos)
        attn_mixed = unheads(attn_mixed)
    own_grad, hidden_in, attn_out, mlp_all, act, der, hidden = attn_out_and_up(
        C, F, attn_mixed, w_out, own_input, gains[2:3], w_gate_up,
        cotangent.reshape(local_rows, width),
    )
    by_layer = None
    if kernels:
        by_layer = jnp.concatenate(
            [mom_attn[:, None].astype(bf16), jnp.transpose(mom_ffn.astype(bf16), (2, 0, 1, 3))], axis=1
        )
    result, mlp_gain, grad_mlp_all, grad_ffn_in, mom_own, p_down = down_and_back(
        C, F, hidden, w_down, hidden_in, own_grad, gains[3:4], act, der, by_layer
    )
    if kernels:
        mom_own = jnp.swapaxes(mom_own, 0, 1)
    else:
        p_down = product(block_count, 1, (grad_mlp_all, hidden))
    g_down = scatter(p_down)
    p_gate_up = product(block_count, 2, (mlp_all, grad_ffn_in))
    if kernels:
        grad_ffn_in, p_gate_up = lax.optimization_barrier((grad_ffn_in, p_gate_up))
    g_gate_up = scatter(p_gate_up)
    grad_resid, attn_gain, grad_attn_all, grad_mixed = back_to_attn(
        C, F, grad_ffn_in, w_gate_up, own_grad, attn_out, gains[2:3], w_out
    )
    if kernels:
        grad_mixed = after(grad_mixed, g_down)
        weighted_q, weighted_k, grad_value, inner, gain_cols = attend_back_call(
            F, projected, query_rows, key_rows, grad_mixed, log_total, stats, *tables
        )
        inner = jnp.transpose(
            jnp.sum(inner, axis=1).reshape(per, 8, chips, local_rows), (1, 2, 0, 3)
        ).reshape(8, tokens)
        gain_cols = jnp.sum(gain_cols, axis=0)
        query_gain_cols = gain_cols[:, 0].reshape(head_cols)
        key_gain_cols = gain_cols[:, 1].reshape(head_cols)
        flat = (tokens, head_cols)
        zero = jnp.zeros((width,), f32)
        gain_local = jnp.stack(
            [
                lax.dynamic_update_slice(zero, query_gain_cols, (f * head_cols,)),
                lax.dynamic_update_slice(zero, key_gain_cols, (f * head_cols,)),
                attn_gain[0],
                mlp_gain[0],
                *[zero] * 4,
            ]
        )
        grad_rows, grad_projected, gain_layer = last_call(
            F, weighted_q.reshape(flat), weighted_k.reshape(flat), grad_value.reshape(flat),
            projected, stats, inner, w_qkv, grad_resid, gain_local,
        )
    else:
        grad_query, grad_key, grad_value = attend_back(
            query_rows, key_rows, value_rows, pos, heads(grad_mixed), log_total
        )
        grad_query_norm = unheads(unrotate(grad_query * HEAD_DIM ** (-0.5), cosine_table, sine_table))
        grad_key_norm = unheads(unrotate(grad_key, cosine_table, sine_table))
        query_gain_cols = jnp.sum(grad_query_norm * query_hat, axis=0)
        key_gain_cols = jnp.sum(grad_key_norm * key_hat, axis=0)
        query_weighted = grad_query_norm * gain_query
        key_weighted = grad_key_norm * gain_key
        query_inner, key_inner = norm_stats(
            jnp.sum(query_weighted * query_hat, axis=-1), jnp.sum(key_weighted * key_hat, axis=-1)
        )
        grad_query_raw = query_scale * (query_weighted - query_hat * (query_inner / width)[..., None])
        grad_key_raw = key_scale * (key_weighted - key_hat * (key_inner / width)[..., None])
        grad_projected = jnp.concatenate(
            [grad_query_raw.astype(bf16), grad_key_raw.astype(bf16), unheads(grad_value).astype(bf16)],
            axis=1,
        )
        grad_rows = back_to_input(C, F, grad_projected, w_qkv, grad_resid)
    g_attn = scatter(
        product(UNITS_ATTN, 1, (input_all, grad_projected), (grad_attn_all, attn_mixed))
    )
    if not kernels:
        grad_input = from_layer(C, F, grad_rows)
        result = from_layer(C, F, result)
        zero = jnp.zeros((width,), f32)
        gain_local = jnp.stack(
            [
                lax.dynamic_update_slice(zero, query_gain_cols, (f * head_cols,)),
                lax.dynamic_update_slice(zero, key_gain_cols, (f * head_cols,)),
                attn_gain[0],
                mlp_gain[0],
            ]
        )
        gain_total = jnp.sum(lax.all_gather(gain_local, BOTH, axis=0, tiled=False), axis=0)

    if kernels:
        early = jnp.stack([jnp.zeros_like(g_down[0]), g_gate_up[0], g_gate_up[1], g_down[0]])
        mom = momentum * mom_own.reshape(early.shape).astype(f32)
        owned = (mom + early.astype(f32)).astype(bf16)
        mom_first = mom[0]
        early = jnp.swapaxes(early.reshape(UNITS_ATTN, C, dz, head_cols), 0, 1)
        early, owned, mom_first, grad_rows = lax.optimization_barrier((early, owned, mom_first, grad_rows))
        late = (mom_first + g_attn[0].astype(f32)).astype(bf16)
        owned = lax.dynamic_update_slice(owned, late[None], (0, 0, 0))
        got = lax.dynamic_update_slice(early, g_attn.reshape(C, 1, dz, head_cols), (0, 0, 0, 0))
        sent_back = lax.all_to_all(got, "ctx", split_axis=0, concat_axis=0, tiled=True).astype(f32)
        grad_attn = sent_back[:, 0]
        grad_ffn = jnp.transpose(sent_back[:, 1:], (1, 2, 0, 3))
        own, leaving, gain_total = newton_call(C, owned, jnp.stack([result, grad_rows]), gain_layer)
        homing = go_home(C, F, leaving)
        gain_total = gain_total[:4]
    else:
        grad_attn = g_attn[:, 0].astype(f32)
        grad_ffn = jnp.transpose(
            jnp.concatenate([g_gate_up, g_down], axis=1).astype(f32), (1, 2, 0, 3)
        )
    new_attn = momentum * mom_attn + grad_attn
    new_ffn = momentum * mom_ffn + grad_ffn
    if kernels:
        homing, new_attn, new_ffn, grad_attn, grad_ffn = lax.optimization_barrier(
            (homing, new_attn, new_ffn, grad_attn, grad_ffn)
        )
        back_rows = at_home(C, homing)
        result, grad_input = back_rows[0], back_rows[1]
    if not kernels:
        send = jnp.concatenate(
            [
                new_attn.astype(bf16),
                jnp.transpose(new_ffn.astype(bf16), (0, 2, 1, 3)).reshape(3 * block_count, dz, head_cols),
            ],
            axis=0,
        ).reshape(C * F, dz // parts, head_cols)
        own = lax.all_to_all(send, BOTH, split_axis=0, concat_axis=0, tiled=True)
        own = jnp.transpose(own.reshape(C, F, dz // parts, head_cols), (0, 2, 1, 3)).reshape(
            C * dz // parts, F * head_cols
        )

        def peers(a):
            out = [a]
            for s in range(1, parts):
                pairs = [(i, i - i % parts + (i + parts - s) % parts) for i in range(C * F)]
                out.append(lax.ppermute(a, BOTH, pairs))
            return out

        own32 = own.astype(f32)
        square = jnp.sum(own32 * own32)
        total = sum(peers(square.reshape(1, 1)))
        inv = 1.0 / (jnp.sqrt(total) + 1e-07)
        for iteration in range(NS_STEPS):
            factor = inv if iteration == 0 else 1.0
            every = peers(own)
            gram = [(dot(own, b, 1, 1) * (factor * factor)).astype(bf16) for b in every]
            product = sum(dot(g, b, 1, 0) for g, b in zip(gram, every)) * factor
            product_all = peers(product.astype(bf16))
            product_two = sum(dot(g, b, 1, 0) for g, b in zip(gram, product_all))
            own = (
                quintic_one * factor * own.astype(f32) + quintic_two * product + quintic_three * product_two
            ).astype(bf16)
    if kernels:
        home = own
    else:
        home = jnp.transpose(own.reshape(C, dz // parts, F, head_cols), (0, 2, 1, 3)).reshape(
            C * F, dz // parts, head_cols
        )
    steps = lax.all_to_all(home, BOTH, split_axis=0, concat_axis=0, tiled=True)
    steps = -muon_rate * steps.astype(f32)
    if kernels:
        steps = steps.reshape(C, UNITS_ATTN, dz, head_cols)
        step_attn = steps[:, 0]
        step_ffn = jnp.transpose(steps[:, 1:], (1, 2, 0, 3))
    else:
        steps = steps.reshape(units, dz, head_cols)
        step_attn = steps[:UNITS_ATTN]
        step_ffn = jnp.transpose(
            steps[UNITS_ATTN:].reshape(3, block_count, dz, head_cols), (0, 2, 1, 3)
        )
    new_gain_mom = momentum * gain_mom + gain_total
    return (
        result.reshape(layer_input.shape),
        grad_input.astype(f32).reshape(layer_input.shape),
        grad_attn,
        grad_ffn,
        gain_total,
        new_attn,
        new_ffn,
        new_gain_mom,
        step_attn,
        step_ffn,
        -gain_rate * new_gain_mom,
    )


def solution(mesh):
    tokens = P("fsdp", "ctx", None)
    attn = P(None, "ctx", "fsdp")
    ffn = P(None, "ctx", None, "fsdp")
    in_specs = (tokens, tokens, P(), attn, ffn, P(), attn, ffn, P())
    out_specs = (tokens, tokens, attn, ffn, P(), attn, ffn, P(), attn, ffn, P())
    body = functools.partial(shards, mesh.shape["ctx"], mesh.shape["fsdp"])
    return jax.shard_map(body, mesh=mesh, in_specs=in_specs, out_specs=out_specs, check_vma=False)
```

```python
import functools
import jax
import jax.numpy as jnp
from jax import lax
from jax.experimental import pallas as pl
from jax.experimental.pallas import tpu as pltpu
from jax.sharding import PartitionSpec as P

NS_STEPS = 3
HEAD_DIM = 128
UNITS_ATTN = 4

epsilon = 1e-06
rope_theta = 500000.0
quintic_one = 3.4445
quintic_two = -4.775
quintic_three = 2.0315
momentum = 0.95
muon_rate = 1.0
gain_rate = 0.0005
BOTH = ("ctx", "fsdp")
bf16 = jnp.bfloat16
f32 = jnp.float32


def dot(a, b, ca, cb):
    return lax.dot_general(a, b, (((ca,), (cb,)), ((), ())), preferred_element_type=f32)


def token_rows(operand):
    return lax.all_gather(operand, "fsdp", axis=0, tiled=True)


def token_sums(operand):
    return lax.psum_scatter(operand.astype(bf16), "fsdp", scatter_dimension=0, tiled=True).astype(f32)


def norm_stats(first_sum, second_sum):
    got = lax.all_gather(jnp.stack([first_sum, second_sum]), "fsdp", axis=0, tiled=False)
    total = jnp.sum(got, axis=0)
    return total[0], total[1]


def rms_back(upstream, normed, inv_scale):
    return inv_scale * (upstream - normed * jnp.mean(upstream * normed, axis=-1, keepdims=True))


def rotary_tables(slot_order):
    half_dim = HEAD_DIM // 2
    inverse = rope_theta ** (-(jnp.arange(half_dim, dtype=f32) * 2.0) / HEAD_DIM)
    angles = slot_order.astype(f32)[..., None] * inverse
    angles = jnp.concatenate([angles, angles], axis=-1)
    return (jnp.cos(angles)[..., None, :], jnp.sin(angles)[..., None, :])


def rotate(operand, cosine_table, sine_table):
    half_dim = operand.shape[-1] // 2
    flipped = jnp.concatenate([-operand[..., half_dim:], operand[..., :half_dim]], axis=-1)
    return operand * cosine_table + flipped * sine_table


def unrotate(upstream, cosine_table, sine_table):
    half_dim = upstream.shape[-1] // 2
    shifted = upstream * sine_table
    flipped = jnp.concatenate([shifted[..., half_dim:], -shifted[..., :half_dim]], axis=-1)
    return upstream * cosine_table + flipped


def masked_scores(query_rows, key_rows, pos):
    scores = jnp.einsum("gqhe,gkhe->ghqk", query_rows, key_rows, preferred_element_type=f32)
    causal = pos[:, None, :, None] >= pos[:, None, None, :]
    return jnp.where(causal, scores, -1e30)


def attend(query_rows, key_rows, value_rows, pos):
    scores = masked_scores(query_rows, key_rows, pos)
    row_max = jnp.max(scores, axis=-1, keepdims=True)
    weights = jnp.exp(scores - row_max)
    row_total = jnp.sum(weights, axis=-1, keepdims=True)
    probabilities = (weights / row_total).astype(bf16)
    attn_mixed = jnp.einsum("ghqk,gkhe->gqhe", probabilities, value_rows, preferred_element_type=f32)
    return attn_mixed.astype(bf16), row_max + jnp.log(row_total)


def attend_back(query_rows, key_rows, value_rows, pos, grad_mixed, log_total):
    scores = masked_scores(query_rows, key_rows, pos)
    probabilities = jnp.exp(scores - log_total)
    grad_probs = jnp.einsum("gqhe,gkhe->ghqk", grad_mixed, value_rows, preferred_element_type=f32)
    grad_value = jnp.einsum(
        "ghqk,gqhe->gkhe", probabilities.astype(bf16), grad_mixed, preferred_element_type=f32
    )
    inner_sum = jnp.sum(grad_probs * probabilities, axis=-1, keepdims=True)
    grad_scores = (probabilities * (grad_probs - inner_sum)).astype(bf16)
    grad_query = jnp.einsum("ghqk,gkhe->gqhe", grad_scores, key_rows, preferred_element_type=f32)
    grad_key = jnp.einsum("ghqk,gqhe->gkhe", grad_scores, query_rows, preferred_element_type=f32)
    return grad_query, grad_key, grad_value


MESH = pl.DeviceIdType.MESH
VMEM_LIMIT = 60 * 1024 * 1024
ANY = pl.BlockSpec(memory_space=pl.ANY)


class Plane:
    def __init__(self):
        f = lax.axis_index("fsdp")
        self.f, self.c, self.chip = f, f % 2, f // 2
        x, y = self.chip % 2, self.chip // 2
        self.qx = self.chip + 1 - 2 * x
        self.qy = self.chip + 2 - 4 * y
        self.qd = self.qx + 2 - 4 * y
        self.fc = f + 1 - 2 * self.c
        self.fx = 2 * self.qx + self.c
        self.fy = 2 * self.qy + self.c
        self.fd = 2 * self.qd + self.c
        self.other = 1 - self.c

    def greet(self):
        barrier = pltpu.get_barrier_semaphore()
        for to in (self.fc, self.fx, self.fy):
            pl.semaphore_signal(barrier, inc=1, device_id={"fsdp": to}, device_id_type=MESH)
        pl.semaphore_wait(barrier, 3)


def partner(i, k):
    if k == 3:
        return 3 - i
    if k == 2:
        return (i + 2) % 4
    return i + 1 - 2 * (i % 2)


FAR_FIRST = (3, 2, 1)


def remote(src, dst, send, recv, i, to, axis="fsdp"):
    return pltpu.make_async_remote_copy(
        src_ref=src, dst_ref=dst, send_sem=send.at[i], recv_sem=recv.at[i],
        device_id={axis: to}, device_id_type=MESH,
    )


def local(src, dst, sems, i):
    copy = pltpu.make_async_copy(src, dst, sems.at[i])
    copy.start()
    return copy


def nn(a, b):
    return lax.dot_general(a, b, (((1,), (0,)), ((), ())), preferred_element_type=f32)


def nt(a, b):
    return lax.dot_general(a, b, (((1,), (1,)), ((), ())), preferred_element_type=f32)


def gather_phase(at, rows, send, recv, base, on_rows):
    half = rows.shape[1] // 2
    A, B = pl.ds(0, half), pl.ds(half, half)

    def cp(i, slot, part, to):
        ref = rows.at[slot] if part is None else rows.at[slot, part]
        return remote(ref, ref, send, recv, base + i, to)

    fcx, fcy, fcd = 2 * at.qx + at.other, 2 * at.qy + at.other, 2 * at.qd + at.other
    sent = []

    def go(*a):
        c = cp(*a)
        c.start()
        sent.append(c)

    def arrived(i, slot, part, frm):
        cp(i, slot, part, frm).wait_recv()

    go(0, at.f, None, at.fc)
    go(1, at.f, A, at.fx)
    go(3, at.f, B, at.fy)
    go(2, at.f, B, at.fx)
    go(4, at.f, A, at.fy)
    arrived(0, at.fc, None, at.fc)
    on_rows(2 * at.chip, 2)
    arrived(1, at.fx, A, at.fx)
    go(5, at.fx, A, at.fy)
    go(7, at.fx, A, at.fc)
    arrived(3, at.fy, B, at.fy)
    go(6, at.fy, B, at.fx)
    go(8, at.fy, B, at.fc)
    arrived(2, at.fx, B, at.fx)
    go(9, at.fx, B, at.fc)
    arrived(4, at.fy, A, at.fy)
    go(10, at.fy, A, at.fc)
    arrived(7, fcx, A, at.fc)
    arrived(9, fcx, B, at.fc)
    on_rows(2 * at.qx, 2)
    arrived(8, fcy, B, at.fc)
    arrived(10, fcy, A, at.fc)
    on_rows(2 * at.qy, 2)
    arrived(5, at.fd, A, at.fy)
    go(11, at.fd, A, at.fc)
    arrived(6, at.fd, B, at.fx)
    go(12, at.fd, B, at.fc)
    on_rows(at.fd, 1)
    arrived(11, fcd, A, at.fc)
    arrived(12, fcd, B, at.fc)
    on_rows(fcd, 1)
    for c in sent:
        c.wait_send()


GATHER_COPIES = 13
SCATTER_COPIES = 10


def scatter_scratch(R, D):
    return [
        pltpu.VMEM((4, R, D), bf16),
        pltpu.VMEM((4, R, D), bf16),
        pltpu.VMEM((2, R, D), f32),
        pltpu.VMEM((3, R, D), bf16),
        pltpu.VMEM((3, R, D), bf16),
    ]


def scatter_phase(at, partial, bufs, send, recv, base, between=None):
    to_core, from_core, mine, out, inc = bufs
    R, D = to_core.shape[1], to_core.shape[2]
    half = R // 2
    A, B = pl.ds(0, half), pl.ds(half, half)
    tile = 512
    step = 16
    sent = []

    def go(i, src, dst, to):
        c = remote(src, dst, send, recv, base + i, to)
        c.start()
        sent.append(c)

    def arrived(i, dst, frm):
        remote(dst, dst, send, recv, base + i, frm).wait_recv()

    def compute(order, chip, slot):
        @pl.loop(0, D // tile)
        def _(n):
            cols = pl.ds(pl.multiple_of(n * tile, tile), tile)
            got = partial(chip, cols)
            lo, hi = got[:R], got[R:]
            first = at.c == 0
            mine[slot, :, cols] = jnp.where(first, lo, hi)
            to_core[order, :, cols] = jnp.where(first, hi, lo).astype(bf16)

        go(order, to_core.at[order], from_core.at[order], at.fc)

    def chip_sum(order, slot):
        arrived(order, from_core.at[order], at.fc)

        @pl.loop(0, R // step)
        def _(r):
            rows = pl.ds(pl.multiple_of(r * step, step), step)
            out[order, rows, :] = (mine[slot, rows, :] + from_core[order, rows, :].astype(f32)).astype(bf16)

    def relay(order, start, src):
        @pl.loop(0, half // step)
        def _(r):
            rows = pl.ds(pl.multiple_of(start + r * step, step), step)
            out[order, rows, :] = (out[order, rows, :].astype(f32) + inc[src, rows, :].astype(f32)).astype(bf16)

    compute(0, at.qd, 0)
    compute(1, at.qx, 1)
    if between is not None:
        between()
    chip_sum(0, 0)
    go(4, out.at[0, A], inc.at[0, A], at.fx)
    go(5, out.at[0, B], inc.at[0, B], at.fy)
    compute(2, at.qy, 0)
    chip_sum(1, 1)
    go(6, out.at[1, A], inc.at[1, A], at.fx)
    compute(3, at.chip, 1)
    chip_sum(2, 0)
    go(8, out.at[2, B], inc.at[2, B], at.fy)
    arrived(5, inc.at[0, B], at.fy)
    relay(1, half, 0)
    go(7, out.at[1, B], inc.at[1, B], at.fx)
    arrived(4, inc.at[0, A], at.fx)
    relay(2, 0, 0)
    go(9, out.at[2, A], inc.at[2, A], at.fy)
    arrived(3, from_core.at[3], at.fc)
    arrived(6, inc.at[1, A], at.fx)
    arrived(8, inc.at[2, B], at.fy)
    arrived(7, inc.at[1, B], at.fx)
    arrived(9, inc.at[2, A], at.fy)
    for c in sent:
        c.wait_send()

    def total(rows):
        return (
            mine[1, rows, :]
            + from_core[3, rows, :].astype(f32)
            + inc[1, rows, :].astype(f32)
            + inc[2, rows, :].astype(f32)
        )

    return total


def rms(v):
    return lax.rsqrt(jnp.mean(v * v, axis=-1, keepdims=True) + epsilon)


def back(weighted, normed, scale):
    return scale * (weighted - normed * jnp.mean(weighted * normed, axis=-1, keepdims=True))


def row_loop(R, body, step=16):
    @pl.loop(0, R // step)
    def _(r):
        body(pl.ds(pl.multiple_of(r * step, step), step))


def pair_loop(rows, w_cols, total_cols, body):
    @pl.loop(0, total_cols // w_cols)
    def _(t):
        body(pl.ds(pl.multiple_of(t * w_cols, w_cols), w_cols))


class Stores:
    def __init__(self, sems):
        self.sems, self.steps, self.n = sems, [], 0

    def slot(self):
        if len(self.steps) >= 2:
            for c in self.steps[-2]:
                c.wait()
            self.steps[-2] = []
        return len(self.steps) % 2

    def put(self, pairs):
        done = []
        for src, dst in pairs:
            done.append(local(src, dst, self.sems, self.n))
            self.n += 1
        self.steps.append(done)

    def finish(self):
        for step in self.steps:
            for c in step:
                c.wait()


class Moving:
    def __init__(self, at, C, mine, stage, landing, lsem, base, send, recv):
        self.at, self.C, self.mine, self.stage, self.landing = at, C, mine, stage, landing
        self.lsem, self.base, self.send, self.recv = lsem, base, send, recv
        self.z = lax.axis_index("ctx")
        self.piece = mine.shape[0] // C
        self.sent = []

    def greet(self, barrier):
        at, C = self.at, self.C
        for k in range(1, C):
            pl.semaphore_signal(barrier, inc=1, device_id={"ctx": (self.z + k) % C}, device_id_type=MESH)
            pl.semaphore_signal(
                barrier, inc=1, device_id={"fsdp": 2 * ((at.chip + k) % C) + at.c}, device_id_type=MESH
            )

    def first(self):
        at, C, piece = self.at, self.C, self.piece
        for k in FAR_FIRST:
            j = partner(at.chip, k)
            src = self.mine.at[pl.ds(j * piece, piece)]
            c = remote(src, self.stage.at[at.chip], self.send, self.recv, k, 2 * j + at.c)
            c.start()
            self.sent.append(c)
        src = self.mine.at[pl.ds(at.chip * piece, piece)]
        self.keep = local(src, self.stage.at[at.chip], self.lsem, self.base)

    def land(self, layer):
        return self.landing.at[pl.ds(layer * self.piece, self.piece)]

    def second(self):
        at, C, z = self.at, self.C, self.z
        self.keep.wait()
        for k in FAR_FIRST:
            frm = partner(at.chip, k)
            remote(self.stage.at[frm], self.stage.at[frm], self.send, self.recv, k, 2 * frm + at.c).wait_recv()
        for k in FAR_FIRST:
            to = partner(z, k)
            c = remote(self.stage.at[to], self.land(z), self.send, self.recv, C + k, to, "ctx")
            c.start()
            self.sent.append(c)
        self.keep = local(self.stage.at[z], self.land(z), self.lsem, self.base + 1)

    def finish(self):
        C, z = self.C, self.z
        self.keep.wait()
        for k in FAR_FIRST:
            frm = partner(z, k)
            remote(self.land(frm), self.land(frm), self.send, self.recv, C + k, frm, "ctx").wait_recv()
        for c in self.sent:
            c.wait_send()


def enter_kernel(C, x_ref, own_ref, all_ref, stage, mine, rows, lsem, osem, send, recv, tsend, trecv):
    at = Plane()
    load = local(x_ref, mine, lsem, 0)
    moving = Moving(at, C, mine, stage, rows.at[at.f], lsem, 1, tsend, trecv)
    barrier = pltpu.get_barrier_semaphore()
    moving.greet(barrier)
    pl.semaphore_signal(barrier, inc=1, device_id={"fsdp": at.fc}, device_id_type=MESH)
    pl.semaphore_wait(barrier, 2 * (C - 1) + 1)
    load.wait()
    moving.first()
    moving.second()
    moving.finish()
    save = local(rows.at[at.f], own_ref, lsem, 3)
    stores = []

    def on_rows(first, count):
        stores.append(local(rows.at[pl.ds(first, count)], all_ref.at[pl.ds(first, count)], osem, len(stores)))

    gather_phase(at, rows, send, recv, 0, on_rows)
    save.wait()
    for c in stores:
        c.wait()


def enter_call(C, F, x):
    R, D = x.shape
    return pl.pallas_call(
        functools.partial(enter_kernel, C),
        out_shape=[jax.ShapeDtypeStruct((R, D), bf16), jax.ShapeDtypeStruct((F, R, D), bf16)],
        in_specs=[ANY],
        out_specs=[ANY] * 2,
        scratch_shapes=[
            pltpu.VMEM((C, R // C, D), bf16),
            pltpu.VMEM((R, D), bf16),
            pltpu.VMEM((F, R, D), bf16),
            dma(4), dma(5), dma(GATHER_COPIES), dma(GATHER_COPIES), dma(2 * C), dma(2 * C),
        ],
        compiler_params=params(1),
        cost_estimate=cost(70),
    )(x)


def move_kernel(C, x_ref, own_ref, stage, mine, own, lsem, send, recv):
    at = Plane()
    load = local(x_ref, mine, lsem, 0)
    moving = Moving(at, C, mine, stage, own, lsem, 1, send, recv)
    barrier = pltpu.get_barrier_semaphore()
    moving.greet(barrier)
    pl.semaphore_wait(barrier, 2 * (C - 1))
    load.wait()
    moving.first()
    moving.second()
    moving.finish()
    local(own, own_ref, lsem, 3).wait()


def move_call(C, x):
    R, D = x.shape
    return pl.pallas_call(
        functools.partial(move_kernel, C),
        out_shape=jax.ShapeDtypeStruct((R, D), bf16),
        in_specs=[ANY],
        out_specs=ANY,
        scratch_shapes=[
            pltpu.VMEM((C, R // C, D), bf16),
            pltpu.VMEM((R, D), bf16),
            pltpu.VMEM((R, D), bf16),
            dma(4), dma(2 * C), dma(2 * C),
        ],
        compiler_params=params(9),
        cost_estimate=cost(50),
    )(x)


def qkv_kernel(all_ref, w_ref, proj_ref, st_ref, rows, w, acc, st, lsem, osem, ssend, srecv):
    at = Plane()
    F, R = rows.shape[0], rows.shape[1]
    e = w.shape[1] // 3
    m = 2 * R
    loads = [local(w_ref.at[:, pl.ds(0, 3 * e)], w, lsem, 0)] + [
        local(all_ref.at[pl.ds(2 * p, 2)], rows.at[pl.ds(2 * p, 2)], lsem, 1 + p) for p in range(F // 2)
    ]
    barrier = pltpu.get_barrier_semaphore()
    for k in range(1, F):
        pl.semaphore_signal(barrier, inc=1, device_id={"fsdp": (at.f + k) % F}, device_id_type=MESH)
    pl.semaphore_wait(barrier, F - 1)
    loads[0].wait()
    stores = Stores(osem)
    for p in range(F // 2):
        loads[1 + p].wait()
        s = stores.slot()

        def tile(c):
            acc[s, :, c] = nn(rows[pl.ds(2 * p, 2)].reshape(m, rows.shape[2]), w[:, c])

        pair_loop(m, 256, w.shape[1], tile)
        q, k = acc[s, :, :e], acc[s, :, e : 2 * e]
        st[at.f, :, pl.ds(p * m, m)] = row_sums(q * q, k * k)
        stores.put([(acc.at[s], proj_ref.at[pl.ds(p * m, m)])])
    share_stats(at, F, st, ssend, srecv, 0)
    local(st, st_ref, lsem, 1 + F // 2).wait()
    stores.finish()


def params(number):
    return pltpu.CompilerParams(
        collective_id=number, has_side_effects=True, vmem_limit_bytes=VMEM_LIMIT
    )


def cost(us):
    return pl.CostEstimate(flops=int(us * 1e9), bytes_accessed=2**20, transcendentals=0)


def dma(n):
    return pltpu.SemaphoreType.DMA((n,))


def qkv_call(F, rows, w):
    _, R, D = rows.shape
    n = w.shape[1] // 4 * 3
    return pl.pallas_call(
        qkv_kernel,
        out_shape=[
            jax.ShapeDtypeStruct((F * R, n), f32),
            jax.ShapeDtypeStruct((F, 8, F * R), f32),
        ],
        in_specs=[ANY] * 2,
        out_specs=[ANY] * 2,
        scratch_shapes=[
            pltpu.VMEM((F, R, D), bf16),
            pltpu.VMEM((D, n), bf16),
            pltpu.VMEM((2, 2 * R, n), f32),
            pltpu.VMEM((F, 8, F * R), f32),
            dma(6), dma(4), dma(F), dma(F),
        ],
        compiler_params=params(7),
        cost_estimate=cost(22),
    )(rows, w)


def out_kernel(
    mixed_ref, wo_ref, x_ref, gain_ref, hid_ref, ao_ref, in_ref,
    mixed, wo, x, gain, hid, ao, inp, b0, b1, b2, b3, b4, lsem, send, recv,
):
    at = Plane()
    e = wo.shape[1]
    pairs = [(mixed_ref, mixed), (wo_ref.at[:, pl.ds(3 * e, e)], wo), (x_ref, x), (gain_ref, gain)]
    loads = [local(s, d, lsem, i) for i, (s, d) in enumerate(pairs)]
    at.greet()
    R = x.shape[0]
    loads[0].wait()
    loads[1].wait()

    def partial(chip, cols):
        return nt(mixed[pl.ds(pl.multiple_of(chip * 2 * R, 2 * R), 2 * R), :], wo[cols, :])

    total = scatter_phase(at, partial, (b0, b1, b2, b3, b4), send, recv, 0)
    loads[2].wait()
    loads[3].wait()

    def finish(r):
        out = total(r)
        ao[r, :] = out
        hidden_in = x[r, :].astype(f32) + out * rms(out) * gain[...]
        hid[r, :] = hidden_in
        inp[r, :] = hidden_in.astype(bf16)

    row_loop(R, finish)
    for c in [local(ao, ao_ref, lsem, 4), local(hid, hid_ref, lsem, 5), local(inp, in_ref, lsem, 6)]:
        c.wait()


def out_call(F, mixed, wo, x, gain):
    R, D = x.shape
    e = wo.shape[1] // 4
    return pl.pallas_call(
        out_kernel,
        out_shape=[
            jax.ShapeDtypeStruct((R, D), f32),
            jax.ShapeDtypeStruct((R, D), f32),
            jax.ShapeDtypeStruct((R, D), bf16),
        ],
        in_specs=[ANY] * 4,
        out_specs=[ANY] * 3,
        scratch_shapes=[
            pltpu.VMEM((F * R, e), bf16),
            pltpu.VMEM((D, e), bf16),
            pltpu.VMEM((R, D), bf16),
            pltpu.VMEM((1, D), f32),
            pltpu.VMEM((R, D), f32),
            pltpu.VMEM((R, D), f32),
            pltpu.VMEM((R, D), bf16),
        ]
        + scatter_scratch(R, D)
        + [dma(7), dma(SCATTER_COPIES), dma(SCATTER_COPIES)],
        compiler_params=params(8),
        cost_estimate=cost(46),
    )(mixed, wo, x, gain)


def up_kernel(
    in_ref, w_ref, all_ref, act_ref, der_ref, h_ref,
    w, rows, act, der, h, lsem, osem, send, recv,
):
    at = Plane()
    own = local(in_ref, rows.at[at.f], lsem, 0)
    n = act.shape[2]
    loads = [local(w_ref, w, lsem, 1)]
    width = 256
    at.greet()
    R = rows.shape[1]
    own.wait()
    waited = []
    stores = Stores(osem)

    def on_rows(first, count):
        s = stores.slot()
        m = count * R
        if not waited:
            for c in loads:
                c.wait()
            waited.append(1)

        @pl.loop(0, n // width)
        def _(t):
            c = pl.ds(pl.multiple_of(t * width, width), width)
            lhs = rows[pl.ds(first, count)].reshape(m, rows.shape[2])
            g = nn(lhs, w[:, c])
            u = nn(lhs, w[:, pl.ds(pl.multiple_of(n + t * width, width), width)])
            sig = jax.nn.sigmoid(g)
            a = g * sig
            act[s, pl.ds(0, m), c] = a.astype(bf16)
            der[s, pl.ds(0, m), c] = (u * (sig * (1.0 + g * (1.0 - sig)))).astype(bf16)
            h[s, pl.ds(0, m), c] = (a * u).astype(bf16)

        start = pl.multiple_of(first * R, R)
        stores.put(
            [
                (act.at[s, pl.ds(0, m)], act_ref.at[pl.ds(start, m)]),
                (der.at[s, pl.ds(0, m)], der_ref.at[pl.ds(start, m)]),
                (h.at[s, pl.ds(0, m)], h_ref.at[pl.ds(start, m)]),
                (rows.at[pl.ds(first, count)], all_ref.at[pl.ds(first, count)]),
            ]
        )

    gather_phase(at, rows, send, recv, 0, on_rows)
    stores.finish()


def up_call(F, inp, w):
    R, D = inp.shape
    n = w.shape[1] // 2
    T = F * R
    wide = jax.ShapeDtypeStruct((T, n), bf16)
    return pl.pallas_call(
        up_kernel,
        out_shape=[jax.ShapeDtypeStruct((F, R, D), bf16), wide, wide, wide],
        in_specs=[ANY] * 2,
        out_specs=[ANY] * 4,
        scratch_shapes=[
            pltpu.VMEM((D, 2 * n), bf16),
            pltpu.VMEM((F, R, D), bf16),
            pltpu.VMEM((2, 2 * R, n), bf16),
            pltpu.VMEM((2, 2 * R, n), bf16),
            pltpu.VMEM((2, 2 * R, n), bf16),
        ]
        + [dma(2), dma(20), dma(GATHER_COPIES), dma(GATHER_COPIES)],
        compiler_params=params(2),
        cost_estimate=cost(46),
    )(inp, w)


def down_kernel(
    C, h_ref, wd_ref, hid_ref, cot_ref, gain_ref, act_ref, der_ref, unit_ref,
    res_ref, gg_ref, all_ref, grad_ref, mom_ref, p_ref,
    h, wd, hid, cot, gain, act, der, res, gacc, rows, grad, prod, b0, b1, b2, b3, b4,
    lsem, osem, asem, psem, send, recv, usend, urecv,
):
    at = Plane()
    loads = [
        local(s, d, lsem, i)
        for i, (s, d) in enumerate(
            [(h_ref, h), (wd_ref, wd), (hid_ref, hid), (gain_ref, gain), (cot_ref, cot)]
        )
    ]
    z = lax.axis_index("ctx")
    barrier = pltpu.get_barrier_semaphore()
    for to in (at.fc, at.fx, at.fy):
        pl.semaphore_signal(barrier, inc=1, device_id={"fsdp": to}, device_id_type=MESH)
    for k in FAR_FIRST:
        pl.semaphore_signal(barrier, inc=1, device_id={"ctx": partner(z, k)}, device_id_type=MESH)
    pl.semaphore_wait(barrier, C + 2)
    R = rows.shape[1]
    n = wd.shape[1]
    units = []

    def send_units(k):
        to = partner(z, k)
        c = remote(unit_ref.at[to], mom_ref.at[z], usend, urecv, k, to, "ctx")
        c.start()
        units.append(c)

    for k in FAR_FIRST:
        send_units(k)
    units.append(local(unit_ref.at[z], mom_ref.at[z], lsem, 5))
    loads[0].wait()
    loads[1].wait()

    def partial(chip, cols):
        return nt(h[pl.ds(pl.multiple_of(chip * 2 * R, 2 * R), 2 * R), :], wd[cols, :])

    total = scatter_phase(at, partial, (b0, b1, b2, b3, b4), send, recv, 0)
    for c in loads[2:]:
        c.wait()
    gacc[...] = jnp.zeros_like(gacc)

    def finish(r):
        out = total(r)
        scale = rms(out)
        hat = out * scale
        res[r, :] = (hid[r, :] + hat * gain[...]).astype(bf16)
        g = cot[r, :].astype(f32)
        gacc[...] += jnp.sum(g * hat, axis=0, keepdims=True)
        rows[at.f, r, :] = back(g * gain[...], hat, scale).astype(bf16)

    row_loop(R, finish)
    saves = [local(res, res_ref, lsem, 6), local(gacc, gg_ref, lsem, 7)]
    stores = Stores(osem)

    def on_rows(first, count):
        s = stores.slot()
        m = count * R
        start = pl.multiple_of(first * R, R)
        k = len(stores.steps)
        la = local(act_ref.at[pl.ds(start, m)], act.at[s, pl.ds(0, m)], asem, 2 * k)
        ld = local(der_ref.at[pl.ds(start, m)], der.at[s, pl.ds(0, m)], asem, 2 * k + 1)
        la.wait()
        ld.wait()

        width = 512

        @pl.loop(0, n // width)
        def _(t):
            c = pl.ds(pl.multiple_of(t * width, width), width)
            up = pl.ds(pl.multiple_of(n + t * width, width), width)
            gh = nn(rows[pl.ds(first, count)].reshape(m, rows.shape[2]), wd[:, c])
            grad[s, pl.ds(0, m), up] = (gh * act[s, pl.ds(0, m), c].astype(f32)).astype(bf16)
            grad[s, pl.ds(0, m), c] = (gh * der[s, pl.ds(0, m), c].astype(f32)).astype(bf16)

        stores.put(
            [
                (grad.at[s, pl.ds(0, m)], grad_ref.at[pl.ds(start, m)]),
                (rows.at[pl.ds(first, count)], all_ref.at[pl.ds(first, count)]),
            ]
        )

    gather_phase(at, rows, send, recv, SCATTER_COPIES, on_rows)
    F, D = rows.shape[0], rows.shape[2]
    tile, cols = prod.shape[1], p_ref.shape[3]
    puts = []
    for t in range(D // tile):
        if t >= 2:
            for c in puts[t - 2]:
                c.wait()
        rhs = rows[:, :, t * tile : (t + 1) * tile].reshape(F * R, tile)
        prod[t % 2] = lax.dot_general(
            rhs, h[...], (((0,), (0,)), ((), ())), preferred_element_type=f32
        ).astype(bf16)
        puts.append(
            [
                local(
                    prod.at[t % 2, :, pl.ds(b * cols, cols)],
                    p_ref.at[b, 0, pl.ds(t * tile, tile)],
                    psem,
                    t * (n // cols) + b,
                )
                for b in range(n // cols)
            ]
        )
    for step in puts[-2:]:
        for c in step:
            c.wait()
    for k in FAR_FIRST:
        frm = partner(z, k)
        remote(mom_ref.at[frm], mom_ref.at[frm], usend, urecv, k, frm, "ctx").wait_recv()
    for c in units[:-1]:
        c.wait_send()
    units[-1].wait()
    for s in saves:
        s.wait()
    stores.finish()


def down_call(C, F, h, wd, hid, cot, gain, act, der, units):
    R, D = hid.shape
    n = wd.shape[1]
    T = F * R
    copies = SCATTER_COPIES + GATHER_COPIES
    one = jax.ShapeDtypeStruct((R, D), bf16)
    return pl.pallas_call(
        functools.partial(down_kernel, C),
        out_shape=[
            one,
            jax.ShapeDtypeStruct((1, D), f32),
            jax.ShapeDtypeStruct((F, R, D), bf16),
            jax.ShapeDtypeStruct((T, 2 * n), bf16),
            jax.ShapeDtypeStruct(units.shape, bf16),
            jax.ShapeDtypeStruct((units.shape[1], 1, D, units.shape[3]), bf16),
        ],
        in_specs=[ANY] * 8,
        out_specs=[ANY] * 6,
        scratch_shapes=[
            pltpu.VMEM((T, n), bf16),
            pltpu.VMEM((D, n), bf16),
            pltpu.VMEM((R, D), f32),
            pltpu.VMEM((R, D), bf16),
            pltpu.VMEM((1, D), f32),
            pltpu.VMEM((2, 2 * R, n), bf16),
            pltpu.VMEM((2, 2 * R, n), bf16),
            pltpu.VMEM((R, D), bf16),
            pltpu.VMEM((1, D), f32),
            pltpu.VMEM((F, R, D), bf16),
            pltpu.VMEM((2, 2 * R, 2 * n), bf16),
            pltpu.VMEM((2, 512, n), bf16),
        ]
        + scatter_scratch(R, D)
        + [dma(8), dma(15), dma(10), dma(16), dma(copies), dma(copies), dma(C), dma(C)],
        compiler_params=params(3),
        cost_estimate=cost(108),
    )(h, wd, hid, cot, gain, act, der, units)


def mid_kernel(
    grad_ref, w_ref, cot_ref, ao_ref, gain_ref, wo_ref,
    res_ref, gg_ref, all_ref, gm_ref,
    grad, w, cot, ao, gain, wo, res, gacc, rows, gm, b0, b1, b2, b3, b4,
    lsem, osem, send, recv,
):
    at = Plane()
    e = wo.shape[1]
    pairs = [
        (grad_ref, grad), (w_ref, w),
        (cot_ref, cot), (ao_ref, ao), (gain_ref, gain), (wo_ref.at[:, pl.ds(3 * e, e)], wo),
    ]
    loads = [local(s, d, lsem, i) for i, (s, d) in enumerate(pairs)]
    at.greet()
    R = rows.shape[1]
    for c in loads[:2]:
        c.wait()

    def partial(chip, cols):
        return nt(grad[pl.ds(pl.multiple_of(chip * 2 * R, 2 * R), 2 * R), :], w[cols, :])

    total = scatter_phase(at, partial, (b0, b1, b2, b3, b4), send, recv, 0)
    for c in loads[2:]:
        c.wait()
    gacc[...] = jnp.zeros_like(gacc)

    def finish(r):
        resid = cot[r, :].astype(f32) + total(r)
        res[r, :] = resid
        out = ao[r, :]
        scale = rms(out)
        hat = out * scale
        gacc[...] += jnp.sum(resid * hat, axis=0, keepdims=True)
        rows[at.f, r, :] = back(resid * gain[...], hat, scale).astype(bf16)

    row_loop(R, finish)
    saves = [local(res, res_ref, lsem, 8), local(gacc, gg_ref, lsem, 9)]
    stores = Stores(osem)

    def on_rows(first, count):
        s = stores.slot()
        m = count * R
        start = pl.multiple_of(first * R, R)
        lhs = rows[pl.ds(first, count)].reshape(m, rows.shape[2])
        gm[s, pl.ds(0, m), :] = nn(lhs, wo[...]).astype(bf16)
        stores.put(
            [
                (gm.at[s, pl.ds(0, m)], gm_ref.at[pl.ds(start, m)]),
                (rows.at[pl.ds(first, count)], all_ref.at[pl.ds(first, count)]),
            ]
        )

    gather_phase(at, rows, send, recv, SCATTER_COPIES, on_rows)
    for s in saves:
        s.wait()
    stores.finish()


def mid_call(F, grad, w, cot, ao, gain, wo):
    R, D = cot.shape
    n, e = w.shape[1], wo.shape[1] // 4
    T = F * R
    copies = SCATTER_COPIES + GATHER_COPIES
    return pl.pallas_call(
        mid_kernel,
        out_shape=[
            jax.ShapeDtypeStruct((R, D), f32),
            jax.ShapeDtypeStruct((1, D), f32),
            jax.ShapeDtypeStruct((F, R, D), bf16),
            jax.ShapeDtypeStruct((T, e), bf16),
        ],
        in_specs=[ANY] * 6,
        out_specs=[ANY] * 4,
        scratch_shapes=[
            pltpu.VMEM((T, n), bf16),
            pltpu.VMEM((D, n), bf16),
            pltpu.VMEM((R, D), bf16),
            pltpu.VMEM((R, D), f32),
            pltpu.VMEM((1, D), f32),
            pltpu.VMEM((D, e), bf16),
            pltpu.VMEM((R, D), f32),
            pltpu.VMEM((1, D), f32),
            pltpu.VMEM((F, R, D), bf16),
            pltpu.VMEM((2, 2 * R, e), bf16),
        ]
        + scatter_scratch(R, D)
        + [dma(10), dma(10), dma(copies), dma(copies)],
        compiler_params=params(4),
        cost_estimate=cost(92),
    )(grad, w, cot, ao, gain, wo)


def last_kernel(
    width, q_ref, k_ref, v_ref, proj_ref, st_ref, in_ref, w_ref, res_ref, gain_ref,
    out_ref, gp_ref, gsum_ref,
    q, k, proj, st, ins, gains, gsum, gp, w, res, out, b0, b1, b2, b3, b4,
    lsem, send, recv, ssend, srecv, gsend, grecv,
):
    at = Plane()
    F, T = st.shape[0], st.shape[2]
    e = q.shape[1]
    R = res.shape[0]
    pairs = [
        (in_ref, ins.at[at.f]), (st_ref, st), (q_ref, q), (k_ref, k),
        (v_ref, gp.at[:, pl.ds(2 * e, e)]), (proj_ref.at[:, pl.ds(0, 2 * e)], proj), (w_ref.at[:, pl.ds(0, 3 * e)], w), (res_ref, res),
        (gain_ref, gains.at[at.f]),
    ]
    loads = [local(s, d, lsem, i) for i, (s, d) in enumerate(pairs)]
    barrier = pltpu.get_barrier_semaphore()
    for s in range(1, F):
        pl.semaphore_signal(barrier, inc=1, device_id={"fsdp": (at.f + s) % F}, device_id_type=MESH)
    pl.semaphore_wait(barrier, F - 1)
    loads[0].wait()
    share_stats(at, F, ins, ssend, srecv, 0)
    for c in loads[1:6]:
        c.wait()
    step = 256

    @pl.loop(0, T // step)
    def _(t):
        r = pl.ds(pl.multiple_of(t * step, step), step)
        sums = jnp.sum(st[:, :, r], axis=0)
        inner = jnp.sum(ins[:, :, r], axis=0) / width
        for row, grad in ((0, q), (1, k)):
            scale = lax.rsqrt(column(sums[row : row + 1], HEAD_DIM) / width + epsilon)
            mean = column(inner[row : row + 1], HEAD_DIM)
            for h in range(e // HEAD_DIM):
                hat = proj[r, row * e + h * HEAD_DIM : row * e + (h + 1) * HEAD_DIM] * scale
                got = scale * (grad[r, h * HEAD_DIM : (h + 1) * HEAD_DIM] - hat * mean)
                gp[r, row * e + h * HEAD_DIM : row * e + (h + 1) * HEAD_DIM] = got.astype(bf16)

    save = local(gp, gp_ref, lsem, 9)
    loads[6].wait()

    def partial(chip, cols):
        return nt(gp[pl.ds(pl.multiple_of(chip * 2 * R, 2 * R), 2 * R), :], w[cols, :])

    total = scatter_phase(at, partial, (b0, b1, b2, b3, b4), send, recv, 0)
    loads[7].wait()

    def finish(r):
        out[r, :] = (res[r, :] + total(r)).astype(bf16)

    row_loop(R, finish)
    store = local(out, out_ref, lsem, 10)
    loads[8].wait()
    share_stats(at, F, gains, gsend, grecv, 0)
    gsum[...] = jnp.sum(gains[...], axis=0)
    local(gsum, gsum_ref, lsem, 11).wait()
    store.wait()
    save.wait()


def last_call(F, wq, wk, gv, proj, st, ins, w, res, gains):
    R, D = res.shape
    n = w.shape[1] // 4 * 3
    T, e = F * R, n // 3
    return pl.pallas_call(
        functools.partial(last_kernel, D),
        out_shape=[
            jax.ShapeDtypeStruct((R, D), bf16),
            jax.ShapeDtypeStruct((T, n), bf16),
            jax.ShapeDtypeStruct((8, D), f32),
        ],
        in_specs=[ANY] * 9,
        out_specs=[ANY] * 3,
        scratch_shapes=[
            pltpu.VMEM((T, e), f32),
            pltpu.VMEM((T, e), f32),
            pltpu.VMEM((T, 2 * e), f32),
            pltpu.VMEM((F, 8, T), f32),
            pltpu.VMEM((F, 8, T), f32),
            pltpu.VMEM((F, 8, D), f32),
            pltpu.VMEM((8, D), f32),
            pltpu.VMEM((T, n), bf16),
            pltpu.VMEM((D, n), bf16),
            pltpu.VMEM((R, D), f32),
            pltpu.VMEM((R, D), bf16),
        ]
        + scatter_scratch(R, D)
        + [dma(12), dma(SCATTER_COPIES), dma(SCATTER_COPIES), dma(F), dma(F), dma(F), dma(F)],
        compiler_params=params(5),
        cost_estimate=cost(55),
    )(wq, wk, gv, proj, st, ins, w, res, gains)


def tn(a, b):
    return lax.dot_general(a, b, (((0,), (0,)), ((), ())), preferred_element_type=f32)


def grad_kernel(*refs):
    out = refs[-1]
    start = 0
    for x_ref, dy_ref in zip(refs[:-1:2], refs[1:-1:2]):
        got = tn(x_ref[...], dy_ref[...]).astype(bf16)
        units = dy_ref.shape[1] // out.shape[-1]
        for b in range(units):
            out[(start + b,) + (0,) * (len(out.shape) - 3)] = got[:, b * out.shape[-1] : (b + 1) * out.shape[-1]]
        start += units


def grad_call(pairs, units, cols, groups):
    T, D = pairs[0][0].shape
    tile = 512
    specs, args = [], []
    for x, dy in pairs:
        specs += [
            pl.BlockSpec((T, tile), lambda g, d: (0, d)),
            pl.BlockSpec((T, dy.shape[1] // groups), lambda g, d: (0, g)),
        ]
        args += [x, dy]
    return pl.pallas_call(
        grad_kernel,
        out_shape=jax.ShapeDtypeStruct((units, groups, D, cols), bf16),
        grid=(groups, D // tile),
        in_specs=specs,
        out_specs=pl.BlockSpec((units, 1, tile, cols), lambda g, d: (0, g, d, 0)),
        compiler_params=pltpu.CompilerParams(vmem_limit_bytes=VMEM_LIMIT),
        cost_estimate=cost(12 * groups),
    )(*args)


def share_stats(at, F, st, send, recv, base):
    sent = []
    for k in range(1, F):
        to = (at.f + k) % F
        c = remote(st.at[at.f], st.at[at.f], send, recv, base + k, to)
        c.start()
        sent.append(c)
    for k in range(1, F):
        frm = (at.f - k + F) % F
        remote(st.at[frm], st.at[frm], send, recv, base + k, frm).wait_recv()
    for c in sent:
        c.wait_send()


def row_sums(a, b):
    r = lax.broadcasted_iota(jnp.int32, (8, a.shape[1]), 0)
    one, two = (r == 0).astype(f32), (r == 1).astype(f32)

    def half(sel, v):
        return lax.dot_general(
            sel, v, (((1,), (1,)), ((), ())), preferred_element_type=f32, precision=lax.Precision.HIGHEST
        )

    return half(one, a) + half(two, b)


def column(row, lanes):
    return jnp.broadcast_to(row, (lanes, row.shape[1])).T


def turn(v, cos, sin):
    return v * cos + pltpu.roll(v, HEAD_DIM // 2, 1) * sin


def seq_columns(st, c, chips, R):
    return jnp.concatenate([st[:, pl.ds(pl.multiple_of((2 * j + c) * R, R), R)] for j in range(chips)], axis=1)


def attend_kernel(width, q_ref, k_ref, v_ref, st_ref, gq_ref, gk_ref, cos_ref, sin_ref, pos_ref, posc_ref, mix_ref, qr_ref, kr_ref, lse_ref):
    c = pl.program_id(0)
    chips, R = q_ref.shape[0], q_ref.shape[2]
    L = chips * R
    sums = jnp.sum(seq_columns_all(st_ref, c, chips, R), axis=0)
    cos, sin = cos_ref[0], sin_ref[0]

    def norm_turn(ref, row, gain):
        scale = lax.rsqrt(column(sums[row : row + 1], HEAD_DIM) / width + epsilon)
        return turn(ref[...].reshape(L, HEAD_DIM) * scale * gain[...], cos, sin)

    qr = (norm_turn(q_ref, 0, gq_ref) * HEAD_DIM ** (-0.5)).astype(bf16)
    kr = norm_turn(k_ref, 1, gk_ref).astype(bf16)
    v = v_ref[...].reshape(L, HEAD_DIM).astype(bf16)
    qr_ref[...] = qr.reshape(qr_ref.shape)
    kr_ref[...] = kr.reshape(kr_ref.shape)
    pos = pos_ref[0]
    for t in range(chips):
        rows = slice(t * R, (t + 1) * R)
        s = nt(qr[rows], kr)
        s = jnp.where(posc_ref[0, rows, :1] >= pos, s, -1e30)
        top = jnp.max(s, axis=-1, keepdims=True)
        e = jnp.exp(s - top)
        total = jnp.sum(e, axis=-1, keepdims=True)
        p = (e * (1.0 / total)).astype(bf16)
        mix_ref[t, 0] = nn(p, v).astype(bf16)
        lse_ref[0, 0, rows, :] = jnp.broadcast_to(top + jnp.log(total), (R, HEAD_DIM))


def seq_columns_all(st_ref, c, chips, R):
    return jnp.concatenate(
        [st_ref[:, :, pl.ds(pl.multiple_of((2 * j + c) * R, R), R)] for j in range(chips)], axis=2
    )


def attend_specs(chips, R, heads, F, L):
    def at(offset):
        return pl.BlockSpec((chips, 1, R, HEAD_DIM), lambda c, h: (0, c, 0, offset + h))

    gain = pl.BlockSpec((1, HEAD_DIM), lambda c, h: (0, h))
    table = pl.BlockSpec((1, L, HEAD_DIM), lambda c, h: (c, 0, 0))
    stats = pl.BlockSpec((F, 8, F * R), lambda c, h: (0, 0, 0))
    posr = pl.BlockSpec((1, 1, L), lambda c, h: (c, 0, 0))
    lse = pl.BlockSpec((1, 1, L, HEAD_DIM), lambda c, h: (c, h, 0, 0))
    return at, gain, table, stats, posr, lse


def attend_call(F, proj, st, gq, gk, cos, sin, pos, posc):
    R = proj.shape[0] // F
    e = proj.shape[1] // 3
    heads, chips = e // HEAD_DIM, F // 2
    L = chips * R
    at, gain, table, stats, posr, lse = attend_specs(chips, R, heads, F, L)
    view = proj.reshape(chips, 2, R, 3 * e)
    flat = jax.ShapeDtypeStruct((chips, 2, R, e), bf16)
    out = pl.pallas_call(
        functools.partial(attend_kernel, heads * HEAD_DIM * F),
        out_shape=[flat, flat, flat, jax.ShapeDtypeStruct((2, heads, L, HEAD_DIM), f32)],
        grid=(2, heads),
        in_specs=[at(0), at(heads), at(2 * heads), stats, gain, gain, table, table, posr, table],
        out_specs=[at(0), at(0), at(0), lse],
        compiler_params=pltpu.CompilerParams(vmem_limit_bytes=VMEM_LIMIT),
        cost_estimate=cost(15),
    )(view, view, view, st, gq, gk, cos, sin, pos, posc)
    return out


def attend_back_kernel(
    width, q_ref, k_ref, v_ref, qr_ref, kr_ref, gm_ref, lse_ref, st_ref, gq_ref, gk_ref, cos_ref, sin_ref, pos_ref, posc_ref,
    wq_ref, wk_ref, gv_ref, in_ref, gg_ref, dk, dv, dq,
):
    c = pl.program_id(0)
    chips, R = q_ref.shape[0], q_ref.shape[2]
    L = chips * R
    kr = kr_ref[...].reshape(L, HEAD_DIM)
    v = v_ref[...].reshape(L, HEAD_DIM).astype(bf16)
    pos = pos_ref[0]
    dk[...] = jnp.zeros_like(dk)
    dv[...] = jnp.zeros_like(dv)
    for t in range(chips):
        rows = slice(t * R, (t + 1) * R)
        qt, gm = qr_ref[t, 0], gm_ref[t, 0]
        s = nt(qt, kr)
        s = jnp.where(posc_ref[0, rows, :1] >= pos, s, -1e30)
        p = jnp.exp(s - lse_ref[0, 0, rows, :1])
        dp = nt(gm, v)
        dv[...] += lax.dot_general(p.astype(bf16), gm, (((0,), (0,)), ((), ())), preferred_element_type=f32)
        inner = jnp.sum(dp * p, axis=-1, keepdims=True)
        ds = (p * (dp - inner)).astype(bf16)
        dq[rows, :] = nn(ds, kr)
        dk[...] += lax.dot_general(ds, qt, (((0,), (0,)), ((), ())), preferred_element_type=f32)
    gv_ref[...] = dv[...].astype(bf16).reshape(gv_ref.shape)
    sums = jnp.sum(seq_columns_all(st_ref, c, chips, R), axis=0)
    cos, sin = cos_ref[0], sin_ref[0]

    def finish(grad, ref, row, gain, out):
        norm = turn(grad, cos, -sin)
        hat = ref[...].reshape(L, HEAD_DIM) * lax.rsqrt(column(sums[row : row + 1], HEAD_DIM) / width + epsilon)
        gg_ref[0, 0, row : row + 1, :] = jnp.sum(norm * hat, axis=0, keepdims=True)
        weighted = norm * gain[...]
        out[...] = weighted.reshape(out.shape)
        return weighted * hat

    gg_ref[...] = jnp.zeros_like(gg_ref)
    in_ref[0, 0] = row_sums(
        finish(dq[...] * HEAD_DIM ** (-0.5), q_ref, 0, gq_ref, wq_ref), finish(dk[...], k_ref, 1, gk_ref, wk_ref)
    )


def attend_back_call(F, proj, qr, kr, gm, lse_in, st, gq, gk, cos, sin, pos, posc):
    R = proj.shape[0] // F
    e = proj.shape[1] // 3
    heads, chips = e // HEAD_DIM, F // 2
    L = chips * R
    at, gain, table, stats, posr, lse = attend_specs(chips, R, heads, F, L)
    view = proj.reshape(chips, 2, R, 3 * e)
    flat = (chips, 2, R, e)
    small = pl.BlockSpec((1, 1, 8, L), lambda c, h: (c, h, 0, 0))
    tiny = pl.BlockSpec((1, 1, 8, HEAD_DIM), lambda c, h: (c, h, 0, 0))
    wide = jax.ShapeDtypeStruct(flat, f32)
    return pl.pallas_call(
        functools.partial(attend_back_kernel, heads * HEAD_DIM * F),
        out_shape=[
            wide, wide, jax.ShapeDtypeStruct(flat, bf16),
            jax.ShapeDtypeStruct((2, heads, 8, L), f32),
            jax.ShapeDtypeStruct((2, heads, 8, HEAD_DIM), f32),
        ],
        grid=(2, heads),
        in_specs=[
            at(0), at(heads), at(2 * heads), at(0), at(0), at(0), lse, stats, gain, gain, table, table, posr, table,
        ],
        out_specs=[at(0), at(0), at(0), small, tiny],
        scratch_shapes=[pltpu.VMEM((L, HEAD_DIM), f32)] * 3,
        compiler_params=pltpu.CompilerParams(vmem_limit_bytes=VMEM_LIMIT),
        cost_estimate=cost(35),
    )(view, view, view, qr, kr, gm.reshape(flat), lse_in, st, gq, gk, cos, sin, pos, posc)


def newton_kernel(
    C, m_ref, rows_ref, gain_ref, grad_ref, out_ref, stage_ref, gsum_ref, back_ref,
    v, gram, y, yf, stat, gains, gsum,
    lsem, osem, vsend, vrecv, ysend, yrecv, ssend, srecv, tsend, trecv, gsend, grecv, usend, urecv, usem, bsend, brecv,
):
    me = lax.axis_index("fsdp")
    z = lax.axis_index("ctx")
    core, chip = me % 2, me // 2
    peer = me + 1 - 2 * core
    F = 2 * C
    cols = m_ref.shape[2]
    gload = local(gain_ref, gains.at[z], lsem, 1)
    barrier = pltpu.get_barrier_semaphore()
    for k in range(1, C):
        pl.semaphore_signal(barrier, inc=1, device_id={"ctx": (z + k) % C}, device_id_type=MESH)
    for k in range(1, F):
        pl.semaphore_signal(barrier, inc=1, device_id={"fsdp": (me + k) % F}, device_id_type=MESH)
    pl.semaphore_wait(barrier, C + F - 2)
    rows_in = v.shape[1] // C
    units_sent, units_kept = [], []
    for k in range(F):
        to = (me + k) % F
        for b in range(C):
            src = m_ref.at[to // 2, pl.ds((2 * b + to % 2) * rows_in, rows_in)]
            dst = v.at[0, pl.ds(b * rows_in, rows_in), pl.ds(me * cols, cols)]
            if k == 0:
                units_kept.append(local(src, dst, usem, b))
            else:
                c = remote(src, dst, usend, urecv, k * C + b, to)
                c.start()
                units_sent.append(c)
    piece = rows_ref.shape[1] // C

    def part(j):
        return pl.ds(j * piece, piece)

    sent, keep = [], [local(grad_ref.at[z], back_ref.at[z], lsem, 4)]
    for k in FAR_FIRST:
        to = partner(z, k)
        c = remote(grad_ref.at[to], back_ref.at[z], bsend, brecv, k, to, "ctx")
        c.start()
        sent.append(c)
    for a in range(2):
        for k in FAR_FIRST:
            to = partner(z, k)
            c = remote(rows_ref.at[a, part(to)], stage_ref.at[a, z], tsend, trecv, C * a + k, to, "ctx")
            c.start()
            sent.append(c)
        keep.append(local(rows_ref.at[a, part(z)], stage_ref.at[a, z], lsem, 2 + a))
    gload.wait()
    for k in range(1, C):
        c = remote(gains.at[z], gains.at[z], gsend, grecv, k, (z + k) % C, "ctx")
        c.start()
        sent.append(c)

    def rows_arrived():
        for c in keep:
            c.wait()
        for k in FAR_FIRST:
            dst = back_ref.at[partner(z, k)]
            remote(dst, dst, bsend, brecv, k, partner(z, k), "ctx").wait_recv()
        for a in range(2):
            for k in FAR_FIRST:
                dst = stage_ref.at[a, partner(z, k)]
                remote(dst, dst, tsend, trecv, C * a + k, partner(z, k), "ctx").wait_recv()
        for k in range(1, C):
            frm = (z - k + C) % C
            remote(gains.at[frm], gains.at[frm], gsend, grecv, k, frm, "ctx").wait_recv()
        gsum[...] = jnp.sum(gains[...], axis=0)
        local(gsum, gsum_ref, lsem, 6).wait()
        for c in sent:
            c.wait_send()

    for k in range(1, F):
        frm = (me - k + F) % F
        for b in range(C):
            dst = v.at[0, pl.ds(b * rows_in, rows_in), pl.ds(frm * cols, cols)]
            remote(dst, dst, usend, urecv, k * C + b, frm).wait_recv()
    for c in units_sent:
        c.wait_send()
    for c in units_kept:
        c.wait()
    M, D = v.shape[1], v.shape[2]
    tile, col = 512, 1024
    tiles = M // tile

    def block(i):
        return pl.ds(pl.multiple_of(i * tile, tile), tile)

    halves = D // col

    def swap(buf, n, i, sends, recvs):
        part = (block(i), pl.ds(n * col, col))
        return remote(buf.at[(0, *part)], buf.at[(1, *part)], sends, recvs, n * tiles + i, peer)

    pending = [swap(v, n, i, vsend, vrecv) for n in range(halves) for i in range(tiles)]
    for c in pending:
        c.start()
    stat[0] = jnp.zeros_like(stat[0])

    def add(r):
        part = v[0, r, :].astype(f32)
        stat[0] += jnp.sum((part * part).reshape(-1, 8, D // 128, 128), axis=(0, 2))

    row_loop(M, add)
    share = remote(stat.at[0], stat.at[1], ssend, srecv, 0, peer)
    share.start()
    share.wait()
    inv = 1.0 / (jnp.sqrt(jnp.sum(stat[0] + stat[1])) + 1e-07)

    for iteration in range(NS_STEPS):
        factor = inv if iteration == 0 else 1.0

        def grams(h, n):
            rhs = pl.ds(pl.multiple_of(n * col, col), col)
            cols = pl.ds(pl.multiple_of(h * M + n * col, col), col)

            @pl.loop(0, tiles)
            def _(i):
                rows = pl.ds(pl.multiple_of(i * tile, tile), tile)
                got = nt(v[0, rows, :], v[h, rhs, :])
                if iteration == 0:
                    got = got * (factor * factor)
                gram[rows, cols] = got.astype(bf16)

        @pl.loop(0, M // col)
        def _(n):
            grams(0, n)

        for c in pending:
            c.wait()

        @pl.loop(0, M // col)
        def _(n):
            grams(1, n)

        def times(src, i, n):
            rows, c = block(i), pl.ds(n * col, col)
            return nn(gram[rows, :M], src[0, :, c]) + nn(gram[rows, M:], src[1, :, c])

        swaps = []
        for n in range(halves):

            @pl.loop(0, tiles)
            def _(i):
                at = (block(i), pl.ds(n * col, col))
                got = times(v, i, n)
                if iteration == 0:
                    got = got * factor
                yf[at] = got
                y[(0, *at)] = got.astype(bf16)
                swap(y, n, i, ysend, yrecv).start()

            swaps += [swap(y, n, i, ysend, yrecv) for i in range(tiles)]
        pending = []
        for n in range(halves):
            for c in swaps[n * tiles : (n + 1) * tiles]:
                c.wait()

            @pl.loop(0, tiles)
            def _(i):
                at = (block(i), pl.ds(n * col, col))
                got = times(y, i, n)
                old = v[(0, *at)].astype(f32)
                if iteration == 0:
                    old = old * factor
                v[(0, *at)] = (quintic_one * old + quintic_two * yf[at] + quintic_three * got).astype(bf16)
                if iteration < NS_STEPS - 1:
                    swap(v, n, i, vsend, vrecv).start()

            if iteration < NS_STEPS - 1:
                pending += [swap(v, n, i, vsend, vrecv) for i in range(tiles)]
            else:
                for b in range(C):
                    for g in range(n * col // cols, (n + 1) * col // cols):
                        src = v.at[0, pl.ds(b * rows_in, rows_in), pl.ds(g * cols, cols)]
                        pending.append(local(src, out_ref.at[b * F + g], osem, b * F + g))
    rows_arrived()
    for c in pending:
        c.wait()


def newton_call(C, x, rows, gains, grads):
    _, D, cols = x.shape
    M = D // 2
    _, R, _ = rows.shape
    n = 4
    return pl.pallas_call(
        functools.partial(newton_kernel, C),
        out_shape=[
            jax.ShapeDtypeStruct((2 * C * C, M // C, cols), bf16),
            jax.ShapeDtypeStruct((2, C, R // C, D), bf16),
            jax.ShapeDtypeStruct((8, D), f32),
            jax.ShapeDtypeStruct(grads.shape, bf16),
        ],
        in_specs=[ANY] * 4,
        out_specs=[ANY] * 4,
        scratch_shapes=[
            pltpu.VMEM((2, M, D), bf16),
            pltpu.VMEM((M, 2 * M), bf16),
            pltpu.VMEM((2, M, D), bf16),
            pltpu.VMEM((M, D), f32),
            pltpu.VMEM((2, 8, 128), f32),
            pltpu.VMEM((C, 8, D), f32),
            pltpu.VMEM((8, D), f32),
            dma(7), dma(2 * C * C), dma(n), dma(n), dma(n), dma(n), dma(1), dma(1),
            dma(2 * C), dma(2 * C), dma(C), dma(C), dma(2 * C * C), dma(2 * C * C), dma(C), dma(C), dma(C),
        ],
        compiler_params=params(6),
        cost_estimate=cost(95),
    )(x, rows, gains, grads)


def project(C, F, x, w):
    own = to_layer(C, F, x)
    rows = token_rows(own)
    return own, rows, dot(rows, w, 1, 0)


def attn_out_and_up(C, F, mixed, wo, x, gain, w, cot):
    if kernels_fit(C, F):
        hidden_in, out, inp = out_call(F, mixed, wo, x, gain)
        cot, inp = lax.optimization_barrier((cot, inp))
        cot, inp = lax.optimization_barrier((move_call(C, cot), inp))
        return (cot, hidden_in, out, *up_call(F, inp, w))
    out = token_sums(dot(mixed, wo, 1, 1))
    hidden_in = x.astype(f32) + out * rms(out) * gain
    rows = token_rows(hidden_in.astype(bf16))
    g, u = jnp.split(dot(rows, w, 1, 0), 2, axis=1)
    sig = jax.nn.sigmoid(g)
    der = u * (sig * (1.0 + g * (1.0 - sig)))
    act = g * sig
    cot = to_layer(C, F, cot)
    return cot, hidden_in, out, rows, act.astype(bf16), der.astype(bf16), (act * u).astype(bf16)


def down_and_back(C, F, h, wd, hidden_in, cot, gain, act, der, units):
    if kernels_fit(C, F):
        return down_call(C, F, h, wd, hidden_in, cot, gain, act, der, units)
    out = token_sums(dot(h, wd, 1, 1))
    scale = rms(out)
    hat = out * scale
    g = cot.astype(f32)
    rows = token_rows(back(g * gain, hat, scale).astype(bf16))
    gh = dot(rows, wd, 1, 0)
    return (
        (hidden_in + hat * gain).astype(bf16),
        jnp.sum(g * hat, axis=0, keepdims=True),
        rows,
        jnp.concatenate([(gh * der.astype(f32)).astype(bf16), (gh * act.astype(f32)).astype(bf16)], axis=1),
        None,
        None,
    )


def back_to_attn(C, F, grad, w, cot, out, gain, wo):
    if kernels_fit(C, F):
        return mid_call(F, grad, w, cot, out, gain, wo)
    resid = cot.astype(f32) + token_sums(dot(grad, w, 1, 1))
    scale = rms(out)
    hat = out * scale
    rows = token_rows(back(resid * gain, hat, scale).astype(bf16))
    return resid, jnp.sum(resid * hat, axis=0, keepdims=True), rows, dot(rows, wo, 1, 0).astype(bf16)


def back_to_input(C, F, grad_projected, w, resid):
    return (resid + token_sums(dot(grad_projected, w, 1, 1))).astype(bf16)


def kernels_fit(C, F):
    return C == 4 and F == 8 and UNITS_ATTN * 4 * 2 == C * F


def to_layer(C, F, x):
    z, chip = lax.axis_index("ctx"), lax.axis_index("fsdp") // 2
    x = x.reshape(C, x.shape[0] // C, x.shape[1])
    got = []
    for k in range(C):
        pairs = [
            (s * F + f, (f // 2) * F + 2 * ((s + k) % C) + f % 2) for s in range(C) for f in range(F)
        ]
        block = lax.dynamic_index_in_dim(x, (z + k) % C, 0, keepdims=False)
        got.append(lax.ppermute(block, BOTH, pairs))
    got = jnp.stack(got)
    got = [lax.dynamic_index_in_dim(got, (chip - s + C) % C, 0, keepdims=False) for s in range(C)]
    return jnp.concatenate(got, axis=0)


def go_home(C, F, stage):
    chip = lax.axis_index("fsdp") // 2
    got = [lax.dynamic_index_in_dim(stage, chip, 1, keepdims=False)]
    for k in range(1, C):
        pairs = [(f, 2 * ((f // 2 + k) % C) + f % 2) for f in range(F)]
        block = lax.dynamic_index_in_dim(stage, (chip + k) % C, 1, keepdims=False)
        got.append(lax.ppermute(block, "fsdp", pairs))
    return got


def at_home(C, got):
    chip = lax.axis_index("fsdp") // 2
    got = jnp.stack(got)
    got = [lax.dynamic_index_in_dim(got, (chip - j + C) % C, 0, keepdims=False) for j in range(C)]
    return jnp.concatenate(got, axis=1)


def from_layer(C, F, x):
    z, chip = lax.axis_index("ctx"), lax.axis_index("fsdp") // 2
    x = x.reshape(C, x.shape[0] // C, x.shape[1])
    got = []
    for k in range(C):
        pairs = [
            ((f // 2) * F + 2 * ((s + k) % C) + f % 2, s * F + f) for s in range(C) for f in range(F)
        ]
        block = lax.dynamic_index_in_dim(x, (chip - k + C) % C, 0, keepdims=False)
        got.append(lax.ppermute(block, BOTH, pairs))
    got = jnp.stack(got)
    got = [lax.dynamic_index_in_dim(got, (j - z + C) % C, 0, keepdims=False) for j in range(C)]
    return jnp.concatenate(got, axis=0)


def shards(C, F, layer_input, cotangent, positions, w_attn, w_ffn, gains, mom_attn, mom_ffn, gain_mom):
    z = lax.axis_index("ctx")
    f = lax.axis_index("fsdp")
    local_rows, width = layer_input.shape[1], layer_input.shape[2]
    seq_total, seq_length = positions.shape
    dz, head_cols = w_attn.shape[1], w_attn.shape[2]
    local_heads = head_cols // HEAD_DIM
    block_count = w_ffn.shape[2]
    per = seq_total // C
    piece = local_rows // C
    chips = F // per
    tokens = F * local_rows
    hidden_cols = block_count * head_cols
    units = UNITS_ATTN + 3 * block_count
    parts = C * F // units

    def after(a, b):
        return lax.optimization_barrier((a, b))[0]

    def rows_gather(shard):
        return lax.all_gather(shard, "ctx", axis=0, tiled=True)

    def product(units, groups, *pairs):
        pairs = [(x.reshape(tokens, width), dy) for x, dy in pairs]
        if kernels:
            return grad_call(pairs, units, head_cols, groups)
        grad = jnp.concatenate([dot(x, dy, 0, 0).astype(bf16) for x, dy in pairs], axis=1)
        return jnp.transpose(grad.reshape(width, groups, units, head_cols), (2, 1, 0, 3))

    def scatter(grad):
        if kernels:
            return lax.psum_scatter(grad, "ctx", scatter_dimension=0, tiled=True)[0]
        return lax.psum_scatter(grad, "ctx", scatter_dimension=2, tiled=True)

    kernels = kernels_fit(C, F)
    w_heads = rows_gather(jnp.concatenate([w_attn[i] for i in range(UNITS_ATTN)], axis=1))
    w_qkv, w_out = (w_heads, w_heads) if kernels else (w_heads[:, : 3 * head_cols], w_heads[:, 3 * head_cols :])
    ffn_flat = w_ffn.reshape(3, dz, hidden_cols)
    w_gate_up = rows_gather(jnp.concatenate([ffn_flat[0], ffn_flat[1]], axis=1))
    w_down = rows_gather(ffn_flat[2])

    gain_query = lax.dynamic_slice_in_dim(gains[0], f * head_cols, head_cols)
    gain_key = lax.dynamic_slice_in_dim(gains[1], f * head_cols, head_cols)
    pos = lax.dynamic_slice_in_dim(positions, z * per, per, 0)
    pos = jnp.transpose(pos.reshape(per, C, chips, piece), (0, 2, 1, 3)).reshape(per, seq_length)
    cosine_table, sine_table = rotary_tables(pos)

    def heads(a):
        return jnp.transpose(
            a.reshape(chips, per, local_rows, local_heads, HEAD_DIM), (1, 0, 2, 3, 4)
        ).reshape(per, seq_length, local_heads, HEAD_DIM)

    def unheads(a):
        return jnp.transpose(
            a.reshape(per, chips, local_rows, local_heads, HEAD_DIM), (1, 0, 2, 3, 4)
        ).reshape(tokens, head_cols)

    if kernels:
        sign = jnp.where(jnp.arange(HEAD_DIM) < HEAD_DIM // 2, -1.0, 1.0)
        tables = (
            gain_query[None],
            gain_key[None],
            jnp.broadcast_to(cosine_table[:, :, 0], (per, seq_length, HEAD_DIM)),
            sine_table[:, :, 0] * sign,
            pos.astype(f32)[:, None, :],
            jnp.broadcast_to(pos.astype(f32)[..., None], (per, seq_length, HEAD_DIM)),
        )
        own_input, input_all = enter_call(C, F, layer_input.reshape(local_rows, width))
        projected, stats = qkv_call(F, input_all, w_qkv)
        attn_mixed, query_rows, key_rows, log_total = attend_call(F, projected, stats, *tables)
        attn_mixed = attn_mixed.reshape(tokens, head_cols)
    else:
        own_input, input_all, projected = project(C, F, layer_input.reshape(local_rows, width), w_qkv)
        query_raw = projected[:, :head_cols]
        key_raw = projected[:, head_cols : 2 * head_cols]
        value_raw = projected[:, 2 * head_cols :]
        query_total, key_total = norm_stats(
            jnp.sum(query_raw * query_raw, axis=-1), jnp.sum(key_raw * key_raw, axis=-1)
        )
        query_scale = lax.rsqrt(query_total / width + epsilon)[..., None]
        key_scale = lax.rsqrt(key_total / width + epsilon)[..., None]
        query_hat = query_raw * query_scale
        key_hat = key_raw * key_scale
        query_rows = (
            rotate(heads(query_hat * gain_query), cosine_table, sine_table) * HEAD_DIM ** (-0.5)
        ).astype(bf16)
        key_rows = rotate(heads(key_hat * gain_key), cosine_table, sine_table).astype(bf16)
        value_rows = heads(value_raw.astype(bf16))
        attn_mixed, log_total = attend(query_rows, key_rows, value_rows, pos)
        attn_mixed = unheads(attn_mixed)
    own_grad, hidden_in, attn_out, mlp_all, act, der, hidden = attn_out_and_up(
        C, F, attn_mixed, w_out, own_input, gains[2:3], w_gate_up,
        cotangent.reshape(local_rows, width),
    )
    by_layer = None
    if kernels:
        by_layer = jnp.concatenate(
            [mom_attn[:, None].astype(bf16), jnp.transpose(mom_ffn.astype(bf16), (2, 0, 1, 3))], axis=1
        )
    result, mlp_gain, grad_mlp_all, grad_ffn_in, mom_own, p_down = down_and_back(
        C, F, hidden, w_down, hidden_in, own_grad, gains[3:4], act, der, by_layer
    )
    if kernels:
        mom_own = jnp.swapaxes(mom_own, 0, 1)
    else:
        p_down = product(block_count, 1, (grad_mlp_all, hidden))
    g_down = scatter(p_down)
    p_gate_up = product(block_count, 2, (mlp_all, grad_ffn_in))
    if kernels:
        grad_ffn_in, p_gate_up = lax.optimization_barrier((grad_ffn_in, p_gate_up))
    g_gate_up = scatter(p_gate_up)
    grad_resid, attn_gain, grad_attn_all, grad_mixed = back_to_attn(
        C, F, grad_ffn_in, w_gate_up, own_grad, attn_out, gains[2:3], w_out
    )
    if kernels:
        grad_mixed = after(grad_mixed, g_down)
        weighted_q, weighted_k, grad_value, inner, gain_cols = attend_back_call(
            F, projected, query_rows, key_rows, grad_mixed, log_total, stats, *tables
        )
        inner = jnp.transpose(
            jnp.sum(inner, axis=1).reshape(per, 8, chips, local_rows), (1, 2, 0, 3)
        ).reshape(8, tokens)
        gain_cols = jnp.sum(gain_cols, axis=0)
        query_gain_cols = gain_cols[:, 0].reshape(head_cols)
        key_gain_cols = gain_cols[:, 1].reshape(head_cols)
        flat = (tokens, head_cols)
        zero = jnp.zeros((width,), f32)
        gain_local = jnp.stack(
            [
                lax.dynamic_update_slice(zero, query_gain_cols, (f * head_cols,)),
                lax.dynamic_update_slice(zero, key_gain_cols, (f * head_cols,)),
                attn_gain[0],
                mlp_gain[0],
                *[zero] * 4,
            ]
        )
        grad_rows, grad_projected, gain_layer = last_call(
            F, weighted_q.reshape(flat), weighted_k.reshape(flat), grad_value.reshape(flat),
            projected, stats, inner, w_qkv, grad_resid, gain_local,
        )
    else:
        grad_query, grad_key, grad_value = attend_back(
            query_rows, key_rows, value_rows, pos, heads(grad_mixed), log_total
        )
        grad_query_norm = unheads(unrotate(grad_query * HEAD_DIM ** (-0.5), cosine_table, sine_table))
        grad_key_norm = unheads(unrotate(grad_key, cosine_table, sine_table))
        query_gain_cols = jnp.sum(grad_query_norm * query_hat, axis=0)
        key_gain_cols = jnp.sum(grad_key_norm * key_hat, axis=0)
        query_weighted = grad_query_norm * gain_query
        key_weighted = grad_key_norm * gain_key
        query_inner, key_inner = norm_stats(
            jnp.sum(query_weighted * query_hat, axis=-1), jnp.sum(key_weighted * key_hat, axis=-1)
        )
        grad_query_raw = query_scale * (query_weighted - query_hat * (query_inner / width)[..., None])
        grad_key_raw = key_scale * (key_weighted - key_hat * (key_inner / width)[..., None])
        grad_projected = jnp.concatenate(
            [grad_query_raw.astype(bf16), grad_key_raw.astype(bf16), unheads(grad_value).astype(bf16)],
            axis=1,
        )
        grad_rows = back_to_input(C, F, grad_projected, w_qkv, grad_resid)
    g_attn = scatter(
        product(UNITS_ATTN, 1, (input_all, grad_projected), (grad_attn_all, attn_mixed))
    )
    if not kernels:
        grad_input = from_layer(C, F, grad_rows)
        result = from_layer(C, F, result)
        zero = jnp.zeros((width,), f32)
        gain_local = jnp.stack(
            [
                lax.dynamic_update_slice(zero, query_gain_cols, (f * head_cols,)),
                lax.dynamic_update_slice(zero, key_gain_cols, (f * head_cols,)),
                attn_gain[0],
                mlp_gain[0],
            ]
        )
        gain_total = jnp.sum(lax.all_gather(gain_local, BOTH, axis=0, tiled=False), axis=0)

    if kernels:
        early = jnp.stack([jnp.zeros_like(g_down[0]), g_gate_up[0], g_gate_up[1], g_down[0]])
        mom = momentum * mom_own.reshape(early.shape).astype(f32)
        owned = (mom + early.astype(f32)).astype(bf16)
        mom_first = mom[0]
        early = jnp.swapaxes(early.reshape(UNITS_ATTN, C, dz, head_cols), 0, 1)
        early, owned, mom_first, grad_rows = lax.optimization_barrier((early, owned, mom_first, grad_rows))
        late = (mom_first + g_attn[0].astype(f32)).astype(bf16)
        owned = lax.dynamic_update_slice(owned, late[None], (0, 0, 0))
        got = lax.dynamic_update_slice(early, g_attn.reshape(C, 1, dz, head_cols), (0, 0, 0, 0))
        own, leaving, gain_total, sent_back = newton_call(
            C, owned, jnp.stack([result, grad_rows]), gain_layer, got
        )
        sent_back = sent_back.astype(f32)
        grad_attn = sent_back[:, 0]
        grad_ffn = jnp.transpose(sent_back[:, 1:], (1, 2, 0, 3))
        homing = go_home(C, F, leaving)
        gain_total = gain_total[:4]
    else:
        grad_attn = g_attn[:, 0].astype(f32)
        grad_ffn = jnp.transpose(
            jnp.concatenate([g_gate_up, g_down], axis=1).astype(f32), (1, 2, 0, 3)
        )
    new_attn = momentum * mom_attn + grad_attn
    new_ffn = momentum * mom_ffn + grad_ffn
    if kernels:
        homing, new_attn, new_ffn, grad_attn, grad_ffn = lax.optimization_barrier(
            (homing, new_attn, new_ffn, grad_attn, grad_ffn)
        )
        back_rows = at_home(C, homing)
        result, grad_input = back_rows[0], back_rows[1]
    if not kernels:
        send = jnp.concatenate(
            [
                new_attn.astype(bf16),
                jnp.transpose(new_ffn.astype(bf16), (0, 2, 1, 3)).reshape(3 * block_count, dz, head_cols),
            ],
            axis=0,
        ).reshape(C * F, dz // parts, head_cols)
        own = lax.all_to_all(send, BOTH, split_axis=0, concat_axis=0, tiled=True)
        own = jnp.transpose(own.reshape(C, F, dz // parts, head_cols), (0, 2, 1, 3)).reshape(
            C * dz // parts, F * head_cols
        )

        def peers(a):
            out = [a]
            for s in range(1, parts):
                pairs = [(i, i - i % parts + (i + parts - s) % parts) for i in range(C * F)]
                out.append(lax.ppermute(a, BOTH, pairs))
            return out

        own32 = own.astype(f32)
        square = jnp.sum(own32 * own32)
        total = sum(peers(square.reshape(1, 1)))
        inv = 1.0 / (jnp.sqrt(total) + 1e-07)
        for iteration in range(NS_STEPS):
            factor = inv if iteration == 0 else 1.0
            every = peers(own)
            gram = [(dot(own, b, 1, 1) * (factor * factor)).astype(bf16) for b in every]
            product = sum(dot(g, b, 1, 0) for g, b in zip(gram, every)) * factor
            product_all = peers(product.astype(bf16))
            product_two = sum(dot(g, b, 1, 0) for g, b in zip(gram, product_all))
            own = (
                quintic_one * factor * own.astype(f32) + quintic_two * product + quintic_three * product_two
            ).astype(bf16)
    if kernels:
        home = own
    else:
        home = jnp.transpose(own.reshape(C, dz // parts, F, head_cols), (0, 2, 1, 3)).reshape(
            C * F, dz // parts, head_cols
        )
    steps = lax.all_to_all(home, BOTH, split_axis=0, concat_axis=0, tiled=True)
    if kernels:
        steps = steps.reshape(C, UNITS_ATTN, dz, head_cols)
        arranged = lax.optimization_barrier(jnp.transpose(steps[:, 1:], (1, 2, 0, 3)))
        step_attn = -muon_rate * steps[:, 0].astype(f32)
        step_ffn = -muon_rate * arranged.astype(f32)
    else:
        steps = -muon_rate * steps.astype(f32)
        steps = steps.reshape(units, dz, head_cols)
        step_attn = steps[:UNITS_ATTN]
        step_ffn = jnp.transpose(
            steps[UNITS_ATTN:].reshape(3, block_count, dz, head_cols), (0, 2, 1, 3)
        )
    new_gain_mom = momentum * gain_mom + gain_total
    return (
        result.reshape(layer_input.shape),
        grad_input.astype(f32).reshape(layer_input.shape),
        grad_attn,
        grad_ffn,
        gain_total,
        new_attn,
        new_ffn,
        new_gain_mom,
        step_attn,
        step_ffn,
        -gain_rate * new_gain_mom,
    )


def solution(mesh):
    tokens = P("fsdp", "ctx", None)
    attn = P(None, "ctx", "fsdp")
    ffn = P(None, "ctx", None, "fsdp")
    in_specs = (tokens, tokens, P(), attn, ffn, P(), attn, ffn, P())
    out_specs = (tokens, tokens, attn, ffn, P(), attn, ffn, P(), attn, ffn, P())
    body = functools.partial(shards, mesh.shape["ctx"], mesh.shape["fsdp"])
    return jax.shard_map(body, mesh=mesh, in_specs=in_specs, out_specs=out_specs, check_vma=False)
```

```python
import functools
import jax
import jax.numpy as jnp
from jax import lax
from jax.experimental import pallas as pl
from jax.experimental.pallas import tpu as pltpu
from jax.sharding import PartitionSpec as P

NS_STEPS = 3
HEAD_DIM = 128
UNITS_ATTN = 4

epsilon = 1e-06
rope_theta = 500000.0
quintic_one = 3.4445
quintic_two = -4.775
quintic_three = 2.0315
momentum = 0.95
muon_rate = 1.0
gain_rate = 0.0005
BOTH = ("ctx", "fsdp")
bf16 = jnp.bfloat16
f32 = jnp.float32


def dot(a, b, ca, cb):
    return lax.dot_general(a, b, (((ca,), (cb,)), ((), ())), preferred_element_type=f32)


def token_rows(operand):
    return lax.all_gather(operand, "fsdp", axis=0, tiled=True)


def token_sums(operand):
    return lax.psum_scatter(operand.astype(bf16), "fsdp", scatter_dimension=0, tiled=True).astype(f32)


def norm_stats(first_sum, second_sum):
    got = lax.all_gather(jnp.stack([first_sum, second_sum]), "fsdp", axis=0, tiled=False)
    total = jnp.sum(got, axis=0)
    return total[0], total[1]


def rms_back(upstream, normed, inv_scale):
    return inv_scale * (upstream - normed * jnp.mean(upstream * normed, axis=-1, keepdims=True))


def rotary_tables(slot_order):
    half_dim = HEAD_DIM // 2
    inverse = rope_theta ** (-(jnp.arange(half_dim, dtype=f32) * 2.0) / HEAD_DIM)
    angles = slot_order.astype(f32)[..., None] * inverse
    angles = jnp.concatenate([angles, angles], axis=-1)
    return (jnp.cos(angles)[..., None, :], jnp.sin(angles)[..., None, :])


def rotate(operand, cosine_table, sine_table):
    half_dim = operand.shape[-1] // 2
    flipped = jnp.concatenate([-operand[..., half_dim:], operand[..., :half_dim]], axis=-1)
    return operand * cosine_table + flipped * sine_table


def unrotate(upstream, cosine_table, sine_table):
    half_dim = upstream.shape[-1] // 2
    shifted = upstream * sine_table
    flipped = jnp.concatenate([shifted[..., half_dim:], -shifted[..., :half_dim]], axis=-1)
    return upstream * cosine_table + flipped


def masked_scores(query_rows, key_rows, pos):
    scores = jnp.einsum("gqhe,gkhe->ghqk", query_rows, key_rows, preferred_element_type=f32)
    causal = pos[:, None, :, None] >= pos[:, None, None, :]
    return jnp.where(causal, scores, -1e30)


def attend(query_rows, key_rows, value_rows, pos):
    scores = masked_scores(query_rows, key_rows, pos)
    row_max = jnp.max(scores, axis=-1, keepdims=True)
    weights = jnp.exp(scores - row_max)
    row_total = jnp.sum(weights, axis=-1, keepdims=True)
    probabilities = (weights / row_total).astype(bf16)
    attn_mixed = jnp.einsum("ghqk,gkhe->gqhe", probabilities, value_rows, preferred_element_type=f32)
    return attn_mixed.astype(bf16), row_max + jnp.log(row_total)


def attend_back(query_rows, key_rows, value_rows, pos, grad_mixed, log_total):
    scores = masked_scores(query_rows, key_rows, pos)
    probabilities = jnp.exp(scores - log_total)
    grad_probs = jnp.einsum("gqhe,gkhe->ghqk", grad_mixed, value_rows, preferred_element_type=f32)
    grad_value = jnp.einsum(
        "ghqk,gqhe->gkhe", probabilities.astype(bf16), grad_mixed, preferred_element_type=f32
    )
    inner_sum = jnp.sum(grad_probs * probabilities, axis=-1, keepdims=True)
    grad_scores = (probabilities * (grad_probs - inner_sum)).astype(bf16)
    grad_query = jnp.einsum("ghqk,gkhe->gqhe", grad_scores, key_rows, preferred_element_type=f32)
    grad_key = jnp.einsum("ghqk,gqhe->gkhe", grad_scores, query_rows, preferred_element_type=f32)
    return grad_query, grad_key, grad_value


MESH = pl.DeviceIdType.MESH
VMEM_LIMIT = 60 * 1024 * 1024
ANY = pl.BlockSpec(memory_space=pl.ANY)


class Plane:
    def __init__(self):
        f = lax.axis_index("fsdp")
        self.f, self.c, self.chip = f, f % 2, f // 2
        x, y = self.chip % 2, self.chip // 2
        self.qx = self.chip + 1 - 2 * x
        self.qy = self.chip + 2 - 4 * y
        self.qd = self.qx + 2 - 4 * y
        self.fc = f + 1 - 2 * self.c
        self.fx = 2 * self.qx + self.c
        self.fy = 2 * self.qy + self.c
        self.fd = 2 * self.qd + self.c
        self.other = 1 - self.c

    def greet(self):
        barrier = pltpu.get_barrier_semaphore()
        for to in (self.fc, self.fx, self.fy):
            pl.semaphore_signal(barrier, inc=1, device_id={"fsdp": to}, device_id_type=MESH)
        pl.semaphore_wait(barrier, 3)


def partner(i, k):
    if k == 3:
        return 3 - i
    if k == 2:
        return (i + 2) % 4
    return i + 1 - 2 * (i % 2)


FAR_FIRST = (3, 2, 1)


def remote(src, dst, send, recv, i, to, axis="fsdp"):
    return pltpu.make_async_remote_copy(
        src_ref=src, dst_ref=dst, send_sem=send.at[i], recv_sem=recv.at[i],
        device_id={axis: to}, device_id_type=MESH,
    )


def local(src, dst, sems, i):
    copy = pltpu.make_async_copy(src, dst, sems.at[i])
    copy.start()
    return copy


def nn(a, b):
    return lax.dot_general(a, b, (((1,), (0,)), ((), ())), preferred_element_type=f32)


def nt(a, b):
    return lax.dot_general(a, b, (((1,), (1,)), ((), ())), preferred_element_type=f32)


def gather_phase(at, rows, send, recv, base, on_rows):
    half = rows.shape[1] // 2
    A, B = pl.ds(0, half), pl.ds(half, half)

    def cp(i, slot, part, to):
        ref = rows.at[slot] if part is None else rows.at[slot, part]
        return remote(ref, ref, send, recv, base + i, to)

    fcx, fcy, fcd = 2 * at.qx + at.other, 2 * at.qy + at.other, 2 * at.qd + at.other
    sent = []

    def go(*a):
        c = cp(*a)
        c.start()
        sent.append(c)

    def arrived(i, slot, part, frm):
        cp(i, slot, part, frm).wait_recv()

    go(0, at.f, None, at.fc)
    go(1, at.f, A, at.fx)
    go(3, at.f, B, at.fy)
    go(2, at.f, B, at.fx)
    go(4, at.f, A, at.fy)
    arrived(0, at.fc, None, at.fc)
    on_rows(2 * at.chip, 2)
    arrived(1, at.fx, A, at.fx)
    go(5, at.fx, A, at.fy)
    go(7, at.fx, A, at.fc)
    arrived(3, at.fy, B, at.fy)
    go(6, at.fy, B, at.fx)
    go(8, at.fy, B, at.fc)
    arrived(2, at.fx, B, at.fx)
    go(9, at.fx, B, at.fc)
    arrived(4, at.fy, A, at.fy)
    go(10, at.fy, A, at.fc)
    arrived(7, fcx, A, at.fc)
    arrived(9, fcx, B, at.fc)
    on_rows(2 * at.qx, 2)
    arrived(8, fcy, B, at.fc)
    arrived(10, fcy, A, at.fc)
    on_rows(2 * at.qy, 2)
    arrived(5, at.fd, A, at.fy)
    go(11, at.fd, A, at.fc)
    arrived(6, at.fd, B, at.fx)
    go(12, at.fd, B, at.fc)
    on_rows(at.fd, 1)
    arrived(11, fcd, A, at.fc)
    arrived(12, fcd, B, at.fc)
    on_rows(fcd, 1)
    for c in sent:
        c.wait_send()


GATHER_COPIES = 13
SCATTER_COPIES = 10


def scatter_scratch(R, D):
    return [
        pltpu.VMEM((4, R, D), bf16),
        pltpu.VMEM((4, R, D), bf16),
        pltpu.VMEM((2, R, D), f32),
        pltpu.VMEM((3, R, D), bf16),
        pltpu.VMEM((3, R, D), bf16),
    ]


def scatter_phase(at, partial, bufs, send, recv, base, between=None):
    to_core, from_core, mine, out, inc = bufs
    R, D = to_core.shape[1], to_core.shape[2]
    half = R // 2
    A, B = pl.ds(0, half), pl.ds(half, half)
    tile = 512
    step = 16
    sent = []

    def go(i, src, dst, to):
        c = remote(src, dst, send, recv, base + i, to)
        c.start()
        sent.append(c)

    def arrived(i, dst, frm):
        remote(dst, dst, send, recv, base + i, frm).wait_recv()

    def compute(order, chip, slot):
        @pl.loop(0, D // tile)
        def _(n):
            cols = pl.ds(pl.multiple_of(n * tile, tile), tile)
            got = partial(chip, cols)
            lo, hi = got[:R], got[R:]
            first = at.c == 0
            mine[slot, :, cols] = jnp.where(first, lo, hi)
            to_core[order, :, cols] = jnp.where(first, hi, lo).astype(bf16)

        go(order, to_core.at[order], from_core.at[order], at.fc)

    def chip_sum(order, slot):
        arrived(order, from_core.at[order], at.fc)

        @pl.loop(0, R // step)
        def _(r):
            rows = pl.ds(pl.multiple_of(r * step, step), step)
            out[order, rows, :] = (mine[slot, rows, :] + from_core[order, rows, :].astype(f32)).astype(bf16)

    def relay(order, start, src):
        @pl.loop(0, half // step)
        def _(r):
            rows = pl.ds(pl.multiple_of(start + r * step, step), step)
            out[order, rows, :] = (out[order, rows, :].astype(f32) + inc[src, rows, :].astype(f32)).astype(bf16)

    compute(0, at.qd, 0)
    compute(1, at.qx, 1)
    if between is not None:
        between()
    chip_sum(0, 0)
    go(4, out.at[0, A], inc.at[0, A], at.fx)
    go(5, out.at[0, B], inc.at[0, B], at.fy)
    compute(2, at.qy, 0)
    chip_sum(1, 1)
    go(6, out.at[1, A], inc.at[1, A], at.fx)
    compute(3, at.chip, 1)
    chip_sum(2, 0)
    go(8, out.at[2, B], inc.at[2, B], at.fy)
    arrived(5, inc.at[0, B], at.fy)
    relay(1, half, 0)
    go(7, out.at[1, B], inc.at[1, B], at.fx)
    arrived(4, inc.at[0, A], at.fx)
    relay(2, 0, 0)
    go(9, out.at[2, A], inc.at[2, A], at.fy)
    arrived(3, from_core.at[3], at.fc)
    arrived(6, inc.at[1, A], at.fx)
    arrived(8, inc.at[2, B], at.fy)
    arrived(7, inc.at[1, B], at.fx)
    arrived(9, inc.at[2, A], at.fy)
    for c in sent:
        c.wait_send()

    def total(rows):
        return (
            mine[1, rows, :]
            + from_core[3, rows, :].astype(f32)
            + inc[1, rows, :].astype(f32)
            + inc[2, rows, :].astype(f32)
        )

    return total


def rms(v):
    return lax.rsqrt(jnp.mean(v * v, axis=-1, keepdims=True) + epsilon)


def back(weighted, normed, scale):
    return scale * (weighted - normed * jnp.mean(weighted * normed, axis=-1, keepdims=True))


def row_loop(R, body, step=16):
    @pl.loop(0, R // step)
    def _(r):
        body(pl.ds(pl.multiple_of(r * step, step), step))


def pair_loop(rows, w_cols, total_cols, body):
    @pl.loop(0, total_cols // w_cols)
    def _(t):
        body(pl.ds(pl.multiple_of(t * w_cols, w_cols), w_cols))


class Stores:
    def __init__(self, sems):
        self.sems, self.steps, self.n = sems, [], 0

    def slot(self):
        if len(self.steps) >= 2:
            for c in self.steps[-2]:
                c.wait()
            self.steps[-2] = []
        return len(self.steps) % 2

    def put(self, pairs):
        done = []
        for src, dst in pairs:
            done.append(local(src, dst, self.sems, self.n))
            self.n += 1
        self.steps.append(done)

    def finish(self):
        for step in self.steps:
            for c in step:
                c.wait()


class Moving:
    def __init__(self, at, C, mine, stage, landing, lsem, base, send, recv):
        self.at, self.C, self.mine, self.stage, self.landing = at, C, mine, stage, landing
        self.lsem, self.base, self.send, self.recv = lsem, base, send, recv
        self.z = lax.axis_index("ctx")
        self.piece = mine.shape[0] // C
        self.sent = []

    def greet(self, barrier):
        at, C = self.at, self.C
        for k in range(1, C):
            pl.semaphore_signal(barrier, inc=1, device_id={"ctx": (self.z + k) % C}, device_id_type=MESH)
            pl.semaphore_signal(
                barrier, inc=1, device_id={"fsdp": 2 * ((at.chip + k) % C) + at.c}, device_id_type=MESH
            )

    def first(self):
        at, C, piece = self.at, self.C, self.piece
        for k in FAR_FIRST:
            j = partner(at.chip, k)
            src = self.mine.at[pl.ds(j * piece, piece)]
            c = remote(src, self.stage.at[at.chip], self.send, self.recv, k, 2 * j + at.c)
            c.start()
            self.sent.append(c)
        src = self.mine.at[pl.ds(at.chip * piece, piece)]
        self.keep = local(src, self.stage.at[at.chip], self.lsem, self.base)

    def land(self, layer):
        return self.landing.at[pl.ds(layer * self.piece, self.piece)]

    def second(self):
        at, C, z = self.at, self.C, self.z
        self.keep.wait()
        for k in FAR_FIRST:
            frm = partner(at.chip, k)
            remote(self.stage.at[frm], self.stage.at[frm], self.send, self.recv, k, 2 * frm + at.c).wait_recv()
        for k in FAR_FIRST:
            to = partner(z, k)
            c = remote(self.stage.at[to], self.land(z), self.send, self.recv, C + k, to, "ctx")
            c.start()
            self.sent.append(c)
        self.keep = local(self.stage.at[z], self.land(z), self.lsem, self.base + 1)

    def finish(self):
        C, z = self.C, self.z
        self.keep.wait()
        for k in FAR_FIRST:
            frm = partner(z, k)
            remote(self.land(frm), self.land(frm), self.send, self.recv, C + k, frm, "ctx").wait_recv()
        for c in self.sent:
            c.wait_send()


def enter_kernel(C, x_ref, own_ref, all_ref, stage, mine, rows, lsem, osem, send, recv, tsend, trecv):
    at = Plane()
    load = local(x_ref, mine, lsem, 0)
    moving = Moving(at, C, mine, stage, rows.at[at.f], lsem, 1, tsend, trecv)
    barrier = pltpu.get_barrier_semaphore()
    moving.greet(barrier)
    pl.semaphore_signal(barrier, inc=1, device_id={"fsdp": at.fc}, device_id_type=MESH)
    pl.semaphore_wait(barrier, 2 * (C - 1) + 1)
    load.wait()
    moving.first()
    moving.second()
    moving.finish()
    save = local(rows.at[at.f], own_ref, lsem, 3)
    stores = []

    def on_rows(first, count):
        stores.append(local(rows.at[pl.ds(first, count)], all_ref.at[pl.ds(first, count)], osem, len(stores)))

    gather_phase(at, rows, send, recv, 0, on_rows)
    save.wait()
    for c in stores:
        c.wait()


def enter_call(C, F, x):
    R, D = x.shape
    return pl.pallas_call(
        functools.partial(enter_kernel, C),
        out_shape=[jax.ShapeDtypeStruct((R, D), bf16), jax.ShapeDtypeStruct((F, R, D), bf16)],
        in_specs=[ANY],
        out_specs=[ANY] * 2,
        scratch_shapes=[
            pltpu.VMEM((C, R // C, D), bf16),
            pltpu.VMEM((R, D), bf16),
            pltpu.VMEM((F, R, D), bf16),
            dma(4), dma(5), dma(GATHER_COPIES), dma(GATHER_COPIES), dma(2 * C), dma(2 * C),
        ],
        compiler_params=params(1),
        cost_estimate=cost(70),
    )(x)


def qkv_kernel(all_ref, w_ref, proj_ref, st_ref, rows, w, acc, st, lsem, osem, ssend, srecv):
    at = Plane()
    F, R = rows.shape[0], rows.shape[1]
    e = w.shape[1] // 3
    m = 2 * R
    loads = [local(w_ref.at[:, pl.ds(0, 3 * e)], w, lsem, 0)] + [
        local(all_ref.at[pl.ds(2 * p, 2)], rows.at[pl.ds(2 * p, 2)], lsem, 1 + p) for p in range(F // 2)
    ]
    barrier = pltpu.get_barrier_semaphore()
    for k in range(1, F):
        pl.semaphore_signal(barrier, inc=1, device_id={"fsdp": (at.f + k) % F}, device_id_type=MESH)
    pl.semaphore_wait(barrier, F - 1)
    loads[0].wait()
    stores = Stores(osem)
    for p in range(F // 2):
        loads[1 + p].wait()
        s = stores.slot()

        def tile(c):
            acc[s, :, c] = nn(rows[pl.ds(2 * p, 2)].reshape(m, rows.shape[2]), w[:, c])

        pair_loop(m, 256, w.shape[1], tile)
        q, k = acc[s, :, :e], acc[s, :, e : 2 * e]
        st[at.f, :, pl.ds(p * m, m)] = row_sums(q * q, k * k)
        stores.put([(acc.at[s], proj_ref.at[pl.ds(p * m, m)])])
    share_stats(at, F, st, ssend, srecv, 0)
    local(st, st_ref, lsem, 1 + F // 2).wait()
    stores.finish()


def params(number):
    return pltpu.CompilerParams(
        collective_id=number, has_side_effects=True, vmem_limit_bytes=VMEM_LIMIT
    )


def cost(us):
    return pl.CostEstimate(flops=int(us * 1e9), bytes_accessed=2**20, transcendentals=0)


def dma(n):
    return pltpu.SemaphoreType.DMA((n,))


def qkv_call(F, rows, w):
    _, R, D = rows.shape
    n = w.shape[1] // 4 * 3
    return pl.pallas_call(
        qkv_kernel,
        out_shape=[
            jax.ShapeDtypeStruct((F * R, n), f32),
            jax.ShapeDtypeStruct((F, 8, F * R), f32),
        ],
        in_specs=[ANY] * 2,
        out_specs=[ANY] * 2,
        scratch_shapes=[
            pltpu.VMEM((F, R, D), bf16),
            pltpu.VMEM((D, n), bf16),
            pltpu.VMEM((2, 2 * R, n), f32),
            pltpu.VMEM((F, 8, F * R), f32),
            dma(6), dma(4), dma(F), dma(F),
        ],
        compiler_params=params(7),
        cost_estimate=cost(22),
    )(rows, w)


def out_kernel(
    mixed_ref, wo_ref, x_ref, gain_ref, hid_ref, ao_ref, in_ref,
    mixed, wo, x, gain, hid, ao, inp, b0, b1, b2, b3, b4, lsem, send, recv,
):
    at = Plane()
    e = wo.shape[1]
    pairs = [(mixed_ref, mixed), (wo_ref.at[:, pl.ds(3 * e, e)], wo), (x_ref, x), (gain_ref, gain)]
    loads = [local(s, d, lsem, i) for i, (s, d) in enumerate(pairs)]
    at.greet()
    R = x.shape[0]
    loads[0].wait()
    loads[1].wait()

    def partial(chip, cols):
        return nt(mixed[pl.ds(pl.multiple_of(chip * 2 * R, 2 * R), 2 * R), :], wo[cols, :])

    total = scatter_phase(at, partial, (b0, b1, b2, b3, b4), send, recv, 0)
    loads[2].wait()
    loads[3].wait()

    def finish(r):
        out = total(r)
        ao[r, :] = out
        hidden_in = x[r, :].astype(f32) + out * rms(out) * gain[...]
        hid[r, :] = hidden_in
        inp[r, :] = hidden_in.astype(bf16)

    row_loop(R, finish)
    for c in [local(ao, ao_ref, lsem, 4), local(hid, hid_ref, lsem, 5), local(inp, in_ref, lsem, 6)]:
        c.wait()


def out_call(F, mixed, wo, x, gain):
    R, D = x.shape
    e = wo.shape[1] // 4
    return pl.pallas_call(
        out_kernel,
        out_shape=[
            jax.ShapeDtypeStruct((R, D), f32),
            jax.ShapeDtypeStruct((R, D), f32),
            jax.ShapeDtypeStruct((R, D), bf16),
        ],
        in_specs=[ANY] * 4,
        out_specs=[ANY] * 3,
        scratch_shapes=[
            pltpu.VMEM((F * R, e), bf16),
            pltpu.VMEM((D, e), bf16),
            pltpu.VMEM((R, D), bf16),
            pltpu.VMEM((1, D), f32),
            pltpu.VMEM((R, D), f32),
            pltpu.VMEM((R, D), f32),
            pltpu.VMEM((R, D), bf16),
        ]
        + scatter_scratch(R, D)
        + [dma(7), dma(SCATTER_COPIES), dma(SCATTER_COPIES)],
        compiler_params=params(8),
        cost_estimate=cost(46),
    )(mixed, wo, x, gain)


def up_kernel(
    C, in_ref, w_ref, cot_ref, all_ref, act_ref, der_ref, h_ref, moved_ref,
    w, rows, act, der, h, mine, moved, stage, lsem, osem, send, recv, tsend, trecv,
):
    at = Plane()
    cot = local(cot_ref, mine, lsem, 2)
    moving = Moving(at, C, mine, stage, moved, lsem, 3, tsend, trecv)
    own = local(in_ref, rows.at[at.f], lsem, 0)
    n = act.shape[2]
    loads = [local(w_ref, w, lsem, 1)]
    width = 256
    barrier = pltpu.get_barrier_semaphore()
    moving.greet(barrier)
    pl.semaphore_signal(barrier, inc=1, device_id={"fsdp": at.fc}, device_id_type=MESH)
    pl.semaphore_wait(barrier, 2 * (C - 1) + 1)
    R = rows.shape[1]
    cot.wait()
    moving.first()
    own.wait()
    waited = []
    stores = Stores(osem)

    def on_rows(first, count):
        s = stores.slot()
        m = count * R
        if not waited:
            for c in loads:
                c.wait()
            moving.second()
            waited.append(1)

        @pl.loop(0, n // width)
        def _(t):
            c = pl.ds(pl.multiple_of(t * width, width), width)
            lhs = rows[pl.ds(first, count)].reshape(m, rows.shape[2])
            g = nn(lhs, w[:, c])
            u = nn(lhs, w[:, pl.ds(pl.multiple_of(n + t * width, width), width)])
            sig = jax.nn.sigmoid(g)
            a = g * sig
            act[s, pl.ds(0, m), c] = a.astype(bf16)
            der[s, pl.ds(0, m), c] = (u * (sig * (1.0 + g * (1.0 - sig)))).astype(bf16)
            h[s, pl.ds(0, m), c] = (a * u).astype(bf16)

        start = pl.multiple_of(first * R, R)
        stores.put(
            [
                (act.at[s, pl.ds(0, m)], act_ref.at[pl.ds(start, m)]),
                (der.at[s, pl.ds(0, m)], der_ref.at[pl.ds(start, m)]),
                (h.at[s, pl.ds(0, m)], h_ref.at[pl.ds(start, m)]),
                (rows.at[pl.ds(first, count)], all_ref.at[pl.ds(first, count)]),
            ]
        )

    gather_phase(at, rows, send, recv, 0, on_rows)
    moving.finish()
    local(moved, moved_ref, lsem, 5).wait()
    stores.finish()


def up_call(C, F, inp, w, cot):
    R, D = inp.shape
    n = w.shape[1] // 2
    T = F * R
    wide = jax.ShapeDtypeStruct((T, n), bf16)
    return pl.pallas_call(
        functools.partial(up_kernel, C),
        out_shape=[
            jax.ShapeDtypeStruct((F, R, D), bf16), wide, wide, wide, jax.ShapeDtypeStruct((R, D), bf16),
        ],
        in_specs=[ANY] * 3,
        out_specs=[ANY] * 5,
        scratch_shapes=[
            pltpu.VMEM((D, 2 * n), bf16),
            pltpu.VMEM((F, R, D), bf16),
            pltpu.VMEM((2, 2 * R, n), bf16),
            pltpu.VMEM((2, 2 * R, n), bf16),
            pltpu.VMEM((2, 2 * R, n), bf16),
            pltpu.VMEM((R, D), bf16),
            pltpu.VMEM((R, D), bf16),
            pltpu.VMEM((C, R // C, D), bf16),
        ]
        + [dma(6), dma(20), dma(GATHER_COPIES), dma(GATHER_COPIES), dma(2 * C), dma(2 * C)],
        compiler_params=params(2),
        cost_estimate=cost(56),
    )(inp, w, cot)


def down_kernel(
    C, h_ref, wd_ref, hid_ref, cot_ref, gain_ref, act_ref, der_ref, unit_ref,
    res_ref, gg_ref, all_ref, grad_ref, mom_ref, p_ref,
    h, wd, hid, cot, gain, act, der, res, gacc, rows, grad, prod, b0, b1, b2, b3, b4,
    lsem, osem, asem, psem, send, recv, usend, urecv,
):
    at = Plane()
    loads = [
        local(s, d, lsem, i)
        for i, (s, d) in enumerate(
            [(h_ref, h), (wd_ref, wd), (hid_ref, hid), (gain_ref, gain), (cot_ref, cot)]
        )
    ]
    z = lax.axis_index("ctx")
    barrier = pltpu.get_barrier_semaphore()
    for to in (at.fc, at.fx, at.fy):
        pl.semaphore_signal(barrier, inc=1, device_id={"fsdp": to}, device_id_type=MESH)
    for k in FAR_FIRST:
        pl.semaphore_signal(barrier, inc=1, device_id={"ctx": partner(z, k)}, device_id_type=MESH)
    pl.semaphore_wait(barrier, C + 2)
    R = rows.shape[1]
    n = wd.shape[1]
    units = []

    def send_units(k):
        to = partner(z, k)
        c = remote(unit_ref.at[to], mom_ref.at[z], usend, urecv, k, to, "ctx")
        c.start()
        units.append(c)

    for k in FAR_FIRST:
        send_units(k)
    units.append(local(unit_ref.at[z], mom_ref.at[z], lsem, 5))
    loads[0].wait()
    loads[1].wait()

    def partial(chip, cols):
        return nt(h[pl.ds(pl.multiple_of(chip * 2 * R, 2 * R), 2 * R), :], wd[cols, :])

    total = scatter_phase(at, partial, (b0, b1, b2, b3, b4), send, recv, 0)
    for c in loads[2:]:
        c.wait()
    gacc[...] = jnp.zeros_like(gacc)

    def finish(r):
        out = total(r)
        scale = rms(out)
        hat = out * scale
        res[r, :] = (hid[r, :] + hat * gain[...]).astype(bf16)
        g = cot[r, :].astype(f32)
        gacc[...] += jnp.sum(g * hat, axis=0, keepdims=True)
        rows[at.f, r, :] = back(g * gain[...], hat, scale).astype(bf16)

    row_loop(R, finish)
    saves = [local(res, res_ref, lsem, 6), local(gacc, gg_ref, lsem, 7)]
    stores = Stores(osem)

    def on_rows(first, count):
        s = stores.slot()
        m = count * R
        start = pl.multiple_of(first * R, R)
        k = len(stores.steps)
        la = local(act_ref.at[pl.ds(start, m)], act.at[s, pl.ds(0, m)], asem, 2 * k)
        ld = local(der_ref.at[pl.ds(start, m)], der.at[s, pl.ds(0, m)], asem, 2 * k + 1)
        la.wait()
        ld.wait()

        width = 512

        @pl.loop(0, n // width)
        def _(t):
            c = pl.ds(pl.multiple_of(t * width, width), width)
            up = pl.ds(pl.multiple_of(n + t * width, width), width)
            gh = nn(rows[pl.ds(first, count)].reshape(m, rows.shape[2]), wd[:, c])
            grad[s, pl.ds(0, m), up] = (gh * act[s, pl.ds(0, m), c].astype(f32)).astype(bf16)
            grad[s, pl.ds(0, m), c] = (gh * der[s, pl.ds(0, m), c].astype(f32)).astype(bf16)

        stores.put(
            [
                (grad.at[s, pl.ds(0, m)], grad_ref.at[pl.ds(start, m)]),
                (rows.at[pl.ds(first, count)], all_ref.at[pl.ds(first, count)]),
            ]
        )

    gather_phase(at, rows, send, recv, SCATTER_COPIES, on_rows)
    F, D = rows.shape[0], rows.shape[2]
    tile, cols = prod.shape[1], p_ref.shape[3]
    puts = []
    for t in range(D // tile):
        if t >= 2:
            for c in puts[t - 2]:
                c.wait()
        rhs = rows[:, :, t * tile : (t + 1) * tile].reshape(F * R, tile)
        prod[t % 2] = lax.dot_general(
            rhs, h[...], (((0,), (0,)), ((), ())), preferred_element_type=f32
        ).astype(bf16)
        puts.append(
            [
                local(
                    prod.at[t % 2, :, pl.ds(b * cols, cols)],
                    p_ref.at[b, 0, pl.ds(t * tile, tile)],
                    psem,
                    t * (n // cols) + b,
                )
                for b in range(n // cols)
            ]
        )
    for step in puts[-2:]:
        for c in step:
            c.wait()
    for k in FAR_FIRST:
        frm = partner(z, k)
        remote(mom_ref.at[frm], mom_ref.at[frm], usend, urecv, k, frm, "ctx").wait_recv()
    for c in units[:-1]:
        c.wait_send()
    units[-1].wait()
    for s in saves:
        s.wait()
    stores.finish()


def down_call(C, F, h, wd, hid, cot, gain, act, der, units):
    R, D = hid.shape
    n = wd.shape[1]
    T = F * R
    copies = SCATTER_COPIES + GATHER_COPIES
    one = jax.ShapeDtypeStruct((R, D), bf16)
    return pl.pallas_call(
        functools.partial(down_kernel, C),
        out_shape=[
            one,
            jax.ShapeDtypeStruct((1, D), f32),
            jax.ShapeDtypeStruct((F, R, D), bf16),
            jax.ShapeDtypeStruct((T, 2 * n), bf16),
            jax.ShapeDtypeStruct(units.shape, bf16),
            jax.ShapeDtypeStruct((units.shape[1], 1, D, units.shape[3]), bf16),
        ],
        in_specs=[ANY] * 8,
        out_specs=[ANY] * 6,
        scratch_shapes=[
            pltpu.VMEM((T, n), bf16),
            pltpu.VMEM((D, n), bf16),
            pltpu.VMEM((R, D), f32),
            pltpu.VMEM((R, D), bf16),
            pltpu.VMEM((1, D), f32),
            pltpu.VMEM((2, 2 * R, n), bf16),
            pltpu.VMEM((2, 2 * R, n), bf16),
            pltpu.VMEM((R, D), bf16),
            pltpu.VMEM((1, D), f32),
            pltpu.VMEM((F, R, D), bf16),
            pltpu.VMEM((2, 2 * R, 2 * n), bf16),
            pltpu.VMEM((2, 512, n), bf16),
        ]
        + scatter_scratch(R, D)
        + [dma(8), dma(15), dma(10), dma(16), dma(copies), dma(copies), dma(C), dma(C)],
        compiler_params=params(3),
        cost_estimate=cost(108),
    )(h, wd, hid, cot, gain, act, der, units)


def mid_kernel(
    grad_ref, w_ref, cot_ref, ao_ref, gain_ref, wo_ref,
    res_ref, gg_ref, all_ref, gm_ref,
    grad, w, cot, ao, gain, wo, res, gacc, rows, gm, b0, b1, b2, b3, b4,
    lsem, osem, send, recv,
):
    at = Plane()
    e = wo.shape[1]
    pairs = [
        (grad_ref, grad), (w_ref, w),
        (cot_ref, cot), (ao_ref, ao), (gain_ref, gain), (wo_ref.at[:, pl.ds(3 * e, e)], wo),
    ]
    loads = [local(s, d, lsem, i) for i, (s, d) in enumerate(pairs)]
    at.greet()
    R = rows.shape[1]
    for c in loads[:2]:
        c.wait()

    def partial(chip, cols):
        return nt(grad[pl.ds(pl.multiple_of(chip * 2 * R, 2 * R), 2 * R), :], w[cols, :])

    total = scatter_phase(at, partial, (b0, b1, b2, b3, b4), send, recv, 0)
    for c in loads[2:]:
        c.wait()
    gacc[...] = jnp.zeros_like(gacc)

    def finish(r):
        resid = cot[r, :].astype(f32) + total(r)
        res[r, :] = resid
        out = ao[r, :]
        scale = rms(out)
        hat = out * scale
        gacc[...] += jnp.sum(resid * hat, axis=0, keepdims=True)
        rows[at.f, r, :] = back(resid * gain[...], hat, scale).astype(bf16)

    row_loop(R, finish)
    saves = [local(res, res_ref, lsem, 8), local(gacc, gg_ref, lsem, 9)]
    stores = Stores(osem)

    def on_rows(first, count):
        s = stores.slot()
        m = count * R
        start = pl.multiple_of(first * R, R)
        lhs = rows[pl.ds(first, count)].reshape(m, rows.shape[2])
        gm[s, pl.ds(0, m), :] = nn(lhs, wo[...]).astype(bf16)
        stores.put(
            [
                (gm.at[s, pl.ds(0, m)], gm_ref.at[pl.ds(start, m)]),
                (rows.at[pl.ds(first, count)], all_ref.at[pl.ds(first, count)]),
            ]
        )

    gather_phase(at, rows, send, recv, SCATTER_COPIES, on_rows)
    for s in saves:
        s.wait()
    stores.finish()


def mid_call(F, grad, w, cot, ao, gain, wo):
    R, D = cot.shape
    n, e = w.shape[1], wo.shape[1] // 4
    T = F * R
    copies = SCATTER_COPIES + GATHER_COPIES
    return pl.pallas_call(
        mid_kernel,
        out_shape=[
            jax.ShapeDtypeStruct((R, D), f32),
            jax.ShapeDtypeStruct((1, D), f32),
            jax.ShapeDtypeStruct((F, R, D), bf16),
            jax.ShapeDtypeStruct((T, e), bf16),
        ],
        in_specs=[ANY] * 6,
        out_specs=[ANY] * 4,
        scratch_shapes=[
            pltpu.VMEM((T, n), bf16),
            pltpu.VMEM((D, n), bf16),
            pltpu.VMEM((R, D), bf16),
            pltpu.VMEM((R, D), f32),
            pltpu.VMEM((1, D), f32),
            pltpu.VMEM((D, e), bf16),
            pltpu.VMEM((R, D), f32),
            pltpu.VMEM((1, D), f32),
            pltpu.VMEM((F, R, D), bf16),
            pltpu.VMEM((2, 2 * R, e), bf16),
        ]
        + scatter_scratch(R, D)
        + [dma(10), dma(10), dma(copies), dma(copies)],
        compiler_params=params(4),
        cost_estimate=cost(92),
    )(grad, w, cot, ao, gain, wo)


def last_kernel(
    width, q_ref, k_ref, v_ref, proj_ref, st_ref, in_ref, w_ref, res_ref, gain_ref,
    out_ref, gp_ref, gsum_ref,
    q, k, proj, st, ins, gains, gsum, gp, w, res, out, b0, b1, b2, b3, b4,
    lsem, send, recv, ssend, srecv, gsend, grecv,
):
    at = Plane()
    F, T = st.shape[0], st.shape[2]
    e = q.shape[1]
    R = res.shape[0]
    pairs = [
        (in_ref, ins.at[at.f]), (st_ref, st), (q_ref, q), (k_ref, k),
        (v_ref, gp.at[:, pl.ds(2 * e, e)]), (proj_ref.at[:, pl.ds(0, 2 * e)], proj), (w_ref.at[:, pl.ds(0, 3 * e)], w), (res_ref, res),
        (gain_ref, gains.at[at.f]),
    ]
    loads = [local(s, d, lsem, i) for i, (s, d) in enumerate(pairs)]
    barrier = pltpu.get_barrier_semaphore()
    for s in range(1, F):
        pl.semaphore_signal(barrier, inc=1, device_id={"fsdp": (at.f + s) % F}, device_id_type=MESH)
    pl.semaphore_wait(barrier, F - 1)
    loads[0].wait()
    share_stats(at, F, ins, ssend, srecv, 0)
    for c in loads[1:6]:
        c.wait()
    step = 256

    @pl.loop(0, T // step)
    def _(t):
        r = pl.ds(pl.multiple_of(t * step, step), step)
        sums = jnp.sum(st[:, :, r], axis=0)
        inner = jnp.sum(ins[:, :, r], axis=0) / width
        for row, grad in ((0, q), (1, k)):
            scale = lax.rsqrt(column(sums[row : row + 1], HEAD_DIM) / width + epsilon)
            mean = column(inner[row : row + 1], HEAD_DIM)
            for h in range(e // HEAD_DIM):
                hat = proj[r, row * e + h * HEAD_DIM : row * e + (h + 1) * HEAD_DIM] * scale
                got = scale * (grad[r, h * HEAD_DIM : (h + 1) * HEAD_DIM] - hat * mean)
                gp[r, row * e + h * HEAD_DIM : row * e + (h + 1) * HEAD_DIM] = got.astype(bf16)

    save = local(gp, gp_ref, lsem, 9)
    loads[6].wait()

    def partial(chip, cols):
        return nt(gp[pl.ds(pl.multiple_of(chip * 2 * R, 2 * R), 2 * R), :], w[cols, :])

    total = scatter_phase(at, partial, (b0, b1, b2, b3, b4), send, recv, 0)
    loads[7].wait()

    def finish(r):
        out[r, :] = (res[r, :] + total(r)).astype(bf16)

    row_loop(R, finish)
    store = local(out, out_ref, lsem, 10)
    loads[8].wait()
    share_stats(at, F, gains, gsend, grecv, 0)
    gsum[...] = jnp.sum(gains[...], axis=0)
    local(gsum, gsum_ref, lsem, 11).wait()
    store.wait()
    save.wait()


def last_call(F, wq, wk, gv, proj, st, ins, w, res, gains):
    R, D = res.shape
    n = w.shape[1] // 4 * 3
    T, e = F * R, n // 3
    return pl.pallas_call(
        functools.partial(last_kernel, D),
        out_shape=[
            jax.ShapeDtypeStruct((R, D), bf16),
            jax.ShapeDtypeStruct((T, n), bf16),
            jax.ShapeDtypeStruct((8, D), f32),
        ],
        in_specs=[ANY] * 9,
        out_specs=[ANY] * 3,
        scratch_shapes=[
            pltpu.VMEM((T, e), f32),
            pltpu.VMEM((T, e), f32),
            pltpu.VMEM((T, 2 * e), f32),
            pltpu.VMEM((F, 8, T), f32),
            pltpu.VMEM((F, 8, T), f32),
            pltpu.VMEM((F, 8, D), f32),
            pltpu.VMEM((8, D), f32),
            pltpu.VMEM((T, n), bf16),
            pltpu.VMEM((D, n), bf16),
            pltpu.VMEM((R, D), f32),
            pltpu.VMEM((R, D), bf16),
        ]
        + scatter_scratch(R, D)
        + [dma(12), dma(SCATTER_COPIES), dma(SCATTER_COPIES), dma(F), dma(F), dma(F), dma(F)],
        compiler_params=params(5),
        cost_estimate=cost(55),
    )(wq, wk, gv, proj, st, ins, w, res, gains)


def tn(a, b):
    return lax.dot_general(a, b, (((0,), (0,)), ((), ())), preferred_element_type=f32)


def grad_kernel(*refs):
    out = refs[-1]
    start = 0
    for x_ref, dy_ref in zip(refs[:-1:2], refs[1:-1:2]):
        got = tn(x_ref[...], dy_ref[...]).astype(bf16)
        units = dy_ref.shape[1] // out.shape[-1]
        for b in range(units):
            out[(start + b,) + (0,) * (len(out.shape) - 3)] = got[:, b * out.shape[-1] : (b + 1) * out.shape[-1]]
        start += units


def grad_call(pairs, units, cols, groups):
    T, D = pairs[0][0].shape
    tile = 512
    specs, args = [], []
    for x, dy in pairs:
        specs += [
            pl.BlockSpec((T, tile), lambda g, d: (0, d)),
            pl.BlockSpec((T, dy.shape[1] // groups), lambda g, d: (0, g)),
        ]
        args += [x, dy]
    return pl.pallas_call(
        grad_kernel,
        out_shape=jax.ShapeDtypeStruct((units, groups, D, cols), bf16),
        grid=(groups, D // tile),
        in_specs=specs,
        out_specs=pl.BlockSpec((units, 1, tile, cols), lambda g, d: (0, g, d, 0)),
        compiler_params=pltpu.CompilerParams(vmem_limit_bytes=VMEM_LIMIT),
        cost_estimate=cost(12 * groups),
    )(*args)


def share_stats(at, F, st, send, recv, base):
    sent = []
    for k in range(1, F):
        to = (at.f + k) % F
        c = remote(st.at[at.f], st.at[at.f], send, recv, base + k, to)
        c.start()
        sent.append(c)
    for k in range(1, F):
        frm = (at.f - k + F) % F
        remote(st.at[frm], st.at[frm], send, recv, base + k, frm).wait_recv()
    for c in sent:
        c.wait_send()


def row_sums(a, b):
    r = lax.broadcasted_iota(jnp.int32, (8, a.shape[1]), 0)
    one, two = (r == 0).astype(f32), (r == 1).astype(f32)

    def half(sel, v):
        return lax.dot_general(
            sel, v, (((1,), (1,)), ((), ())), preferred_element_type=f32, precision=lax.Precision.HIGHEST
        )

    return half(one, a) + half(two, b)


def column(row, lanes):
    return jnp.broadcast_to(row, (lanes, row.shape[1])).T


def turn(v, cos, sin):
    return v * cos + pltpu.roll(v, HEAD_DIM // 2, 1) * sin


def seq_columns(st, c, chips, R):
    return jnp.concatenate([st[:, pl.ds(pl.multiple_of((2 * j + c) * R, R), R)] for j in range(chips)], axis=1)


def attend_kernel(width, q_ref, k_ref, v_ref, st_ref, gq_ref, gk_ref, cos_ref, sin_ref, pos_ref, posc_ref, mix_ref, qr_ref, kr_ref, lse_ref):
    c = pl.program_id(0)
    chips, R = q_ref.shape[0], q_ref.shape[2]
    L = chips * R
    sums = jnp.sum(seq_columns_all(st_ref, c, chips, R), axis=0)
    cos, sin = cos_ref[0], sin_ref[0]

    def norm_turn(ref, row, gain):
        scale = lax.rsqrt(column(sums[row : row + 1], HEAD_DIM) / width + epsilon)
        return turn(ref[...].reshape(L, HEAD_DIM) * scale * gain[...], cos, sin)

    qr = (norm_turn(q_ref, 0, gq_ref) * HEAD_DIM ** (-0.5)).astype(bf16)
    kr = norm_turn(k_ref, 1, gk_ref).astype(bf16)
    v = v_ref[...].reshape(L, HEAD_DIM).astype(bf16)
    qr_ref[...] = qr.reshape(qr_ref.shape)
    kr_ref[...] = kr.reshape(kr_ref.shape)
    pos = pos_ref[0]
    for t in range(chips):
        rows = slice(t * R, (t + 1) * R)
        s = nt(qr[rows], kr)
        s = jnp.where(posc_ref[0, rows, :1] >= pos, s, -1e30)
        top = jnp.max(s, axis=-1, keepdims=True)
        e = jnp.exp(s - top)
        total = jnp.sum(e, axis=-1, keepdims=True)
        p = (e * (1.0 / total)).astype(bf16)
        mix_ref[t, 0] = nn(p, v).astype(bf16)
        lse_ref[0, 0, rows, :] = jnp.broadcast_to(top + jnp.log(total), (R, HEAD_DIM))


def seq_columns_all(st_ref, c, chips, R):
    return jnp.concatenate(
        [st_ref[:, :, pl.ds(pl.multiple_of((2 * j + c) * R, R), R)] for j in range(chips)], axis=2
    )


def attend_specs(chips, R, heads, F, L):
    def at(offset):
        return pl.BlockSpec((chips, 1, R, HEAD_DIM), lambda c, h: (0, c, 0, offset + h))

    gain = pl.BlockSpec((1, HEAD_DIM), lambda c, h: (0, h))
    table = pl.BlockSpec((1, L, HEAD_DIM), lambda c, h: (c, 0, 0))
    stats = pl.BlockSpec((F, 8, F * R), lambda c, h: (0, 0, 0))
    posr = pl.BlockSpec((1, 1, L), lambda c, h: (c, 0, 0))
    lse = pl.BlockSpec((1, 1, L, HEAD_DIM), lambda c, h: (c, h, 0, 0))
    return at, gain, table, stats, posr, lse


def attend_call(F, proj, st, gq, gk, cos, sin, pos, posc):
    R = proj.shape[0] // F
    e = proj.shape[1] // 3
    heads, chips = e // HEAD_DIM, F // 2
    L = chips * R
    at, gain, table, stats, posr, lse = attend_specs(chips, R, heads, F, L)
    view = proj.reshape(chips, 2, R, 3 * e)
    flat = jax.ShapeDtypeStruct((chips, 2, R, e), bf16)
    out = pl.pallas_call(
        functools.partial(attend_kernel, heads * HEAD_DIM * F),
        out_shape=[flat, flat, flat, jax.ShapeDtypeStruct((2, heads, L, HEAD_DIM), f32)],
        grid=(2, heads),
        in_specs=[at(0), at(heads), at(2 * heads), stats, gain, gain, table, table, posr, table],
        out_specs=[at(0), at(0), at(0), lse],
        compiler_params=pltpu.CompilerParams(vmem_limit_bytes=VMEM_LIMIT),
        cost_estimate=cost(15),
    )(view, view, view, st, gq, gk, cos, sin, pos, posc)
    return out


def attend_back_kernel(
    width, q_ref, k_ref, v_ref, qr_ref, kr_ref, gm_ref, lse_ref, st_ref, gq_ref, gk_ref, cos_ref, sin_ref, pos_ref, posc_ref,
    wq_ref, wk_ref, gv_ref, in_ref, gg_ref, dk, dv, dq,
):
    c = pl.program_id(0)
    chips, R = q_ref.shape[0], q_ref.shape[2]
    L = chips * R
    kr = kr_ref[...].reshape(L, HEAD_DIM)
    v = v_ref[...].reshape(L, HEAD_DIM).astype(bf16)
    pos = pos_ref[0]
    dk[...] = jnp.zeros_like(dk)
    dv[...] = jnp.zeros_like(dv)
    for t in range(chips):
        rows = slice(t * R, (t + 1) * R)
        qt, gm = qr_ref[t, 0], gm_ref[t, 0]
        s = nt(qt, kr)
        s = jnp.where(posc_ref[0, rows, :1] >= pos, s, -1e30)
        p = jnp.exp(s - lse_ref[0, 0, rows, :1])
        dp = nt(gm, v)
        dv[...] += lax.dot_general(p.astype(bf16), gm, (((0,), (0,)), ((), ())), preferred_element_type=f32)
        inner = jnp.sum(dp * p, axis=-1, keepdims=True)
        ds = (p * (dp - inner)).astype(bf16)
        dq[rows, :] = nn(ds, kr)
        dk[...] += lax.dot_general(ds, qt, (((0,), (0,)), ((), ())), preferred_element_type=f32)
    gv_ref[...] = dv[...].astype(bf16).reshape(gv_ref.shape)
    sums = jnp.sum(seq_columns_all(st_ref, c, chips, R), axis=0)
    cos, sin = cos_ref[0], sin_ref[0]

    def finish(grad, ref, row, gain, out):
        norm = turn(grad, cos, -sin)
        hat = ref[...].reshape(L, HEAD_DIM) * lax.rsqrt(column(sums[row : row + 1], HEAD_DIM) / width + epsilon)
        gg_ref[0, 0, row : row + 1, :] = jnp.sum(norm * hat, axis=0, keepdims=True)
        weighted = norm * gain[...]
        out[...] = weighted.reshape(out.shape)
        return weighted * hat

    gg_ref[...] = jnp.zeros_like(gg_ref)
    in_ref[0, 0] = row_sums(
        finish(dq[...] * HEAD_DIM ** (-0.5), q_ref, 0, gq_ref, wq_ref), finish(dk[...], k_ref, 1, gk_ref, wk_ref)
    )


def attend_back_call(F, proj, qr, kr, gm, lse_in, st, gq, gk, cos, sin, pos, posc):
    R = proj.shape[0] // F
    e = proj.shape[1] // 3
    heads, chips = e // HEAD_DIM, F // 2
    L = chips * R
    at, gain, table, stats, posr, lse = attend_specs(chips, R, heads, F, L)
    view = proj.reshape(chips, 2, R, 3 * e)
    flat = (chips, 2, R, e)
    small = pl.BlockSpec((1, 1, 8, L), lambda c, h: (c, h, 0, 0))
    tiny = pl.BlockSpec((1, 1, 8, HEAD_DIM), lambda c, h: (c, h, 0, 0))
    wide = jax.ShapeDtypeStruct(flat, f32)
    return pl.pallas_call(
        functools.partial(attend_back_kernel, heads * HEAD_DIM * F),
        out_shape=[
            wide, wide, jax.ShapeDtypeStruct(flat, bf16),
            jax.ShapeDtypeStruct((2, heads, 8, L), f32),
            jax.ShapeDtypeStruct((2, heads, 8, HEAD_DIM), f32),
        ],
        grid=(2, heads),
        in_specs=[
            at(0), at(heads), at(2 * heads), at(0), at(0), at(0), lse, stats, gain, gain, table, table, posr, table,
        ],
        out_specs=[at(0), at(0), at(0), small, tiny],
        scratch_shapes=[pltpu.VMEM((L, HEAD_DIM), f32)] * 3,
        compiler_params=pltpu.CompilerParams(vmem_limit_bytes=VMEM_LIMIT),
        cost_estimate=cost(35),
    )(view, view, view, qr, kr, gm.reshape(flat), lse_in, st, gq, gk, cos, sin, pos, posc)


def newton_kernel(
    C, m_ref, rows_ref, gain_ref, grad_ref, out_ref, stage_ref, gsum_ref, back_ref,
    v, gram, y, yf, stat, gains, gsum,
    lsem, osem, vsend, vrecv, ysend, yrecv, ssend, srecv, tsend, trecv, gsend, grecv, usend, urecv, usem, bsend, brecv,
):
    me = lax.axis_index("fsdp")
    z = lax.axis_index("ctx")
    core, chip = me % 2, me // 2
    peer = me + 1 - 2 * core
    F = 2 * C
    cols = m_ref.shape[2]
    gload = local(gain_ref, gains.at[z], lsem, 1)
    barrier = pltpu.get_barrier_semaphore()
    for k in range(1, C):
        pl.semaphore_signal(barrier, inc=1, device_id={"ctx": (z + k) % C}, device_id_type=MESH)
    for k in range(1, F):
        pl.semaphore_signal(barrier, inc=1, device_id={"fsdp": (me + k) % F}, device_id_type=MESH)
    pl.semaphore_wait(barrier, C + F - 2)
    rows_in = v.shape[1] // C
    units_sent, units_kept = [], []
    for k in range(F):
        to = (me + k) % F
        for b in range(C):
            src = m_ref.at[to // 2, pl.ds((2 * b + to % 2) * rows_in, rows_in)]
            dst = v.at[0, pl.ds(b * rows_in, rows_in), pl.ds(me * cols, cols)]
            if k == 0:
                units_kept.append(local(src, dst, usem, b))
            else:
                c = remote(src, dst, usend, urecv, k * C + b, to)
                c.start()
                units_sent.append(c)
    piece = rows_ref.shape[1] // C

    def part(j):
        return pl.ds(j * piece, piece)

    sent, keep = [], [local(grad_ref.at[z], back_ref.at[z], lsem, 4)]
    for k in FAR_FIRST:
        to = partner(z, k)
        c = remote(grad_ref.at[to], back_ref.at[z], bsend, brecv, k, to, "ctx")
        c.start()
        sent.append(c)
    for a in range(2):
        for k in FAR_FIRST:
            to = partner(z, k)
            c = remote(rows_ref.at[a, part(to)], stage_ref.at[a, z], tsend, trecv, C * a + k, to, "ctx")
            c.start()
            sent.append(c)
        keep.append(local(rows_ref.at[a, part(z)], stage_ref.at[a, z], lsem, 2 + a))
    gload.wait()
    for k in range(1, C):
        c = remote(gains.at[z], gains.at[z], gsend, grecv, k, (z + k) % C, "ctx")
        c.start()
        sent.append(c)

    def rows_arrived():
        for c in keep:
            c.wait()
        for k in FAR_FIRST:
            dst = back_ref.at[partner(z, k)]
            remote(dst, dst, bsend, brecv, k, partner(z, k), "ctx").wait_recv()
        for a in range(2):
            for k in FAR_FIRST:
                dst = stage_ref.at[a, partner(z, k)]
                remote(dst, dst, tsend, trecv, C * a + k, partner(z, k), "ctx").wait_recv()
        for k in range(1, C):
            frm = (z - k + C) % C
            remote(gains.at[frm], gains.at[frm], gsend, grecv, k, frm, "ctx").wait_recv()
        gsum[...] = jnp.sum(gains[...], axis=0)
        local(gsum, gsum_ref, lsem, 6).wait()
        for c in sent:
            c.wait_send()

    for k in range(1, F):
        frm = (me - k + F) % F
        for b in range(C):
            dst = v.at[0, pl.ds(b * rows_in, rows_in), pl.ds(frm * cols, cols)]
            remote(dst, dst, usend, urecv, k * C + b, frm).wait_recv()
    for c in units_sent:
        c.wait_send()
    for c in units_kept:
        c.wait()
    M, D = v.shape[1], v.shape[2]
    tile, col = 512, 1024
    tiles = M // tile

    def block(i):
        return pl.ds(pl.multiple_of(i * tile, tile), tile)

    halves = D // col

    def swap(buf, n, i, sends, recvs):
        part = (block(i), pl.ds(n * col, col))
        return remote(buf.at[(0, *part)], buf.at[(1, *part)], sends, recvs, n * tiles + i, peer)

    pending = [swap(v, n, i, vsend, vrecv) for n in range(halves) for i in range(tiles)]
    for c in pending:
        c.start()
    stat[0] = jnp.zeros_like(stat[0])

    def add(r):
        part = v[0, r, :].astype(f32)
        stat[0] += jnp.sum((part * part).reshape(-1, 8, D // 128, 128), axis=(0, 2))

    row_loop(M, add)
    share = remote(stat.at[0], stat.at[1], ssend, srecv, 0, peer)
    share.start()
    share.wait()
    inv = 1.0 / (jnp.sqrt(jnp.sum(stat[0] + stat[1])) + 1e-07)

    for iteration in range(NS_STEPS):
        factor = inv if iteration == 0 else 1.0

        def grams(h, n):
            rhs = pl.ds(pl.multiple_of(n * col, col), col)
            cols = pl.ds(pl.multiple_of(h * M + n * col, col), col)

            @pl.loop(0, tiles)
            def _(i):
                rows = pl.ds(pl.multiple_of(i * tile, tile), tile)
                got = nt(v[0, rows, :], v[h, rhs, :])
                if iteration == 0:
                    got = got * (factor * factor)
                gram[rows, cols] = got.astype(bf16)

        @pl.loop(0, M // col)
        def _(n):
            grams(0, n)

        for c in pending:
            c.wait()

        @pl.loop(0, M // col)
        def _(n):
            grams(1, n)

        def times(src, i, n):
            rows, c = block(i), pl.ds(n * col, col)
            return nn(gram[rows, :M], src[0, :, c]) + nn(gram[rows, M:], src[1, :, c])

        swaps = []
        for n in range(halves):

            @pl.loop(0, tiles)
            def _(i):
                at = (block(i), pl.ds(n * col, col))
                got = times(v, i, n)
                if iteration == 0:
                    got = got * factor
                yf[at] = got
                y[(0, *at)] = got.astype(bf16)
                swap(y, n, i, ysend, yrecv).start()

            swaps += [swap(y, n, i, ysend, yrecv) for i in range(tiles)]
        pending = []
        for n in range(halves):
            for c in swaps[n * tiles : (n + 1) * tiles]:
                c.wait()

            @pl.loop(0, tiles)
            def _(i):
                at = (block(i), pl.ds(n * col, col))
                got = times(y, i, n)
                old = v[(0, *at)].astype(f32)
                if iteration == 0:
                    old = old * factor
                v[(0, *at)] = (quintic_one * old + quintic_two * yf[at] + quintic_three * got).astype(bf16)
                if iteration < NS_STEPS - 1:
                    swap(v, n, i, vsend, vrecv).start()

            if iteration < NS_STEPS - 1:
                pending += [swap(v, n, i, vsend, vrecv) for i in range(tiles)]
            else:
                for b in range(C):
                    for g in range(n * col // cols, (n + 1) * col // cols):
                        src = v.at[0, pl.ds(b * rows_in, rows_in), pl.ds(g * cols, cols)]
                        pending.append(local(src, out_ref.at[b * F + g], osem, b * F + g))
    rows_arrived()
    for c in pending:
        c.wait()


def newton_call(C, x, rows, gains, grads):
    _, D, cols = x.shape
    M = D // 2
    _, R, _ = rows.shape
    n = 4
    return pl.pallas_call(
        functools.partial(newton_kernel, C),
        out_shape=[
            jax.ShapeDtypeStruct((2 * C * C, M // C, cols), bf16),
            jax.ShapeDtypeStruct((2, C, R // C, D), bf16),
            jax.ShapeDtypeStruct((8, D), f32),
            jax.ShapeDtypeStruct(grads.shape, bf16),
        ],
        in_specs=[ANY] * 4,
        out_specs=[ANY] * 4,
        scratch_shapes=[
            pltpu.VMEM((2, M, D), bf16),
            pltpu.VMEM((M, 2 * M), bf16),
            pltpu.VMEM((2, M, D), bf16),
            pltpu.VMEM((M, D), f32),
            pltpu.VMEM((2, 8, 128), f32),
            pltpu.VMEM((C, 8, D), f32),
            pltpu.VMEM((8, D), f32),
            dma(7), dma(2 * C * C), dma(n), dma(n), dma(n), dma(n), dma(1), dma(1),
            dma(2 * C), dma(2 * C), dma(C), dma(C), dma(2 * C * C), dma(2 * C * C), dma(C), dma(C), dma(C),
        ],
        compiler_params=params(6),
        cost_estimate=cost(95),
    )(x, rows, gains, grads)


def project(C, F, x, w):
    own = to_layer(C, F, x)
    rows = token_rows(own)
    return own, rows, dot(rows, w, 1, 0)


def attn_out_and_up(C, F, mixed, wo, x, gain, w, cot):
    if kernels_fit(C, F):
        hidden_in, out, inp = out_call(F, mixed, wo, x, gain)
        rows, act, der, h, cot = up_call(C, F, inp, w, cot)
        return cot, hidden_in, out, rows, act, der, h
    out = token_sums(dot(mixed, wo, 1, 1))
    hidden_in = x.astype(f32) + out * rms(out) * gain
    rows = token_rows(hidden_in.astype(bf16))
    g, u = jnp.split(dot(rows, w, 1, 0), 2, axis=1)
    sig = jax.nn.sigmoid(g)
    der = u * (sig * (1.0 + g * (1.0 - sig)))
    act = g * sig
    cot = to_layer(C, F, cot)
    return cot, hidden_in, out, rows, act.astype(bf16), der.astype(bf16), (act * u).astype(bf16)


def down_and_back(C, F, h, wd, hidden_in, cot, gain, act, der, units):
    if kernels_fit(C, F):
        return down_call(C, F, h, wd, hidden_in, cot, gain, act, der, units)
    out = token_sums(dot(h, wd, 1, 1))
    scale = rms(out)
    hat = out * scale
    g = cot.astype(f32)
    rows = token_rows(back(g * gain, hat, scale).astype(bf16))
    gh = dot(rows, wd, 1, 0)
    return (
        (hidden_in + hat * gain).astype(bf16),
        jnp.sum(g * hat, axis=0, keepdims=True),
        rows,
        jnp.concatenate([(gh * der.astype(f32)).astype(bf16), (gh * act.astype(f32)).astype(bf16)], axis=1),
        None,
        None,
    )


def back_to_attn(C, F, grad, w, cot, out, gain, wo):
    if kernels_fit(C, F):
        return mid_call(F, grad, w, cot, out, gain, wo)
    resid = cot.astype(f32) + token_sums(dot(grad, w, 1, 1))
    scale = rms(out)
    hat = out * scale
    rows = token_rows(back(resid * gain, hat, scale).astype(bf16))
    return resid, jnp.sum(resid * hat, axis=0, keepdims=True), rows, dot(rows, wo, 1, 0).astype(bf16)


def back_to_input(C, F, grad_projected, w, resid):
    return (resid + token_sums(dot(grad_projected, w, 1, 1))).astype(bf16)


def kernels_fit(C, F):
    return C == 4 and F == 8 and UNITS_ATTN * 4 * 2 == C * F


def to_layer(C, F, x):
    z, chip = lax.axis_index("ctx"), lax.axis_index("fsdp") // 2
    x = x.reshape(C, x.shape[0] // C, x.shape[1])
    got = []
    for k in range(C):
        pairs = [
            (s * F + f, (f // 2) * F + 2 * ((s + k) % C) + f % 2) for s in range(C) for f in range(F)
        ]
        block = lax.dynamic_index_in_dim(x, (z + k) % C, 0, keepdims=False)
        got.append(lax.ppermute(block, BOTH, pairs))
    got = jnp.stack(got)
    got = [lax.dynamic_index_in_dim(got, (chip - s + C) % C, 0, keepdims=False) for s in range(C)]
    return jnp.concatenate(got, axis=0)


def go_home(C, F, stage):
    chip = lax.axis_index("fsdp") // 2
    got = [lax.dynamic_index_in_dim(stage, chip, 1, keepdims=False)]
    for k in range(1, C):
        pairs = [(f, 2 * ((f // 2 + k) % C) + f % 2) for f in range(F)]
        block = lax.dynamic_index_in_dim(stage, (chip + k) % C, 1, keepdims=False)
        got.append(lax.ppermute(block, "fsdp", pairs))
    return got


def at_home(C, got):
    chip = lax.axis_index("fsdp") // 2
    got = jnp.stack(got)
    got = [lax.dynamic_index_in_dim(got, (chip - j + C) % C, 0, keepdims=False) for j in range(C)]
    return jnp.concatenate(got, axis=1)


def from_layer(C, F, x):
    z, chip = lax.axis_index("ctx"), lax.axis_index("fsdp") // 2
    x = x.reshape(C, x.shape[0] // C, x.shape[1])
    got = []
    for k in range(C):
        pairs = [
            ((f // 2) * F + 2 * ((s + k) % C) + f % 2, s * F + f) for s in range(C) for f in range(F)
        ]
        block = lax.dynamic_index_in_dim(x, (chip - k + C) % C, 0, keepdims=False)
        got.append(lax.ppermute(block, BOTH, pairs))
    got = jnp.stack(got)
    got = [lax.dynamic_index_in_dim(got, (j - z + C) % C, 0, keepdims=False) for j in range(C)]
    return jnp.concatenate(got, axis=0)


def shards(C, F, layer_input, cotangent, positions, w_attn, w_ffn, gains, mom_attn, mom_ffn, gain_mom):
    z = lax.axis_index("ctx")
    f = lax.axis_index("fsdp")
    local_rows, width = layer_input.shape[1], layer_input.shape[2]
    seq_total, seq_length = positions.shape
    dz, head_cols = w_attn.shape[1], w_attn.shape[2]
    local_heads = head_cols // HEAD_DIM
    block_count = w_ffn.shape[2]
    per = seq_total // C
    piece = local_rows // C
    chips = F // per
    tokens = F * local_rows
    hidden_cols = block_count * head_cols
    units = UNITS_ATTN + 3 * block_count
    parts = C * F // units

    def after(a, b):
        return lax.optimization_barrier((a, b))[0]

    def rows_gather(shard):
        return lax.all_gather(shard, "ctx", axis=0, tiled=True)

    def product(units, groups, *pairs):
        pairs = [(x.reshape(tokens, width), dy) for x, dy in pairs]
        if kernels:
            return grad_call(pairs, units, head_cols, groups)
        grad = jnp.concatenate([dot(x, dy, 0, 0).astype(bf16) for x, dy in pairs], axis=1)
        return jnp.transpose(grad.reshape(width, groups, units, head_cols), (2, 1, 0, 3))

    def scatter(grad):
        if kernels:
            return lax.psum_scatter(grad, "ctx", scatter_dimension=0, tiled=True)[0]
        return lax.psum_scatter(grad, "ctx", scatter_dimension=2, tiled=True)

    kernels = kernels_fit(C, F)
    w_heads = rows_gather(jnp.concatenate([w_attn[i] for i in range(UNITS_ATTN)], axis=1))
    w_qkv, w_out = (w_heads, w_heads) if kernels else (w_heads[:, : 3 * head_cols], w_heads[:, 3 * head_cols :])
    ffn_flat = w_ffn.reshape(3, dz, hidden_cols)
    w_gate_up = rows_gather(jnp.concatenate([ffn_flat[0], ffn_flat[1]], axis=1))
    w_down = rows_gather(ffn_flat[2])

    gain_query = lax.dynamic_slice_in_dim(gains[0], f * head_cols, head_cols)
    gain_key = lax.dynamic_slice_in_dim(gains[1], f * head_cols, head_cols)
    pos = lax.dynamic_slice_in_dim(positions, z * per, per, 0)
    pos = jnp.transpose(pos.reshape(per, C, chips, piece), (0, 2, 1, 3)).reshape(per, seq_length)
    cosine_table, sine_table = rotary_tables(pos)

    def heads(a):
        return jnp.transpose(
            a.reshape(chips, per, local_rows, local_heads, HEAD_DIM), (1, 0, 2, 3, 4)
        ).reshape(per, seq_length, local_heads, HEAD_DIM)

    def unheads(a):
        return jnp.transpose(
            a.reshape(per, chips, local_rows, local_heads, HEAD_DIM), (1, 0, 2, 3, 4)
        ).reshape(tokens, head_cols)

    if kernels:
        sign = jnp.where(jnp.arange(HEAD_DIM) < HEAD_DIM // 2, -1.0, 1.0)
        tables = (
            gain_query[None],
            gain_key[None],
            jnp.broadcast_to(cosine_table[:, :, 0], (per, seq_length, HEAD_DIM)),
            sine_table[:, :, 0] * sign,
            pos.astype(f32)[:, None, :],
            jnp.broadcast_to(pos.astype(f32)[..., None], (per, seq_length, HEAD_DIM)),
        )
        own_input, input_all = enter_call(C, F, layer_input.reshape(local_rows, width))
        projected, stats = qkv_call(F, input_all, w_qkv)
        attn_mixed, query_rows, key_rows, log_total = attend_call(F, projected, stats, *tables)
        attn_mixed = attn_mixed.reshape(tokens, head_cols)
    else:
        own_input, input_all, projected = project(C, F, layer_input.reshape(local_rows, width), w_qkv)
        query_raw = projected[:, :head_cols]
        key_raw = projected[:, head_cols : 2 * head_cols]
        value_raw = projected[:, 2 * head_cols :]
        query_total, key_total = norm_stats(
            jnp.sum(query_raw * query_raw, axis=-1), jnp.sum(key_raw * key_raw, axis=-1)
        )
        query_scale = lax.rsqrt(query_total / width + epsilon)[..., None]
        key_scale = lax.rsqrt(key_total / width + epsilon)[..., None]
        query_hat = query_raw * query_scale
        key_hat = key_raw * key_scale
        query_rows = (
            rotate(heads(query_hat * gain_query), cosine_table, sine_table) * HEAD_DIM ** (-0.5)
        ).astype(bf16)
        key_rows = rotate(heads(key_hat * gain_key), cosine_table, sine_table).astype(bf16)
        value_rows = heads(value_raw.astype(bf16))
        attn_mixed, log_total = attend(query_rows, key_rows, value_rows, pos)
        attn_mixed = unheads(attn_mixed)
    own_grad, hidden_in, attn_out, mlp_all, act, der, hidden = attn_out_and_up(
        C, F, attn_mixed, w_out, own_input, gains[2:3], w_gate_up,
        cotangent.reshape(local_rows, width),
    )
    by_layer = None
    if kernels:
        by_layer = jnp.concatenate(
            [mom_attn[:, None].astype(bf16), jnp.transpose(mom_ffn.astype(bf16), (2, 0, 1, 3))], axis=1
        )
    result, mlp_gain, grad_mlp_all, grad_ffn_in, mom_own, p_down = down_and_back(
        C, F, hidden, w_down, hidden_in, own_grad, gains[3:4], act, der, by_layer
    )
    if kernels:
        mom_own = jnp.swapaxes(mom_own, 0, 1)
    else:
        p_down = product(block_count, 1, (grad_mlp_all, hidden))
    g_down = scatter(p_down)
    p_gate_up = product(block_count, 2, (mlp_all, grad_ffn_in))
    if kernels:
        grad_ffn_in, p_gate_up = lax.optimization_barrier((grad_ffn_in, p_gate_up))
    g_gate_up = scatter(p_gate_up)
    grad_resid, attn_gain, grad_attn_all, grad_mixed = back_to_attn(
        C, F, grad_ffn_in, w_gate_up, own_grad, attn_out, gains[2:3], w_out
    )
    if kernels:
        grad_mixed = after(grad_mixed, g_down)
        weighted_q, weighted_k, grad_value, inner, gain_cols = attend_back_call(
            F, projected, query_rows, key_rows, grad_mixed, log_total, stats, *tables
        )
        inner = jnp.transpose(
            jnp.sum(inner, axis=1).reshape(per, 8, chips, local_rows), (1, 2, 0, 3)
        ).reshape(8, tokens)
        gain_cols = jnp.sum(gain_cols, axis=0)
        query_gain_cols = gain_cols[:, 0].reshape(head_cols)
        key_gain_cols = gain_cols[:, 1].reshape(head_cols)
        flat = (tokens, head_cols)
        zero = jnp.zeros((width,), f32)
        gain_local = jnp.stack(
            [
                lax.dynamic_update_slice(zero, query_gain_cols, (f * head_cols,)),
                lax.dynamic_update_slice(zero, key_gain_cols, (f * head_cols,)),
                attn_gain[0],
                mlp_gain[0],
                *[zero] * 4,
            ]
        )
        grad_rows, grad_projected, gain_layer = last_call(
            F, weighted_q.reshape(flat), weighted_k.reshape(flat), grad_value.reshape(flat),
            projected, stats, inner, w_qkv, grad_resid, gain_local,
        )
    else:
        grad_query, grad_key, grad_value = attend_back(
            query_rows, key_rows, value_rows, pos, heads(grad_mixed), log_total
        )
        grad_query_norm = unheads(unrotate(grad_query * HEAD_DIM ** (-0.5), cosine_table, sine_table))
        grad_key_norm = unheads(unrotate(grad_key, cosine_table, sine_table))
        query_gain_cols = jnp.sum(grad_query_norm * query_hat, axis=0)
        key_gain_cols = jnp.sum(grad_key_norm * key_hat, axis=0)
        query_weighted = grad_query_norm * gain_query
        key_weighted = grad_key_norm * gain_key
        query_inner, key_inner = norm_stats(
            jnp.sum(query_weighted * query_hat, axis=-1), jnp.sum(key_weighted * key_hat, axis=-1)
        )
        grad_query_raw = query_scale * (query_weighted - query_hat * (query_inner / width)[..., None])
        grad_key_raw = key_scale * (key_weighted - key_hat * (key_inner / width)[..., None])
        grad_projected = jnp.concatenate(
            [grad_query_raw.astype(bf16), grad_key_raw.astype(bf16), unheads(grad_value).astype(bf16)],
            axis=1,
        )
        grad_rows = back_to_input(C, F, grad_projected, w_qkv, grad_resid)
    g_attn = scatter(
        product(UNITS_ATTN, 1, (input_all, grad_projected), (grad_attn_all, attn_mixed))
    )
    if not kernels:
        grad_input = from_layer(C, F, grad_rows)
        result = from_layer(C, F, result)
        zero = jnp.zeros((width,), f32)
        gain_local = jnp.stack(
            [
                lax.dynamic_update_slice(zero, query_gain_cols, (f * head_cols,)),
                lax.dynamic_update_slice(zero, key_gain_cols, (f * head_cols,)),
                attn_gain[0],
                mlp_gain[0],
            ]
        )
        gain_total = jnp.sum(lax.all_gather(gain_local, BOTH, axis=0, tiled=False), axis=0)

    if kernels:
        early = jnp.stack([jnp.zeros_like(g_down[0]), g_gate_up[0], g_gate_up[1], g_down[0]])
        mom = momentum * mom_own.reshape(early.shape).astype(f32)
        owned = (mom + early.astype(f32)).astype(bf16)
        mom_first = mom[0]
        early = jnp.swapaxes(early.reshape(UNITS_ATTN, C, dz, head_cols), 0, 1)
        early, owned, mom_first, grad_rows = lax.optimization_barrier((early, owned, mom_first, grad_rows))
        late = (mom_first + g_attn[0].astype(f32)).astype(bf16)
        owned = lax.dynamic_update_slice(owned, late[None], (0, 0, 0))
        got = lax.dynamic_update_slice(early, g_attn.reshape(C, 1, dz, head_cols), (0, 0, 0, 0))
        own, leaving, gain_total, sent_back = newton_call(
            C, owned, jnp.stack([result, grad_rows]), gain_layer, got
        )
        sent_back = sent_back.astype(f32)
        grad_attn = sent_back[:, 0]
        grad_ffn = jnp.transpose(sent_back[:, 1:], (1, 2, 0, 3))
        homing = go_home(C, F, leaving)
        gain_total = gain_total[:4]
    else:
        grad_attn = g_attn[:, 0].astype(f32)
        grad_ffn = jnp.transpose(
            jnp.concatenate([g_gate_up, g_down], axis=1).astype(f32), (1, 2, 0, 3)
        )
    new_attn = momentum * mom_attn + grad_attn
    new_ffn = momentum * mom_ffn + grad_ffn
    if kernels:
        homing, new_attn, new_ffn, grad_attn, grad_ffn = lax.optimization_barrier(
            (homing, new_attn, new_ffn, grad_attn, grad_ffn)
        )
        back_rows = at_home(C, homing)
        result, grad_input = back_rows[0], back_rows[1]
    if not kernels:
        send = jnp.concatenate(
            [
                new_attn.astype(bf16),
                jnp.transpose(new_ffn.astype(bf16), (0, 2, 1, 3)).reshape(3 * block_count, dz, head_cols),
            ],
            axis=0,
        ).reshape(C * F, dz // parts, head_cols)
        own = lax.all_to_all(send, BOTH, split_axis=0, concat_axis=0, tiled=True)
        own = jnp.transpose(own.reshape(C, F, dz // parts, head_cols), (0, 2, 1, 3)).reshape(
            C * dz // parts, F * head_cols
        )

        def peers(a):
            out = [a]
            for s in range(1, parts):
                pairs = [(i, i - i % parts + (i + parts - s) % parts) for i in range(C * F)]
                out.append(lax.ppermute(a, BOTH, pairs))
            return out

        own32 = own.astype(f32)
        square = jnp.sum(own32 * own32)
        total = sum(peers(square.reshape(1, 1)))
        inv = 1.0 / (jnp.sqrt(total) + 1e-07)
        for iteration in range(NS_STEPS):
            factor = inv if iteration == 0 else 1.0
            every = peers(own)
            gram = [(dot(own, b, 1, 1) * (factor * factor)).astype(bf16) for b in every]
            product = sum(dot(g, b, 1, 0) for g, b in zip(gram, every)) * factor
            product_all = peers(product.astype(bf16))
            product_two = sum(dot(g, b, 1, 0) for g, b in zip(gram, product_all))
            own = (
                quintic_one * factor * own.astype(f32) + quintic_two * product + quintic_three * product_two
            ).astype(bf16)
    if kernels:
        home = own
    else:
        home = jnp.transpose(own.reshape(C, dz // parts, F, head_cols), (0, 2, 1, 3)).reshape(
            C * F, dz // parts, head_cols
        )
    steps = lax.all_to_all(home, BOTH, split_axis=0, concat_axis=0, tiled=True)
    if kernels:
        steps = steps.reshape(C, UNITS_ATTN, dz, head_cols)
        arranged = lax.optimization_barrier(jnp.transpose(steps[:, 1:], (1, 2, 0, 3)))
        step_attn = -muon_rate * steps[:, 0].astype(f32)
        step_ffn = -muon_rate * arranged.astype(f32)
    else:
        steps = -muon_rate * steps.astype(f32)
        steps = steps.reshape(units, dz, head_cols)
        step_attn = steps[:UNITS_ATTN]
        step_ffn = jnp.transpose(
            steps[UNITS_ATTN:].reshape(3, block_count, dz, head_cols), (0, 2, 1, 3)
        )
    new_gain_mom = momentum * gain_mom + gain_total
    return (
        result.reshape(layer_input.shape),
        grad_input.astype(f32).reshape(layer_input.shape),
        grad_attn,
        grad_ffn,
        gain_total,
        new_attn,
        new_ffn,
        new_gain_mom,
        step_attn,
        step_ffn,
        -gain_rate * new_gain_mom,
    )


def solution(mesh):
    tokens = P("fsdp", "ctx", None)
    attn = P(None, "ctx", "fsdp")
    ffn = P(None, "ctx", None, "fsdp")
    in_specs = (tokens, tokens, P(), attn, ffn, P(), attn, ffn, P())
    out_specs = (tokens, tokens, attn, ffn, P(), attn, ffn, P(), attn, ffn, P())
    body = functools.partial(shards, mesh.shape["ctx"], mesh.shape["fsdp"])
    return jax.shard_map(body, mesh=mesh, in_specs=in_specs, out_specs=out_specs, check_vma=False)
```

```python
import functools
import jax
import jax.numpy as jnp
from jax import lax
from jax.experimental import pallas as pl
from jax.experimental.pallas import tpu as pltpu
from jax.sharding import PartitionSpec as P

NS_STEPS = 3
HEAD_DIM = 128
UNITS_ATTN = 4

epsilon = 1e-06
rope_theta = 500000.0
quintic_one = 3.4445
quintic_two = -4.775
quintic_three = 2.0315
momentum = 0.95
muon_rate = 1.0
gain_rate = 0.0005
BOTH = ("ctx", "fsdp")
bf16 = jnp.bfloat16
f32 = jnp.float32


def dot(a, b, ca, cb):
    return lax.dot_general(a, b, (((ca,), (cb,)), ((), ())), preferred_element_type=f32)


def token_rows(operand):
    return lax.all_gather(operand, "fsdp", axis=0, tiled=True)


def token_sums(operand):
    return lax.psum_scatter(operand.astype(bf16), "fsdp", scatter_dimension=0, tiled=True).astype(f32)


def norm_stats(first_sum, second_sum):
    got = lax.all_gather(jnp.stack([first_sum, second_sum]), "fsdp", axis=0, tiled=False)
    total = jnp.sum(got, axis=0)
    return total[0], total[1]


def rms_back(upstream, normed, inv_scale):
    return inv_scale * (upstream - normed * jnp.mean(upstream * normed, axis=-1, keepdims=True))


def rotary_tables(slot_order):
    half_dim = HEAD_DIM // 2
    inverse = rope_theta ** (-(jnp.arange(half_dim, dtype=f32) * 2.0) / HEAD_DIM)
    angles = slot_order.astype(f32)[..., None] * inverse
    angles = jnp.concatenate([angles, angles], axis=-1)
    return (jnp.cos(angles)[..., None, :], jnp.sin(angles)[..., None, :])


def rotate(operand, cosine_table, sine_table):
    half_dim = operand.shape[-1] // 2
    flipped = jnp.concatenate([-operand[..., half_dim:], operand[..., :half_dim]], axis=-1)
    return operand * cosine_table + flipped * sine_table


def unrotate(upstream, cosine_table, sine_table):
    half_dim = upstream.shape[-1] // 2
    shifted = upstream * sine_table
    flipped = jnp.concatenate([shifted[..., half_dim:], -shifted[..., :half_dim]], axis=-1)
    return upstream * cosine_table + flipped


def masked_scores(query_rows, key_rows, pos):
    scores = jnp.einsum("gqhe,gkhe->ghqk", query_rows, key_rows, preferred_element_type=f32)
    causal = pos[:, None, :, None] >= pos[:, None, None, :]
    return jnp.where(causal, scores, -1e30)


def attend(query_rows, key_rows, value_rows, pos):
    scores = masked_scores(query_rows, key_rows, pos)
    row_max = jnp.max(scores, axis=-1, keepdims=True)
    weights = jnp.exp(scores - row_max)
    row_total = jnp.sum(weights, axis=-1, keepdims=True)
    probabilities = (weights / row_total).astype(bf16)
    attn_mixed = jnp.einsum("ghqk,gkhe->gqhe", probabilities, value_rows, preferred_element_type=f32)
    return attn_mixed.astype(bf16), row_max + jnp.log(row_total)


def attend_back(query_rows, key_rows, value_rows, pos, grad_mixed, log_total):
    scores = masked_scores(query_rows, key_rows, pos)
    probabilities = jnp.exp(scores - log_total)
    grad_probs = jnp.einsum("gqhe,gkhe->ghqk", grad_mixed, value_rows, preferred_element_type=f32)
    grad_value = jnp.einsum(
        "ghqk,gqhe->gkhe", probabilities.astype(bf16), grad_mixed, preferred_element_type=f32
    )
    inner_sum = jnp.sum(grad_probs * probabilities, axis=-1, keepdims=True)
    grad_scores = (probabilities * (grad_probs - inner_sum)).astype(bf16)
    grad_query = jnp.einsum("ghqk,gkhe->gqhe", grad_scores, key_rows, preferred_element_type=f32)
    grad_key = jnp.einsum("ghqk,gqhe->gkhe", grad_scores, query_rows, preferred_element_type=f32)
    return grad_query, grad_key, grad_value


MESH = pl.DeviceIdType.MESH
VMEM_LIMIT = 60 * 1024 * 1024
ANY = pl.BlockSpec(memory_space=pl.ANY)


class Plane:
    def __init__(self):
        f = lax.axis_index("fsdp")
        self.f, self.c, self.chip = f, f % 2, f // 2
        x, y = self.chip % 2, self.chip // 2
        self.qx = self.chip + 1 - 2 * x
        self.qy = self.chip + 2 - 4 * y
        self.qd = self.qx + 2 - 4 * y
        self.fc = f + 1 - 2 * self.c
        self.fx = 2 * self.qx + self.c
        self.fy = 2 * self.qy + self.c
        self.fd = 2 * self.qd + self.c
        self.other = 1 - self.c

    def greet(self):
        barrier = pltpu.get_barrier_semaphore()
        for to in (self.fc, self.fx, self.fy):
            pl.semaphore_signal(barrier, inc=1, device_id={"fsdp": to}, device_id_type=MESH)
        pl.semaphore_wait(barrier, 3)


def partner(i, k):
    if k == 3:
        return 3 - i
    if k == 2:
        return (i + 2) % 4
    return i + 1 - 2 * (i % 2)


FAR_FIRST = (3, 2, 1)


def remote(src, dst, send, recv, i, to, axis="fsdp"):
    return pltpu.make_async_remote_copy(
        src_ref=src, dst_ref=dst, send_sem=send.at[i], recv_sem=recv.at[i],
        device_id={axis: to}, device_id_type=MESH,
    )


def local(src, dst, sems, i):
    copy = pltpu.make_async_copy(src, dst, sems.at[i])
    copy.start()
    return copy


def nn(a, b):
    return lax.dot_general(a, b, (((1,), (0,)), ((), ())), preferred_element_type=f32)


def nt(a, b):
    return lax.dot_general(a, b, (((1,), (1,)), ((), ())), preferred_element_type=f32)


def gather_phase(at, rows, send, recv, base, on_rows):
    half = rows.shape[1] // 2
    A, B = pl.ds(0, half), pl.ds(half, half)

    def cp(i, slot, part, to):
        ref = rows.at[slot] if part is None else rows.at[slot, part]
        return remote(ref, ref, send, recv, base + i, to)

    fcx, fcy, fcd = 2 * at.qx + at.other, 2 * at.qy + at.other, 2 * at.qd + at.other
    sent = []

    def go(*a):
        c = cp(*a)
        c.start()
        sent.append(c)

    def arrived(i, slot, part, frm):
        cp(i, slot, part, frm).wait_recv()

    go(0, at.f, None, at.fc)
    go(1, at.f, A, at.fx)
    go(3, at.f, B, at.fy)
    go(2, at.f, B, at.fx)
    go(4, at.f, A, at.fy)
    arrived(0, at.fc, None, at.fc)
    on_rows(2 * at.chip, 2)
    arrived(1, at.fx, A, at.fx)
    go(5, at.fx, A, at.fy)
    go(7, at.fx, A, at.fc)
    arrived(3, at.fy, B, at.fy)
    go(6, at.fy, B, at.fx)
    go(8, at.fy, B, at.fc)
    arrived(2, at.fx, B, at.fx)
    go(9, at.fx, B, at.fc)
    arrived(4, at.fy, A, at.fy)
    go(10, at.fy, A, at.fc)
    arrived(7, fcx, A, at.fc)
    arrived(9, fcx, B, at.fc)
    on_rows(2 * at.qx, 2)
    arrived(8, fcy, B, at.fc)
    arrived(10, fcy, A, at.fc)
    on_rows(2 * at.qy, 2)
    arrived(5, at.fd, A, at.fy)
    go(11, at.fd, A, at.fc)
    arrived(6, at.fd, B, at.fx)
    go(12, at.fd, B, at.fc)
    on_rows(at.fd, 1)
    arrived(11, fcd, A, at.fc)
    arrived(12, fcd, B, at.fc)
    on_rows(fcd, 1)
    for c in sent:
        c.wait_send()


GATHER_COPIES = 13
SCATTER_COPIES = 10


def scatter_scratch(R, D):
    return [
        pltpu.VMEM((4, R, D), bf16),
        pltpu.VMEM((4, R, D), bf16),
        pltpu.VMEM((2, R, D), f32),
        pltpu.VMEM((3, R, D), bf16),
        pltpu.VMEM((3, R, D), bf16),
    ]


def scatter_phase(at, partial, bufs, send, recv, base, between=None):
    to_core, from_core, mine, out, inc = bufs
    R, D = to_core.shape[1], to_core.shape[2]
    half = R // 2
    A, B = pl.ds(0, half), pl.ds(half, half)
    tile = 512
    step = 16
    sent = []

    def go(i, src, dst, to):
        c = remote(src, dst, send, recv, base + i, to)
        c.start()
        sent.append(c)

    def arrived(i, dst, frm):
        remote(dst, dst, send, recv, base + i, frm).wait_recv()

    def compute(order, chip, slot):
        @pl.loop(0, D // tile)
        def _(n):
            cols = pl.ds(pl.multiple_of(n * tile, tile), tile)
            got = partial(chip, cols)
            lo, hi = got[:R], got[R:]
            first = at.c == 0
            mine[slot, :, cols] = jnp.where(first, lo, hi)
            to_core[order, :, cols] = jnp.where(first, hi, lo).astype(bf16)

        go(order, to_core.at[order], from_core.at[order], at.fc)

    def chip_sum(order, slot):
        arrived(order, from_core.at[order], at.fc)

        @pl.loop(0, R // step)
        def _(r):
            rows = pl.ds(pl.multiple_of(r * step, step), step)
            out[order, rows, :] = (mine[slot, rows, :] + from_core[order, rows, :].astype(f32)).astype(bf16)

    def relay(order, start, src):
        @pl.loop(0, half // step)
        def _(r):
            rows = pl.ds(pl.multiple_of(start + r * step, step), step)
            out[order, rows, :] = (out[order, rows, :].astype(f32) + inc[src, rows, :].astype(f32)).astype(bf16)

    compute(0, at.qd, 0)
    compute(1, at.qx, 1)
    if between is not None:
        between()
    chip_sum(0, 0)
    go(4, out.at[0, A], inc.at[0, A], at.fx)
    go(5, out.at[0, B], inc.at[0, B], at.fy)
    compute(2, at.qy, 0)
    chip_sum(1, 1)
    go(6, out.at[1, A], inc.at[1, A], at.fx)
    compute(3, at.chip, 1)
    chip_sum(2, 0)
    go(8, out.at[2, B], inc.at[2, B], at.fy)
    arrived(5, inc.at[0, B], at.fy)
    relay(1, half, 0)
    go(7, out.at[1, B], inc.at[1, B], at.fx)
    arrived(4, inc.at[0, A], at.fx)
    relay(2, 0, 0)
    go(9, out.at[2, A], inc.at[2, A], at.fy)
    arrived(3, from_core.at[3], at.fc)
    arrived(6, inc.at[1, A], at.fx)
    arrived(8, inc.at[2, B], at.fy)
    arrived(7, inc.at[1, B], at.fx)
    arrived(9, inc.at[2, A], at.fy)
    for c in sent:
        c.wait_send()

    def total(rows):
        return (
            mine[1, rows, :]
            + from_core[3, rows, :].astype(f32)
            + inc[1, rows, :].astype(f32)
            + inc[2, rows, :].astype(f32)
        )

    return total


def rms(v):
    return lax.rsqrt(jnp.mean(v * v, axis=-1, keepdims=True) + epsilon)


def back(weighted, normed, scale):
    return scale * (weighted - normed * jnp.mean(weighted * normed, axis=-1, keepdims=True))


def row_loop(R, body, step=16):
    @pl.loop(0, R // step)
    def _(r):
        body(pl.ds(pl.multiple_of(r * step, step), step))


def pair_loop(rows, w_cols, total_cols, body):
    @pl.loop(0, total_cols // w_cols)
    def _(t):
        body(pl.ds(pl.multiple_of(t * w_cols, w_cols), w_cols))


class Stores:
    def __init__(self, sems):
        self.sems, self.steps, self.n = sems, [], 0

    def slot(self):
        if len(self.steps) >= 2:
            for c in self.steps[-2]:
                c.wait()
            self.steps[-2] = []
        return len(self.steps) % 2

    def put(self, pairs):
        done = []
        for src, dst in pairs:
            done.append(local(src, dst, self.sems, self.n))
            self.n += 1
        self.steps.append(done)

    def finish(self):
        for step in self.steps:
            for c in step:
                c.wait()


class Moving:
    def __init__(self, at, C, mine, stage, landing, lsem, base, send, recv):
        self.at, self.C, self.mine, self.stage, self.landing = at, C, mine, stage, landing
        self.lsem, self.base, self.send, self.recv = lsem, base, send, recv
        self.z = lax.axis_index("ctx")
        self.piece = mine.shape[0] // C
        self.sent = []

    def greet(self, barrier):
        at, C = self.at, self.C
        for k in range(1, C):
            pl.semaphore_signal(barrier, inc=1, device_id={"ctx": (self.z + k) % C}, device_id_type=MESH)
            pl.semaphore_signal(
                barrier, inc=1, device_id={"fsdp": 2 * ((at.chip + k) % C) + at.c}, device_id_type=MESH
            )

    def first(self):
        at, C, piece = self.at, self.C, self.piece
        for k in FAR_FIRST:
            j = partner(at.chip, k)
            src = self.mine.at[pl.ds(j * piece, piece)]
            c = remote(src, self.stage.at[at.chip], self.send, self.recv, k, 2 * j + at.c)
            c.start()
            self.sent.append(c)
        src = self.mine.at[pl.ds(at.chip * piece, piece)]
        self.keep = local(src, self.stage.at[at.chip], self.lsem, self.base)

    def land(self, layer):
        return self.landing.at[pl.ds(layer * self.piece, self.piece)]

    def second(self):
        at, C, z = self.at, self.C, self.z
        self.keep.wait()
        for k in FAR_FIRST:
            frm = partner(at.chip, k)
            remote(self.stage.at[frm], self.stage.at[frm], self.send, self.recv, k, 2 * frm + at.c).wait_recv()
        for k in FAR_FIRST:
            to = partner(z, k)
            c = remote(self.stage.at[to], self.land(z), self.send, self.recv, C + k, to, "ctx")
            c.start()
            self.sent.append(c)
        self.keep = local(self.stage.at[z], self.land(z), self.lsem, self.base + 1)

    def finish(self):
        C, z = self.C, self.z
        self.keep.wait()
        for k in FAR_FIRST:
            frm = partner(z, k)
            remote(self.land(frm), self.land(frm), self.send, self.recv, C + k, frm, "ctx").wait_recv()
        for c in self.sent:
            c.wait_send()


def enter_kernel(C, x_ref, own_ref, all_ref, stage, mine, rows, lsem, osem, send, recv, tsend, trecv):
    at = Plane()
    load = local(x_ref, mine, lsem, 0)
    moving = Moving(at, C, mine, stage, rows.at[at.f], lsem, 1, tsend, trecv)
    barrier = pltpu.get_barrier_semaphore()
    moving.greet(barrier)
    pl.semaphore_signal(barrier, inc=1, device_id={"fsdp": at.fc}, device_id_type=MESH)
    pl.semaphore_wait(barrier, 2 * (C - 1) + 1)
    load.wait()
    moving.first()
    moving.second()
    moving.finish()
    save = local(rows.at[at.f], own_ref, lsem, 3)
    stores = []

    def on_rows(first, count):
        stores.append(local(rows.at[pl.ds(first, count)], all_ref.at[pl.ds(first, count)], osem, len(stores)))

    gather_phase(at, rows, send, recv, 0, on_rows)
    save.wait()
    for c in stores:
        c.wait()


def enter_call(C, F, x):
    R, D = x.shape
    return pl.pallas_call(
        functools.partial(enter_kernel, C),
        out_shape=[jax.ShapeDtypeStruct((R, D), bf16), jax.ShapeDtypeStruct((F, R, D), bf16)],
        in_specs=[ANY],
        out_specs=[ANY] * 2,
        scratch_shapes=[
            pltpu.VMEM((C, R // C, D), bf16),
            pltpu.VMEM((R, D), bf16),
            pltpu.VMEM((F, R, D), bf16),
            dma(4), dma(5), dma(GATHER_COPIES), dma(GATHER_COPIES), dma(2 * C), dma(2 * C),
        ],
        compiler_params=params(1),
        cost_estimate=cost(70),
    )(x)


def qkv_kernel(all_ref, w_ref, proj_ref, st_ref, rows, w, acc, st, lsem, osem, ssend, srecv):
    at = Plane()
    F, R = rows.shape[0], rows.shape[1]
    e = w.shape[1] // 3
    m = 2 * R
    loads = [local(w_ref.at[:, pl.ds(0, 3 * e)], w, lsem, 0)] + [
        local(all_ref.at[pl.ds(2 * p, 2)], rows.at[pl.ds(2 * p, 2)], lsem, 1 + p) for p in range(F // 2)
    ]
    barrier = pltpu.get_barrier_semaphore()
    for k in range(1, F):
        pl.semaphore_signal(barrier, inc=1, device_id={"fsdp": (at.f + k) % F}, device_id_type=MESH)
    pl.semaphore_wait(barrier, F - 1)
    loads[0].wait()
    stores = Stores(osem)
    for p in range(F // 2):
        loads[1 + p].wait()
        s = stores.slot()

        def tile(c):
            acc[s, :, c] = nn(rows[pl.ds(2 * p, 2)].reshape(m, rows.shape[2]), w[:, c])

        pair_loop(m, 256, w.shape[1], tile)
        q, k = acc[s, :, :e], acc[s, :, e : 2 * e]
        st[at.f, :, pl.ds(p * m, m)] = row_sums(q * q, k * k)
        stores.put([(acc.at[s], proj_ref.at[pl.ds(p * m, m)])])
    share_stats(at, F, st, ssend, srecv, 0)
    local(st, st_ref, lsem, 1 + F // 2).wait()
    stores.finish()


def params(number):
    return pltpu.CompilerParams(
        collective_id=number, has_side_effects=True, vmem_limit_bytes=VMEM_LIMIT
    )


def cost(us):
    return pl.CostEstimate(flops=int(us * 1e9), bytes_accessed=2**20, transcendentals=0)


def dma(n):
    return pltpu.SemaphoreType.DMA((n,))


def qkv_call(F, rows, w):
    _, R, D = rows.shape
    n = w.shape[1] // 4 * 3
    return pl.pallas_call(
        qkv_kernel,
        out_shape=[
            jax.ShapeDtypeStruct((F * R, n), f32),
            jax.ShapeDtypeStruct((F, 8, F * R), f32),
        ],
        in_specs=[ANY] * 2,
        out_specs=[ANY] * 2,
        scratch_shapes=[
            pltpu.VMEM((F, R, D), bf16),
            pltpu.VMEM((D, n), bf16),
            pltpu.VMEM((2, 2 * R, n), f32),
            pltpu.VMEM((F, 8, F * R), f32),
            dma(6), dma(4), dma(F), dma(F),
        ],
        compiler_params=params(7),
        cost_estimate=cost(22),
    )(rows, w)


def out_kernel(
    mixed_ref, wo_ref, x_ref, gain_ref, hid_ref, ao_ref, in_ref,
    mixed, wo, x, gain, hid, ao, inp, b0, b1, b2, b3, b4, lsem, send, recv,
):
    at = Plane()
    e = wo.shape[1]
    pairs = [(mixed_ref, mixed), (wo_ref.at[:, pl.ds(3 * e, e)], wo), (x_ref, x), (gain_ref, gain)]
    loads = [local(s, d, lsem, i) for i, (s, d) in enumerate(pairs)]
    at.greet()
    R = x.shape[0]
    loads[0].wait()
    loads[1].wait()

    def partial(chip, cols):
        return nt(mixed[pl.ds(pl.multiple_of(chip * 2 * R, 2 * R), 2 * R), :], wo[cols, :])

    total = scatter_phase(at, partial, (b0, b1, b2, b3, b4), send, recv, 0)
    loads[2].wait()
    loads[3].wait()

    def finish(r):
        out = total(r)
        ao[r, :] = out
        hidden_in = x[r, :].astype(f32) + out * rms(out) * gain[...]
        hid[r, :] = hidden_in
        inp[r, :] = hidden_in.astype(bf16)

    row_loop(R, finish)
    for c in [local(ao, ao_ref, lsem, 4), local(hid, hid_ref, lsem, 5), local(inp, in_ref, lsem, 6)]:
        c.wait()


def out_call(F, mixed, wo, x, gain):
    R, D = x.shape
    e = wo.shape[1] // 4
    return pl.pallas_call(
        out_kernel,
        out_shape=[
            jax.ShapeDtypeStruct((R, D), f32),
            jax.ShapeDtypeStruct((R, D), f32),
            jax.ShapeDtypeStruct((R, D), bf16),
        ],
        in_specs=[ANY] * 4,
        out_specs=[ANY] * 3,
        scratch_shapes=[
            pltpu.VMEM((F * R, e), bf16),
            pltpu.VMEM((D, e), bf16),
            pltpu.VMEM((R, D), bf16),
            pltpu.VMEM((1, D), f32),
            pltpu.VMEM((R, D), f32),
            pltpu.VMEM((R, D), f32),
            pltpu.VMEM((R, D), bf16),
        ]
        + scatter_scratch(R, D)
        + [dma(7), dma(SCATTER_COPIES), dma(SCATTER_COPIES)],
        compiler_params=params(8),
        cost_estimate=cost(46),
    )(mixed, wo, x, gain)


def up_kernel(
    C, in_ref, w_ref, cot_ref, all_ref, act_ref, der_ref, h_ref, moved_ref,
    w, rows, act, der, h, mine, moved, stage, lsem, osem, send, recv, tsend, trecv,
):
    at = Plane()
    cot = local(cot_ref, mine, lsem, 2)
    moving = Moving(at, C, mine, stage, moved, lsem, 3, tsend, trecv)
    own = local(in_ref, rows.at[at.f], lsem, 0)
    n = act.shape[2]
    loads = [local(w_ref, w, lsem, 1)]
    width = 256
    barrier = pltpu.get_barrier_semaphore()
    moving.greet(barrier)
    pl.semaphore_signal(barrier, inc=1, device_id={"fsdp": at.fc}, device_id_type=MESH)
    pl.semaphore_wait(barrier, 2 * (C - 1) + 1)
    R = rows.shape[1]
    cot.wait()
    moving.first()
    own.wait()
    waited = []
    stores = Stores(osem)

    def on_rows(first, count):
        s = stores.slot()
        m = count * R
        if not waited:
            for c in loads:
                c.wait()
            moving.second()
            waited.append(1)

        @pl.loop(0, n // width)
        def _(t):
            c = pl.ds(pl.multiple_of(t * width, width), width)
            lhs = rows[pl.ds(first, count)].reshape(m, rows.shape[2])
            g = nn(lhs, w[:, c])
            u = nn(lhs, w[:, pl.ds(pl.multiple_of(n + t * width, width), width)])
            sig = jax.nn.sigmoid(g)
            a = g * sig
            act[s, pl.ds(0, m), c] = a.astype(bf16)
            der[s, pl.ds(0, m), c] = (u * (sig * (1.0 + g * (1.0 - sig)))).astype(bf16)
            h[s, pl.ds(0, m), c] = (a * u).astype(bf16)

        start = pl.multiple_of(first * R, R)
        stores.put(
            [
                (act.at[s, pl.ds(0, m)], act_ref.at[pl.ds(start, m)]),
                (der.at[s, pl.ds(0, m)], der_ref.at[pl.ds(start, m)]),
                (h.at[s, pl.ds(0, m)], h_ref.at[pl.ds(start, m)]),
                (rows.at[pl.ds(first, count)], all_ref.at[pl.ds(first, count)]),
            ]
        )

    gather_phase(at, rows, send, recv, 0, on_rows)
    moving.finish()
    local(moved, moved_ref, lsem, 5).wait()
    stores.finish()


def up_call(C, F, inp, w, cot):
    R, D = inp.shape
    n = w.shape[1] // 2
    T = F * R
    wide = jax.ShapeDtypeStruct((T, n), bf16)
    return pl.pallas_call(
        functools.partial(up_kernel, C),
        out_shape=[
            jax.ShapeDtypeStruct((F, R, D), bf16), wide, wide, wide, jax.ShapeDtypeStruct((R, D), bf16),
        ],
        in_specs=[ANY] * 3,
        out_specs=[ANY] * 5,
        scratch_shapes=[
            pltpu.VMEM((D, 2 * n), bf16),
            pltpu.VMEM((F, R, D), bf16),
            pltpu.VMEM((2, 2 * R, n), bf16),
            pltpu.VMEM((2, 2 * R, n), bf16),
            pltpu.VMEM((2, 2 * R, n), bf16),
            pltpu.VMEM((R, D), bf16),
            pltpu.VMEM((R, D), bf16),
            pltpu.VMEM((C, R // C, D), bf16),
        ]
        + [dma(6), dma(20), dma(GATHER_COPIES), dma(GATHER_COPIES), dma(2 * C), dma(2 * C)],
        compiler_params=params(2),
        cost_estimate=cost(56),
    )(inp, w, cot)


def down_kernel(
    C, h_ref, wd_ref, hid_ref, cot_ref, gain_ref, act_ref, der_ref, unit_ref,
    res_ref, gg_ref, all_ref, grad_ref, mom_ref, p_ref,
    h, wd, hid, cot, gain, act, der, res, gacc, rows, grad, prod, b0, b1, b2, b3, b4,
    lsem, osem, asem, psem, send, recv, usend, urecv,
):
    at = Plane()
    loads = [
        local(s, d, lsem, i)
        for i, (s, d) in enumerate(
            [(h_ref, h), (wd_ref, wd), (hid_ref, hid), (gain_ref, gain), (cot_ref, cot)]
        )
    ]
    z = lax.axis_index("ctx")
    barrier = pltpu.get_barrier_semaphore()
    for to in (at.fc, at.fx, at.fy):
        pl.semaphore_signal(barrier, inc=1, device_id={"fsdp": to}, device_id_type=MESH)
    for k in FAR_FIRST:
        pl.semaphore_signal(barrier, inc=1, device_id={"ctx": partner(z, k)}, device_id_type=MESH)
    pl.semaphore_wait(barrier, C + 2)
    R = rows.shape[1]
    n = wd.shape[1]
    units = []

    def send_units(k):
        to = partner(z, k)
        c = remote(unit_ref.at[to], mom_ref.at[z], usend, urecv, k, to, "ctx")
        c.start()
        units.append(c)

    for k in FAR_FIRST:
        send_units(k)
    units.append(local(unit_ref.at[z], mom_ref.at[z], lsem, 5))
    loads[0].wait()
    loads[1].wait()

    def partial(chip, cols):
        return nt(h[pl.ds(pl.multiple_of(chip * 2 * R, 2 * R), 2 * R), :], wd[cols, :])

    total = scatter_phase(at, partial, (b0, b1, b2, b3, b4), send, recv, 0)
    for c in loads[2:]:
        c.wait()
    gacc[...] = jnp.zeros_like(gacc)

    def finish(r):
        out = total(r)
        scale = rms(out)
        hat = out * scale
        res[r, :] = (hid[r, :] + hat * gain[...]).astype(bf16)
        g = cot[r, :].astype(f32)
        gacc[...] += jnp.sum(g * hat, axis=0, keepdims=True)
        rows[at.f, r, :] = back(g * gain[...], hat, scale).astype(bf16)

    row_loop(R, finish)
    saves = [local(res, res_ref, lsem, 6), local(gacc, gg_ref, lsem, 7)]
    stores = Stores(osem)

    def on_rows(first, count):
        s = stores.slot()
        m = count * R
        start = pl.multiple_of(first * R, R)
        k = len(stores.steps)
        la = local(act_ref.at[pl.ds(start, m)], act.at[s, pl.ds(0, m)], asem, 2 * k)
        ld = local(der_ref.at[pl.ds(start, m)], der.at[s, pl.ds(0, m)], asem, 2 * k + 1)
        la.wait()
        ld.wait()

        width = 512

        @pl.loop(0, n // width)
        def _(t):
            c = pl.ds(pl.multiple_of(t * width, width), width)
            up = pl.ds(pl.multiple_of(n + t * width, width), width)
            gh = nn(rows[pl.ds(first, count)].reshape(m, rows.shape[2]), wd[:, c])
            grad[s, pl.ds(0, m), up] = (gh * act[s, pl.ds(0, m), c].astype(f32)).astype(bf16)
            grad[s, pl.ds(0, m), c] = (gh * der[s, pl.ds(0, m), c].astype(f32)).astype(bf16)

        stores.put(
            [
                (grad.at[s, pl.ds(0, m)], grad_ref.at[pl.ds(start, m)]),
                (rows.at[pl.ds(first, count)], all_ref.at[pl.ds(first, count)]),
            ]
        )

    gather_phase(at, rows, send, recv, SCATTER_COPIES, on_rows)
    F, D = rows.shape[0], rows.shape[2]
    tile, cols = prod.shape[1], p_ref.shape[3]
    puts = []
    for t in range(D // tile):
        if t >= 2:
            for c in puts[t - 2]:
                c.wait()
        rhs = rows[:, :, t * tile : (t + 1) * tile].reshape(F * R, tile)
        prod[t % 2] = lax.dot_general(
            rhs, h[...], (((0,), (0,)), ((), ())), preferred_element_type=f32
        ).astype(bf16)
        puts.append(
            [
                local(
                    prod.at[t % 2, :, pl.ds(b * cols, cols)],
                    p_ref.at[b, 0, pl.ds(t * tile, tile)],
                    psem,
                    t * (n // cols) + b,
                )
                for b in range(n // cols)
            ]
        )
    for step in puts[-2:]:
        for c in step:
            c.wait()
    for k in FAR_FIRST:
        frm = partner(z, k)
        remote(mom_ref.at[frm], mom_ref.at[frm], usend, urecv, k, frm, "ctx").wait_recv()
    for c in units[:-1]:
        c.wait_send()
    units[-1].wait()
    for s in saves:
        s.wait()
    stores.finish()


def down_call(C, F, h, wd, hid, cot, gain, act, der, units):
    R, D = hid.shape
    n = wd.shape[1]
    T = F * R
    copies = SCATTER_COPIES + GATHER_COPIES
    one = jax.ShapeDtypeStruct((R, D), bf16)
    return pl.pallas_call(
        functools.partial(down_kernel, C),
        out_shape=[
            one,
            jax.ShapeDtypeStruct((1, D), f32),
            jax.ShapeDtypeStruct((F, R, D), bf16),
            jax.ShapeDtypeStruct((T, 2 * n), bf16),
            jax.ShapeDtypeStruct(units.shape, bf16),
            jax.ShapeDtypeStruct((units.shape[1], 1, D, units.shape[3]), bf16),
        ],
        in_specs=[ANY] * 8,
        out_specs=[ANY] * 6,
        scratch_shapes=[
            pltpu.VMEM((T, n), bf16),
            pltpu.VMEM((D, n), bf16),
            pltpu.VMEM((R, D), f32),
            pltpu.VMEM((R, D), bf16),
            pltpu.VMEM((1, D), f32),
            pltpu.VMEM((2, 2 * R, n), bf16),
            pltpu.VMEM((2, 2 * R, n), bf16),
            pltpu.VMEM((R, D), bf16),
            pltpu.VMEM((1, D), f32),
            pltpu.VMEM((F, R, D), bf16),
            pltpu.VMEM((2, 2 * R, 2 * n), bf16),
            pltpu.VMEM((2, 512, n), bf16),
        ]
        + scatter_scratch(R, D)
        + [dma(8), dma(15), dma(10), dma(16), dma(copies), dma(copies), dma(C), dma(C)],
        compiler_params=params(3),
        cost_estimate=cost(108),
    )(h, wd, hid, cot, gain, act, der, units)


def mid_kernel(
    grad_ref, w_ref, cot_ref, ao_ref, gain_ref, wo_ref,
    res_ref, gg_ref, all_ref, gm_ref,
    grad, w, cot, ao, gain, wo, res, gacc, rows, gm, b0, b1, b2, b3, b4,
    lsem, osem, send, recv,
):
    at = Plane()
    e = wo.shape[1]
    pairs = [
        (grad_ref, grad), (w_ref, w),
        (cot_ref, cot), (ao_ref, ao), (gain_ref, gain), (wo_ref.at[:, pl.ds(3 * e, e)], wo),
    ]
    loads = [local(s, d, lsem, i) for i, (s, d) in enumerate(pairs)]
    at.greet()
    R = rows.shape[1]
    for c in loads[:2]:
        c.wait()

    def partial(chip, cols):
        return nt(grad[pl.ds(pl.multiple_of(chip * 2 * R, 2 * R), 2 * R), :], w[cols, :])

    total = scatter_phase(at, partial, (b0, b1, b2, b3, b4), send, recv, 0)
    for c in loads[2:]:
        c.wait()
    gacc[...] = jnp.zeros_like(gacc)

    def finish(r):
        resid = cot[r, :].astype(f32) + total(r)
        res[r, :] = resid
        out = ao[r, :]
        scale = rms(out)
        hat = out * scale
        gacc[...] += jnp.sum(resid * hat, axis=0, keepdims=True)
        rows[at.f, r, :] = back(resid * gain[...], hat, scale).astype(bf16)

    row_loop(R, finish)
    saves = [local(res, res_ref, lsem, 8), local(gacc, gg_ref, lsem, 9)]
    stores = Stores(osem)

    def on_rows(first, count):
        s = stores.slot()
        m = count * R
        start = pl.multiple_of(first * R, R)
        lhs = rows[pl.ds(first, count)].reshape(m, rows.shape[2])
        gm[s, pl.ds(0, m), :] = nn(lhs, wo[...]).astype(bf16)
        stores.put(
            [
                (gm.at[s, pl.ds(0, m)], gm_ref.at[pl.ds(start, m)]),
                (rows.at[pl.ds(first, count)], all_ref.at[pl.ds(first, count)]),
            ]
        )

    gather_phase(at, rows, send, recv, SCATTER_COPIES, on_rows)
    for s in saves:
        s.wait()
    stores.finish()


def mid_call(F, grad, w, cot, ao, gain, wo):
    R, D = cot.shape
    n, e = w.shape[1], wo.shape[1] // 4
    T = F * R
    copies = SCATTER_COPIES + GATHER_COPIES
    return pl.pallas_call(
        mid_kernel,
        out_shape=[
            jax.ShapeDtypeStruct((R, D), f32),
            jax.ShapeDtypeStruct((1, D), f32),
            jax.ShapeDtypeStruct((F, R, D), bf16),
            jax.ShapeDtypeStruct((T, e), bf16),
        ],
        in_specs=[ANY] * 6,
        out_specs=[ANY] * 4,
        scratch_shapes=[
            pltpu.VMEM((T, n), bf16),
            pltpu.VMEM((D, n), bf16),
            pltpu.VMEM((R, D), bf16),
            pltpu.VMEM((R, D), f32),
            pltpu.VMEM((1, D), f32),
            pltpu.VMEM((D, e), bf16),
            pltpu.VMEM((R, D), f32),
            pltpu.VMEM((1, D), f32),
            pltpu.VMEM((F, R, D), bf16),
            pltpu.VMEM((2, 2 * R, e), bf16),
        ]
        + scatter_scratch(R, D)
        + [dma(10), dma(10), dma(copies), dma(copies)],
        compiler_params=params(4),
        cost_estimate=cost(92),
    )(grad, w, cot, ao, gain, wo)


def last_kernel(
    width, q_ref, k_ref, v_ref, proj_ref, st_ref, in_ref, w_ref, res_ref, gain_ref,
    out_ref, gp_ref, gsum_ref,
    q, k, proj, st, ins, gains, gsum, gp, w, res, out, b0, b1, b2, b3, b4,
    lsem, send, recv, ssend, srecv, gsend, grecv,
):
    at = Plane()
    F, T = st.shape[0], st.shape[2]
    e = q.shape[1]
    R = res.shape[0]
    pairs = [
        (in_ref, ins.at[at.f]), (st_ref, st), (q_ref, q), (k_ref, k),
        (v_ref, gp.at[:, pl.ds(2 * e, e)]), (proj_ref.at[:, pl.ds(0, 2 * e)], proj), (w_ref.at[:, pl.ds(0, 3 * e)], w), (res_ref, res),
        (gain_ref, gains.at[at.f]),
    ]
    loads = [local(s, d, lsem, i) for i, (s, d) in enumerate(pairs)]
    barrier = pltpu.get_barrier_semaphore()
    for s in range(1, F):
        pl.semaphore_signal(barrier, inc=1, device_id={"fsdp": (at.f + s) % F}, device_id_type=MESH)
    pl.semaphore_wait(barrier, F - 1)
    loads[0].wait()
    share_stats(at, F, ins, ssend, srecv, 0)
    for c in loads[1:6]:
        c.wait()
    step = 256

    @pl.loop(0, T // step)
    def _(t):
        r = pl.ds(pl.multiple_of(t * step, step), step)
        sums = jnp.sum(st[:, :, r], axis=0)
        inner = jnp.sum(ins[:, :, r], axis=0) / width
        for row, grad in ((0, q), (1, k)):
            scale = lax.rsqrt(column(sums[row : row + 1], HEAD_DIM) / width + epsilon)
            mean = column(inner[row : row + 1], HEAD_DIM)
            for h in range(e // HEAD_DIM):
                hat = proj[r, row * e + h * HEAD_DIM : row * e + (h + 1) * HEAD_DIM] * scale
                got = scale * (grad[r, h * HEAD_DIM : (h + 1) * HEAD_DIM] - hat * mean)
                gp[r, row * e + h * HEAD_DIM : row * e + (h + 1) * HEAD_DIM] = got.astype(bf16)

    save = local(gp, gp_ref, lsem, 9)
    loads[6].wait()

    def partial(chip, cols):
        return nt(gp[pl.ds(pl.multiple_of(chip * 2 * R, 2 * R), 2 * R), :], w[cols, :])

    total = scatter_phase(at, partial, (b0, b1, b2, b3, b4), send, recv, 0)
    loads[7].wait()

    def finish(r):
        out[r, :] = (res[r, :] + total(r)).astype(bf16)

    row_loop(R, finish)
    store = local(out, out_ref, lsem, 10)
    loads[8].wait()
    share_stats(at, F, gains, gsend, grecv, 0)
    gsum[...] = jnp.sum(gains[...], axis=0)
    local(gsum, gsum_ref, lsem, 11).wait()
    store.wait()
    save.wait()


def last_call(F, wq, wk, gv, proj, st, ins, w, res, gains):
    R, D = res.shape
    n = w.shape[1] // 4 * 3
    T, e = F * R, n // 3
    return pl.pallas_call(
        functools.partial(last_kernel, D),
        out_shape=[
            jax.ShapeDtypeStruct((R, D), bf16),
            jax.ShapeDtypeStruct((T, n), bf16),
            jax.ShapeDtypeStruct((8, D), f32),
        ],
        in_specs=[ANY] * 9,
        out_specs=[ANY] * 3,
        scratch_shapes=[
            pltpu.VMEM((T, e), f32),
            pltpu.VMEM((T, e), f32),
            pltpu.VMEM((T, 2 * e), f32),
            pltpu.VMEM((F, 8, T), f32),
            pltpu.VMEM((F, 8, T), f32),
            pltpu.VMEM((F, 8, D), f32),
            pltpu.VMEM((8, D), f32),
            pltpu.VMEM((T, n), bf16),
            pltpu.VMEM((D, n), bf16),
            pltpu.VMEM((R, D), f32),
            pltpu.VMEM((R, D), bf16),
        ]
        + scatter_scratch(R, D)
        + [dma(12), dma(SCATTER_COPIES), dma(SCATTER_COPIES), dma(F), dma(F), dma(F), dma(F)],
        compiler_params=params(5),
        cost_estimate=cost(55),
    )(wq, wk, gv, proj, st, ins, w, res, gains)


def tn(a, b):
    return lax.dot_general(a, b, (((0,), (0,)), ((), ())), preferred_element_type=f32)


def grad_kernel(*refs):
    out = refs[-1]
    start = 0
    for x_ref, dy_ref in zip(refs[:-1:2], refs[1:-1:2]):
        got = tn(x_ref[...], dy_ref[...]).astype(bf16)
        units = dy_ref.shape[1] // out.shape[-1]
        for b in range(units):
            out[(start + b,) + (0,) * (len(out.shape) - 3)] = got[:, b * out.shape[-1] : (b + 1) * out.shape[-1]]
        start += units


def grad_call(pairs, units, cols, groups):
    T, D = pairs[0][0].shape
    tile = 512
    specs, args = [], []
    for x, dy in pairs:
        specs += [
            pl.BlockSpec((T, tile), lambda g, d: (0, d)),
            pl.BlockSpec((T, dy.shape[1] // groups), lambda g, d: (0, g)),
        ]
        args += [x, dy]
    return pl.pallas_call(
        grad_kernel,
        out_shape=jax.ShapeDtypeStruct((units, groups, D, cols), bf16),
        grid=(groups, D // tile),
        in_specs=specs,
        out_specs=pl.BlockSpec((units, 1, tile, cols), lambda g, d: (0, g, d, 0)),
        compiler_params=pltpu.CompilerParams(vmem_limit_bytes=VMEM_LIMIT),
        cost_estimate=cost(12 * groups),
    )(*args)


def share_stats(at, F, st, send, recv, base):
    sent = []
    for k in range(1, F):
        to = (at.f + k) % F
        c = remote(st.at[at.f], st.at[at.f], send, recv, base + k, to)
        c.start()
        sent.append(c)
    for k in range(1, F):
        frm = (at.f - k + F) % F
        remote(st.at[frm], st.at[frm], send, recv, base + k, frm).wait_recv()
    for c in sent:
        c.wait_send()


def row_sums(a, b):
    r = lax.broadcasted_iota(jnp.int32, (8, a.shape[1]), 0)
    one, two = (r == 0).astype(f32), (r == 1).astype(f32)

    def half(sel, v):
        return lax.dot_general(
            sel, v, (((1,), (1,)), ((), ())), preferred_element_type=f32, precision=lax.Precision.HIGHEST
        )

    return half(one, a) + half(two, b)


def column(row, lanes):
    return jnp.broadcast_to(row, (lanes, row.shape[1])).T


def turn(v, cos, sin):
    return v * cos + pltpu.roll(v, HEAD_DIM // 2, 1) * sin


def seq_columns(st, c, chips, R):
    return jnp.concatenate([st[:, pl.ds(pl.multiple_of((2 * j + c) * R, R), R)] for j in range(chips)], axis=1)


def attend_kernel(width, q_ref, k_ref, v_ref, st_ref, gq_ref, gk_ref, cos_ref, sin_ref, pos_ref, posc_ref, mix_ref, qr_ref, kr_ref, lse_ref):
    c = pl.program_id(0)
    chips, R = q_ref.shape[0], q_ref.shape[2]
    L = chips * R
    sums = jnp.sum(seq_columns_all(st_ref, c, chips, R), axis=0)
    cos, sin = cos_ref[0], sin_ref[0]

    def norm_turn(ref, row, gain):
        scale = lax.rsqrt(column(sums[row : row + 1], HEAD_DIM) / width + epsilon)
        return turn(ref[...].reshape(L, HEAD_DIM) * scale * gain[...], cos, sin)

    qr = (norm_turn(q_ref, 0, gq_ref) * HEAD_DIM ** (-0.5)).astype(bf16)
    kr = norm_turn(k_ref, 1, gk_ref).astype(bf16)
    v = v_ref[...].reshape(L, HEAD_DIM).astype(bf16)
    qr_ref[...] = qr.reshape(qr_ref.shape)
    kr_ref[...] = kr.reshape(kr_ref.shape)
    pos = pos_ref[0]
    for t in range(chips):
        rows = slice(t * R, (t + 1) * R)
        s = nt(qr[rows], kr)
        s = jnp.where(posc_ref[0, rows, :1] >= pos, s, -1e30)
        top = jnp.max(s, axis=-1, keepdims=True)
        e = jnp.exp(s - top)
        total = jnp.sum(e, axis=-1, keepdims=True)
        p = (e * (1.0 / total)).astype(bf16)
        mix_ref[t, 0] = nn(p, v).astype(bf16)
        lse_ref[0, 0, rows, :] = jnp.broadcast_to(top + jnp.log(total), (R, HEAD_DIM))


def seq_columns_all(st_ref, c, chips, R):
    return jnp.concatenate(
        [st_ref[:, :, pl.ds(pl.multiple_of((2 * j + c) * R, R), R)] for j in range(chips)], axis=2
    )


def attend_specs(chips, R, heads, F, L):
    def at(offset):
        return pl.BlockSpec((chips, 1, R, HEAD_DIM), lambda c, h: (0, c, 0, offset + h))

    gain = pl.BlockSpec((1, HEAD_DIM), lambda c, h: (0, h))
    table = pl.BlockSpec((1, L, HEAD_DIM), lambda c, h: (c, 0, 0))
    stats = pl.BlockSpec((F, 8, F * R), lambda c, h: (0, 0, 0))
    posr = pl.BlockSpec((1, 1, L), lambda c, h: (c, 0, 0))
    lse = pl.BlockSpec((1, 1, L, HEAD_DIM), lambda c, h: (c, h, 0, 0))
    return at, gain, table, stats, posr, lse


def attend_call(F, proj, st, gq, gk, cos, sin, pos, posc):
    R = proj.shape[0] // F
    e = proj.shape[1] // 3
    heads, chips = e // HEAD_DIM, F // 2
    L = chips * R
    at, gain, table, stats, posr, lse = attend_specs(chips, R, heads, F, L)
    view = proj.reshape(chips, 2, R, 3 * e)
    flat = jax.ShapeDtypeStruct((chips, 2, R, e), bf16)
    out = pl.pallas_call(
        functools.partial(attend_kernel, heads * HEAD_DIM * F),
        out_shape=[flat, flat, flat, jax.ShapeDtypeStruct((2, heads, L, HEAD_DIM), f32)],
        grid=(2, heads),
        in_specs=[at(0), at(heads), at(2 * heads), stats, gain, gain, table, table, posr, table],
        out_specs=[at(0), at(0), at(0), lse],
        compiler_params=pltpu.CompilerParams(vmem_limit_bytes=VMEM_LIMIT),
        cost_estimate=cost(15),
    )(view, view, view, st, gq, gk, cos, sin, pos, posc)
    return out


def attend_back_kernel(
    width, q_ref, k_ref, v_ref, qr_ref, kr_ref, gm_ref, lse_ref, st_ref, gq_ref, gk_ref, cos_ref, sin_ref, pos_ref, posc_ref,
    wq_ref, wk_ref, gv_ref, in_ref, gg_ref, dk, dv, dq,
):
    c = pl.program_id(0)
    chips, R = q_ref.shape[0], q_ref.shape[2]
    L = chips * R
    kr = kr_ref[...].reshape(L, HEAD_DIM)
    v = v_ref[...].reshape(L, HEAD_DIM).astype(bf16)
    pos = pos_ref[0]
    dk[...] = jnp.zeros_like(dk)
    dv[...] = jnp.zeros_like(dv)
    for t in range(chips):
        rows = slice(t * R, (t + 1) * R)
        qt, gm = qr_ref[t, 0], gm_ref[t, 0]
        s = nt(qt, kr)
        s = jnp.where(posc_ref[0, rows, :1] >= pos, s, -1e30)
        p = jnp.exp(s - lse_ref[0, 0, rows, :1])
        dp = nt(gm, v)
        dv[...] += lax.dot_general(p.astype(bf16), gm, (((0,), (0,)), ((), ())), preferred_element_type=f32)
        inner = jnp.sum(dp * p, axis=-1, keepdims=True)
        ds = (p * (dp - inner)).astype(bf16)
        dq[rows, :] = nn(ds, kr)
        dk[...] += lax.dot_general(ds, qt, (((0,), (0,)), ((), ())), preferred_element_type=f32)
    gv_ref[...] = dv[...].astype(bf16).reshape(gv_ref.shape)
    sums = jnp.sum(seq_columns_all(st_ref, c, chips, R), axis=0)
    cos, sin = cos_ref[0], sin_ref[0]

    def finish(grad, ref, row, gain, out):
        norm = turn(grad, cos, -sin)
        hat = ref[...].reshape(L, HEAD_DIM) * lax.rsqrt(column(sums[row : row + 1], HEAD_DIM) / width + epsilon)
        gg_ref[0, 0, row : row + 1, :] = jnp.sum(norm * hat, axis=0, keepdims=True)
        weighted = norm * gain[...]
        out[...] = weighted.reshape(out.shape)
        return weighted * hat

    gg_ref[...] = jnp.zeros_like(gg_ref)
    in_ref[0, 0] = row_sums(
        finish(dq[...] * HEAD_DIM ** (-0.5), q_ref, 0, gq_ref, wq_ref), finish(dk[...], k_ref, 1, gk_ref, wk_ref)
    )


def attend_back_call(F, proj, qr, kr, gm, lse_in, st, gq, gk, cos, sin, pos, posc):
    R = proj.shape[0] // F
    e = proj.shape[1] // 3
    heads, chips = e // HEAD_DIM, F // 2
    L = chips * R
    at, gain, table, stats, posr, lse = attend_specs(chips, R, heads, F, L)
    view = proj.reshape(chips, 2, R, 3 * e)
    flat = (chips, 2, R, e)
    small = pl.BlockSpec((1, 1, 8, L), lambda c, h: (c, h, 0, 0))
    tiny = pl.BlockSpec((1, 1, 8, HEAD_DIM), lambda c, h: (c, h, 0, 0))
    wide = jax.ShapeDtypeStruct(flat, f32)
    return pl.pallas_call(
        functools.partial(attend_back_kernel, heads * HEAD_DIM * F),
        out_shape=[
            wide, wide, jax.ShapeDtypeStruct(flat, bf16),
            jax.ShapeDtypeStruct((2, heads, 8, L), f32),
            jax.ShapeDtypeStruct((2, heads, 8, HEAD_DIM), f32),
        ],
        grid=(2, heads),
        in_specs=[
            at(0), at(heads), at(2 * heads), at(0), at(0), at(0), lse, stats, gain, gain, table, table, posr, table,
        ],
        out_specs=[at(0), at(0), at(0), small, tiny],
        scratch_shapes=[pltpu.VMEM((L, HEAD_DIM), f32)] * 3,
        compiler_params=pltpu.CompilerParams(vmem_limit_bytes=VMEM_LIMIT),
        cost_estimate=cost(35),
    )(view, view, view, qr, kr, gm.reshape(flat), lse_in, st, gq, gk, cos, sin, pos, posc)


class Sides:
    def __init__(self, out, into):
        self.out, self.into = out, into

    def wait(self):
        self.out.wait_send()
        self.into.wait_recv()


def newton_kernel(
    C, m_ref, res_ref, gin_ref, gain_ref, grad_ref, late_ref, out_ref, stage_ref, gsum_ref, back_ref,
    v, gram, y, yf, stat, gains, gsum,
    lsem, osem, vsend, vrecv, ysend, yrecv, ssend, srecv, tsend, trecv, gsend, grecv, usend, urecv, usem, bsend, brecv, isend, irecv,
):
    me = lax.axis_index("fsdp")
    z = lax.axis_index("ctx")
    core, chip = me % 2, me // 2
    peer = me + 1 - 2 * core
    F = 2 * C
    cols = m_ref.shape[2]
    gload = local(gain_ref, gains.at[z], lsem, 1)
    barrier = pltpu.get_barrier_semaphore()
    for k in range(1, C):
        pl.semaphore_signal(barrier, inc=1, device_id={"ctx": (z + k) % C}, device_id_type=MESH)
    for k in range(1, F):
        pl.semaphore_signal(barrier, inc=1, device_id={"fsdp": (me + k) % F}, device_id_type=MESH)
    pl.semaphore_wait(barrier, C + F - 2)
    rows_in = v.shape[1] // C
    def fellow(a, other):
        to = partner(chip, a) if a else chip
        return 2 * to + (1 - core if other else core)

    units_sent, units_kept = [], []
    for a in (3, 1, 2, 0):
        for other in range(2):
            to = fellow(a, other)
            for b in range(C):
                src = m_ref.at[to // 2, pl.ds((2 * b + to % 2) * rows_in, rows_in)]
                dst = v.at[0, pl.ds(b * rows_in, rows_in), pl.ds(me * cols, cols)]
                if a == 0 and other == 0:
                    units_kept.append(local(src, dst, usem, b))
                else:
                    c = remote(src, dst, usend, urecv, (2 * a + other) * C + b, to)
                    c.start()
                    units_sent.append(c)
    piece = res_ref.shape[0] // C

    def part(j):
        return pl.ds(j * piece, piece)

    late = grad_ref.shape[2]

    def back_to(layer, frm, k, kind):
        if kind == 0:
            src = late_ref.at[pl.ds(pl.multiple_of(layer * late, late), late)]
            return src, back_ref.at[frm, 0], k
        return grad_ref.at[layer], back_ref.at[frm, pl.ds(1, grad_ref.shape[1])], C + k

    sent, keep = [], []
    for kind in range(2):
        src, dst, _ = back_to(z, z, 0, kind)
        keep.append(local(src, dst, lsem, (0, 4)[kind]))
        for k in FAR_FIRST:
            to = partner(z, k)
            src, dst, i = back_to(to, z, k, kind)
            c = remote(src, dst, bsend, brecv, i, to, "ctx")
            c.start()
            sent.append(c)
    for a, rows_ref in enumerate((res_ref, gin_ref)):
        for k in FAR_FIRST:
            to = partner(z, k)
            c = remote(rows_ref.at[part(to)], stage_ref.at[a, z], tsend, trecv, C * a + k, to, "ctx")
            c.start()
            sent.append(c)
        keep.append(local(rows_ref.at[part(z)], stage_ref.at[a, z], lsem, 2 + a))
    gload.wait()
    for k in range(1, C):
        c = remote(gains.at[z], gains.at[z], gsend, grecv, k, (z + k) % C, "ctx")
        c.start()
        sent.append(c)

    def rows_arrived():
        for c in keep:
            c.wait()
        for kind in range(2):
            for k in FAR_FIRST:
                _, dst, i = back_to(z, partner(z, k), k, kind)
                remote(dst, dst, bsend, brecv, i, partner(z, k), "ctx").wait_recv()
        for a in range(2):
            for k in FAR_FIRST:
                dst = stage_ref.at[a, partner(z, k)]
                remote(dst, dst, tsend, trecv, C * a + k, partner(z, k), "ctx").wait_recv()
        for k in range(1, C):
            frm = (z - k + C) % C
            remote(gains.at[frm], gains.at[frm], gsend, grecv, k, frm, "ctx").wait_recv()
        gsum[...] = jnp.sum(gains[...], axis=0)
        local(gsum, gsum_ref, lsem, 6).wait()
        for c in sent:
            c.wait_send()

    stat[0] = jnp.zeros_like(stat[0])

    def columns(owner):
        return pl.ds(pl.multiple_of(owner * cols, cols), cols)

    def pass_on(a, other, owner=None):
        i = 2 * a + other
        c = columns(fellow(a, other if owner is None else owner))
        return remote(v.at[0, :, c], v.at[1, :, c], isend, irecv, i, peer)

    pending = []
    for a in range(C):
        for other in range(2):
            frm = fellow(a, other)
            if a == 0 and other == 0:
                for c in units_kept:
                    c.wait()
            else:
                for b in range(C):
                    dst = v.at[0, pl.ds(b * rows_in, rows_in), columns(frm)]
                    remote(dst, dst, usend, urecv, (2 * a + other) * C + b, frm).wait_recv()
            c = pass_on(a, other)
            c.start()
            pending.append(Sides(c, pass_on(a, other, 1 - other)))

            @pl.loop(0, v.shape[1] // 128)
            def _(r):
                block = v[0, pl.ds(pl.multiple_of(r * 128, 128), 128), columns(frm)].astype(f32)
                stat[0] += jnp.sum((block * block).reshape(-1, 8, cols // 128, 128), axis=(0, 2))

    for c in units_sent:
        c.wait_send()
    M, D = v.shape[1], v.shape[2]
    tile, col = 512, 1024
    tiles = M // tile

    def block(i):
        return pl.ds(pl.multiple_of(i * tile, tile), tile)

    halves = D // col

    def swap(buf, n, i, sends, recvs):
        part = (block(i), pl.ds(n * col, col))
        return remote(buf.at[(0, *part)], buf.at[(1, *part)], sends, recvs, n * tiles + i, peer)

    share = remote(stat.at[0], stat.at[1], ssend, srecv, 0, peer)
    share.start()
    share.wait()
    inv = 1.0 / (jnp.sqrt(jnp.sum(stat[0] + stat[1])) + 1e-07)

    for iteration in range(NS_STEPS):
        factor = inv if iteration == 0 else 1.0

        def grams(h, n):
            rhs = pl.ds(pl.multiple_of(n * col, col), col)
            cols = pl.ds(pl.multiple_of(h * M + n * col, col), col)

            @pl.loop(0, tiles)
            def _(i):
                rows = pl.ds(pl.multiple_of(i * tile, tile), tile)
                got = nt(v[0, rows, :], v[h, rhs, :])
                if iteration == 0:
                    got = got * (factor * factor)
                gram[rows, cols] = got.astype(bf16)

        @pl.loop(0, M // col)
        def _(n):
            grams(0, n)

        for c in pending:
            c.wait()

        @pl.loop(0, M // col)
        def _(n):
            grams(1, n)

        def times(src, i, n):
            rows, c = block(i), pl.ds(n * col, col)
            return nn(gram[rows, :M], src[0, :, c]) + nn(gram[rows, M:], src[1, :, c])

        swaps = []
        for n in range(halves):

            @pl.loop(0, tiles)
            def _(i):
                at = (block(i), pl.ds(n * col, col))
                got = times(v, i, n)
                if iteration == 0:
                    got = got * factor
                yf[at] = got
                y[(0, *at)] = got.astype(bf16)
                swap(y, n, i, ysend, yrecv).start()

            swaps += [swap(y, n, i, ysend, yrecv) for i in range(tiles)]
        pending = []
        for n in range(halves):
            for c in swaps[n * tiles : (n + 1) * tiles]:
                c.wait()

            @pl.loop(0, tiles)
            def _(i):
                at = (block(i), pl.ds(n * col, col))
                got = times(y, i, n)
                old = v[(0, *at)].astype(f32)
                if iteration == 0:
                    old = old * factor
                v[(0, *at)] = (quintic_one * old + quintic_two * yf[at] + quintic_three * got).astype(bf16)
                if iteration < NS_STEPS - 1:
                    swap(v, n, i, vsend, vrecv).start()

            if iteration < NS_STEPS - 1:
                pending += [swap(v, n, i, vsend, vrecv) for i in range(tiles)]
            else:
                for b in range(C):
                    for g in range(n * col // cols, (n + 1) * col // cols):
                        src = v.at[0, pl.ds(b * rows_in, rows_in), pl.ds(g * cols, cols)]
                        pending.append(local(src, out_ref.at[b * F + g], osem, b * F + g))
    rows_arrived()
    for c in pending:
        c.wait()


def newton_call(C, x, result, grad_rows, gains, grads, late):
    _, D, cols = x.shape
    M = D // 2
    R = result.shape[0]
    n = 4
    return pl.pallas_call(
        functools.partial(newton_kernel, C),
        out_shape=[
            jax.ShapeDtypeStruct((2 * C * C, M // C, cols), bf16),
            jax.ShapeDtypeStruct((2, C, R // C, D), bf16),
            jax.ShapeDtypeStruct((8, D), f32),
            jax.ShapeDtypeStruct((C, C, *grads.shape[2:]), bf16),
        ],
        in_specs=[ANY] * 6,
        out_specs=[ANY] * 4,
        scratch_shapes=[
            pltpu.VMEM((2, M, D), bf16),
            pltpu.VMEM((M, 2 * M), bf16),
            pltpu.VMEM((2, M, D), bf16),
            pltpu.VMEM((M, D), f32),
            pltpu.VMEM((2, 8, 128), f32),
            pltpu.VMEM((C, 8, D), f32),
            pltpu.VMEM((8, D), f32),
            dma(7), dma(2 * C * C), dma(n), dma(n), dma(n), dma(n), dma(1), dma(1),
            dma(2 * C), dma(2 * C), dma(C), dma(C), dma(2 * C * C), dma(2 * C * C), dma(C), dma(2 * C), dma(2 * C), dma(2 * C), dma(2 * C),
        ],
        compiler_params=params(6),
        cost_estimate=cost(95),
    )(x, result, grad_rows, gains, grads, late)


def project(C, F, x, w):
    own = to_layer(C, F, x)
    rows = token_rows(own)
    return own, rows, dot(rows, w, 1, 0)


def attn_out_and_up(C, F, mixed, wo, x, gain, w, cot):
    if kernels_fit(C, F):
        hidden_in, out, inp = out_call(F, mixed, wo, x, gain)
        rows, act, der, h, cot = up_call(C, F, inp, w, cot)
        return cot, hidden_in, out, rows, act, der, h
    out = token_sums(dot(mixed, wo, 1, 1))
    hidden_in = x.astype(f32) + out * rms(out) * gain
    rows = token_rows(hidden_in.astype(bf16))
    g, u = jnp.split(dot(rows, w, 1, 0), 2, axis=1)
    sig = jax.nn.sigmoid(g)
    der = u * (sig * (1.0 + g * (1.0 - sig)))
    act = g * sig
    cot = to_layer(C, F, cot)
    return cot, hidden_in, out, rows, act.astype(bf16), der.astype(bf16), (act * u).astype(bf16)


def down_and_back(C, F, h, wd, hidden_in, cot, gain, act, der, units):
    if kernels_fit(C, F):
        return down_call(C, F, h, wd, hidden_in, cot, gain, act, der, units)
    out = token_sums(dot(h, wd, 1, 1))
    scale = rms(out)
    hat = out * scale
    g = cot.astype(f32)
    rows = token_rows(back(g * gain, hat, scale).astype(bf16))
    gh = dot(rows, wd, 1, 0)
    return (
        (hidden_in + hat * gain).astype(bf16),
        jnp.sum(g * hat, axis=0, keepdims=True),
        rows,
        jnp.concatenate([(gh * der.astype(f32)).astype(bf16), (gh * act.astype(f32)).astype(bf16)], axis=1),
        None,
        None,
    )


def back_to_attn(C, F, grad, w, cot, out, gain, wo):
    if kernels_fit(C, F):
        return mid_call(F, grad, w, cot, out, gain, wo)
    resid = cot.astype(f32) + token_sums(dot(grad, w, 1, 1))
    scale = rms(out)
    hat = out * scale
    rows = token_rows(back(resid * gain, hat, scale).astype(bf16))
    return resid, jnp.sum(resid * hat, axis=0, keepdims=True), rows, dot(rows, wo, 1, 0).astype(bf16)


def back_to_input(C, F, grad_projected, w, resid):
    return (resid + token_sums(dot(grad_projected, w, 1, 1))).astype(bf16)


def kernels_fit(C, F):
    return C == 4 and F == 8 and UNITS_ATTN * 4 * 2 == C * F


def to_layer(C, F, x):
    z, chip = lax.axis_index("ctx"), lax.axis_index("fsdp") // 2
    x = x.reshape(C, x.shape[0] // C, x.shape[1])
    got = []
    for k in range(C):
        pairs = [
            (s * F + f, (f // 2) * F + 2 * ((s + k) % C) + f % 2) for s in range(C) for f in range(F)
        ]
        block = lax.dynamic_index_in_dim(x, (z + k) % C, 0, keepdims=False)
        got.append(lax.ppermute(block, BOTH, pairs))
    got = jnp.stack(got)
    got = [lax.dynamic_index_in_dim(got, (chip - s + C) % C, 0, keepdims=False) for s in range(C)]
    return jnp.concatenate(got, axis=0)


def go_home(C, F, stage):
    chip = lax.axis_index("fsdp") // 2
    got = [lax.dynamic_index_in_dim(stage, chip, 1, keepdims=False)]
    for k in range(1, C):
        pairs = [(f, 2 * ((f // 2 + k) % C) + f % 2) for f in range(F)]
        block = lax.dynamic_index_in_dim(stage, (chip + k) % C, 1, keepdims=False)
        got.append(lax.ppermute(block, "fsdp", pairs))
    return got


def at_home(C, got):
    chip = lax.axis_index("fsdp") // 2
    got = jnp.stack(got)
    got = [lax.dynamic_index_in_dim(got, (chip - j + C) % C, 0, keepdims=False) for j in range(C)]
    return jnp.concatenate(got, axis=1)


def from_layer(C, F, x):
    z, chip = lax.axis_index("ctx"), lax.axis_index("fsdp") // 2
    x = x.reshape(C, x.shape[0] // C, x.shape[1])
    got = []
    for k in range(C):
        pairs = [
            ((f // 2) * F + 2 * ((s + k) % C) + f % 2, s * F + f) for s in range(C) for f in range(F)
        ]
        block = lax.dynamic_index_in_dim(x, (chip - k + C) % C, 0, keepdims=False)
        got.append(lax.ppermute(block, BOTH, pairs))
    got = jnp.stack(got)
    got = [lax.dynamic_index_in_dim(got, (j - z + C) % C, 0, keepdims=False) for j in range(C)]
    return jnp.concatenate(got, axis=0)


def shards(C, F, layer_input, cotangent, positions, w_attn, w_ffn, gains, mom_attn, mom_ffn, gain_mom):
    z = lax.axis_index("ctx")
    f = lax.axis_index("fsdp")
    local_rows, width = layer_input.shape[1], layer_input.shape[2]
    seq_total, seq_length = positions.shape
    dz, head_cols = w_attn.shape[1], w_attn.shape[2]
    local_heads = head_cols // HEAD_DIM
    block_count = w_ffn.shape[2]
    per = seq_total // C
    piece = local_rows // C
    chips = F // per
    tokens = F * local_rows
    hidden_cols = block_count * head_cols
    units = UNITS_ATTN + 3 * block_count
    parts = C * F // units

    def after(a, b):
        return lax.optimization_barrier((a, b))[0]

    def rows_gather(shard):
        return lax.all_gather(shard, "ctx", axis=0, tiled=True)

    def product(units, groups, *pairs):
        pairs = [(x.reshape(tokens, width), dy) for x, dy in pairs]
        if kernels:
            return grad_call(pairs, units, head_cols, groups)
        grad = jnp.concatenate([dot(x, dy, 0, 0).astype(bf16) for x, dy in pairs], axis=1)
        return jnp.transpose(grad.reshape(width, groups, units, head_cols), (2, 1, 0, 3))

    def scatter(grad):
        if kernels:
            return lax.psum_scatter(grad, "ctx", scatter_dimension=0, tiled=True)[0]
        return lax.psum_scatter(grad, "ctx", scatter_dimension=2, tiled=True)

    kernels = kernels_fit(C, F)
    w_heads = rows_gather(jnp.concatenate([w_attn[i] for i in range(UNITS_ATTN)], axis=1))
    w_qkv, w_out = (w_heads, w_heads) if kernels else (w_heads[:, : 3 * head_cols], w_heads[:, 3 * head_cols :])
    ffn_flat = w_ffn.reshape(3, dz, hidden_cols)
    w_gate_up = rows_gather(jnp.concatenate([ffn_flat[0], ffn_flat[1]], axis=1))
    w_down = rows_gather(ffn_flat[2])

    gain_query = lax.dynamic_slice_in_dim(gains[0], f * head_cols, head_cols)
    gain_key = lax.dynamic_slice_in_dim(gains[1], f * head_cols, head_cols)
    pos = lax.dynamic_slice_in_dim(positions, z * per, per, 0)
    pos = jnp.transpose(pos.reshape(per, C, chips, piece), (0, 2, 1, 3)).reshape(per, seq_length)
    cosine_table, sine_table = rotary_tables(pos)

    def heads(a):
        return jnp.transpose(
            a.reshape(chips, per, local_rows, local_heads, HEAD_DIM), (1, 0, 2, 3, 4)
        ).reshape(per, seq_length, local_heads, HEAD_DIM)

    def unheads(a):
        return jnp.transpose(
            a.reshape(per, chips, local_rows, local_heads, HEAD_DIM), (1, 0, 2, 3, 4)
        ).reshape(tokens, head_cols)

    if kernels:
        sign = jnp.where(jnp.arange(HEAD_DIM) < HEAD_DIM // 2, -1.0, 1.0)
        tables = (
            gain_query[None],
            gain_key[None],
            jnp.broadcast_to(cosine_table[:, :, 0], (per, seq_length, HEAD_DIM)),
            sine_table[:, :, 0] * sign,
            pos.astype(f32)[:, None, :],
            jnp.broadcast_to(pos.astype(f32)[..., None], (per, seq_length, HEAD_DIM)),
        )
        own_input, input_all = enter_call(C, F, layer_input.reshape(local_rows, width))
        projected, stats = qkv_call(F, input_all, w_qkv)
        attn_mixed, query_rows, key_rows, log_total = attend_call(F, projected, stats, *tables)
        attn_mixed = attn_mixed.reshape(tokens, head_cols)
    else:
        own_input, input_all, projected = project(C, F, layer_input.reshape(local_rows, width), w_qkv)
        query_raw = projected[:, :head_cols]
        key_raw = projected[:, head_cols : 2 * head_cols]
        value_raw = projected[:, 2 * head_cols :]
        query_total, key_total = norm_stats(
            jnp.sum(query_raw * query_raw, axis=-1), jnp.sum(key_raw * key_raw, axis=-1)
        )
        query_scale = lax.rsqrt(query_total / width + epsilon)[..., None]
        key_scale = lax.rsqrt(key_total / width + epsilon)[..., None]
        query_hat = query_raw * query_scale
        key_hat = key_raw * key_scale
        query_rows = (
            rotate(heads(query_hat * gain_query), cosine_table, sine_table) * HEAD_DIM ** (-0.5)
        ).astype(bf16)
        key_rows = rotate(heads(key_hat * gain_key), cosine_table, sine_table).astype(bf16)
        value_rows = heads(value_raw.astype(bf16))
        attn_mixed, log_total = attend(query_rows, key_rows, value_rows, pos)
        attn_mixed = unheads(attn_mixed)
    own_grad, hidden_in, attn_out, mlp_all, act, der, hidden = attn_out_and_up(
        C, F, attn_mixed, w_out, own_input, gains[2:3], w_gate_up,
        cotangent.reshape(local_rows, width),
    )
    by_layer = None
    if kernels:
        by_layer = jnp.concatenate(
            [mom_attn[:, None].astype(bf16), jnp.transpose(mom_ffn.astype(bf16), (2, 0, 1, 3))], axis=1
        )
    result, mlp_gain, grad_mlp_all, grad_ffn_in, mom_own, p_down = down_and_back(
        C, F, hidden, w_down, hidden_in, own_grad, gains[3:4], act, der, by_layer
    )
    if kernels:
        mom_own = jnp.swapaxes(mom_own, 0, 1)
    else:
        p_down = product(block_count, 1, (grad_mlp_all, hidden))
    g_down = scatter(p_down)
    p_gate_up = product(block_count, 2, (mlp_all, grad_ffn_in))
    if kernels:
        grad_ffn_in, p_gate_up = lax.optimization_barrier((grad_ffn_in, p_gate_up))
    g_gate_up = scatter(p_gate_up)
    grad_resid, attn_gain, grad_attn_all, grad_mixed = back_to_attn(
        C, F, grad_ffn_in, w_gate_up, own_grad, attn_out, gains[2:3], w_out
    )
    if kernels:
        grad_mixed = after(grad_mixed, g_down)
        weighted_q, weighted_k, grad_value, inner, gain_cols = attend_back_call(
            F, projected, query_rows, key_rows, grad_mixed, log_total, stats, *tables
        )
        inner = jnp.transpose(
            jnp.sum(inner, axis=1).reshape(per, 8, chips, local_rows), (1, 2, 0, 3)
        ).reshape(8, tokens)
        gain_cols = jnp.sum(gain_cols, axis=0)
        query_gain_cols = gain_cols[:, 0].reshape(head_cols)
        key_gain_cols = gain_cols[:, 1].reshape(head_cols)
        flat = (tokens, head_cols)
        zero = jnp.zeros((width,), f32)
        gain_local = jnp.stack(
            [
                lax.dynamic_update_slice(zero, query_gain_cols, (f * head_cols,)),
                lax.dynamic_update_slice(zero, key_gain_cols, (f * head_cols,)),
                attn_gain[0],
                mlp_gain[0],
                *[zero] * 4,
            ]
        )
        grad_rows, grad_projected, gain_layer = last_call(
            F, weighted_q.reshape(flat), weighted_k.reshape(flat), grad_value.reshape(flat),
            projected, stats, inner, w_qkv, grad_resid, gain_local,
        )
    else:
        grad_query, grad_key, grad_value = attend_back(
            query_rows, key_rows, value_rows, pos, heads(grad_mixed), log_total
        )
        grad_query_norm = unheads(unrotate(grad_query * HEAD_DIM ** (-0.5), cosine_table, sine_table))
        grad_key_norm = unheads(unrotate(grad_key, cosine_table, sine_table))
        query_gain_cols = jnp.sum(grad_query_norm * query_hat, axis=0)
        key_gain_cols = jnp.sum(grad_key_norm * key_hat, axis=0)
        query_weighted = grad_query_norm * gain_query
        key_weighted = grad_key_norm * gain_key
        query_inner, key_inner = norm_stats(
            jnp.sum(query_weighted * query_hat, axis=-1), jnp.sum(key_weighted * key_hat, axis=-1)
        )
        grad_query_raw = query_scale * (query_weighted - query_hat * (query_inner / width)[..., None])
        grad_key_raw = key_scale * (key_weighted - key_hat * (key_inner / width)[..., None])
        grad_projected = jnp.concatenate(
            [grad_query_raw.astype(bf16), grad_key_raw.astype(bf16), unheads(grad_value).astype(bf16)],
            axis=1,
        )
        grad_rows = back_to_input(C, F, grad_projected, w_qkv, grad_resid)
    g_attn = scatter(
        product(UNITS_ATTN, 1, (input_all, grad_projected), (grad_attn_all, attn_mixed))
    )
    if not kernels:
        grad_input = from_layer(C, F, grad_rows)
        result = from_layer(C, F, result)
        zero = jnp.zeros((width,), f32)
        gain_local = jnp.stack(
            [
                lax.dynamic_update_slice(zero, query_gain_cols, (f * head_cols,)),
                lax.dynamic_update_slice(zero, key_gain_cols, (f * head_cols,)),
                attn_gain[0],
                mlp_gain[0],
            ]
        )
        gain_total = jnp.sum(lax.all_gather(gain_local, BOTH, axis=0, tiled=False), axis=0)

    if kernels:
        early = jnp.stack([g_gate_up[0], g_gate_up[1], g_down[0]])
        mom = momentum * mom_own.reshape(UNITS_ATTN, width, head_cols).astype(f32)
        owned = jnp.concatenate([jnp.zeros_like(early[:1]), (mom[1:] + early.astype(f32)).astype(bf16)], axis=0)
        mom_first = mom[0]
        early = jnp.swapaxes(early.reshape(3, C, dz, head_cols), 0, 1)
        early, owned, mom_first, grad_rows = lax.optimization_barrier((early, owned, mom_first, grad_rows))
        late = (mom_first + g_attn[0].astype(f32)).astype(bf16)
        owned = lax.dynamic_update_slice(owned, late[None], (0, 0, 0))
        own, leaving, gain_total, sent_back = newton_call(
            C, owned, result, grad_rows, gain_layer, early, g_attn[0]
        )
        sent_back = sent_back.astype(f32)
        grad_attn = sent_back[:, 0]
        grad_ffn = jnp.transpose(sent_back[:, 1:], (1, 2, 0, 3))
        homing = go_home(C, F, leaving)
        gain_total = gain_total[:4]
    else:
        grad_attn = g_attn[:, 0].astype(f32)
        grad_ffn = jnp.transpose(
            jnp.concatenate([g_gate_up, g_down], axis=1).astype(f32), (1, 2, 0, 3)
        )
    new_attn = momentum * mom_attn + grad_attn
    new_ffn = momentum * mom_ffn + grad_ffn
    if kernels:
        homing, new_attn, new_ffn, grad_attn, grad_ffn = lax.optimization_barrier(
            (homing, new_attn, new_ffn, grad_attn, grad_ffn)
        )
        back_rows = at_home(C, homing)
        result, grad_input = back_rows[0], back_rows[1]
    if not kernels:
        send = jnp.concatenate(
            [
                new_attn.astype(bf16),
                jnp.transpose(new_ffn.astype(bf16), (0, 2, 1, 3)).reshape(3 * block_count, dz, head_cols),
            ],
            axis=0,
        ).reshape(C * F, dz // parts, head_cols)
        own = lax.all_to_all(send, BOTH, split_axis=0, concat_axis=0, tiled=True)
        own = jnp.transpose(own.reshape(C, F, dz // parts, head_cols), (0, 2, 1, 3)).reshape(
            C * dz // parts, F * head_cols
        )

        def peers(a):
            out = [a]
            for s in range(1, parts):
                pairs = [(i, i - i % parts + (i + parts - s) % parts) for i in range(C * F)]
                out.append(lax.ppermute(a, BOTH, pairs))
            return out

        own32 = own.astype(f32)
        square = jnp.sum(own32 * own32)
        total = sum(peers(square.reshape(1, 1)))
        inv = 1.0 / (jnp.sqrt(total) + 1e-07)
        for iteration in range(NS_STEPS):
            factor = inv if iteration == 0 else 1.0
            every = peers(own)
            gram = [(dot(own, b, 1, 1) * (factor * factor)).astype(bf16) for b in every]
            product = sum(dot(g, b, 1, 0) for g, b in zip(gram, every)) * factor
            product_all = peers(product.astype(bf16))
            product_two = sum(dot(g, b, 1, 0) for g, b in zip(gram, product_all))
            own = (
                quintic_one * factor * own.astype(f32) + quintic_two * product + quintic_three * product_two
            ).astype(bf16)
    if kernels:
        home = own
    else:
        home = jnp.transpose(own.reshape(C, dz // parts, F, head_cols), (0, 2, 1, 3)).reshape(
            C * F, dz // parts, head_cols
        )
    steps = lax.all_to_all(home, BOTH, split_axis=0, concat_axis=0, tiled=True)
    if kernels:
        steps = steps.reshape(C, UNITS_ATTN, dz, head_cols)
        arranged = lax.optimization_barrier(jnp.transpose(steps[:, 1:], (1, 2, 0, 3)))
        step_attn = -muon_rate * steps[:, 0].astype(f32)
        step_ffn = -muon_rate * arranged.astype(f32)
    else:
        steps = -muon_rate * steps.astype(f32)
        steps = steps.reshape(units, dz, head_cols)
        step_attn = steps[:UNITS_ATTN]
        step_ffn = jnp.transpose(
            steps[UNITS_ATTN:].reshape(3, block_count, dz, head_cols), (0, 2, 1, 3)
        )
    new_gain_mom = momentum * gain_mom + gain_total
    return (
        result.reshape(layer_input.shape),
        grad_input.astype(f32).reshape(layer_input.shape),
        grad_attn,
        grad_ffn,
        gain_total,
        new_attn,
        new_ffn,
        new_gain_mom,
        step_attn,
        step_ffn,
        -gain_rate * new_gain_mom,
    )


def solution(mesh):
    tokens = P("fsdp", "ctx", None)
    attn = P(None, "ctx", "fsdp")
    ffn = P(None, "ctx", None, "fsdp")
    in_specs = (tokens, tokens, P(), attn, ffn, P(), attn, ffn, P())
    out_specs = (tokens, tokens, attn, ffn, P(), attn, ffn, P(), attn, ffn, P())
    body = functools.partial(shards, mesh.shape["ctx"], mesh.shape["fsdp"])
    return jax.shard_map(body, mesh=mesh, in_specs=in_specs, out_specs=out_specs, check_vma=False)
```

```python
import functools
import jax
import jax.numpy as jnp
from jax import lax
from jax.experimental import pallas as pl
from jax.experimental.pallas import tpu as pltpu
from jax.sharding import PartitionSpec as P

NS_STEPS = 3
HEAD_DIM = 128
UNITS_ATTN = 4

epsilon = 1e-06
rope_theta = 500000.0
quintic_one = 3.4445
quintic_two = -4.775
quintic_three = 2.0315
momentum = 0.95
muon_rate = 1.0
gain_rate = 0.0005
BOTH = ("ctx", "fsdp")
bf16 = jnp.bfloat16
f32 = jnp.float32


def dot(a, b, ca, cb):
    return lax.dot_general(a, b, (((ca,), (cb,)), ((), ())), preferred_element_type=f32)


def token_rows(operand):
    return lax.all_gather(operand, "fsdp", axis=0, tiled=True)


def token_sums(operand):
    return lax.psum_scatter(operand.astype(bf16), "fsdp", scatter_dimension=0, tiled=True).astype(f32)


def norm_stats(first_sum, second_sum):
    got = lax.all_gather(jnp.stack([first_sum, second_sum]), "fsdp", axis=0, tiled=False)
    total = jnp.sum(got, axis=0)
    return total[0], total[1]


def rms_back(upstream, normed, inv_scale):
    return inv_scale * (upstream - normed * jnp.mean(upstream * normed, axis=-1, keepdims=True))


def rotary_tables(slot_order):
    half_dim = HEAD_DIM // 2
    inverse = rope_theta ** (-(jnp.arange(half_dim, dtype=f32) * 2.0) / HEAD_DIM)
    angles = slot_order.astype(f32)[..., None] * inverse
    angles = jnp.concatenate([angles, angles], axis=-1)
    return (jnp.cos(angles)[..., None, :], jnp.sin(angles)[..., None, :])


def rotate(operand, cosine_table, sine_table):
    half_dim = operand.shape[-1] // 2
    flipped = jnp.concatenate([-operand[..., half_dim:], operand[..., :half_dim]], axis=-1)
    return operand * cosine_table + flipped * sine_table


def unrotate(upstream, cosine_table, sine_table):
    half_dim = upstream.shape[-1] // 2
    shifted = upstream * sine_table
    flipped = jnp.concatenate([shifted[..., half_dim:], -shifted[..., :half_dim]], axis=-1)
    return upstream * cosine_table + flipped


def masked_scores(query_rows, key_rows, pos):
    scores = jnp.einsum("gqhe,gkhe->ghqk", query_rows, key_rows, preferred_element_type=f32)
    causal = pos[:, None, :, None] >= pos[:, None, None, :]
    return jnp.where(causal, scores, -1e30)


def attend(query_rows, key_rows, value_rows, pos):
    scores = masked_scores(query_rows, key_rows, pos)
    row_max = jnp.max(scores, axis=-1, keepdims=True)
    weights = jnp.exp(scores - row_max)
    row_total = jnp.sum(weights, axis=-1, keepdims=True)
    probabilities = (weights / row_total).astype(bf16)
    attn_mixed = jnp.einsum("ghqk,gkhe->gqhe", probabilities, value_rows, preferred_element_type=f32)
    return attn_mixed.astype(bf16), row_max + jnp.log(row_total)


def attend_back(query_rows, key_rows, value_rows, pos, grad_mixed, log_total):
    scores = masked_scores(query_rows, key_rows, pos)
    probabilities = jnp.exp(scores - log_total)
    grad_probs = jnp.einsum("gqhe,gkhe->ghqk", grad_mixed, value_rows, preferred_element_type=f32)
    grad_value = jnp.einsum(
        "ghqk,gqhe->gkhe", probabilities.astype(bf16), grad_mixed, preferred_element_type=f32
    )
    inner_sum = jnp.sum(grad_probs * probabilities, axis=-1, keepdims=True)
    grad_scores = (probabilities * (grad_probs - inner_sum)).astype(bf16)
    grad_query = jnp.einsum("ghqk,gkhe->gqhe", grad_scores, key_rows, preferred_element_type=f32)
    grad_key = jnp.einsum("ghqk,gqhe->gkhe", grad_scores, query_rows, preferred_element_type=f32)
    return grad_query, grad_key, grad_value


MESH = pl.DeviceIdType.MESH
VMEM_LIMIT = 60 * 1024 * 1024
ANY = pl.BlockSpec(memory_space=pl.ANY)


class Plane:
    def __init__(self):
        f = lax.axis_index("fsdp")
        self.f, self.c, self.chip = f, f % 2, f // 2
        x, y = self.chip % 2, self.chip // 2
        self.qx = self.chip + 1 - 2 * x
        self.qy = self.chip + 2 - 4 * y
        self.qd = self.qx + 2 - 4 * y
        self.fc = f + 1 - 2 * self.c
        self.fx = 2 * self.qx + self.c
        self.fy = 2 * self.qy + self.c
        self.fd = 2 * self.qd + self.c
        self.other = 1 - self.c

    def greet(self):
        barrier = pltpu.get_barrier_semaphore()
        for to in (self.fc, self.fx, self.fy):
            pl.semaphore_signal(barrier, inc=1, device_id={"fsdp": to}, device_id_type=MESH)
        pl.semaphore_wait(barrier, 3)


def partner(i, k):
    if k == 3:
        return 3 - i
    if k == 2:
        return (i + 2) % 4
    return i + 1 - 2 * (i % 2)


FAR_FIRST = (3, 2, 1)


def remote(src, dst, send, recv, i, to, axis="fsdp"):
    return pltpu.make_async_remote_copy(
        src_ref=src, dst_ref=dst, send_sem=send.at[i], recv_sem=recv.at[i],
        device_id={axis: to}, device_id_type=MESH,
    )


def local(src, dst, sems, i):
    copy = pltpu.make_async_copy(src, dst, sems.at[i])
    copy.start()
    return copy


def nn(a, b):
    return lax.dot_general(a, b, (((1,), (0,)), ((), ())), preferred_element_type=f32)


def nt(a, b):
    return lax.dot_general(a, b, (((1,), (1,)), ((), ())), preferred_element_type=f32)


def gather_phase(at, rows, send, recv, base, on_rows):
    half = rows.shape[1] // 2
    A, B = pl.ds(0, half), pl.ds(half, half)

    def cp(i, slot, part, to):
        ref = rows.at[slot] if part is None else rows.at[slot, part]
        return remote(ref, ref, send, recv, base + i, to)

    fcx, fcy, fcd = 2 * at.qx + at.other, 2 * at.qy + at.other, 2 * at.qd + at.other
    sent = []

    def go(*a):
        c = cp(*a)
        c.start()
        sent.append(c)

    def arrived(i, slot, part, frm):
        cp(i, slot, part, frm).wait_recv()

    go(0, at.f, None, at.fc)
    go(1, at.f, A, at.fx)
    go(3, at.f, B, at.fy)
    go(2, at.f, B, at.fx)
    go(4, at.f, A, at.fy)
    arrived(0, at.fc, None, at.fc)
    on_rows(2 * at.chip, 2)
    arrived(1, at.fx, A, at.fx)
    go(5, at.fx, A, at.fy)
    go(7, at.fx, A, at.fc)
    arrived(3, at.fy, B, at.fy)
    go(6, at.fy, B, at.fx)
    go(8, at.fy, B, at.fc)
    arrived(2, at.fx, B, at.fx)
    go(9, at.fx, B, at.fc)
    arrived(4, at.fy, A, at.fy)
    go(10, at.fy, A, at.fc)
    arrived(7, fcx, A, at.fc)
    arrived(9, fcx, B, at.fc)
    on_rows(2 * at.qx, 2)
    arrived(8, fcy, B, at.fc)
    arrived(10, fcy, A, at.fc)
    on_rows(2 * at.qy, 2)
    arrived(5, at.fd, A, at.fy)
    go(11, at.fd, A, at.fc)
    arrived(6, at.fd, B, at.fx)
    go(12, at.fd, B, at.fc)
    on_rows(at.fd, 1)
    arrived(11, fcd, A, at.fc)
    arrived(12, fcd, B, at.fc)
    on_rows(fcd, 1)
    for c in sent:
        c.wait_send()


GATHER_COPIES = 13
SCATTER_COPIES = 10


def scatter_scratch(R, D):
    return [
        pltpu.VMEM((4, R, D), bf16),
        pltpu.VMEM((4, R, D), bf16),
        pltpu.VMEM((2, R, D), f32),
        pltpu.VMEM((3, R, D), bf16),
        pltpu.VMEM((3, R, D), bf16),
    ]


def scatter_phase(at, partial, bufs, send, recv, base, between=None):
    to_core, from_core, mine, out, inc = bufs
    R, D = to_core.shape[1], to_core.shape[2]
    half = R // 2
    A, B = pl.ds(0, half), pl.ds(half, half)
    tile = 512
    step = 16
    sent = []

    def go(i, src, dst, to):
        c = remote(src, dst, send, recv, base + i, to)
        c.start()
        sent.append(c)

    def arrived(i, dst, frm):
        remote(dst, dst, send, recv, base + i, frm).wait_recv()

    def compute(order, chip, slot):
        @pl.loop(0, D // tile)
        def _(n):
            cols = pl.ds(pl.multiple_of(n * tile, tile), tile)
            got = partial(chip, cols)
            lo, hi = got[:R], got[R:]
            first = at.c == 0
            mine[slot, :, cols] = jnp.where(first, lo, hi)
            to_core[order, :, cols] = jnp.where(first, hi, lo).astype(bf16)

        go(order, to_core.at[order], from_core.at[order], at.fc)

    def chip_sum(order, slot):
        arrived(order, from_core.at[order], at.fc)

        @pl.loop(0, R // step)
        def _(r):
            rows = pl.ds(pl.multiple_of(r * step, step), step)
            out[order, rows, :] = (mine[slot, rows, :] + from_core[order, rows, :].astype(f32)).astype(bf16)

    def relay(order, start, src):
        @pl.loop(0, half // step)
        def _(r):
            rows = pl.ds(pl.multiple_of(start + r * step, step), step)
            out[order, rows, :] = (out[order, rows, :].astype(f32) + inc[src, rows, :].astype(f32)).astype(bf16)

    compute(0, at.qd, 0)
    compute(1, at.qx, 1)
    if between is not None:
        between()
    chip_sum(0, 0)
    go(4, out.at[0, A], inc.at[0, A], at.fx)
    go(5, out.at[0, B], inc.at[0, B], at.fy)
    compute(2, at.qy, 0)
    chip_sum(1, 1)
    go(6, out.at[1, A], inc.at[1, A], at.fx)
    compute(3, at.chip, 1)
    chip_sum(2, 0)
    go(8, out.at[2, B], inc.at[2, B], at.fy)
    arrived(5, inc.at[0, B], at.fy)
    relay(1, half, 0)
    go(7, out.at[1, B], inc.at[1, B], at.fx)
    arrived(4, inc.at[0, A], at.fx)
    relay(2, 0, 0)
    go(9, out.at[2, A], inc.at[2, A], at.fy)
    arrived(3, from_core.at[3], at.fc)
    arrived(6, inc.at[1, A], at.fx)
    arrived(8, inc.at[2, B], at.fy)
    arrived(7, inc.at[1, B], at.fx)
    arrived(9, inc.at[2, A], at.fy)
    for c in sent:
        c.wait_send()

    def total(rows):
        return (
            mine[1, rows, :]
            + from_core[3, rows, :].astype(f32)
            + inc[1, rows, :].astype(f32)
            + inc[2, rows, :].astype(f32)
        )

    return total


def rms(v):
    return lax.rsqrt(jnp.mean(v * v, axis=-1, keepdims=True) + epsilon)


def back(weighted, normed, scale):
    return scale * (weighted - normed * jnp.mean(weighted * normed, axis=-1, keepdims=True))


def row_loop(R, body, step=16):
    @pl.loop(0, R // step)
    def _(r):
        body(pl.ds(pl.multiple_of(r * step, step), step))


def pair_loop(rows, w_cols, total_cols, body):
    @pl.loop(0, total_cols // w_cols)
    def _(t):
        body(pl.ds(pl.multiple_of(t * w_cols, w_cols), w_cols))


class Stores:
    def __init__(self, sems):
        self.sems, self.steps, self.n = sems, [], 0

    def slot(self):
        if len(self.steps) >= 2:
            for c in self.steps[-2]:
                c.wait()
            self.steps[-2] = []
        return len(self.steps) % 2

    def put(self, pairs):
        done = []
        for src, dst in pairs:
            done.append(local(src, dst, self.sems, self.n))
            self.n += 1
        self.steps.append(done)

    def finish(self):
        for step in self.steps:
            for c in step:
                c.wait()


class Moving:
    def __init__(self, at, C, mine, stage, landing, lsem, base, send, recv):
        self.at, self.C, self.mine, self.stage, self.landing = at, C, mine, stage, landing
        self.lsem, self.base, self.send, self.recv = lsem, base, send, recv
        self.z = lax.axis_index("ctx")
        self.piece = mine.shape[0] // C
        self.sent = []

    def greet(self, barrier):
        at, C = self.at, self.C
        for k in range(1, C):
            pl.semaphore_signal(barrier, inc=1, device_id={"ctx": (self.z + k) % C}, device_id_type=MESH)
            pl.semaphore_signal(
                barrier, inc=1, device_id={"fsdp": 2 * ((at.chip + k) % C) + at.c}, device_id_type=MESH
            )

    def first(self):
        at, C, piece = self.at, self.C, self.piece
        for k in FAR_FIRST:
            j = partner(at.chip, k)
            src = self.mine.at[pl.ds(j * piece, piece)]
            c = remote(src, self.stage.at[at.chip], self.send, self.recv, k, 2 * j + at.c)
            c.start()
            self.sent.append(c)
        src = self.mine.at[pl.ds(at.chip * piece, piece)]
        self.keep = local(src, self.stage.at[at.chip], self.lsem, self.base)

    def land(self, layer):
        return self.landing.at[pl.ds(layer * self.piece, self.piece)]

    def second(self):
        at, C, z = self.at, self.C, self.z
        self.keep.wait()
        for k in FAR_FIRST:
            frm = partner(at.chip, k)
            remote(self.stage.at[frm], self.stage.at[frm], self.send, self.recv, k, 2 * frm + at.c).wait_recv()
        for k in FAR_FIRST:
            to = partner(z, k)
            c = remote(self.stage.at[to], self.land(z), self.send, self.recv, C + k, to, "ctx")
            c.start()
            self.sent.append(c)
        self.keep = local(self.stage.at[z], self.land(z), self.lsem, self.base + 1)

    def finish(self):
        C, z = self.C, self.z
        self.keep.wait()
        for k in FAR_FIRST:
            frm = partner(z, k)
            remote(self.land(frm), self.land(frm), self.send, self.recv, C + k, frm, "ctx").wait_recv()
        for c in self.sent:
            c.wait_send()


def enter_kernel(C, x_ref, own_ref, all_ref, stage, mine, rows, lsem, osem, send, recv, tsend, trecv):
    at = Plane()
    load = local(x_ref, mine, lsem, 0)
    moving = Moving(at, C, mine, stage, rows.at[at.f], lsem, 1, tsend, trecv)
    barrier = pltpu.get_barrier_semaphore()
    moving.greet(barrier)
    pl.semaphore_signal(barrier, inc=1, device_id={"fsdp": at.fc}, device_id_type=MESH)
    pl.semaphore_wait(barrier, 2 * (C - 1) + 1)
    load.wait()
    moving.first()
    moving.second()
    moving.finish()
    save = local(rows.at[at.f], own_ref, lsem, 3)
    stores = []

    def on_rows(first, count):
        stores.append(local(rows.at[pl.ds(first, count)], all_ref.at[pl.ds(first, count)], osem, len(stores)))

    gather_phase(at, rows, send, recv, 0, on_rows)
    save.wait()
    for c in stores:
        c.wait()


def enter_call(C, F, x):
    R, D = x.shape
    return pl.pallas_call(
        functools.partial(enter_kernel, C),
        out_shape=[jax.ShapeDtypeStruct((R, D), bf16), jax.ShapeDtypeStruct((F, R, D), bf16)],
        in_specs=[ANY],
        out_specs=[ANY] * 2,
        scratch_shapes=[
            pltpu.VMEM((C, R // C, D), bf16),
            pltpu.VMEM((R, D), bf16),
            pltpu.VMEM((F, R, D), bf16),
            dma(4), dma(5), dma(GATHER_COPIES), dma(GATHER_COPIES), dma(2 * C), dma(2 * C),
        ],
        compiler_params=params(1),
        cost_estimate=cost(70),
    )(x)


def qkv_kernel(all_ref, w_ref, proj_ref, st_ref, rows, w, acc, st, lsem, osem, ssend, srecv):
    at = Plane()
    F, R = rows.shape[0], rows.shape[1]
    e = w.shape[1] // 3
    m = 2 * R
    loads = [local(w_ref.at[:, pl.ds(0, 3 * e)], w, lsem, 0)] + [
        local(all_ref.at[pl.ds(2 * p, 2)], rows.at[pl.ds(2 * p, 2)], lsem, 1 + p) for p in range(F // 2)
    ]
    barrier = pltpu.get_barrier_semaphore()
    for k in range(1, F):
        pl.semaphore_signal(barrier, inc=1, device_id={"fsdp": (at.f + k) % F}, device_id_type=MESH)
    pl.semaphore_wait(barrier, F - 1)
    loads[0].wait()
    stores = Stores(osem)
    for p in range(F // 2):
        loads[1 + p].wait()
        s = stores.slot()

        def tile(c):
            acc[s, :, c] = nn(rows[pl.ds(2 * p, 2)].reshape(m, rows.shape[2]), w[:, c])

        pair_loop(m, 256, w.shape[1], tile)
        q, k = acc[s, :, :e], acc[s, :, e : 2 * e]
        st[at.f, :, pl.ds(p * m, m)] = row_sums(q * q, k * k)
        stores.put([(acc.at[s], proj_ref.at[pl.ds(p * m, m)])])
    share_stats(at, F, st, ssend, srecv, 0)
    local(st, st_ref, lsem, 1 + F // 2).wait()
    stores.finish()


def params(number):
    return pltpu.CompilerParams(
        collective_id=number, has_side_effects=True, vmem_limit_bytes=VMEM_LIMIT
    )


def cost(us):
    return pl.CostEstimate(flops=int(us * 1e9), bytes_accessed=2**20, transcendentals=0)


def dma(n):
    return pltpu.SemaphoreType.DMA((n,))


def qkv_call(F, rows, w):
    _, R, D = rows.shape
    n = w.shape[1] // 4 * 3
    return pl.pallas_call(
        qkv_kernel,
        out_shape=[
            jax.ShapeDtypeStruct((F * R, n), f32),
            jax.ShapeDtypeStruct((F, 8, F * R), f32),
        ],
        in_specs=[ANY] * 2,
        out_specs=[ANY] * 2,
        scratch_shapes=[
            pltpu.VMEM((F, R, D), bf16),
            pltpu.VMEM((D, n), bf16),
            pltpu.VMEM((2, 2 * R, n), f32),
            pltpu.VMEM((F, 8, F * R), f32),
            dma(6), dma(4), dma(F), dma(F),
        ],
        compiler_params=params(7),
        cost_estimate=cost(22),
    )(rows, w)


def out_kernel(
    mixed_ref, wo_ref, x_ref, gain_ref, hid_ref, ao_ref, in_ref,
    mixed, wo, x, gain, hid, ao, inp, b0, b1, b2, b3, b4, lsem, send, recv,
):
    at = Plane()
    e = wo.shape[1]
    pairs = [(mixed_ref, mixed), (wo_ref.at[:, pl.ds(3 * e, e)], wo), (x_ref, x), (gain_ref, gain)]
    loads = [local(s, d, lsem, i) for i, (s, d) in enumerate(pairs)]
    at.greet()
    R = x.shape[0]
    loads[0].wait()
    loads[1].wait()

    def partial(chip, cols):
        return nt(mixed[pl.ds(pl.multiple_of(chip * 2 * R, 2 * R), 2 * R), :], wo[cols, :])

    total = scatter_phase(at, partial, (b0, b1, b2, b3, b4), send, recv, 0)
    loads[2].wait()
    loads[3].wait()

    def finish(r):
        out = total(r)
        ao[r, :] = out
        hidden_in = x[r, :].astype(f32) + out * rms(out) * gain[...]
        hid[r, :] = hidden_in
        inp[r, :] = hidden_in.astype(bf16)

    row_loop(R, finish)
    for c in [local(ao, ao_ref, lsem, 4), local(hid, hid_ref, lsem, 5), local(inp, in_ref, lsem, 6)]:
        c.wait()


def out_call(F, mixed, wo, x, gain):
    R, D = x.shape
    e = wo.shape[1] // 4
    return pl.pallas_call(
        out_kernel,
        out_shape=[
            jax.ShapeDtypeStruct((R, D), f32),
            jax.ShapeDtypeStruct((R, D), f32),
            jax.ShapeDtypeStruct((R, D), bf16),
        ],
        in_specs=[ANY] * 4,
        out_specs=[ANY] * 3,
        scratch_shapes=[
            pltpu.VMEM((F * R, e), bf16),
            pltpu.VMEM((D, e), bf16),
            pltpu.VMEM((R, D), bf16),
            pltpu.VMEM((1, D), f32),
            pltpu.VMEM((R, D), f32),
            pltpu.VMEM((R, D), f32),
            pltpu.VMEM((R, D), bf16),
        ]
        + scatter_scratch(R, D)
        + [dma(7), dma(SCATTER_COPIES), dma(SCATTER_COPIES)],
        compiler_params=params(8),
        cost_estimate=cost(46),
    )(mixed, wo, x, gain)


def up_kernel(
    C, in_ref, w_ref, cot_ref, all_ref, act_ref, der_ref, h_ref, moved_ref,
    w, rows, act, der, h, mine, moved, stage, lsem, osem, send, recv, tsend, trecv,
):
    at = Plane()
    cot = local(cot_ref, mine, lsem, 2)
    moving = Moving(at, C, mine, stage, moved, lsem, 3, tsend, trecv)
    own = local(in_ref, rows.at[at.f], lsem, 0)
    n = act.shape[2]
    loads = [local(w_ref, w, lsem, 1)]
    width = 256
    barrier = pltpu.get_barrier_semaphore()
    moving.greet(barrier)
    pl.semaphore_signal(barrier, inc=1, device_id={"fsdp": at.fc}, device_id_type=MESH)
    pl.semaphore_wait(barrier, 2 * (C - 1) + 1)
    R = rows.shape[1]
    cot.wait()
    moving.first()
    own.wait()
    waited = []
    stores = Stores(osem)

    def on_rows(first, count):
        s = stores.slot()
        m = count * R
        if not waited:
            for c in loads:
                c.wait()
            moving.second()
            waited.append(1)

        @pl.loop(0, n // width)
        def _(t):
            c = pl.ds(pl.multiple_of(t * width, width), width)
            lhs = rows[pl.ds(first, count)].reshape(m, rows.shape[2])
            g = nn(lhs, w[:, c])
            u = nn(lhs, w[:, pl.ds(pl.multiple_of(n + t * width, width), width)])
            sig = jax.nn.sigmoid(g)
            a = g * sig
            act[s, pl.ds(0, m), c] = a.astype(bf16)
            der[s, pl.ds(0, m), c] = (u * (sig * (1.0 + g * (1.0 - sig)))).astype(bf16)
            h[s, pl.ds(0, m), c] = (a * u).astype(bf16)

        start = pl.multiple_of(first * R, R)
        stores.put(
            [
                (act.at[s, pl.ds(0, m)], act_ref.at[pl.ds(start, m)]),
                (der.at[s, pl.ds(0, m)], der_ref.at[pl.ds(start, m)]),
                (h.at[s, pl.ds(0, m)], h_ref.at[pl.ds(start, m)]),
                (rows.at[pl.ds(first, count)], all_ref.at[pl.ds(first, count)]),
            ]
        )

    gather_phase(at, rows, send, recv, 0, on_rows)
    moving.finish()
    local(moved, moved_ref, lsem, 5).wait()
    stores.finish()


def up_call(C, F, inp, w, cot):
    R, D = inp.shape
    n = w.shape[1] // 2
    T = F * R
    wide = jax.ShapeDtypeStruct((T, n), bf16)
    return pl.pallas_call(
        functools.partial(up_kernel, C),
        out_shape=[
            jax.ShapeDtypeStruct((F, R, D), bf16), wide, wide, wide, jax.ShapeDtypeStruct((R, D), bf16),
        ],
        in_specs=[ANY] * 3,
        out_specs=[ANY] * 5,
        scratch_shapes=[
            pltpu.VMEM((D, 2 * n), bf16),
            pltpu.VMEM((F, R, D), bf16),
            pltpu.VMEM((2, 2 * R, n), bf16),
            pltpu.VMEM((2, 2 * R, n), bf16),
            pltpu.VMEM((2, 2 * R, n), bf16),
            pltpu.VMEM((R, D), bf16),
            pltpu.VMEM((R, D), bf16),
            pltpu.VMEM((C, R // C, D), bf16),
        ]
        + [dma(6), dma(20), dma(GATHER_COPIES), dma(GATHER_COPIES), dma(2 * C), dma(2 * C)],
        compiler_params=params(2),
        cost_estimate=cost(56),
    )(inp, w, cot)


def down_kernel(
    C, h_ref, wd_ref, hid_ref, cot_ref, gain_ref, act_ref, der_ref, unit_ref,
    res_ref, gg_ref, all_ref, grad_ref, mom_ref, p_ref,
    h, wd, hid, cot, gain, act, der, res, gacc, rows, grad, prod, acc, b0, b1, b2, b3, b4,
    lsem, osem, asem, psem, send, recv, usend, urecv,
):
    at = Plane()
    loads = [
        local(s, d, lsem, i)
        for i, (s, d) in enumerate(
            [(h_ref, h), (wd_ref, wd), (hid_ref, hid), (gain_ref, gain), (cot_ref, cot)]
        )
    ]
    z = lax.axis_index("ctx")
    barrier = pltpu.get_barrier_semaphore()
    for to in (at.fc, at.fx, at.fy):
        pl.semaphore_signal(barrier, inc=1, device_id={"fsdp": to}, device_id_type=MESH)
    for k in FAR_FIRST:
        pl.semaphore_signal(barrier, inc=1, device_id={"ctx": partner(z, k)}, device_id_type=MESH)
    pl.semaphore_wait(barrier, C + 2)
    R = rows.shape[1]
    n = wd.shape[1]
    units = []

    def send_units(k):
        to = partner(z, k)
        c = remote(unit_ref.at[to], mom_ref.at[z], usend, urecv, k, to, "ctx")
        c.start()
        units.append(c)

    for k in FAR_FIRST:
        send_units(k)
    units.append(local(unit_ref.at[z], mom_ref.at[z], lsem, 5))
    loads[0].wait()
    loads[1].wait()

    def partial(chip, cols):
        return nt(h[pl.ds(pl.multiple_of(chip * 2 * R, 2 * R), 2 * R), :], wd[cols, :])

    total = scatter_phase(at, partial, (b0, b1, b2, b3, b4), send, recv, 0)
    for c in loads[2:]:
        c.wait()
    gacc[...] = jnp.zeros_like(gacc)

    def finish(r):
        out = total(r)
        scale = rms(out)
        hat = out * scale
        res[r, :] = (hid[r, :] + hat * gain[...]).astype(bf16)
        g = cot[r, :].astype(f32)
        gacc[...] += jnp.sum(g * hat, axis=0, keepdims=True)
        rows[at.f, r, :] = back(g * gain[...], hat, scale).astype(bf16)

    row_loop(R, finish)
    saves = [local(res, res_ref, lsem, 6), local(gacc, gg_ref, lsem, 7)]
    stores = Stores(osem)

    def on_rows(first, count):
        s = stores.slot()
        m = count * R
        start = pl.multiple_of(first * R, R)
        k = len(stores.steps)
        la = local(act_ref.at[pl.ds(start, m)], act.at[s, pl.ds(0, m)], asem, 2 * k)
        ld = local(der_ref.at[pl.ds(start, m)], der.at[s, pl.ds(0, m)], asem, 2 * k + 1)
        la.wait()
        ld.wait()

        width = 512

        @pl.loop(0, n // width)
        def _(t):
            c = pl.ds(pl.multiple_of(t * width, width), width)
            up = pl.ds(pl.multiple_of(n + t * width, width), width)
            gh = nn(rows[pl.ds(first, count)].reshape(m, rows.shape[2]), wd[:, c])
            grad[s, pl.ds(0, m), up] = (gh * act[s, pl.ds(0, m), c].astype(f32)).astype(bf16)
            grad[s, pl.ds(0, m), c] = (gh * der[s, pl.ds(0, m), c].astype(f32)).astype(bf16)

        begun = len(stores.steps) > 0
        part = prod.shape[1]

        @pl.loop(0, rows.shape[2] // part)
        def _(t):
            c = pl.ds(pl.multiple_of(t * part, part), part)
            got = lax.dot_general(
                rows[pl.ds(first, count), :, c].reshape(m, part), h[pl.ds(start, m), :],
                (((0,), (0,)), ((), ())), preferred_element_type=f32,
            )
            acc[c, :] = acc[c, :] + got if begun else got

        stores.put(
            [
                (grad.at[s, pl.ds(0, m)], grad_ref.at[pl.ds(start, m)]),
                (rows.at[pl.ds(first, count)], all_ref.at[pl.ds(first, count)]),
            ]
        )

    gather_phase(at, rows, send, recv, SCATTER_COPIES, on_rows)
    D = rows.shape[2]
    tile, cols = prod.shape[1], p_ref.shape[3]
    puts = []
    for t in range(D // tile):
        if t >= 2:
            for c in puts[t - 2]:
                c.wait()
        prod[t % 2] = acc[pl.ds(t * tile, tile), :].astype(bf16)
        puts.append(
            [
                local(
                    prod.at[t % 2, :, pl.ds(b * cols, cols)],
                    p_ref.at[b, 0, pl.ds(t * tile, tile)],
                    psem,
                    t * (n // cols) + b,
                )
                for b in range(n // cols)
            ]
        )
    for step in puts[-2:]:
        for c in step:
            c.wait()
    for k in FAR_FIRST:
        frm = partner(z, k)
        remote(mom_ref.at[frm], mom_ref.at[frm], usend, urecv, k, frm, "ctx").wait_recv()
    for c in units[:-1]:
        c.wait_send()
    units[-1].wait()
    for s in saves:
        s.wait()
    stores.finish()


def down_call(C, F, h, wd, hid, cot, gain, act, der, units):
    R, D = hid.shape
    n = wd.shape[1]
    T = F * R
    copies = SCATTER_COPIES + GATHER_COPIES
    one = jax.ShapeDtypeStruct((R, D), bf16)
    return pl.pallas_call(
        functools.partial(down_kernel, C),
        out_shape=[
            one,
            jax.ShapeDtypeStruct((1, D), f32),
            jax.ShapeDtypeStruct((F, R, D), bf16),
            jax.ShapeDtypeStruct((T, 2 * n), bf16),
            jax.ShapeDtypeStruct(units.shape, bf16),
            jax.ShapeDtypeStruct((units.shape[1], 1, D, units.shape[3]), bf16),
        ],
        in_specs=[ANY] * 8,
        out_specs=[ANY] * 6,
        scratch_shapes=[
            pltpu.VMEM((T, n), bf16),
            pltpu.VMEM((D, n), bf16),
            pltpu.VMEM((R, D), f32),
            pltpu.VMEM((R, D), bf16),
            pltpu.VMEM((1, D), f32),
            pltpu.VMEM((2, 2 * R, n), bf16),
            pltpu.VMEM((2, 2 * R, n), bf16),
            pltpu.VMEM((R, D), bf16),
            pltpu.VMEM((1, D), f32),
            pltpu.VMEM((F, R, D), bf16),
            pltpu.VMEM((2, 2 * R, 2 * n), bf16),
            pltpu.VMEM((2, 512, n), bf16),
            pltpu.VMEM((D, n), f32),
        ]
        + scatter_scratch(R, D)
        + [dma(8), dma(15), dma(10), dma(16), dma(copies), dma(copies), dma(C), dma(C)],
        compiler_params=params(3),
        cost_estimate=cost(108),
    )(h, wd, hid, cot, gain, act, der, units)


def mid_kernel(
    grad_ref, w_ref, cot_ref, ao_ref, gain_ref, wo_ref,
    res_ref, gg_ref, all_ref, gm_ref,
    grad, w, cot, ao, gain, wo, res, gacc, rows, gm, b0, b1, b2, b3, b4,
    lsem, osem, send, recv,
):
    at = Plane()
    e = wo.shape[1]
    pairs = [
        (grad_ref, grad), (w_ref, w),
        (cot_ref, cot), (ao_ref, ao), (gain_ref, gain), (wo_ref.at[:, pl.ds(3 * e, e)], wo),
    ]
    loads = [local(s, d, lsem, i) for i, (s, d) in enumerate(pairs)]
    at.greet()
    R = rows.shape[1]
    for c in loads[:2]:
        c.wait()

    def partial(chip, cols):
        return nt(grad[pl.ds(pl.multiple_of(chip * 2 * R, 2 * R), 2 * R), :], w[cols, :])

    total = scatter_phase(at, partial, (b0, b1, b2, b3, b4), send, recv, 0)
    for c in loads[2:]:
        c.wait()
    gacc[...] = jnp.zeros_like(gacc)

    def finish(r):
        resid = cot[r, :].astype(f32) + total(r)
        res[r, :] = resid
        out = ao[r, :]
        scale = rms(out)
        hat = out * scale
        gacc[...] += jnp.sum(resid * hat, axis=0, keepdims=True)
        rows[at.f, r, :] = back(resid * gain[...], hat, scale).astype(bf16)

    row_loop(R, finish)
    saves = [local(res, res_ref, lsem, 8), local(gacc, gg_ref, lsem, 9)]
    stores = Stores(osem)

    def on_rows(first, count):
        s = stores.slot()
        m = count * R
        start = pl.multiple_of(first * R, R)
        lhs = rows[pl.ds(first, count)].reshape(m, rows.shape[2])
        gm[s, pl.ds(0, m), :] = nn(lhs, wo[...]).astype(bf16)
        stores.put(
            [
                (gm.at[s, pl.ds(0, m)], gm_ref.at[pl.ds(start, m)]),
                (rows.at[pl.ds(first, count)], all_ref.at[pl.ds(first, count)]),
            ]
        )

    gather_phase(at, rows, send, recv, SCATTER_COPIES, on_rows)
    for s in saves:
        s.wait()
    stores.finish()


def mid_call(F, grad, w, cot, ao, gain, wo):
    R, D = cot.shape
    n, e = w.shape[1], wo.shape[1] // 4
    T = F * R
    copies = SCATTER_COPIES + GATHER_COPIES
    return pl.pallas_call(
        mid_kernel,
        out_shape=[
            jax.ShapeDtypeStruct((R, D), f32),
            jax.ShapeDtypeStruct((1, D), f32),
            jax.ShapeDtypeStruct((F, R, D), bf16),
            jax.ShapeDtypeStruct((T, e), bf16),
        ],
        in_specs=[ANY] * 6,
        out_specs=[ANY] * 4,
        scratch_shapes=[
            pltpu.VMEM((T, n), bf16),
            pltpu.VMEM((D, n), bf16),
            pltpu.VMEM((R, D), bf16),
            pltpu.VMEM((R, D), f32),
            pltpu.VMEM((1, D), f32),
            pltpu.VMEM((D, e), bf16),
            pltpu.VMEM((R, D), f32),
            pltpu.VMEM((1, D), f32),
            pltpu.VMEM((F, R, D), bf16),
            pltpu.VMEM((2, 2 * R, e), bf16),
        ]
        + scatter_scratch(R, D)
        + [dma(10), dma(10), dma(copies), dma(copies)],
        compiler_params=params(4),
        cost_estimate=cost(92),
    )(grad, w, cot, ao, gain, wo)


def last_kernel(
    width, q_ref, k_ref, v_ref, proj_ref, st_ref, in_ref, w_ref, res_ref, gain_ref,
    out_ref, gp_ref, gsum_ref,
    q, k, proj, st, ins, gains, gsum, gp, w, res, out, b0, b1, b2, b3, b4,
    lsem, send, recv, ssend, srecv, gsend, grecv,
):
    at = Plane()
    F, T = st.shape[0], st.shape[2]
    e = q.shape[1]
    R = res.shape[0]
    pairs = [
        (in_ref, ins.at[at.f]), (st_ref, st), (q_ref, q), (k_ref, k),
        (v_ref, gp.at[:, pl.ds(2 * e, e)]), (proj_ref.at[:, pl.ds(0, 2 * e)], proj), (w_ref.at[:, pl.ds(0, 3 * e)], w), (res_ref, res),
        (gain_ref, gains.at[at.f]),
    ]
    loads = [local(s, d, lsem, i) for i, (s, d) in enumerate(pairs)]
    barrier = pltpu.get_barrier_semaphore()
    for s in range(1, F):
        pl.semaphore_signal(barrier, inc=1, device_id={"fsdp": (at.f + s) % F}, device_id_type=MESH)
    pl.semaphore_wait(barrier, F - 1)
    loads[0].wait()
    share_stats(at, F, ins, ssend, srecv, 0)
    for c in loads[1:6]:
        c.wait()
    step = 256

    @pl.loop(0, T // step)
    def _(t):
        r = pl.ds(pl.multiple_of(t * step, step), step)
        sums = jnp.sum(st[:, :, r], axis=0)
        inner = jnp.sum(ins[:, :, r], axis=0) / width
        for row, grad in ((0, q), (1, k)):
            scale = lax.rsqrt(column(sums[row : row + 1], HEAD_DIM) / width + epsilon)
            mean = column(inner[row : row + 1], HEAD_DIM)
            for h in range(e // HEAD_DIM):
                hat = proj[r, row * e + h * HEAD_DIM : row * e + (h + 1) * HEAD_DIM] * scale
                got = scale * (grad[r, h * HEAD_DIM : (h + 1) * HEAD_DIM] - hat * mean)
                gp[r, row * e + h * HEAD_DIM : row * e + (h + 1) * HEAD_DIM] = got.astype(bf16)

    save = local(gp, gp_ref, lsem, 9)
    loads[6].wait()

    def partial(chip, cols):
        return nt(gp[pl.ds(pl.multiple_of(chip * 2 * R, 2 * R), 2 * R), :], w[cols, :])

    total = scatter_phase(at, partial, (b0, b1, b2, b3, b4), send, recv, 0)
    loads[7].wait()

    def finish(r):
        out[r, :] = (res[r, :] + total(r)).astype(bf16)

    row_loop(R, finish)
    store = local(out, out_ref, lsem, 10)
    loads[8].wait()
    share_stats(at, F, gains, gsend, grecv, 0)
    gsum[...] = jnp.sum(gains[...], axis=0)
    local(gsum, gsum_ref, lsem, 11).wait()
    store.wait()
    save.wait()


def last_call(F, wq, wk, gv, proj, st, ins, w, res, gains):
    R, D = res.shape
    n = w.shape[1] // 4 * 3
    T, e = F * R, n // 3
    return pl.pallas_call(
        functools.partial(last_kernel, D),
        out_shape=[
            jax.ShapeDtypeStruct((R, D), bf16),
            jax.ShapeDtypeStruct((T, n), bf16),
            jax.ShapeDtypeStruct((8, D), f32),
        ],
        in_specs=[ANY] * 9,
        out_specs=[ANY] * 3,
        scratch_shapes=[
            pltpu.VMEM((T, e), f32),
            pltpu.VMEM((T, e), f32),
            pltpu.VMEM((T, 2 * e), f32),
            pltpu.VMEM((F, 8, T), f32),
            pltpu.VMEM((F, 8, T), f32),
            pltpu.VMEM((F, 8, D), f32),
            pltpu.VMEM((8, D), f32),
            pltpu.VMEM((T, n), bf16),
            pltpu.VMEM((D, n), bf16),
            pltpu.VMEM((R, D), f32),
            pltpu.VMEM((R, D), bf16),
        ]
        + scatter_scratch(R, D)
        + [dma(12), dma(SCATTER_COPIES), dma(SCATTER_COPIES), dma(F), dma(F), dma(F), dma(F)],
        compiler_params=params(5),
        cost_estimate=cost(55),
    )(wq, wk, gv, proj, st, ins, w, res, gains)


def tn(a, b):
    return lax.dot_general(a, b, (((0,), (0,)), ((), ())), preferred_element_type=f32)


def grad_kernel(*refs):
    out = refs[-1]
    start = 0
    for x_ref, dy_ref in zip(refs[:-1:2], refs[1:-1:2]):
        got = tn(x_ref[...], dy_ref[...]).astype(bf16)
        units = dy_ref.shape[1] // out.shape[-1]
        for b in range(units):
            out[(start + b,) + (0,) * (len(out.shape) - 3)] = got[:, b * out.shape[-1] : (b + 1) * out.shape[-1]]
        start += units


def grad_call(pairs, units, cols, groups):
    T, D = pairs[0][0].shape
    tile = 512
    specs, args = [], []
    for x, dy in pairs:
        specs += [
            pl.BlockSpec((T, tile), lambda g, d: (0, d)),
            pl.BlockSpec((T, dy.shape[1] // groups), lambda g, d: (0, g)),
        ]
        args += [x, dy]
    return pl.pallas_call(
        grad_kernel,
        out_shape=jax.ShapeDtypeStruct((units, groups, D, cols), bf16),
        grid=(groups, D // tile),
        in_specs=specs,
        out_specs=pl.BlockSpec((units, 1, tile, cols), lambda g, d: (0, g, d, 0)),
        compiler_params=pltpu.CompilerParams(vmem_limit_bytes=VMEM_LIMIT),
        cost_estimate=cost(12 * groups),
    )(*args)


def share_stats(at, F, st, send, recv, base):
    sent = []
    for k in range(1, F):
        to = (at.f + k) % F
        c = remote(st.at[at.f], st.at[at.f], send, recv, base + k, to)
        c.start()
        sent.append(c)
    for k in range(1, F):
        frm = (at.f - k + F) % F
        remote(st.at[frm], st.at[frm], send, recv, base + k, frm).wait_recv()
    for c in sent:
        c.wait_send()


def row_sums(a, b):
    r = lax.broadcasted_iota(jnp.int32, (8, a.shape[1]), 0)
    one, two = (r == 0).astype(f32), (r == 1).astype(f32)

    def half(sel, v):
        return lax.dot_general(
            sel, v, (((1,), (1,)), ((), ())), preferred_element_type=f32, precision=lax.Precision.HIGHEST
        )

    return half(one, a) + half(two, b)


def column(row, lanes):
    return jnp.broadcast_to(row, (lanes, row.shape[1])).T


def turn(v, cos, sin):
    return v * cos + pltpu.roll(v, HEAD_DIM // 2, 1) * sin


def seq_columns(st, c, chips, R):
    return jnp.concatenate([st[:, pl.ds(pl.multiple_of((2 * j + c) * R, R), R)] for j in range(chips)], axis=1)


def attend_kernel(width, q_ref, k_ref, v_ref, st_ref, gq_ref, gk_ref, cos_ref, sin_ref, pos_ref, posc_ref, mix_ref, qr_ref, kr_ref, lse_ref):
    c = pl.program_id(0)
    chips, R = q_ref.shape[0], q_ref.shape[2]
    L = chips * R
    sums = jnp.sum(seq_columns_all(st_ref, c, chips, R), axis=0)
    cos, sin = cos_ref[0], sin_ref[0]

    def norm_turn(ref, row, gain):
        scale = lax.rsqrt(column(sums[row : row + 1], HEAD_DIM) / width + epsilon)
        return turn(ref[...].reshape(L, HEAD_DIM) * scale * gain[...], cos, sin)

    qr = (norm_turn(q_ref, 0, gq_ref) * HEAD_DIM ** (-0.5)).astype(bf16)
    kr = norm_turn(k_ref, 1, gk_ref).astype(bf16)
    v = v_ref[...].reshape(L, HEAD_DIM).astype(bf16)
    qr_ref[...] = qr.reshape(qr_ref.shape)
    kr_ref[...] = kr.reshape(kr_ref.shape)
    pos = pos_ref[0]
    for t in range(chips):
        rows = slice(t * R, (t + 1) * R)
        s = nt(qr[rows], kr)
        s = jnp.where(posc_ref[0, rows, :1] >= pos, s, -1e30)
        top = jnp.max(s, axis=-1, keepdims=True)
        e = jnp.exp(s - top)
        total = jnp.sum(e, axis=-1, keepdims=True)
        p = (e * (1.0 / total)).astype(bf16)
        mix_ref[t, 0] = nn(p, v).astype(bf16)
        lse_ref[0, 0, rows, :] = jnp.broadcast_to(top + jnp.log(total), (R, HEAD_DIM))


def seq_columns_all(st_ref, c, chips, R):
    return jnp.concatenate(
        [st_ref[:, :, pl.ds(pl.multiple_of((2 * j + c) * R, R), R)] for j in range(chips)], axis=2
    )


def attend_specs(chips, R, heads, F, L):
    def at(offset):
        return pl.BlockSpec((chips, 1, R, HEAD_DIM), lambda c, h: (0, c, 0, offset + h))

    gain = pl.BlockSpec((1, HEAD_DIM), lambda c, h: (0, h))
    table = pl.BlockSpec((1, L, HEAD_DIM), lambda c, h: (c, 0, 0))
    stats = pl.BlockSpec((F, 8, F * R), lambda c, h: (0, 0, 0))
    posr = pl.BlockSpec((1, 1, L), lambda c, h: (c, 0, 0))
    lse = pl.BlockSpec((1, 1, L, HEAD_DIM), lambda c, h: (c, h, 0, 0))
    return at, gain, table, stats, posr, lse


def attend_call(F, proj, st, gq, gk, cos, sin, pos, posc):
    R = proj.shape[0] // F
    e = proj.shape[1] // 3
    heads, chips = e // HEAD_DIM, F // 2
    L = chips * R
    at, gain, table, stats, posr, lse = attend_specs(chips, R, heads, F, L)
    view = proj.reshape(chips, 2, R, 3 * e)
    flat = jax.ShapeDtypeStruct((chips, 2, R, e), bf16)
    out = pl.pallas_call(
        functools.partial(attend_kernel, heads * HEAD_DIM * F),
        out_shape=[flat, flat, flat, jax.ShapeDtypeStruct((2, heads, L, HEAD_DIM), f32)],
        grid=(2, heads),
        in_specs=[at(0), at(heads), at(2 * heads), stats, gain, gain, table, table, posr, table],
        out_specs=[at(0), at(0), at(0), lse],
        compiler_params=pltpu.CompilerParams(vmem_limit_bytes=VMEM_LIMIT),
        cost_estimate=cost(15),
    )(view, view, view, st, gq, gk, cos, sin, pos, posc)
    return out


def attend_back_kernel(
    width, q_ref, k_ref, v_ref, qr_ref, kr_ref, gm_ref, lse_ref, st_ref, gq_ref, gk_ref, cos_ref, sin_ref, pos_ref, posc_ref,
    wq_ref, wk_ref, gv_ref, in_ref, gg_ref, dk, dv, dq,
):
    c = pl.program_id(0)
    chips, R = q_ref.shape[0], q_ref.shape[2]
    L = chips * R
    kr = kr_ref[...].reshape(L, HEAD_DIM)
    v = v_ref[...].reshape(L, HEAD_DIM).astype(bf16)
    pos = pos_ref[0]
    dk[...] = jnp.zeros_like(dk)
    dv[...] = jnp.zeros_like(dv)
    for t in range(chips):
        rows = slice(t * R, (t + 1) * R)
        qt, gm = qr_ref[t, 0], gm_ref[t, 0]
        s = nt(qt, kr)
        s = jnp.where(posc_ref[0, rows, :1] >= pos, s, -1e30)
        p = jnp.exp(s - lse_ref[0, 0, rows, :1])
        dp = nt(gm, v)
        dv[...] += lax.dot_general(p.astype(bf16), gm, (((0,), (0,)), ((), ())), preferred_element_type=f32)
        inner = jnp.sum(dp * p, axis=-1, keepdims=True)
        ds = (p * (dp - inner)).astype(bf16)
        dq[rows, :] = nn(ds, kr)
        dk[...] += lax.dot_general(ds, qt, (((0,), (0,)), ((), ())), preferred_element_type=f32)
    gv_ref[...] = dv[...].astype(bf16).reshape(gv_ref.shape)
    sums = jnp.sum(seq_columns_all(st_ref, c, chips, R), axis=0)
    cos, sin = cos_ref[0], sin_ref[0]

    def finish(grad, ref, row, gain, out):
        norm = turn(grad, cos, -sin)
        hat = ref[...].reshape(L, HEAD_DIM) * lax.rsqrt(column(sums[row : row + 1], HEAD_DIM) / width + epsilon)
        gg_ref[0, 0, row : row + 1, :] = jnp.sum(norm * hat, axis=0, keepdims=True)
        weighted = norm * gain[...]
        out[...] = weighted.reshape(out.shape)
        return weighted * hat

    gg_ref[...] = jnp.zeros_like(gg_ref)
    in_ref[0, 0] = row_sums(
        finish(dq[...] * HEAD_DIM ** (-0.5), q_ref, 0, gq_ref, wq_ref), finish(dk[...], k_ref, 1, gk_ref, wk_ref)
    )


def attend_back_call(F, proj, qr, kr, gm, lse_in, st, gq, gk, cos, sin, pos, posc):
    R = proj.shape[0] // F
    e = proj.shape[1] // 3
    heads, chips = e // HEAD_DIM, F // 2
    L = chips * R
    at, gain, table, stats, posr, lse = attend_specs(chips, R, heads, F, L)
    view = proj.reshape(chips, 2, R, 3 * e)
    flat = (chips, 2, R, e)
    small = pl.BlockSpec((1, 1, 8, L), lambda c, h: (c, h, 0, 0))
    tiny = pl.BlockSpec((1, 1, 8, HEAD_DIM), lambda c, h: (c, h, 0, 0))
    wide = jax.ShapeDtypeStruct(flat, f32)
    return pl.pallas_call(
        functools.partial(attend_back_kernel, heads * HEAD_DIM * F),
        out_shape=[
            wide, wide, jax.ShapeDtypeStruct(flat, bf16),
            jax.ShapeDtypeStruct((2, heads, 8, L), f32),
            jax.ShapeDtypeStruct((2, heads, 8, HEAD_DIM), f32),
        ],
        grid=(2, heads),
        in_specs=[
            at(0), at(heads), at(2 * heads), at(0), at(0), at(0), lse, stats, gain, gain, table, table, posr, table,
        ],
        out_specs=[at(0), at(0), at(0), small, tiny],
        scratch_shapes=[pltpu.VMEM((L, HEAD_DIM), f32)] * 3,
        compiler_params=pltpu.CompilerParams(vmem_limit_bytes=VMEM_LIMIT),
        cost_estimate=cost(35),
    )(view, view, view, qr, kr, gm.reshape(flat), lse_in, st, gq, gk, cos, sin, pos, posc)


class Sides:
    def __init__(self, out, into):
        self.out, self.into = out, into

    def wait(self):
        self.out.wait_send()
        self.into.wait_recv()


def newton_kernel(
    C, m_ref, res_ref, gin_ref, gain_ref, grad_ref, late_ref, out_ref, stage_ref, gsum_ref, back_ref,
    v, gram, y, yf, stat, gains, gsum,
    lsem, osem, vsend, vrecv, ysend, yrecv, ssend, srecv, tsend, trecv, gsend, grecv, usend, urecv, usem, bsend, brecv, isend, irecv,
):
    me = lax.axis_index("fsdp")
    z = lax.axis_index("ctx")
    core, chip = me % 2, me // 2
    peer = me + 1 - 2 * core
    F = 2 * C
    cols = m_ref.shape[2]
    gload = local(gain_ref, gains.at[z], lsem, 1)
    barrier = pltpu.get_barrier_semaphore()
    for k in range(1, C):
        pl.semaphore_signal(barrier, inc=1, device_id={"ctx": (z + k) % C}, device_id_type=MESH)
    for k in range(1, F):
        pl.semaphore_signal(barrier, inc=1, device_id={"fsdp": (me + k) % F}, device_id_type=MESH)
    pl.semaphore_wait(barrier, C + F - 2)
    rows_in = v.shape[1] // C
    def fellow(a, other):
        to = partner(chip, a) if a else chip
        return 2 * to + (1 - core if other else core)

    units_sent, units_kept = [], []
    for a in (3, 1, 2, 0):
        for other in range(2):
            to = fellow(a, other)
            for b in range(C):
                src = m_ref.at[to // 2, pl.ds((2 * b + to % 2) * rows_in, rows_in)]
                dst = v.at[0, pl.ds(b * rows_in, rows_in), pl.ds(me * cols, cols)]
                if a == 0 and other == 0:
                    units_kept.append(local(src, dst, usem, b))
                else:
                    c = remote(src, dst, usend, urecv, (2 * a + other) * C + b, to)
                    c.start()
                    units_sent.append(c)
    piece = res_ref.shape[0] // C

    def part(j):
        return pl.ds(j * piece, piece)

    late = grad_ref.shape[2]

    def back_to(layer, frm, k, kind):
        if kind == 0:
            src = late_ref.at[pl.ds(pl.multiple_of(layer * late, late), late)]
            return src, back_ref.at[frm, 0], k
        return grad_ref.at[layer], back_ref.at[frm, pl.ds(1, grad_ref.shape[1])], C + k

    sent, keep = [], []
    for kind in range(2):
        src, dst, _ = back_to(z, z, 0, kind)
        keep.append(local(src, dst, lsem, (0, 4)[kind]))
        for k in FAR_FIRST:
            to = partner(z, k)
            src, dst, i = back_to(to, z, k, kind)
            c = remote(src, dst, bsend, brecv, i, to, "ctx")
            c.start()
            sent.append(c)
    for a, rows_ref in enumerate((res_ref, gin_ref)):
        for k in FAR_FIRST:
            to = partner(z, k)
            c = remote(rows_ref.at[part(to)], stage_ref.at[a, z], tsend, trecv, C * a + k, to, "ctx")
            c.start()
            sent.append(c)
        keep.append(local(rows_ref.at[part(z)], stage_ref.at[a, z], lsem, 2 + a))
    gload.wait()
    for k in range(1, C):
        c = remote(gains.at[z], gains.at[z], gsend, grecv, k, (z + k) % C, "ctx")
        c.start()
        sent.append(c)

    def rows_arrived():
        for c in keep:
            c.wait()
        for kind in range(2):
            for k in FAR_FIRST:
                _, dst, i = back_to(z, partner(z, k), k, kind)
                remote(dst, dst, bsend, brecv, i, partner(z, k), "ctx").wait_recv()
        for a in range(2):
            for k in FAR_FIRST:
                dst = stage_ref.at[a, partner(z, k)]
                remote(dst, dst, tsend, trecv, C * a + k, partner(z, k), "ctx").wait_recv()
        for k in range(1, C):
            frm = (z - k + C) % C
            remote(gains.at[frm], gains.at[frm], gsend, grecv, k, frm, "ctx").wait_recv()
        gsum[...] = jnp.sum(gains[...], axis=0)
        local(gsum, gsum_ref, lsem, 6).wait()
        for c in sent:
            c.wait_send()

    stat[0] = jnp.zeros_like(stat[0])

    def columns(owner):
        return pl.ds(pl.multiple_of(owner * cols, cols), cols)

    def pass_on(a, other, owner=None):
        i = 2 * a + other
        c = columns(fellow(a, other if owner is None else owner))
        return remote(v.at[0, :, c], v.at[1, :, c], isend, irecv, i, peer)

    pending = []
    for a in range(C):
        for other in range(2):
            frm = fellow(a, other)
            if a == 0 and other == 0:
                for c in units_kept:
                    c.wait()
            else:
                for b in range(C):
                    dst = v.at[0, pl.ds(b * rows_in, rows_in), columns(frm)]
                    remote(dst, dst, usend, urecv, (2 * a + other) * C + b, frm).wait_recv()
            c = pass_on(a, other)
            c.start()
            pending.append(Sides(c, pass_on(a, other, 1 - other)))

            @pl.loop(0, v.shape[1] // 128)
            def _(r):
                block = v[0, pl.ds(pl.multiple_of(r * 128, 128), 128), columns(frm)].astype(f32)
                stat[0] += jnp.sum((block * block).reshape(-1, 8, cols // 128, 128), axis=(0, 2))

    for c in units_sent:
        c.wait_send()
    M, D = v.shape[1], v.shape[2]
    tile, col = 512, 1024
    tiles = M // tile

    def block(i):
        return pl.ds(pl.multiple_of(i * tile, tile), tile)

    halves = D // col

    def swap(buf, n, i, sends, recvs):
        part = (block(i), pl.ds(n * col, col))
        return remote(buf.at[(0, *part)], buf.at[(1, *part)], sends, recvs, n * tiles + i, peer)

    share = remote(stat.at[0], stat.at[1], ssend, srecv, 0, peer)
    share.start()
    share.wait()
    inv = 1.0 / (jnp.sqrt(jnp.sum(stat[0] + stat[1])) + 1e-07)

    for iteration in range(NS_STEPS):
        factor = inv if iteration == 0 else 1.0

        def grams(h, n):
            rhs = pl.ds(pl.multiple_of(n * col, col), col)
            cols = pl.ds(pl.multiple_of(h * M + n * col, col), col)

            @pl.loop(0, tiles)
            def _(i):
                rows = pl.ds(pl.multiple_of(i * tile, tile), tile)
                got = nt(v[0, rows, :], v[h, rhs, :])
                if iteration == 0:
                    got = got * (factor * factor)
                gram[rows, cols] = got.astype(bf16)

        @pl.loop(0, M // col)
        def _(n):
            grams(0, n)

        for c in pending:
            c.wait()

        @pl.loop(0, M // col)
        def _(n):
            grams(1, n)

        def times(src, i, n):
            rows, c = block(i), pl.ds(n * col, col)
            return nn(gram[rows, :M], src[0, :, c]) + nn(gram[rows, M:], src[1, :, c])

        swaps = []
        for n in range(halves):

            @pl.loop(0, tiles)
            def _(i):
                at = (block(i), pl.ds(n * col, col))
                got = times(v, i, n)
                if iteration == 0:
                    got = got * factor
                yf[at] = got
                y[(0, *at)] = got.astype(bf16)
                swap(y, n, i, ysend, yrecv).start()

            swaps += [swap(y, n, i, ysend, yrecv) for i in range(tiles)]
        pending = []
        for n in range(halves):
            for c in swaps[n * tiles : (n + 1) * tiles]:
                c.wait()

            @pl.loop(0, tiles)
            def _(i):
                at = (block(i), pl.ds(n * col, col))
                got = times(y, i, n)
                old = v[(0, *at)].astype(f32)
                if iteration == 0:
                    old = old * factor
                v[(0, *at)] = (quintic_one * old + quintic_two * yf[at] + quintic_three * got).astype(bf16)
                if iteration < NS_STEPS - 1:
                    swap(v, n, i, vsend, vrecv).start()

            if iteration < NS_STEPS - 1:
                pending += [swap(v, n, i, vsend, vrecv) for i in range(tiles)]
            else:
                for b in range(C):
                    for g in range(n * col // cols, (n + 1) * col // cols):
                        src = v.at[0, pl.ds(b * rows_in, rows_in), pl.ds(g * cols, cols)]
                        pending.append(local(src, out_ref.at[b * F + g], osem, b * F + g))
    rows_arrived()
    for c in pending:
        c.wait()


def newton_call(C, x, result, grad_rows, gains, grads, late):
    _, D, cols = x.shape
    M = D // 2
    R = result.shape[0]
    n = 4
    return pl.pallas_call(
        functools.partial(newton_kernel, C),
        out_shape=[
            jax.ShapeDtypeStruct((2 * C * C, M // C, cols), bf16),
            jax.ShapeDtypeStruct((2, C, R // C, D), bf16),
            jax.ShapeDtypeStruct((8, D), f32),
            jax.ShapeDtypeStruct((C, C, *grads.shape[2:]), bf16),
        ],
        in_specs=[ANY] * 6,
        out_specs=[ANY] * 4,
        scratch_shapes=[
            pltpu.VMEM((2, M, D), bf16),
            pltpu.VMEM((M, 2 * M), bf16),
            pltpu.VMEM((2, M, D), bf16),
            pltpu.VMEM((M, D), f32),
            pltpu.VMEM((2, 8, 128), f32),
            pltpu.VMEM((C, 8, D), f32),
            pltpu.VMEM((8, D), f32),
            dma(7), dma(2 * C * C), dma(n), dma(n), dma(n), dma(n), dma(1), dma(1),
            dma(2 * C), dma(2 * C), dma(C), dma(C), dma(2 * C * C), dma(2 * C * C), dma(C), dma(2 * C), dma(2 * C), dma(2 * C), dma(2 * C),
        ],
        compiler_params=params(6),
        cost_estimate=cost(95),
    )(x, result, grad_rows, gains, grads, late)


def project(C, F, x, w):
    own = to_layer(C, F, x)
    rows = token_rows(own)
    return own, rows, dot(rows, w, 1, 0)


def attn_out_and_up(C, F, mixed, wo, x, gain, w, cot):
    if kernels_fit(C, F):
        hidden_in, out, inp = out_call(F, mixed, wo, x, gain)
        rows, act, der, h, cot = up_call(C, F, inp, w, cot)
        return cot, hidden_in, out, rows, act, der, h
    out = token_sums(dot(mixed, wo, 1, 1))
    hidden_in = x.astype(f32) + out * rms(out) * gain
    rows = token_rows(hidden_in.astype(bf16))
    g, u = jnp.split(dot(rows, w, 1, 0), 2, axis=1)
    sig = jax.nn.sigmoid(g)
    der = u * (sig * (1.0 + g * (1.0 - sig)))
    act = g * sig
    cot = to_layer(C, F, cot)
    return cot, hidden_in, out, rows, act.astype(bf16), der.astype(bf16), (act * u).astype(bf16)


def down_and_back(C, F, h, wd, hidden_in, cot, gain, act, der, units):
    if kernels_fit(C, F):
        return down_call(C, F, h, wd, hidden_in, cot, gain, act, der, units)
    out = token_sums(dot(h, wd, 1, 1))
    scale = rms(out)
    hat = out * scale
    g = cot.astype(f32)
    rows = token_rows(back(g * gain, hat, scale).astype(bf16))
    gh = dot(rows, wd, 1, 0)
    return (
        (hidden_in + hat * gain).astype(bf16),
        jnp.sum(g * hat, axis=0, keepdims=True),
        rows,
        jnp.concatenate([(gh * der.astype(f32)).astype(bf16), (gh * act.astype(f32)).astype(bf16)], axis=1),
        None,
        None,
    )


def back_to_attn(C, F, grad, w, cot, out, gain, wo):
    if kernels_fit(C, F):
        return mid_call(F, grad, w, cot, out, gain, wo)
    resid = cot.astype(f32) + token_sums(dot(grad, w, 1, 1))
    scale = rms(out)
    hat = out * scale
    rows = token_rows(back(resid * gain, hat, scale).astype(bf16))
    return resid, jnp.sum(resid * hat, axis=0, keepdims=True), rows, dot(rows, wo, 1, 0).astype(bf16)


def back_to_input(C, F, grad_projected, w, resid):
    return (resid + token_sums(dot(grad_projected, w, 1, 1))).astype(bf16)


def kernels_fit(C, F):
    return C == 4 and F == 8 and UNITS_ATTN * 4 * 2 == C * F


def to_layer(C, F, x):
    z, chip = lax.axis_index("ctx"), lax.axis_index("fsdp") // 2
    x = x.reshape(C, x.shape[0] // C, x.shape[1])
    got = []
    for k in range(C):
        pairs = [
            (s * F + f, (f // 2) * F + 2 * ((s + k) % C) + f % 2) for s in range(C) for f in range(F)
        ]
        block = lax.dynamic_index_in_dim(x, (z + k) % C, 0, keepdims=False)
        got.append(lax.ppermute(block, BOTH, pairs))
    got = jnp.stack(got)
    got = [lax.dynamic_index_in_dim(got, (chip - s + C) % C, 0, keepdims=False) for s in range(C)]
    return jnp.concatenate(got, axis=0)


def go_home(C, F, stage):
    chip = lax.axis_index("fsdp") // 2
    got = [lax.dynamic_index_in_dim(stage, chip, 1, keepdims=False)]
    for k in range(1, C):
        pairs = [(f, 2 * ((f // 2 + k) % C) + f % 2) for f in range(F)]
        block = lax.dynamic_index_in_dim(stage, (chip + k) % C, 1, keepdims=False)
        got.append(lax.ppermute(block, "fsdp", pairs))
    return got


def at_home(C, got):
    chip = lax.axis_index("fsdp") // 2
    got = jnp.stack(got)
    got = [lax.dynamic_index_in_dim(got, (chip - j + C) % C, 0, keepdims=False) for j in range(C)]
    return jnp.concatenate(got, axis=1)


def from_layer(C, F, x):
    z, chip = lax.axis_index("ctx"), lax.axis_index("fsdp") // 2
    x = x.reshape(C, x.shape[0] // C, x.shape[1])
    got = []
    for k in range(C):
        pairs = [
            ((f // 2) * F + 2 * ((s + k) % C) + f % 2, s * F + f) for s in range(C) for f in range(F)
        ]
        block = lax.dynamic_index_in_dim(x, (chip - k + C) % C, 0, keepdims=False)
        got.append(lax.ppermute(block, BOTH, pairs))
    got = jnp.stack(got)
    got = [lax.dynamic_index_in_dim(got, (j - z + C) % C, 0, keepdims=False) for j in range(C)]
    return jnp.concatenate(got, axis=0)


def shards(C, F, layer_input, cotangent, positions, w_attn, w_ffn, gains, mom_attn, mom_ffn, gain_mom):
    z = lax.axis_index("ctx")
    f = lax.axis_index("fsdp")
    local_rows, width = layer_input.shape[1], layer_input.shape[2]
    seq_total, seq_length = positions.shape
    dz, head_cols = w_attn.shape[1], w_attn.shape[2]
    local_heads = head_cols // HEAD_DIM
    block_count = w_ffn.shape[2]
    per = seq_total // C
    piece = local_rows // C
    chips = F // per
    tokens = F * local_rows
    hidden_cols = block_count * head_cols
    units = UNITS_ATTN + 3 * block_count
    parts = C * F // units

    def after(a, b):
        return lax.optimization_barrier((a, b))[0]

    def rows_gather(shard):
        return lax.all_gather(shard, "ctx", axis=0, tiled=True)

    def product(units, groups, *pairs):
        pairs = [(x.reshape(tokens, width), dy) for x, dy in pairs]
        if kernels:
            return grad_call(pairs, units, head_cols, groups)
        grad = jnp.concatenate([dot(x, dy, 0, 0).astype(bf16) for x, dy in pairs], axis=1)
        return jnp.transpose(grad.reshape(width, groups, units, head_cols), (2, 1, 0, 3))

    def scatter(grad):
        if kernels:
            return lax.psum_scatter(grad, "ctx", scatter_dimension=0, tiled=True)[0]
        return lax.psum_scatter(grad, "ctx", scatter_dimension=2, tiled=True)

    kernels = kernels_fit(C, F)
    w_heads = rows_gather(jnp.concatenate([w_attn[i] for i in range(UNITS_ATTN)], axis=1))
    w_qkv, w_out = (w_heads, w_heads) if kernels else (w_heads[:, : 3 * head_cols], w_heads[:, 3 * head_cols :])
    ffn_flat = w_ffn.reshape(3, dz, hidden_cols)
    w_gate_up = rows_gather(jnp.concatenate([ffn_flat[0], ffn_flat[1]], axis=1))
    w_down = rows_gather(ffn_flat[2])

    gain_query = lax.dynamic_slice_in_dim(gains[0], f * head_cols, head_cols)
    gain_key = lax.dynamic_slice_in_dim(gains[1], f * head_cols, head_cols)
    pos = lax.dynamic_slice_in_dim(positions, z * per, per, 0)
    pos = jnp.transpose(pos.reshape(per, C, chips, piece), (0, 2, 1, 3)).reshape(per, seq_length)
    cosine_table, sine_table = rotary_tables(pos)

    def heads(a):
        return jnp.transpose(
            a.reshape(chips, per, local_rows, local_heads, HEAD_DIM), (1, 0, 2, 3, 4)
        ).reshape(per, seq_length, local_heads, HEAD_DIM)

    def unheads(a):
        return jnp.transpose(
            a.reshape(per, chips, local_rows, local_heads, HEAD_DIM), (1, 0, 2, 3, 4)
        ).reshape(tokens, head_cols)

    if kernels:
        sign = jnp.where(jnp.arange(HEAD_DIM) < HEAD_DIM // 2, -1.0, 1.0)
        tables = (
            gain_query[None],
            gain_key[None],
            jnp.broadcast_to(cosine_table[:, :, 0], (per, seq_length, HEAD_DIM)),
            sine_table[:, :, 0] * sign,
            pos.astype(f32)[:, None, :],
            jnp.broadcast_to(pos.astype(f32)[..., None], (per, seq_length, HEAD_DIM)),
        )
        own_input, input_all = enter_call(C, F, layer_input.reshape(local_rows, width))
        projected, stats = qkv_call(F, input_all, w_qkv)
        attn_mixed, query_rows, key_rows, log_total = attend_call(F, projected, stats, *tables)
        attn_mixed = attn_mixed.reshape(tokens, head_cols)
    else:
        own_input, input_all, projected = project(C, F, layer_input.reshape(local_rows, width), w_qkv)
        query_raw = projected[:, :head_cols]
        key_raw = projected[:, head_cols : 2 * head_cols]
        value_raw = projected[:, 2 * head_cols :]
        query_total, key_total = norm_stats(
            jnp.sum(query_raw * query_raw, axis=-1), jnp.sum(key_raw * key_raw, axis=-1)
        )
        query_scale = lax.rsqrt(query_total / width + epsilon)[..., None]
        key_scale = lax.rsqrt(key_total / width + epsilon)[..., None]
        query_hat = query_raw * query_scale
        key_hat = key_raw * key_scale
        query_rows = (
            rotate(heads(query_hat * gain_query), cosine_table, sine_table) * HEAD_DIM ** (-0.5)
        ).astype(bf16)
        key_rows = rotate(heads(key_hat * gain_key), cosine_table, sine_table).astype(bf16)
        value_rows = heads(value_raw.astype(bf16))
        attn_mixed, log_total = attend(query_rows, key_rows, value_rows, pos)
        attn_mixed = unheads(attn_mixed)
    own_grad, hidden_in, attn_out, mlp_all, act, der, hidden = attn_out_and_up(
        C, F, attn_mixed, w_out, own_input, gains[2:3], w_gate_up,
        cotangent.reshape(local_rows, width),
    )
    by_layer = None
    if kernels:
        by_layer = jnp.concatenate(
            [mom_attn[:, None].astype(bf16), jnp.transpose(mom_ffn.astype(bf16), (2, 0, 1, 3))], axis=1
        )
    result, mlp_gain, grad_mlp_all, grad_ffn_in, mom_own, p_down = down_and_back(
        C, F, hidden, w_down, hidden_in, own_grad, gains[3:4], act, der, by_layer
    )
    if kernels:
        mom_own = jnp.swapaxes(mom_own, 0, 1)
    else:
        p_down = product(block_count, 1, (grad_mlp_all, hidden))
    g_down = scatter(p_down)
    p_gate_up = product(block_count, 2, (mlp_all, grad_ffn_in))
    if kernels:
        grad_ffn_in, p_gate_up = lax.optimization_barrier((grad_ffn_in, p_gate_up))
    g_gate_up = scatter(p_gate_up)
    grad_resid, attn_gain, grad_attn_all, grad_mixed = back_to_attn(
        C, F, grad_ffn_in, w_gate_up, own_grad, attn_out, gains[2:3], w_out
    )
    if kernels:
        grad_mixed = after(grad_mixed, g_down)
        weighted_q, weighted_k, grad_value, inner, gain_cols = attend_back_call(
            F, projected, query_rows, key_rows, grad_mixed, log_total, stats, *tables
        )
        inner = jnp.transpose(
            jnp.sum(inner, axis=1).reshape(per, 8, chips, local_rows), (1, 2, 0, 3)
        ).reshape(8, tokens)
        gain_cols = jnp.sum(gain_cols, axis=0)
        query_gain_cols = gain_cols[:, 0].reshape(head_cols)
        key_gain_cols = gain_cols[:, 1].reshape(head_cols)
        flat = (tokens, head_cols)
        zero = jnp.zeros((width,), f32)
        gain_local = jnp.stack(
            [
                lax.dynamic_update_slice(zero, query_gain_cols, (f * head_cols,)),
                lax.dynamic_update_slice(zero, key_gain_cols, (f * head_cols,)),
                attn_gain[0],
                mlp_gain[0],
                *[zero] * 4,
            ]
        )
        grad_rows, grad_projected, gain_layer = last_call(
            F, weighted_q.reshape(flat), weighted_k.reshape(flat), grad_value.reshape(flat),
            projected, stats, inner, w_qkv, grad_resid, gain_local,
        )
    else:
        grad_query, grad_key, grad_value = attend_back(
            query_rows, key_rows, value_rows, pos, heads(grad_mixed), log_total
        )
        grad_query_norm = unheads(unrotate(grad_query * HEAD_DIM ** (-0.5), cosine_table, sine_table))
        grad_key_norm = unheads(unrotate(grad_key, cosine_table, sine_table))
        query_gain_cols = jnp.sum(grad_query_norm * query_hat, axis=0)
        key_gain_cols = jnp.sum(grad_key_norm * key_hat, axis=0)
        query_weighted = grad_query_norm * gain_query
        key_weighted = grad_key_norm * gain_key
        query_inner, key_inner = norm_stats(
            jnp.sum(query_weighted * query_hat, axis=-1), jnp.sum(key_weighted * key_hat, axis=-1)
        )
        grad_query_raw = query_scale * (query_weighted - query_hat * (query_inner / width)[..., None])
        grad_key_raw = key_scale * (key_weighted - key_hat * (key_inner / width)[..., None])
        grad_projected = jnp.concatenate(
            [grad_query_raw.astype(bf16), grad_key_raw.astype(bf16), unheads(grad_value).astype(bf16)],
            axis=1,
        )
        grad_rows = back_to_input(C, F, grad_projected, w_qkv, grad_resid)
    g_attn = scatter(
        product(UNITS_ATTN, 1, (input_all, grad_projected), (grad_attn_all, attn_mixed))
    )
    if not kernels:
        grad_input = from_layer(C, F, grad_rows)
        result = from_layer(C, F, result)
        zero = jnp.zeros((width,), f32)
        gain_local = jnp.stack(
            [
                lax.dynamic_update_slice(zero, query_gain_cols, (f * head_cols,)),
                lax.dynamic_update_slice(zero, key_gain_cols, (f * head_cols,)),
                attn_gain[0],
                mlp_gain[0],
            ]
        )
        gain_total = jnp.sum(lax.all_gather(gain_local, BOTH, axis=0, tiled=False), axis=0)

    if kernels:
        early = jnp.stack([g_gate_up[0], g_gate_up[1], g_down[0]])
        mom = momentum * mom_own.reshape(UNITS_ATTN, width, head_cols).astype(f32)
        owned = jnp.concatenate([jnp.zeros_like(early[:1]), (mom[1:] + early.astype(f32)).astype(bf16)], axis=0)
        mom_first = mom[0]
        early = jnp.swapaxes(early.reshape(3, C, dz, head_cols), 0, 1)
        early, owned, mom_first, grad_rows = lax.optimization_barrier((early, owned, mom_first, grad_rows))
        late = (mom_first + g_attn[0].astype(f32)).astype(bf16)
        owned = lax.dynamic_update_slice(owned, late[None], (0, 0, 0))
        own, leaving, gain_total, sent_back = newton_call(
            C, owned, result, grad_rows, gain_layer, early, g_attn[0]
        )
        sent_back = sent_back.astype(f32)
        grad_attn = sent_back[:, 0]
        grad_ffn = jnp.transpose(sent_back[:, 1:], (1, 2, 0, 3))
        homing = go_home(C, F, leaving)
        gain_total = gain_total[:4]
    else:
        grad_attn = g_attn[:, 0].astype(f32)
        grad_ffn = jnp.transpose(
            jnp.concatenate([g_gate_up, g_down], axis=1).astype(f32), (1, 2, 0, 3)
        )
    new_attn = momentum * mom_attn + grad_attn
    new_ffn = momentum * mom_ffn + grad_ffn
    if kernels:
        homing, new_attn, new_ffn, grad_attn, grad_ffn = lax.optimization_barrier(
            (homing, new_attn, new_ffn, grad_attn, grad_ffn)
        )
        back_rows = at_home(C, homing)
        result, grad_input = back_rows[0], back_rows[1]
    if not kernels:
        send = jnp.concatenate(
            [
                new_attn.astype(bf16),
                jnp.transpose(new_ffn.astype(bf16), (0, 2, 1, 3)).reshape(3 * block_count, dz, head_cols),
            ],
            axis=0,
        ).reshape(C * F, dz // parts, head_cols)
        own = lax.all_to_all(send, BOTH, split_axis=0, concat_axis=0, tiled=True)
        own = jnp.transpose(own.reshape(C, F, dz // parts, head_cols), (0, 2, 1, 3)).reshape(
            C * dz // parts, F * head_cols
        )

        def peers(a):
            out = [a]
            for s in range(1, parts):
                pairs = [(i, i - i % parts + (i + parts - s) % parts) for i in range(C * F)]
                out.append(lax.ppermute(a, BOTH, pairs))
            return out

        own32 = own.astype(f32)
        square = jnp.sum(own32 * own32)
        total = sum(peers(square.reshape(1, 1)))
        inv = 1.0 / (jnp.sqrt(total) + 1e-07)
        for iteration in range(NS_STEPS):
            factor = inv if iteration == 0 else 1.0
            every = peers(own)
            gram = [(dot(own, b, 1, 1) * (factor * factor)).astype(bf16) for b in every]
            product = sum(dot(g, b, 1, 0) for g, b in zip(gram, every)) * factor
            product_all = peers(product.astype(bf16))
            product_two = sum(dot(g, b, 1, 0) for g, b in zip(gram, product_all))
            own = (
                quintic_one * factor * own.astype(f32) + quintic_two * product + quintic_three * product_two
            ).astype(bf16)
    if kernels:
        home = own
    else:
        home = jnp.transpose(own.reshape(C, dz // parts, F, head_cols), (0, 2, 1, 3)).reshape(
            C * F, dz // parts, head_cols
        )
    steps = lax.all_to_all(home, BOTH, split_axis=0, concat_axis=0, tiled=True)
    if kernels:
        steps = steps.reshape(C, UNITS_ATTN, dz, head_cols)
        arranged = lax.optimization_barrier(jnp.transpose(steps[:, 1:], (1, 2, 0, 3)))
        step_attn = -muon_rate * steps[:, 0].astype(f32)
        step_ffn = -muon_rate * arranged.astype(f32)
    else:
        steps = -muon_rate * steps.astype(f32)
        steps = steps.reshape(units, dz, head_cols)
        step_attn = steps[:UNITS_ATTN]
        step_ffn = jnp.transpose(
            steps[UNITS_ATTN:].reshape(3, block_count, dz, head_cols), (0, 2, 1, 3)
        )
    new_gain_mom = momentum * gain_mom + gain_total
    return (
        result.reshape(layer_input.shape),
        grad_input.astype(f32).reshape(layer_input.shape),
        grad_attn,
        grad_ffn,
        gain_total,
        new_attn,
        new_ffn,
        new_gain_mom,
        step_attn,
        step_ffn,
        -gain_rate * new_gain_mom,
    )


def solution(mesh):
    tokens = P("fsdp", "ctx", None)
    attn = P(None, "ctx", "fsdp")
    ffn = P(None, "ctx", None, "fsdp")
    in_specs = (tokens, tokens, P(), attn, ffn, P(), attn, ffn, P())
    out_specs = (tokens, tokens, attn, ffn, P(), attn, ffn, P(), attn, ffn, P())
    body = functools.partial(shards, mesh.shape["ctx"], mesh.shape["fsdp"])
    return jax.shard_map(body, mesh=mesh, in_specs=in_specs, out_specs=out_specs, check_vma=False)
```
